32 devices in a mesh: seq: 8 (over z, x), grp: 4 (over y, core).
Axes of the slice: x: 2, y: 2, z: 4, core: 2. Of those that a mesh axis runs over, the one named last changes fastest.
Arguments:
- query_vecs: bfloat16 [16384, 1024], P(('seq', 'grp')), may hold values from -6 to 6
- key_vecs: bfloat16 [16384, 1024], P(('seq', 'grp')), may hold values from -6 to 6
- value_vecs: bfloat16 [16384, 1024], P(('seq', 'grp')), may hold values from -6 to 6
Outputs:
- attended: bfloat16 [16384, 1024], P(('seq', 'grp'))
The draws below stay inside these ranges and needn't reach their ends.
All inputs are finite; a program needn't handle non-finite values.
Results may differ from the reference program's by a relative error of at most 0.0033.
Values may be sent and summed in bfloat16 or wider, within the bound.
No kernel may reach another device: no remote copies, remote signals or barrier semaphores. Data moves between devices by JAX's collectives and lax.ppermute only.
A program may use at most 128 MiB of HBM per device.

```python
import math
import jax
import jax.numpy as jnp
from jax import lax

HEADS = 8
HEAD_DIM = 128
BLK = 256
LEV = 4
TOKENS = 16384


def smooth_part(key, col_count):
    periods = jax.random.randint(jax.random.fold_in(key, 1), (col_count,), 4 * BLK, 64 * BLK)
    shifts = jax.random.randint(jax.random.fold_in(key, 2), (col_count,), 0, 64 * BLK)
    amplitude = jax.random.uniform(jax.random.fold_in(key, 3), (col_count,), jnp.float32, 0.5, 1.0)
    places = jnp.arange(TOKENS, dtype=jnp.int32)[:, None]
    phase = ((places + shifts[None, :]) % periods[None, :]).astype(jnp.float32) / periods[None, :].astype(jnp.float32)
    return amplitude[None, :] * jnp.sin(2.0 * math.pi * phase)


def rough_part(key, col_count):
    return jax.random.normal(key, (TOKENS, col_count), jnp.float32)


def draw_query_vecs(key, part):
    col_count = HEADS * HEAD_DIM
    base = jax.random.fold_in(key, 101)
    mixed = 0.8 * rough_part(jax.random.fold_in(base, 0), col_count) + 0.6 * smooth_part(jax.random.fold_in(base, 5), col_count)
    return jnp.clip(mixed, -6.0, 6.0).astype(jnp.bfloat16)


def draw_key_vecs(key, part):
    col_count = HEADS * HEAD_DIM
    base = jax.random.fold_in(key, 202)
    mixed = 0.8 * rough_part(jax.random.fold_in(base, 0), col_count) + 0.6 * smooth_part(jax.random.fold_in(base, 5), col_count)
    return jnp.clip(mixed, -6.0, 6.0).astype(jnp.bfloat16)


def draw_value_vecs(key, part):
    col_count = HEADS * HEAD_DIM
    base = jax.random.fold_in(key, 303)
    mixed = rough_part(jax.random.fold_in(base, 0), col_count) + 0.8 * smooth_part(jax.random.fold_in(base, 5), col_count)
    return jnp.clip(mixed, -6.0, 6.0).astype(jnp.bfloat16)


def setup_inputs(seed: int = 0) -> dict:
    key_of = jax.random.split(jax.random.key(seed), 4)
    return {
        "query_vecs": draw_query_vecs(jax.random.fold_in(key_of[3], 71), 0),
        "key_vecs": draw_key_vecs(jax.random.fold_in(key_of[3], 71), 0),
        "value_vecs": draw_value_vecs(jax.random.fold_in(key_of[3], 71), 0),
    }


very_negative = -1e+30

def coarsen_rows(rows_in, factor):
    row_count, col_count = rows_in.shape
    paired = rows_in.reshape(row_count // 2, 2, col_count).astype(jnp.float32)
    return lax.optimization_barrier(((paired[:, 0] + paired[:, 1]) * factor).astype(jnp.bfloat16))

def attend_level(queries, keys_pad, values_pad, height, head_size, first_block, block_total, block_rows):
    row_count, col_count = queries.shape
    head_count = col_count // head_size
    block_count = row_count // block_rows
    group_size = min(block_count, max(1, 512 // block_rows))
    step_count = block_count // group_size
    if height == 0:
        offsets = (0, 1, 2)
    else:
        offsets = (0, 2)
    window = len(offsets) * block_rows
    score_scale = 1.0 / math.sqrt(head_size)
    query_place = jnp.arange(block_rows, dtype=jnp.int32)
    key_place = jnp.arange(window, dtype=jnp.int32)
    key_side = key_place // block_rows
    key_upper = key_place % block_rows >= block_rows // 2
    query_upper = query_place >= block_rows // 2
    below = jnp.logical_and(jnp.logical_not(query_upper)[:, None], key_upper[None, :])
    above = jnp.logical_and(query_upper[:, None], jnp.logical_not(key_upper)[None, :])
    excluded = jnp.where(key_side[None, :] == 0, below, above)
    if height == 0:
        excluded = jnp.zeros_like(excluded)
    shifts = jnp.array([offset - 1 for offset in offsets], dtype=jnp.int32)
    other_shift = jnp.repeat(shifts, block_rows)

    def one_group(group_index):
        start = group_index * group_size * block_rows
        query_blk = lax.dynamic_slice_in_dim(queries, start, group_size * block_rows, 0).reshape(group_size, block_rows, head_count, head_size)
        key_blk = lax.dynamic_slice_in_dim(keys_pad, start, (group_size + 2) * block_rows, 0).reshape(group_size + 2, block_rows, head_count, head_size)
        value_blk = lax.dynamic_slice_in_dim(values_pad, start, (group_size + 2) * block_rows, 0).reshape(group_size + 2, block_rows, head_count, head_size)
        key_win = jnp.concatenate([key_blk[offset:offset + group_size] for offset in offsets], axis=1)
        value_win = jnp.concatenate([value_blk[offset:offset + group_size] for offset in offsets], axis=1)
        scores = jnp.einsum('gqhd,gkhd->ghqk', query_blk.astype(jnp.float32), key_win.astype(jnp.float32)) * score_scale
        own_block = first_block + group_index * group_size + jnp.arange(group_size, dtype=jnp.int32)
        other_block = own_block[:, None] + other_shift[None, :]
        present = jnp.logical_and(other_block >= 0, other_block < block_total)
        allowed = jnp.logical_and(present[:, None, None, :], jnp.logical_not(excluded)[None, None, :, :])
        masked = jnp.where(allowed, scores, very_negative)
        row_max = lax.optimization_barrier(jnp.max(masked, axis=-1))
        weights = jnp.where(allowed, jnp.exp(masked - row_max[..., None]), 0.0)
        row_total = lax.optimization_barrier(jnp.sum(weights, axis=-1)) * 2.0 ** height
        weights_bf = lax.optimization_barrier(weights.astype(jnp.bfloat16))
        weighted = jnp.einsum('ghqk,gkhd->gqhd', weights_bf.astype(jnp.float32), value_win.astype(jnp.float32))
        return (jnp.transpose(row_max, (0, 2, 1)).reshape(group_size * block_rows, head_count), weighted.reshape(group_size * block_rows, col_count), jnp.transpose(row_total, (0, 2, 1)).reshape(group_size * block_rows, head_count))
    row_max, weighted, row_total = lax.map(one_group, jnp.arange(step_count, dtype=jnp.int32))
    return (row_max.reshape(row_count, head_count), weighted.reshape(row_count, col_count), row_total.reshape(row_count, head_count))

def merge_stats(finer, coarser):
    fine_max, fine_sum, fine_total = finer
    coarse_max, coarse_sum, coarse_total = coarser
    row_count, col_count = fine_sum.shape
    head_count = fine_max.shape[1]
    both_max = jnp.maximum(fine_max, coarse_max)
    fine_factor = jnp.exp(fine_max - both_max)
    coarse_factor = jnp.exp(coarse_max - both_max)
    merged = fine_sum.reshape(row_count, head_count, -1) * fine_factor[..., None] + coarse_sum.reshape(row_count, head_count, -1) * coarse_factor[..., None]
    return (both_max, merged.reshape(row_count, col_count), fine_total * fine_factor + coarse_total * coarse_factor)

def widen_stats(stats):
    return tuple((jnp.repeat(member, 2, axis=0) for member in stats))

def finish_output(stats):
    row_max, weighted, row_total = stats
    row_count, col_count = weighted.shape
    head_count = row_total.shape[1]
    return (weighted.reshape(row_count, head_count, -1) / row_total[..., None]).reshape(row_count, col_count).astype(jnp.bfloat16)

def reference(query_vecs, key_vecs, value_vecs):
    col_count = query_vecs.shape[1]
    query_rows, key_rows, value_rows = (query_vecs, key_vecs, value_vecs)
    all_stats = []
    for height in range(LEV):
        if height > 0:
            query_rows = coarsen_rows(query_rows, 0.5)
            key_rows = coarsen_rows(key_rows, 0.5)
            value_rows = coarsen_rows(value_rows, 1.0)
        block_count = query_rows.shape[0] // BLK
        border = jnp.zeros((BLK, col_count), key_rows.dtype)
        key_pad = jnp.concatenate([border, key_rows, border], axis=0)
        value_pad = jnp.concatenate([border, value_rows, border], axis=0)
        all_stats.append(attend_level(query_rows, key_pad, value_pad, height, HEAD_DIM, 0, block_count, BLK))
    running = all_stats[-1]
    for height in range(LEV - 2, -1, -1):
        running = merge_stats(all_stats[height], widen_stats(running))
    return finish_output(running)
```

```python
import math

import jax
import jax.numpy as jnp
from jax import lax
from jax.experimental import pallas as pl
from jax.experimental.pallas import tpu as pltpu
from jax.sharding import PartitionSpec as P

HEADS = 8
HEAD_DIM = 128
BLK = 256
HALF = BLK // 2
SUB = BLK // 8
LEV = 4
EXP_SCALE = math.log2(math.e) / math.sqrt(HEAD_DIM)

very_negative = -1e30
f32 = jnp.float32
bf16 = jnp.bfloat16


def iota(shape, dim):
    return lax.broadcasted_iota(jnp.int32, shape, dim)


def bit(value, place):
    return jnp.bitwise_and(lax.shift_right_logical(value, place), 1)


def low_bits(value):
    step = SUB.bit_length() - 1
    deep = jnp.bitwise_and(value, SUB - 1)
    return 8 * deep + 4 * bit(value, step) + 2 * bit(value, step + 1) + bit(value, step + 2)


def reorder_matrix():
    return (iota((BLK, BLK), 1) == low_bits(iota((BLK, BLK), 0))).astype(bf16)


def restore_matrix():
    return (iota((BLK, BLK), 0) == low_bits(iota((BLK, BLK), 1))).astype(bf16)


def pair_matrix():
    first = low_bits(iota((HALF, BLK), 0))
    place = iota((HALF, BLK), 1)
    return jnp.logical_or(place == first, place == first + 1).astype(bf16)


def mul(left, right):
    return jnp.dot(left, right, preferred_element_type=f32)


def fold(rows, factor):
    half = rows.shape[0] // 2
    total = rows[:half].astype(f32) + rows[half:].astype(f32)
    if factor != 1.0:
        total = total * factor
    return total.astype(bf16)


def fold_chunks(rows, chunk, factor):
    count = rows.shape[0] // chunk
    return jnp.concatenate([fold(rows[i * chunk : (i + 1) * chunk], factor) for i in range(count)], axis=0)


def with_ones(values):
    return jnp.concatenate([values, jnp.ones_like(values)], axis=1)


def attend(query, keys, values, bias=None):
    scores = lax.dot_general(query, keys, (((1,), (1,)), ((), ())), preferred_element_type=f32)
    if bias is not None:
        scores = scores + bias
    top = jnp.max(scores, axis=1, keepdims=True)
    weights = jnp.exp2((scores - top) * EXP_SCALE).astype(bf16)
    return top * EXP_SCALE, mul(weights, with_ones(values))


def twice(rows):
    return jnp.concatenate([rows, rows], axis=0)


def cols(head):
    return slice(head * HEAD_DIM, (head + 1) * HEAD_DIM)


def prepare_body(q_ref, k_ref, v_ref, q0_ref, q1_ref, right_ref, left_ref, swap_ref):
    reorder = reorder_matrix()
    pair = pair_matrix()
    q2, k2, v2 = [], [], []
    for i in range(2):
        rows = slice(i * BLK, (i + 1) * BLK)
        coarse = slice(i * HALF, (i + 1) * HALF)
        q0 = mul(reorder, q_ref[rows, :]).astype(bf16)
        q1 = fold(q0, 0.5)
        q0_ref[rows, :] = q0
        q1_ref[coarse, :] = q1
        q2.append(fold(q1, 0.5))
        k1 = (mul(pair, k_ref[rows, :]) * 0.5).astype(bf16)
        v1 = mul(pair, v_ref[rows, :]).astype(bf16)
        k2.append(fold(k1, 0.5))
        v2.append(fold(v1, 1.0))
        near_ref = left_ref if i == 0 else right_ref
        far_ref = right_ref if i == 0 else left_ref
        near_ref[0:BLK, :] = k_ref[rows, :]
        near_ref[BLK : 2 * BLK, :] = v_ref[rows, :]
        far_ref[2 * BLK : 2 * BLK + HALF, :] = k1
        far_ref[2 * BLK + HALF : 3 * BLK, :] = v1
    for place, parts in enumerate((q2, k2, v2)):
        swap_ref[0, place * HALF : (place + 1) * HALF, :] = jnp.concatenate(parts, axis=0)


def prepare(query_vecs, key_vecs, value_vecs, groups):
    rows, width = query_vecs.shape
    part = width // groups
    block = lambda n: pl.BlockSpec((n, part), lambda g: (0, g))
    shape = lambda n: jax.ShapeDtypeStruct((n, width), bf16)
    return pl.pallas_call(
        prepare_body,
        grid=(groups,),
        in_specs=[block(rows)] * 3,
        out_specs=[
            block(rows),
            block(rows // 2),
            block(3 * BLK),
            block(3 * BLK),
            pl.BlockSpec((1, 3 * HALF, part), lambda g: (g, 0, 0)),
        ],
        out_shape=[
            shape(rows),
            shape(rows // 2),
            shape(3 * BLK),
            shape(3 * BLK),
            jax.ShapeDtypeStruct((groups, 3 * HALF, part), bf16),
        ],
        compiler_params=pltpu.CompilerParams(vmem_limit_bytes=32 << 20),
        cost_estimate=pl.CostEstimate(flops=8 * rows * BLK * width, bytes_accessed=16 * rows * width, transcendentals=0),
        name="prepare",
    )(query_vecs, key_vecs, value_vecs)


def own_body(q_ref, k_ref, v_ref, sum_ref, stat_ref):
    heads = q_ref.shape[1] // HEAD_DIM
    lane = iota((BLK, HEAD_DIM), 1)
    for i in range(2):
        rows = slice(i * BLK, (i + 1) * BLK)
        stat = jnp.zeros((BLK, HEAD_DIM), f32)
        for head in range(heads):
            top, sums = attend(q_ref[rows, cols(head)], k_ref[:, cols(head)], v_ref[:, cols(head)])
            sum_ref[rows, cols(head)] = sums[:, :HEAD_DIM]
            stat = jnp.where(lane == 2 * head, top, stat)
            stat = jnp.where(lane == 2 * head + 1, sums[:, HEAD_DIM:], stat)
        stat_ref[rows, :] = stat


def own_level(q0, key_vecs, value_vecs, groups):
    rows, width = q0.shape
    part = width // groups
    block = lambda n, w: pl.BlockSpec((n, w), lambda g: (0, g))
    return pl.pallas_call(
        own_body,
        grid=(groups,),
        in_specs=[block(rows, part)] * 3,
        out_specs=[block(rows, part), block(rows, HEAD_DIM)],
        out_shape=[
            jax.ShapeDtypeStruct((rows, width), f32),
            jax.ShapeDtypeStruct((rows, groups * HEAD_DIM), f32),
        ],
        compiler_params=pltpu.CompilerParams(vmem_limit_bytes=32 << 20),
        cost_estimate=pl.CostEstimate(
            flops=8 * rows * rows * width, bytes_accessed=12 * rows * width, transcendentals=rows * rows * HEADS
        ),
        name="own_level",
    )(q0, key_vecs, value_vecs)


def halo_body(got_ref, right_ref, left_ref):
    count = got_ref.shape[0]
    pair = count // 2
    for which, factor in ((1, 0.5), (2, 1.0)):
        rows = slice(which * HALF, (which + 1) * HALF)
        near = (which - 1) * BLK
        far = 2 * BLK + (which - 1) * HALF
        for j in range(count):
            level2 = got_ref[j, rows, :]
            level3 = fold_chunks(level2, HALF // 2, factor)
            near_ref, far_ref = (left_ref, right_ref) if j < pair else (right_ref, left_ref)
            spot = j % pair
            near_ref[near + spot * HALF : near + (spot + 1) * HALF, :] = level2
            far_ref[far + spot * HALF // 2 : far + (spot + 1) * HALF // 2, :] = level3


def coarse_halos(got):
    shape = jax.ShapeDtypeStruct((3 * BLK, got.shape[2]), bf16)
    return pl.pallas_call(
        halo_body,
        out_shape=[shape, shape],
        compiler_params=pltpu.CompilerParams(vmem_limit_bytes=32 << 20),
        cost_estimate=pl.CostEstimate(flops=1 << 20, bytes_accessed=6 * got.size, transcendentals=0),
        name="coarse_halos",
    )(got)


def coarse_body(bias_ref, got_ref, prev_ref, next_ref, back_ref):
    count = got_ref.shape[0]
    heads = got_ref.shape[2] // HEAD_DIM
    bias_prev = bias_ref[0]
    bias_next = bias_ref[1]
    key_place = iota((1, 3 * HALF), 1)
    first_is_prev = jnp.where(key_place < HALF, bias_prev, 0.0)
    two_are_prev = jnp.where(key_place < 2 * HALF, bias_prev, 0.0)
    two_are_next = jnp.where(key_place < HALF, 0.0, bias_next)
    last_is_next = jnp.where(key_place < 2 * HALF, 0.0, bias_next)
    third_prev = jnp.where(key_place < HALF, bias_prev, bias_next)
    third_next = jnp.where(key_place < 2 * HALF, bias_prev, bias_next)
    lane = iota((HALF, HEAD_DIM), 1)
    stats = [jnp.zeros((HALF, HEAD_DIM), f32) for _ in range(count)]
    for head in range(heads):
        here = cols(head)

        def own(which, j):
            return got_ref[j, which * HALF : (which + 1) * HALF, here]

        def near(ref, which, spot):
            first = (which - 1) * BLK + spot * HALF
            return ref[first : first + HALF, here]

        def far(ref, which):
            first = 2 * BLK + (which - 1) * HALF
            return ref[first : first + HALF, here]

        def near3(ref, which):
            first = (which - 1) * BLK
            return fold_chunks(ref[first : first + BLK, here], HALF // 2, 0.5 if which == 1 else 1.0)

        level2 = []
        sources = (
            (first_is_prev, lambda w: (near(prev_ref, w, 0), own(w, 2), own(w, 3))),
            (two_are_prev, lambda w: (near(prev_ref, w, 0), near(prev_ref, w, 1), own(w, 3))),
            (two_are_next, lambda w: (own(w, 0), near(next_ref, w, 0), near(next_ref, w, 1))),
            (last_is_next, lambda w: (own(w, 0), own(w, 1), near(next_ref, w, 1))),
        )
        for j, (bias, pick) in enumerate(sources):
            keys = jnp.concatenate(pick(1), axis=0)
            values = jnp.concatenate(pick(2), axis=0)
            level2.append(attend(own(0, j), keys, values, bias))
        level3 = []
        coarser = (
            (third_prev, lambda w: (far(prev_ref, w), near3(next_ref, w), far(next_ref, w))),
            (third_next, lambda w: (far(prev_ref, w), near3(prev_ref, w), far(next_ref, w))),
        )
        for j, (bias, pick) in enumerate(coarser):
            keys = jnp.concatenate(pick(1), axis=0)
            values = jnp.concatenate(pick(2), axis=0)
            query = jnp.concatenate([fold_chunks(own(0, 2 * j + n), HALF // 2, 0.5) for n in range(2)], axis=0)
            level3.append(attend(query, keys, values, bias))
        for j in range(count):
            top2, sum2 = level2[j]
            top3, sum3 = level3[j // 2]

            def spread(rows):
                first = (j % 2) * 2 * SUB
                one = rows[first : first + SUB]
                other = rows[first + SUB : first + 2 * SUB]
                return jnp.concatenate([one, one, other, other], axis=0)

            top3 = spread(top3)
            sum3 = spread(sum3)
            top = jnp.maximum(top2, top3)
            sums = sum2 * (4.0 * jnp.exp2(top2 - top)) + sum3 * (8.0 * jnp.exp2(top3 - top))
            values = sum2[:, :HEAD_DIM] * jnp.exp2(top2 - top) + sum3[:, :HEAD_DIM] * jnp.exp2(top3 - top)
            total = sums[:, HEAD_DIM:]
            back_ref[j, 0:HALF, here] = (values / total).astype(bf16)
            level = top + jnp.log2(total)
            high = level.astype(bf16).astype(f32)
            middle = (level - high).astype(bf16).astype(f32)
            low = level - high - middle
            for n, term in enumerate((high, middle, low)):
                stats[j] = jnp.where(lane == 3 * head + n, term, stats[j])
    for j in range(count):
        turned = stats[j].T[0:16, :].astype(bf16)
        back_ref[j, HALF : HALF + 16, 0:HEAD_DIM] = turned
        back_ref[j, HALF : HALF + 16, HEAD_DIM:] = jnp.zeros((16, back_ref.shape[2] - HEAD_DIM), bf16)


def coarse_levels(bias, got, from_prev, from_next):
    count, _, width = got.shape
    vmem = pl.BlockSpec(memory_space=pltpu.VMEM)
    return pl.pallas_call(
        coarse_body,
        in_specs=[pl.BlockSpec(memory_space=pltpu.SMEM), vmem, vmem, vmem],
        out_specs=vmem,
        out_shape=jax.ShapeDtypeStruct((count, HALF + 16, width), bf16),
        compiler_params=pltpu.CompilerParams(vmem_limit_bytes=32 << 20),
        cost_estimate=pl.CostEstimate(flops=1 << 29, bytes_accessed=8 * got.size, transcendentals=1 << 20),
        name="coarse_levels",
    )(bias, got, from_prev, from_next)


def finish_body(bias_ref, q0_ref, q1_ref, prev_ref, next_ref, sum_ref, stat_ref, back_ref, out_ref):
    heads = q0_ref.shape[1] // HEAD_DIM
    bias_prev = bias_ref[0]
    bias_next = bias_ref[1]
    key_place = iota((1, 3 * HALF), 1)
    one_prev = jnp.where(key_place < HALF, bias_prev, bias_next)
    two_prev = jnp.where(key_place < 2 * HALF, bias_prev, bias_next)
    pair = pair_matrix()
    restore = restore_matrix()
    near_keys = [(mul(pair, ref[0:BLK, :]) * 0.5).astype(bf16) for ref in (prev_ref, next_ref)]
    near_values = [mul(pair, ref[BLK : 2 * BLK, :]).astype(bf16) for ref in (prev_ref, next_ref)]
    packed = back_ref[0, HALF : HALF + 16, 0:HEAD_DIM].astype(f32)
    packed = jnp.concatenate([packed, jnp.zeros((HEAD_DIM - 16, HEAD_DIM), f32)], axis=0).T
    far_keys = slice(2 * BLK, 2 * BLK + HALF)
    far_values = slice(2 * BLK + HALF, 3 * BLK)
    for i in range(2):
        rows = slice(i * BLK, (i + 1) * BLK)
        side_ref, side_bias = (prev_ref, bias_prev) if i == 0 else (next_ref, bias_next)
        results = []
        for head in range(heads):
            here = cols(head)
            side_top, side_sum = attend(q0_ref[rows, here], side_ref[0:BLK, here], side_ref[BLK : 2 * BLK, here])
            side_top = side_top + side_bias
            middle = 1 - i
            keys = jnp.concatenate(
                [prev_ref[far_keys, here], near_keys[middle][:, here], next_ref[far_keys, here]], axis=0
            )
            values = jnp.concatenate(
                [prev_ref[far_values, here], near_values[middle][:, here], next_ref[far_values, here]], axis=0
            )
            top1, sum1 = attend(
                q1_ref[i * HALF : (i + 1) * HALF, here], keys, values, one_prev if i == 0 else two_prev
            )
            spot = slice(i * HALF // 2, (i + 1) * HALF // 2)
            level = packed[spot, 3 * head : 3 * head + 1]
            level = level + packed[spot, 3 * head + 1 : 3 * head + 2]
            level = twice(level + packed[spot, 3 * head + 2 : 3 * head + 3])
            deep = twice(back_ref[0, spot, here].astype(f32))
            top = jnp.maximum(top1, level)
            scale1 = jnp.exp2(top1 - top)
            scale2 = jnp.exp2(level - top)
            number = twice(sum1[:, :HEAD_DIM] * scale1 + deep * scale2)
            total = twice(sum1[:, HEAD_DIM:] * (2.0 * scale1) + scale2)
            top = twice(top)
            own_top = stat_ref[rows, 2 * head : 2 * head + 1]
            own_total = stat_ref[rows, 2 * head + 1 : 2 * head + 2]
            most = jnp.maximum(jnp.maximum(top, own_top), side_top)
            scale = jnp.exp2(top - most)
            own_scale = jnp.exp2(own_top - most)
            side_scale = jnp.exp2(side_top - most)
            number = number * scale + sum_ref[rows, here] * own_scale + side_sum[:, :HEAD_DIM] * side_scale
            total = total * scale + own_total * own_scale + side_sum[:, HEAD_DIM:] * side_scale
            results.append((number / total).astype(bf16))
        out_ref[rows, :] = mul(restore, jnp.concatenate(results, axis=1)).astype(bf16)


def finish(bias, q0, q1, from_prev, from_next, own_sum, own_stat, back):
    groups, back_rows, part = back.shape
    rows, width = q0.shape
    block = lambda n, w: pl.BlockSpec((n, w), lambda g: (0, g))
    return pl.pallas_call(
        finish_body,
        grid=(groups,),
        in_specs=[
            pl.BlockSpec(memory_space=pltpu.SMEM),
            block(rows, part),
            block(rows // 2, part),
            block(3 * BLK, part),
            block(3 * BLK, part),
            block(rows, part),
            block(rows, HEAD_DIM),
            pl.BlockSpec((1, back_rows, part), lambda g: (g, 0, 0)),
        ],
        out_specs=block(rows, part),
        out_shape=jax.ShapeDtypeStruct((rows, width), bf16),
        compiler_params=pltpu.CompilerParams(vmem_limit_bytes=32 << 20),
        cost_estimate=pl.CostEstimate(flops=1 << 30, bytes_accessed=24 * rows * width, transcendentals=1 << 21),
        name="finish",
    )(bias, q0, q1, from_prev, from_next, own_sum, own_stat, back)


def shift(value, axis, steps):
    count = lax.axis_size(axis)
    first, last = (max(0, -steps), min(count, count - steps))
    return lax.ppermute(value, axis, [(source, source + steps) for source in range(first, last)])


def edge_bias(axis):
    place = lax.axis_index(axis)
    last = lax.axis_size(axis) - 1
    at_edge = jnp.stack([place == 0, place == last])
    return jnp.where(at_edge, very_negative, 0.0).astype(f32)


def local(query_vecs, key_vecs, value_vecs):
    groups = lax.axis_size("grp")
    assert query_vecs.shape == (2 * BLK, HEADS * HEAD_DIM) and groups == 4
    everyone = ("seq", "grp")
    q0, q1, to_next, to_prev, swap = prepare(query_vecs, key_vecs, value_vecs, groups)
    got = lax.all_to_all(swap, "grp", split_axis=0, concat_axis=0, tiled=True)
    from_prev = shift(to_next, everyone, 1)
    from_next = shift(to_prev, everyone, -1)
    own_sum, own_stat = own_level(q0, key_vecs, value_vecs, groups)
    coarse_right, coarse_left = coarse_halos(got)
    coarse_prev = shift(coarse_right, "seq", 1)
    coarse_next = shift(coarse_left, "seq", -1)
    back = coarse_levels(edge_bias("seq"), got, coarse_prev, coarse_next)
    back = lax.all_to_all(back, "grp", split_axis=0, concat_axis=0, tiled=True)
    return finish(edge_bias(everyone), q0, q1, from_prev, from_next, own_sum, own_stat, back)


def solution(mesh):
    return jax.shard_map(
        local,
        mesh=mesh,
        in_specs=(P(("seq", "grp"), None), P(("seq", "grp"), None), P(("seq", "grp"), None)),
        out_specs=P(("seq", "grp"), None),
        check_vma=False,
    )
```

```python
import math

import jax
import jax.numpy as jnp
from jax import lax
from jax.experimental import pallas as pl
from jax.experimental.pallas import tpu as pltpu
from jax.sharding import PartitionSpec as P

HEADS = 8
HEAD_DIM = 128
BLK = 256
HALF = BLK // 2
SUB = BLK // 8
LEV = 4
EXP_SCALE = math.log2(math.e) / math.sqrt(HEAD_DIM)

VMEM_GRANT = 24 << 20

very_negative = -1e30
f32 = jnp.float32
bf16 = jnp.bfloat16


def iota(shape, dim):
    return lax.broadcasted_iota(jnp.int32, shape, dim)


def bit(value, place):
    return jnp.bitwise_and(lax.shift_right_logical(value, place), 1)


def low_bits(value):
    step = SUB.bit_length() - 1
    deep = jnp.bitwise_and(value, SUB - 1)
    return 8 * deep + 4 * bit(value, step) + 2 * bit(value, step + 1) + bit(value, step + 2)


def reorder_matrix():
    return (iota((BLK, BLK), 1) == low_bits(iota((BLK, BLK), 0))).astype(bf16)


def restore_matrix():
    return (iota((BLK, BLK), 0) == low_bits(iota((BLK, BLK), 1))).astype(bf16)


def pair_matrix():
    first = low_bits(iota((HALF, BLK), 0))
    place = iota((HALF, BLK), 1)
    return jnp.logical_or(place == first, place == first + 1).astype(bf16)


def mul(left, right):
    return jnp.dot(left, right, preferred_element_type=f32)


def fold(rows, factor):
    half = rows.shape[0] // 2
    total = rows[:half].astype(f32) + rows[half:].astype(f32)
    if factor != 1.0:
        total = total * factor
    return total.astype(bf16)


def fold_chunks(rows, chunk, factor):
    count = rows.shape[0] // chunk
    return jnp.concatenate([fold(rows[i * chunk : (i + 1) * chunk], factor) for i in range(count)], axis=0)


def with_ones(values):
    return jnp.concatenate([values, jnp.ones_like(values)], axis=1)


def attend(units):
    scores = []
    for query, keys, _, bias in units:
        raw = lax.dot_general(query, keys, (((1,), (1,)), ((), ())), preferred_element_type=f32)
        scores.append(raw if bias is None else raw + bias)
    tops = [jnp.max(raw, axis=1, keepdims=True) for raw in scores]
    weights = [jnp.exp2((raw - top) * EXP_SCALE).astype(bf16) for raw, top in zip(scores, tops)]
    sums = [mul(share, with_ones(unit[2])) for share, unit in zip(weights, units)]
    return [(top * EXP_SCALE, total) for top, total in zip(tops, sums)]


def twice(rows):
    return jnp.concatenate([rows, rows], axis=0)


def cols(head):
    return slice(head * HEAD_DIM, (head + 1) * HEAD_DIM)


def prepare_body(q_ref, k_ref, v_ref, q0_ref, q1_ref, near_right, near_left, far_right, far_left, swap_ref):
    reorder = reorder_matrix()
    pair = pair_matrix()
    q2, k2, v2 = [], [], []
    for i in range(2):
        rows = slice(i * BLK, (i + 1) * BLK)
        coarse = slice(i * HALF, (i + 1) * HALF)
        q0 = mul(reorder, q_ref[rows, :]).astype(bf16)
        q1 = fold(q0, 0.5)
        q0_ref[rows, :] = q0
        q1_ref[coarse, :] = q1
        q2.append(fold(q1, 0.5))
        k1 = (mul(pair, k_ref[rows, :]) * 0.5).astype(bf16)
        v1 = mul(pair, v_ref[rows, :]).astype(bf16)
        k2.append(fold(k1, 0.5))
        v2.append(fold(v1, 1.0))
        near_ref = near_left if i == 0 else near_right
        far_ref = far_right if i == 0 else far_left
        near_ref[0:BLK, :] = k_ref[rows, :]
        near_ref[BLK : 2 * BLK, :] = v_ref[rows, :]
        far_ref[0:HALF, :] = k1
        far_ref[HALF:BLK, :] = v1
    for place, parts in enumerate((q2, k2, v2)):
        swap_ref[0, place * HALF : (place + 1) * HALF, :] = jnp.concatenate(parts, axis=0)


def prepare(query_vecs, key_vecs, value_vecs, groups):
    rows, width = query_vecs.shape
    part = width // groups
    block = lambda n: pl.BlockSpec((n, part), lambda g: (0, g))
    shape = lambda n: jax.ShapeDtypeStruct((n, width), bf16)
    tall = (rows, rows // 2, 2 * BLK, 2 * BLK, BLK, BLK)
    return pl.pallas_call(
        prepare_body,
        grid=(groups,),
        in_specs=[block(rows)] * 3,
        out_specs=[block(n) for n in tall] + [pl.BlockSpec((1, 3 * HALF, part), lambda g: (g, 0, 0))],
        out_shape=[shape(n) for n in tall] + [jax.ShapeDtypeStruct((groups, 3 * HALF, part), bf16)],
        compiler_params=pltpu.CompilerParams(vmem_limit_bytes=60 << 20),
        cost_estimate=pl.CostEstimate(flops=8 * rows * BLK * width, bytes_accessed=16 * rows * width, transcendentals=0),
        name="prepare",
    )(query_vecs, key_vecs, value_vecs)


def own_body(q_ref, k_ref, v_ref, sum_ref, stat_ref):
    heads = q_ref.shape[1] // HEAD_DIM
    lane = iota((BLK, HEAD_DIM), 1)
    for i in range(2):
        rows = slice(i * BLK, (i + 1) * BLK)
        stat = jnp.zeros((BLK, HEAD_DIM), f32)
        units = [(q_ref[rows, cols(head)], k_ref[:, cols(head)], v_ref[:, cols(head)], None) for head in range(heads)]
        for head, (top, sums) in enumerate(attend(units)):
            sum_ref[rows, cols(head)] = sums[:, :HEAD_DIM]
            stat = jnp.where(lane == 2 * head, top, stat)
            stat = jnp.where(lane == 2 * head + 1, sums[:, HEAD_DIM:], stat)
        stat_ref[rows, :] = stat


def own_level(q0, key_vecs, value_vecs, groups):
    rows, width = q0.shape
    part = width // groups
    block = lambda n, w: pl.BlockSpec((n, w), lambda g: (0, g))
    return pl.pallas_call(
        own_body,
        grid=(groups,),
        in_specs=[block(rows, part)] * 3,
        out_specs=[block(rows, part), block(rows, HEAD_DIM)],
        out_shape=[
            jax.ShapeDtypeStruct((rows, width), f32),
            jax.ShapeDtypeStruct((rows, groups * HEAD_DIM), f32),
        ],
        compiler_params=pltpu.CompilerParams(vmem_limit_bytes=VMEM_GRANT),
        cost_estimate=pl.CostEstimate(
            flops=8 * rows * rows * width, bytes_accessed=12 * rows * width, transcendentals=rows * rows * HEADS
        ),
        name="own_level",
    )(q0, key_vecs, value_vecs)


def halo_body(got_ref, right_ref, left_ref):
    count = got_ref.shape[0]
    pair = count // 2
    for which, factor in ((1, 0.5), (2, 1.0)):
        rows = slice(which * HALF, (which + 1) * HALF)
        near = (which - 1) * BLK
        far = 2 * BLK + (which - 1) * HALF
        for j in range(count):
            level2 = got_ref[j, rows, :]
            level3 = fold_chunks(level2, HALF // 2, factor)
            near_ref, far_ref = (left_ref, right_ref) if j < pair else (right_ref, left_ref)
            spot = j % pair
            near_ref[near + spot * HALF : near + (spot + 1) * HALF, :] = level2
            far_ref[far + spot * HALF // 2 : far + (spot + 1) * HALF // 2, :] = level3


def coarse_halos(got):
    shape = jax.ShapeDtypeStruct((3 * BLK, got.shape[2]), bf16)
    return pl.pallas_call(
        halo_body,
        out_shape=[shape, shape],
        compiler_params=pltpu.CompilerParams(vmem_limit_bytes=VMEM_GRANT),
        cost_estimate=pl.CostEstimate(flops=1 << 20, bytes_accessed=6 * got.size, transcendentals=0),
        name="coarse_halos",
    )(got)


def coarse_body(bias_ref, got_ref, prev_ref, next_ref, back_ref):
    count = got_ref.shape[0]
    heads = got_ref.shape[2] // HEAD_DIM
    bias_prev = bias_ref[0]
    bias_next = bias_ref[1]
    key_place = iota((1, 3 * HALF), 1)
    first_is_prev = jnp.where(key_place < HALF, bias_prev, 0.0)
    two_are_prev = jnp.where(key_place < 2 * HALF, bias_prev, 0.0)
    two_are_next = jnp.where(key_place < HALF, 0.0, bias_next)
    last_is_next = jnp.where(key_place < 2 * HALF, 0.0, bias_next)
    third_prev = jnp.where(key_place < HALF, bias_prev, bias_next)
    third_next = jnp.where(key_place < 2 * HALF, bias_prev, bias_next)
    lane = iota((HALF, HEAD_DIM), 1)
    stats = [jnp.zeros((HALF, HEAD_DIM), f32) for _ in range(count)]
    for head in range(heads):
        here = cols(head)

        def own(which, j):
            return got_ref[j, which * HALF : (which + 1) * HALF, here]

        def near(ref, which, spot):
            first = (which - 1) * BLK + spot * HALF
            return ref[first : first + HALF, here]

        def far(ref, which):
            first = 2 * BLK + (which - 1) * HALF
            return ref[first : first + HALF, here]

        def near3(ref, which):
            first = (which - 1) * BLK
            return fold_chunks(ref[first : first + BLK, here], HALF // 2, 0.5 if which == 1 else 1.0)

        units = []
        sources = (
            (first_is_prev, lambda w: (near(prev_ref, w, 0), own(w, 2), own(w, 3))),
            (two_are_prev, lambda w: (near(prev_ref, w, 0), near(prev_ref, w, 1), own(w, 3))),
            (two_are_next, lambda w: (own(w, 0), near(next_ref, w, 0), near(next_ref, w, 1))),
            (last_is_next, lambda w: (own(w, 0), own(w, 1), near(next_ref, w, 1))),
        )
        for j, (bias, pick) in enumerate(sources):
            keys = jnp.concatenate(pick(1), axis=0)
            values = jnp.concatenate(pick(2), axis=0)
            units.append((own(0, j), keys, values, bias))
        coarser = (
            (third_prev, lambda w: (far(prev_ref, w), near3(next_ref, w), far(next_ref, w))),
            (third_next, lambda w: (far(prev_ref, w), near3(prev_ref, w), far(next_ref, w))),
        )
        for j, (bias, pick) in enumerate(coarser):
            keys = jnp.concatenate(pick(1), axis=0)
            values = jnp.concatenate(pick(2), axis=0)
            query = jnp.concatenate([fold_chunks(own(0, 2 * j + n), HALF // 2, 0.5) for n in range(2)], axis=0)
            units.append((query, keys, values, bias))
        found = attend(units)
        for j in range(count):
            top2, sum2 = found[j]
            top3, sum3 = found[count + j // 2]

            def spread(rows):
                first = (j % 2) * 2 * SUB
                one = rows[first : first + SUB]
                other = rows[first + SUB : first + 2 * SUB]
                return jnp.concatenate([one, one, other, other], axis=0)

            top3 = spread(top3)
            sum3 = spread(sum3)
            top = jnp.maximum(top2, top3)
            scale2 = jnp.exp2(top2 - top)
            scale3 = jnp.exp2(top3 - top)
            values = sum2[:, :HEAD_DIM] * scale2 + sum3[:, :HEAD_DIM] * scale3
            total = sum2[:, HEAD_DIM:] * (4.0 * scale2) + sum3[:, HEAD_DIM:] * (8.0 * scale3)
            back_ref[j, 0:HALF, here] = (values / total).astype(bf16)
            level = top + jnp.log2(total)
            high = level.astype(bf16).astype(f32)
            middle = (level - high).astype(bf16).astype(f32)
            low = level - high - middle
            for n, term in enumerate((high, middle, low)):
                stats[j] = jnp.where(lane == 3 * head + n, term, stats[j])
    for j in range(count):
        turned = stats[j].T[0:16, :].astype(bf16)
        back_ref[j, HALF : HALF + 16, 0:HEAD_DIM] = turned
        back_ref[j, HALF : HALF + 16, HEAD_DIM:] = jnp.zeros((16, back_ref.shape[2] - HEAD_DIM), bf16)


def coarse_levels(bias, got, from_prev, from_next):
    count, _, width = got.shape
    vmem = pl.BlockSpec(memory_space=pltpu.VMEM)
    return pl.pallas_call(
        coarse_body,
        in_specs=[pl.BlockSpec(memory_space=pltpu.SMEM), vmem, vmem, vmem],
        out_specs=vmem,
        out_shape=jax.ShapeDtypeStruct((count, HALF + 16, width), bf16),
        compiler_params=pltpu.CompilerParams(vmem_limit_bytes=VMEM_GRANT),
        cost_estimate=pl.CostEstimate(flops=1 << 29, bytes_accessed=8 * got.size, transcendentals=1 << 20),
        name="coarse_levels",
    )(bias, got, from_prev, from_next)


def side_body(bias_ref, q0_ref, prev_ref, next_ref, own_sum_ref, own_stat_ref, sum_ref, stat_ref, near_ref):
    heads = q0_ref.shape[1] // HEAD_DIM
    pair = pair_matrix()
    lane = iota((BLK, HEAD_DIM), 1)
    for i, (ref, bias) in enumerate(((prev_ref, bias_ref[0]), (next_ref, bias_ref[1]))):
        rows = slice(i * BLK, (i + 1) * BLK)
        near_ref[i * BLK : i * BLK + HALF, :] = (mul(pair, ref[0:BLK, :]) * 0.5).astype(bf16)
        near_ref[i * BLK + HALF : (i + 1) * BLK, :] = mul(pair, ref[BLK : 2 * BLK, :]).astype(bf16)
        units = [
            (q0_ref[rows, cols(head)], ref[0:BLK, cols(head)], ref[BLK : 2 * BLK, cols(head)], None)
            for head in range(heads)
        ]
        stat = jnp.zeros((BLK, HEAD_DIM), f32)
        for head, (side_top, side_sum) in enumerate(attend(units)):
            side_top = side_top + bias
            own_top = own_stat_ref[rows, 2 * head : 2 * head + 1]
            own_total = own_stat_ref[rows, 2 * head + 1 : 2 * head + 2]
            top = jnp.maximum(own_top, side_top)
            own_scale = jnp.exp2(own_top - top)
            side_scale = jnp.exp2(side_top - top)
            sum_ref[rows, cols(head)] = own_sum_ref[rows, cols(head)] * own_scale + side_sum[:, :HEAD_DIM] * side_scale
            stat = jnp.where(lane == 2 * head, top, stat)
            stat = jnp.where(lane == 2 * head + 1, own_total * own_scale + side_sum[:, HEAD_DIM:] * side_scale, stat)
        stat_ref[rows, :] = stat


def side_level(bias, q0, from_prev, from_next, own_sum, own_stat, groups):
    rows, width = q0.shape
    part = width // groups
    block = lambda n, w: pl.BlockSpec((n, w), lambda g: (0, g))
    return pl.pallas_call(
        side_body,
        grid=(groups,),
        in_specs=[
            pl.BlockSpec(memory_space=pltpu.SMEM),
            block(rows, part),
            block(2 * BLK, part),
            block(2 * BLK, part),
            block(rows, part),
            block(rows, HEAD_DIM),
        ],
        out_specs=[block(rows, part), block(rows, HEAD_DIM), block(2 * BLK, part)],
        out_shape=[
            jax.ShapeDtypeStruct((rows, width), f32),
            jax.ShapeDtypeStruct((rows, groups * HEAD_DIM), f32),
            jax.ShapeDtypeStruct((2 * BLK, width), bf16),
        ],
        compiler_params=pltpu.CompilerParams(vmem_limit_bytes=VMEM_GRANT),
        cost_estimate=pl.CostEstimate(
            flops=8 * rows * BLK * width, bytes_accessed=18 * rows * width, transcendentals=rows * BLK * HEADS
        ),
        name="side_level",
    )(bias, q0, from_prev, from_next, own_sum, own_stat)


def finish_body(bias_ref, q1_ref, near_ref, prev_ref, next_ref, sum_ref, stat_ref, back_ref, out_ref):
    heads = q1_ref.shape[1] // HEAD_DIM
    bias_prev = bias_ref[0]
    bias_next = bias_ref[1]
    key_place = iota((1, 3 * HALF), 1)
    one_prev = jnp.where(key_place < HALF, bias_prev, bias_next)
    two_prev = jnp.where(key_place < 2 * HALF, bias_prev, bias_next)
    restore = restore_matrix()
    packed = back_ref[0, HALF : HALF + 16, 0:HEAD_DIM].astype(f32)
    packed = jnp.concatenate([packed, jnp.zeros((HEAD_DIM - 16, HEAD_DIM), f32)], axis=0).T
    units = []
    for i in range(2):
        for head in range(heads):
            here = cols(head)
            middle = (1 - i) * BLK

            def three(first):
                rows = slice(first, first + HALF)
                near = near_ref[middle + first : middle + first + HALF, here]
                return jnp.concatenate([prev_ref[rows, here], near, next_ref[rows, here]], axis=0)

            query = q1_ref[i * HALF : (i + 1) * HALF, here]
            units.append((query, three(0), three(HALF), one_prev if i == 0 else two_prev))
    found = attend(units)
    for i in range(2):
        rows = slice(i * BLK, (i + 1) * BLK)
        results = []
        for head in range(heads):
            here = cols(head)
            top1, sum1 = found[i * heads + head]
            spot = slice(i * HALF // 2, (i + 1) * HALF // 2)
            level = packed[spot, 3 * head : 3 * head + 1]
            level = level + packed[spot, 3 * head + 1 : 3 * head + 2]
            level = twice(level + packed[spot, 3 * head + 2 : 3 * head + 3])
            deep = twice(back_ref[0, spot, here].astype(f32))
            top = jnp.maximum(top1, level)
            scale1 = jnp.exp2(top1 - top)
            scale2 = jnp.exp2(level - top)
            number = twice(sum1[:, :HEAD_DIM] * scale1 + deep * scale2)
            total = twice(sum1[:, HEAD_DIM:] * (2.0 * scale1) + scale2)
            top = twice(top)
            fine_top = stat_ref[rows, 2 * head : 2 * head + 1]
            fine_total = stat_ref[rows, 2 * head + 1 : 2 * head + 2]
            most = jnp.maximum(top, fine_top)
            scale = jnp.exp2(top - most)
            fine_scale = jnp.exp2(fine_top - most)
            number = number * scale + sum_ref[rows, here] * fine_scale
            total = total * scale + fine_total * fine_scale
            results.append((number / total).astype(bf16))
        out_ref[rows, :] = mul(restore, jnp.concatenate(results, axis=1)).astype(bf16)


def finish(bias, q1, near, from_prev, from_next, fine_sum, fine_stat, back):
    groups, back_rows, part = back.shape
    rows, width = fine_sum.shape
    block = lambda n, w: pl.BlockSpec((n, w), lambda g: (0, g))
    return pl.pallas_call(
        finish_body,
        grid=(groups,),
        in_specs=[
            pl.BlockSpec(memory_space=pltpu.SMEM),
            block(rows // 2, part),
            block(2 * BLK, part),
            block(BLK, part),
            block(BLK, part),
            block(rows, part),
            block(rows, HEAD_DIM),
            pl.BlockSpec((1, back_rows, part), lambda g: (g, 0, 0)),
        ],
        out_specs=block(rows, part),
        out_shape=jax.ShapeDtypeStruct((rows, width), bf16),
        compiler_params=pltpu.CompilerParams(vmem_limit_bytes=VMEM_GRANT),
        cost_estimate=pl.CostEstimate(flops=1 << 29, bytes_accessed=14 * rows * width, transcendentals=1 << 20),
        name="finish",
    )(bias, q1, near, from_prev, from_next, fine_sum, fine_stat, back)


def shift(value, axis, steps):
    count = lax.axis_size(axis)
    first, last = (max(0, -steps), min(count, count - steps))
    return lax.ppermute(value, axis, [(source, source + steps) for source in range(first, last)])


def edge_bias(axis):
    place = lax.axis_index(axis)
    last = lax.axis_size(axis) - 1
    at_edge = jnp.stack([place == 0, place == last])
    return jnp.where(at_edge, very_negative, 0.0).astype(f32)


def local(query_vecs, key_vecs, value_vecs):
    groups = lax.axis_size("grp")
    assert query_vecs.shape == (2 * BLK, HEADS * HEAD_DIM) and groups == 4
    everyone = ("seq", "grp")
    q0, q1, near_right, near_left, far_right, far_left, swap = prepare(query_vecs, key_vecs, value_vecs, groups)
    got = lax.all_to_all(swap, "grp", split_axis=0, concat_axis=0, tiled=True)
    own_sum, own_stat = own_level(q0, key_vecs, value_vecs, groups)
    got, near_right, near_left, own_sum = lax.optimization_barrier((got, near_right, near_left, own_sum))
    coarse_right, coarse_left = coarse_halos(got)
    coarse_prev = shift(coarse_right, "seq", 1)
    coarse_next = shift(coarse_left, "seq", -1)
    near_prev = shift(near_right, everyone, 1)
    near_next = shift(near_left, everyone, -1)
    far_prev = shift(far_right, everyone, 1)
    far_next = shift(far_left, everyone, -1)
    back = coarse_levels(edge_bias("seq"), got, coarse_prev, coarse_next)
    back = lax.all_to_all(back, "grp", split_axis=0, concat_axis=0, tiled=True)
    bias = edge_bias(everyone)
    fine_sum, fine_stat, near = side_level(bias, q0, near_prev, near_next, own_sum, own_stat, groups)
    return finish(bias, q1, near, far_prev, far_next, fine_sum, fine_stat, back)


def solution(mesh):
    return jax.shard_map(
        local,
        mesh=mesh,
        in_specs=(P(("seq", "grp"), None), P(("seq", "grp"), None), P(("seq", "grp"), None)),
        out_specs=P(("seq", "grp"), None),
        check_vma=False,
    )
```

```python
import functools
import functools
import functools
import math

import jax
import jax.numpy as jnp
from jax import lax
from jax.experimental import pallas as pl
from jax.experimental.pallas import tpu as pltpu
from jax.sharding import PartitionSpec as P

HEADS = 8
HEAD_DIM = 128
BLK = 256
HALF = BLK // 2
SUB = BLK // 8
LEV = 4
EXP_SCALE = math.log2(math.e) / math.sqrt(HEAD_DIM)

VMEM_GRANT = 48 << 20

very_negative = -1e30
f32 = jnp.float32
bf16 = jnp.bfloat16


def iota(shape, dim):
    return lax.broadcasted_iota(jnp.int32, shape, dim)


def bit(value, place):
    return jnp.bitwise_and(lax.shift_right_logical(value, place), 1)


def low_bits(value):
    step = SUB.bit_length() - 1
    deep = jnp.bitwise_and(value, SUB - 1)
    return 8 * deep + 4 * bit(value, step) + 2 * bit(value, step + 1) + bit(value, step + 2)


def reorder_matrix():
    return (iota((BLK, BLK), 1) == low_bits(iota((BLK, BLK), 0))).astype(bf16)


def restore_matrix():
    return (iota((BLK, BLK), 0) == low_bits(iota((BLK, BLK), 1))).astype(bf16)


def pair_matrix():
    first = low_bits(iota((HALF, BLK), 0))
    place = iota((HALF, BLK), 1)
    return jnp.logical_or(place == first, place == first + 1).astype(bf16)


def mul(left, right):
    return jnp.dot(left, right, preferred_element_type=f32)


def fold(rows, factor):
    half = rows.shape[0] // 2
    total = rows[:half].astype(f32) + rows[half:].astype(f32)
    if factor != 1.0:
        total = total * factor
    return total.astype(bf16)


def fold_chunks(rows, chunk, factor):
    count = rows.shape[0] // chunk
    return jnp.concatenate([fold(rows[i * chunk : (i + 1) * chunk], factor) for i in range(count)], axis=0)


def twice(rows):
    return jnp.concatenate([rows, rows], axis=0)


def cols(head):
    return slice(head * HEAD_DIM, (head + 1) * HEAD_DIM)


def lane_chunks(rows):
    return [rows[:, first : first + HEAD_DIM] for first in range(0, rows.shape[1], HEAD_DIM)]


def twice(rows):
    return jnp.concatenate([rows, rows], axis=0)


def cols(head):
    return slice(head * HEAD_DIM, (head + 1) * HEAD_DIM)


def lane_chunks(rows):
    return [rows[:, first : first + HEAD_DIM] for first in range(0, rows.shape[1], HEAD_DIM)]


def twice(rows):
    return jnp.concatenate([rows, rows], axis=0)


def cols(head):
    return slice(head * HEAD_DIM, (head + 1) * HEAD_DIM)


def lane_chunks(rows):
    return [rows[:, first : first + HEAD_DIM] for first in range(0, rows.shape[1], HEAD_DIM)]


def with_ones(values):
    return jnp.concatenate([values, jnp.ones_like(values)], axis=1)


def attend(units):
    scores = []
    for query, parts in units:
        chunks = []
        for keys, _, bias in parts:
            raw = lax.dot_general(query, keys, (((1,), (1,)), ((), ())), preferred_element_type=f32)
            chunks.append(lane_chunks(raw if bias is None else raw + bias))
        scores.append(chunks)
    tops = []
    for chunks in scores:
        most = functools.reduce(jnp.maximum, sum(chunks, []))
        tops.append(jnp.broadcast_to(jnp.max(most, axis=1, keepdims=True), most.shape))
    found = []
    for (_, parts), chunks, top in zip(units, scores, tops):
        total = None
        for (_, values, _), pieces in zip(parts, chunks):
            weights = [jnp.exp2((piece - top) * EXP_SCALE).astype(bf16) for piece in pieces]
            one = mul(jnp.concatenate(weights, axis=1), with_ones(values))
            total = one if total is None else total + one
        found.append((top * EXP_SCALE, total))
    return found


def share_of(ref, kind, share, shares, first_row, rows):
    if kind == "lead":
        return ref.at[share]
    width = ref.shape[1] // shares
    first = share * width
    if not isinstance(share, int):
        first = pl.multiple_of(first, HEAD_DIM)
    return ref.at[pl.ds(first_row, rows), pl.ds(first, width)]


class Operand:
    def __init__(self, sources, kind="cols", rows=None, pinned=True):
        self.sources = sources
        self.kind = kind
        self.pinned = pinned
        first = sources[0][0]
        self.rows = first.shape[0] if rows is None else rows
        self.dtype = first.dtype

    def buffer(self, shares):
        shape = self.sources[0][0].shape
        if self.kind == "lead":
            return shape
        pair = (2,) if len(self.sources) == 2 else ()
        return (shares, *pair, self.rows, shape[1] // shares)


def one(value, kind="cols", pinned=True):
    return Operand([(value, 0)], kind, pinned=pinned)


def run_shares(body, name, shares, scalars, ins, outs, flops, exps):
    out_kinds = [kind for _, kind in outs]
    flat = [(i, n) for i, operand in enumerate(ins) for n in range(len(operand.sources))]

    def kernel(*refs):
        refs = list(refs)
        take = lambda count: [refs.pop(0) for _ in range(count)]
        scalar_refs, in_refs, out_refs = take(len(scalars)), take(len(flat)), take(len(outs))
        in_bufs, out_bufs, (in_sems, out_sems) = take(len(ins)), take(len(outs)), take(2)

        def bring(f, share):
            i, n = flat[f]
            operand = ins[i]
            source = share_of(in_refs[f], operand.kind, share, shares, operand.sources[n][1], operand.rows)
            target = in_bufs[i].at[share]
            if len(operand.sources) == 2:
                parity = scalar_refs[0][0]
                target = target.at[parity if n == 0 else 1 - parity]
            return pltpu.make_async_copy(source, target, in_sems.at[f, share])

        def put(i, share):
            rows = out_refs[i].shape[0]
            target = share_of(out_refs[i], out_kinds[i], share, shares, 0, rows)
            return pltpu.make_async_copy(out_bufs[i].at[share], target, out_sems.at[i, share])

        for share in range(shares):
            for f in range(len(flat)):
                bring(f, share).start()

        def step(share, carry):
            for f in range(len(flat)):
                bring(f, share).wait()
            body(scalar_refs, [buf.at[share] for buf in in_bufs], [buf.at[share] for buf in out_bufs])
            for i in range(len(outs)):
                put(i, share).start()
            return carry

        lax.fori_loop(0, shares, step, 0)
        for share in range(shares):
            for i in range(len(outs)):
                put(i, share).wait()

    values, specs = [], []
    for i, n in flat:
        value = ins[i].sources[n][0]
        values.append(pltpu.with_memory_space_constraint(value, pltpu.HBM) if ins[i].pinned else value)
        specs.append(pl.BlockSpec(memory_space=pltpu.HBM if ins[i].pinned else pl.ANY))
    size = sum(value.size * value.dtype.itemsize for value in values + [shape for shape, _ in outs])
    buffers = [pltpu.VMEM(operand.buffer(shares), operand.dtype) for operand in ins]
    for shape, kind in outs:
        width = shape.shape[-1]
        buffers.append(pltpu.VMEM(shape.shape if kind == "lead" else (shares, shape.shape[0], width // shares), shape.dtype))
    return pl.pallas_call(
        kernel,
        in_specs=[pl.BlockSpec(memory_space=pltpu.SMEM)] * len(scalars) + specs,
        out_specs=[pl.BlockSpec(memory_space=pltpu.HBM)] * len(outs),
        out_shape=[pltpu.HBM(shape.shape, shape.dtype) for shape, _ in outs],
        scratch_shapes=buffers
        + [pltpu.SemaphoreType.DMA((len(flat), shares)), pltpu.SemaphoreType.DMA((len(outs), shares))],
        compiler_params=pltpu.CompilerParams(vmem_limit_bytes=VMEM_GRANT),
        cost_estimate=pl.CostEstimate(flops=flops, bytes_accessed=size, transcendentals=exps),
        name=name,
    )(*scalars, *values)


def array(rows, width, dtype):
    return jax.ShapeDtypeStruct((rows, width), dtype)


def swap_body(_, ins, outs):
    pair = pair_matrix()
    for place, (ref, factor) in enumerate(zip(ins, (0.5, 0.5, 1.0))):
        for i in range(2):
            level1 = mul(pair, ref[i * BLK : (i + 1) * BLK, :])
            if factor != 1.0:
                level1 = level1 * factor
            first = place * HALF + i * HALF // 2
            outs[0][first : first + HALF // 2, :] = fold(level1.astype(bf16), factor)


def swap_rows(query_vecs, key_vecs, value_vecs, groups):
    rows, width = query_vecs.shape
    out = jax.ShapeDtypeStruct((groups, 3 * HALF, width // groups), bf16)
    ins = [one(a) for a in (query_vecs, key_vecs, value_vecs)]
    return run_shares(swap_body, "swap_rows", groups, [], ins, [(out, "lead")], 6 * rows * HALF * width, 0)[0]


def rows_body(scalars, ins, outs):
    q_ref, k_ref, v_ref = ins
    q0_ref, q1_ref, near_ref, far_ref, chip_ref = outs
    reorder = reorder_matrix()
    pair = pair_matrix()
    for i in range(2):
        rows = slice(i * BLK, (i + 1) * BLK)
        q0 = mul(reorder, q_ref[rows, :]).astype(bf16)
        q0_ref[rows, :] = q0
        q1_ref[i * HALF : (i + 1) * HALF, :] = fold(q0, 0.5)
    parity = scalars[0][0]
    outer = pl.ds(pl.multiple_of(parity * BLK, BLK), BLK)
    inner = pl.ds(pl.multiple_of((1 - parity) * BLK, BLK), BLK)
    near_ref[0:BLK, :] = k_ref[outer, :]
    near_ref[BLK : 2 * BLK, :] = v_ref[outer, :]
    far_ref[0:HALF, :] = (mul(pair, k_ref[inner, :]) * 0.5).astype(bf16)
    far_ref[HALF:BLK, :] = mul(pair, v_ref[inner, :]).astype(bf16)
    chip_ref[0:BLK, :] = k_ref[inner, :]
    chip_ref[BLK : 2 * BLK, :] = v_ref[inner, :]
    chip_ref[2 * BLK : 2 * BLK + HALF, :] = (mul(pair, k_ref[outer, :]) * 0.5).astype(bf16)
    chip_ref[2 * BLK + HALF : 3 * BLK, :] = mul(pair, v_ref[outer, :]).astype(bf16)


def rows_to_send(parity, query_vecs, key_vecs, value_vecs, groups):
    rows, width = query_vecs.shape
    ins = [one(a) for a in (query_vecs, key_vecs, value_vecs)]
    outs = [(array(n, width, bf16), "cols") for n in (rows, rows // 2, 2 * BLK, BLK, 3 * BLK)]
    return run_shares(rows_body, "rows_to_send", groups, [parity], ins, outs, 8 * rows * BLK * width, 0)


def fine_body(scalars, ins, outs):
    q_ref, k_ref, v_ref, side_ref = ins
    prev_ref, next_ref = side_ref.at[0], side_ref.at[1]
    out_ref, level_ref, near_ref = outs
    heads = q_ref.shape[1] // HEAD_DIM
    pair = pair_matrix()
    for i, ref in enumerate((prev_ref, next_ref)):
        near_ref[i * BLK : i * BLK + HALF, :] = (mul(pair, ref[0:BLK, :]) * 0.5).astype(bf16)
        near_ref[i * BLK + HALF : (i + 1) * BLK, :] = mul(pair, ref[BLK : 2 * BLK, :]).astype(bf16)
    for i, ref in enumerate((prev_ref, next_ref)):
        rows = slice(i * BLK, (i + 1) * BLK)
        units = []
        for head in range(heads):
            here = cols(head)
            own = (k_ref[:, here], v_ref[:, here], None)
            side = (ref[0:BLK, here], ref[BLK : 2 * BLK, here], scalars[1][i])
            units.append((q_ref[rows, here], [own, side]))
        for head, (top, sums) in enumerate(attend(units)):
            total = sums[:, HEAD_DIM:]
            out_ref[rows, cols(head)] = sums[:, :HEAD_DIM] / total
            level_ref[rows, cols(head)] = top + jnp.log2(total)


def fine_level(parity, bias, q0, key_vecs, value_vecs, near, chip, groups):
    rows, width = q0.shape
    ins = [one(a) for a in (q0, key_vecs, value_vecs)] + [Operand([(near, 0), (chip, 0)], rows=2 * BLK, pinned=False)]
    outs = [(array(rows, width, f32), "cols"), (array(rows, width, f32), "cols"), (array(2 * BLK, width, bf16), "cols")]
    flops = 12 * rows * BLK * width
    return run_shares(fine_body, "fine_level", groups, [parity, bias], ins, outs, flops, 3 * rows * BLK * HEADS)


def halo_body(got_ref, right_ref, left_ref):
    count = got_ref.shape[0]
    pair = count // 2
    for which, factor in ((1, 0.5), (2, 1.0)):
        rows = slice(which * HALF, (which + 1) * HALF)
        near = (which - 1) * BLK
        far = 2 * BLK + (which - 1) * HALF
        for j in range(count):
            level2 = got_ref[j, rows, :]
            level3 = fold_chunks(level2, HALF // 2, factor)
            near_ref, far_ref = (left_ref, right_ref) if j < pair else (right_ref, left_ref)
            spot = j % pair
            near_ref[near + spot * HALF : near + (spot + 1) * HALF, :] = level2
            far_ref[far + spot * HALF // 2 : far + (spot + 1) * HALF // 2, :] = level3


def coarse_halos(got):
    shape = jax.ShapeDtypeStruct((3 * BLK, got.shape[2]), bf16)
    return pl.pallas_call(
        halo_body,
        out_shape=[shape, shape],
        compiler_params=pltpu.CompilerParams(vmem_limit_bytes=16 << 20),
        cost_estimate=pl.CostEstimate(flops=1 << 20, bytes_accessed=6 * got.size, transcendentals=0),
        name="coarse_halos",
    )(got)


def coarse_body(bias_ref, got_ref, prev_ref, next_ref, back_ref):
    count = got_ref.shape[0]
    heads = got_ref.shape[2] // HEAD_DIM
    bias_prev = bias_ref[0]
    bias_next = bias_ref[1]
    lane = iota((HALF, HEAD_DIM), 1)

    for head in range(heads):
        here = cols(head)

        def own(which, j):
            return got_ref[j, which * HALF : (which + 1) * HALF, here]

        def near(ref, which, spot):
            first = (which - 1) * BLK + spot * HALF
            return ref[first : first + HALF, here]

        def both(ref, which):
            return ref[(which - 1) * BLK : which * BLK, here]

        def far(ref, which):
            first = 2 * BLK + (which - 1) * HALF
            return ref[first : first + HALF, here]

        def near3(ref, which):
            return fold_chunks(both(ref, which), HALF // 2, 0.5 if which == 1 else 1.0)

        def joined(*rows):
            return jnp.concatenate(rows, axis=0)

        def part(pick, bias):
            return (pick(1), pick(2), bias)

        units = [
            (own(0, 0), [part(lambda w: joined(own(w, 2), own(w, 3)), None), part(lambda w: near(prev_ref, w, 0), bias_prev)]),
            (own(0, 1), [part(lambda w: both(prev_ref, w), bias_prev), part(lambda w: own(w, 3), None)]),
            (own(0, 2), [part(lambda w: both(next_ref, w), bias_next), part(lambda w: own(w, 0), None)]),
            (own(0, 3), [part(lambda w: joined(own(w, 0), own(w, 1)), None), part(lambda w: near(next_ref, w, 1), bias_next)]),
        ]
        for j, (ref, bias, other, other_bias) in enumerate(
            ((next_ref, bias_next, prev_ref, bias_prev), (prev_ref, bias_prev, next_ref, bias_next))
        ):
            query = joined(*[fold_chunks(own(0, 2 * j + n), HALF // 2, 0.5) for n in range(2)])
            units.append(
                (
                    query,
                    [part(lambda w: joined(near3(ref, w), far(ref, w)), bias), part(lambda w: far(other, w), other_bias)],
                )
            )
        found = attend(units)
        for j in range(count):
            top2, sum2 = found[j]
            top3, sum3 = found[count + j // 2]

            def spread(rows):
                first = (j % 2) * 2 * SUB
                one = rows[first : first + SUB]
                other = rows[first + SUB : first + 2 * SUB]
                return joined(one, one, other, other)

            top3 = spread(top3)
            sum3 = spread(sum3)
            top = jnp.maximum(top2, top3)
            scale2 = jnp.exp2(top2 - top)
            scale3 = jnp.exp2(top3 - top)
            values = sum2[:, :HEAD_DIM] * scale2 + sum3[:, :HEAD_DIM] * scale3
            total = sum2[:, HEAD_DIM:] * (4.0 * scale2) + sum3[:, HEAD_DIM:] * (8.0 * scale3)
            back_ref[j, 0:HALF, here] = (values / total).astype(bf16)
            level = top + jnp.log2(total)
            high = level.astype(bf16).astype(f32)
            middle = (level - high).astype(bf16).astype(f32)
            terms = jnp.where(lane == 0, high, jnp.where(lane == 1, middle, level - high - middle))
            back_ref[j, HALF : HALF + 16, here] = terms.T[0:16, :].astype(bf16)


def coarse_levels(bias, got, from_prev, from_next):
    count, _, width = got.shape
    vmem = pl.BlockSpec(memory_space=pltpu.VMEM)
    return pl.pallas_call(
        coarse_body,
        in_specs=[pl.BlockSpec(memory_space=pltpu.SMEM), vmem, vmem, vmem],
        out_specs=vmem,
        out_shape=jax.ShapeDtypeStruct((count, HALF + 16, width), bf16),
        compiler_params=pltpu.CompilerParams(vmem_limit_bytes=16 << 20),
        cost_estimate=pl.CostEstimate(flops=1 << 29, bytes_accessed=8 * got.size, transcendentals=1 << 20),
        name="coarse_levels",
    )(bias, got, from_prev, from_next)


def finish_body(scalars, ins, outs):
    q1_ref, near_ref, fine_ref, level_ref, side_ref, back_ref = ins
    prev_ref, next_ref = side_ref.at[0], side_ref.at[1]
    heads = q1_ref.shape[1] // HEAD_DIM
    bias_prev = scalars[1][0]
    bias_next = scalars[1][1]
    restore = restore_matrix()
    units = []
    for i in range(2):
        for head in range(heads):
            here = cols(head)
            ref, bias, other, other_bias = (
                (next_ref, bias_next, prev_ref, bias_prev) if i == 0 else (prev_ref, bias_prev, next_ref, bias_next)
            )
            middle = (1 - i) * BLK

            def pick(first):
                near = near_ref[middle + first : middle + first + HALF, here]
                return jnp.concatenate([near, ref[first : first + HALF, here]], axis=0)

            both = (pick(0), pick(HALF), bias)
            one = (other[0:HALF, here], other[HALF:BLK, here], other_bias)
            units.append((q1_ref[i * HALF : (i + 1) * HALF, here], [both, one]))
    found = attend(units)
    for i in range(2):
        rows = slice(i * BLK, (i + 1) * BLK)
        spot = slice(i * HALF // 2, (i + 1) * HALF // 2)
        results = []
        for head in range(heads):
            here = cols(head)
            top1, sum1 = found[i * heads + head]
            packed = back_ref[HALF : HALF + 16, here].astype(f32)
            packed = jnp.sum(jnp.where(iota(packed.shape, 0) < 3, packed, 0.0), axis=0, keepdims=True)
            level = jnp.broadcast_to(packed, (HEAD_DIM, HEAD_DIM)).T[spot, :]
            level = twice(level)
            deep = twice(back_ref[spot, here].astype(f32))
            top = jnp.maximum(top1, level)
            scale1 = jnp.exp2(top1 - top)
            scale2 = jnp.exp2(level - top)
            number = twice(sum1[:, :HEAD_DIM] * scale1 + deep * scale2)
            total = twice(sum1[:, HEAD_DIM:] * (2.0 * scale1) + scale2)
            top = twice(top)
            fine = level_ref[rows, here]
            most = jnp.maximum(top, fine)
            scale = jnp.exp2(top - most)
            fine_scale = jnp.exp2(fine - most)
            number = number * scale + fine_ref[rows, here] * fine_scale
            total = total * scale + fine_scale
            results.append((number / total).astype(bf16))
        outs[0][rows, :] = mul(restore, jnp.concatenate(results, axis=1)).astype(bf16)


def finish(parity, bias, q1, near, far, chip, fine, level, back):
    groups = back.shape[0]
    rows, width = fine.shape
    ins = [one(a) for a in (q1, near, fine, level)]
    ins.append(Operand([(far, 0), (chip, 2 * BLK)], rows=BLK, pinned=False))
    ins.append(one(back, "lead", pinned=False))
    outs = [(array(rows, width, bf16), "cols")]
    return run_shares(finish_body, "finish", groups, [parity, bias], ins, outs, 1 << 29, 1 << 20)[0]


def shift(value, axis, steps):
    count = lax.axis_size(axis)
    first, last = (max(0, -steps), min(count, count - steps))
    return lax.ppermute(value, axis, [(source, source + steps) for source in range(first, last)])


def trade(value, axis, first):
    count = lax.axis_size(axis)
    pairs = [(source, source + 1) for source in range(first, count - 1, 2)]
    return lax.ppermute(value, axis, pairs + [(target, source) for source, target in pairs])


def edge_bias(axis):
    place = lax.axis_index(axis)
    last = lax.axis_size(axis) - 1
    at_edge = jnp.stack([place == 0, place == last])
    return jnp.where(at_edge, very_negative, 0.0).astype(f32)


def local(query_vecs, key_vecs, value_vecs):
    groups = lax.axis_size("grp")
    assert query_vecs.shape == (2 * BLK, HEADS * HEAD_DIM) and groups == 4
    everyone = ("seq", "grp")
    parity = jnp.bitwise_and(lax.axis_index(everyone), 1).astype(jnp.int32).reshape(1)
    bias = edge_bias(everyone)
    swap = swap_rows(query_vecs, key_vecs, value_vecs, groups)
    got = lax.all_to_all(swap, "grp", split_axis=0, concat_axis=0, tiled=True)
    query_rows, swap = lax.optimization_barrier((query_vecs, swap))
    q0, q1, near, far, chip = rows_to_send(parity, query_rows, key_vecs, value_vecs, groups)
    got, near, far, chip = lax.optimization_barrier((got, near, far, chip))
    coarse_right, coarse_left = coarse_halos(got)
    coarse_right, coarse_left, near, far, chip = lax.optimization_barrier((coarse_right, coarse_left, near, far, chip))
    coarse_prev = shift(coarse_right, "seq", 1)
    coarse_next = shift(coarse_left, "seq", -1)
    near = trade(near, everyone, 1)
    chip = trade(chip, everyone, 0)
    far = trade(far, everyone, 1)
    fine, level, middle = fine_level(parity, bias, q0, key_vecs, value_vecs, near, chip, groups)
    got, level = lax.optimization_barrier((got, level))
    back = coarse_levels(edge_bias("seq"), got, coarse_prev, coarse_next)
    back = lax.all_to_all(back, "grp", split_axis=0, concat_axis=0, tiled=True)
    return finish(parity, bias, q1, middle, far, chip, fine, level, back)


def solution(mesh):
    return jax.shard_map(
        local,
        mesh=mesh,
        in_specs=(P(("seq", "grp"), None), P(("seq", "grp"), None), P(("seq", "grp"), None)),
        out_specs=P(("seq", "grp"), None),
        check_vma=False,
    )
```

```python
import functools
import functools
import functools
import functools
import math

import jax
import jax.numpy as jnp
from jax import lax
from jax.experimental import pallas as pl
from jax.experimental.pallas import tpu as pltpu
from jax.sharding import PartitionSpec as P

HEADS = 8
HEAD_DIM = 128
BLK = 256
HALF = BLK // 2
SUB = BLK // 8
LEV = 4
EXP_SCALE = math.log2(math.e) / math.sqrt(HEAD_DIM)

VMEM_GRANT = 48 << 20

very_negative = -1e30
f32 = jnp.float32
bf16 = jnp.bfloat16


def iota(shape, dim):
    return lax.broadcasted_iota(jnp.int32, shape, dim)


def bit(value, place):
    return jnp.bitwise_and(lax.shift_right_logical(value, place), 1)


def low_bits(value):
    step = SUB.bit_length() - 1
    deep = jnp.bitwise_and(value, SUB - 1)
    return 8 * deep + 4 * bit(value, step) + 2 * bit(value, step + 1) + bit(value, step + 2)


def reorder_matrix():
    return (iota((BLK, BLK), 1) == low_bits(iota((BLK, BLK), 0))).astype(bf16)


def restore_matrix():
    return (iota((BLK, BLK), 0) == low_bits(iota((BLK, BLK), 1))).astype(bf16)


def pair_matrix():
    first = low_bits(iota((HALF, BLK), 0))
    place = iota((HALF, BLK), 1)
    return jnp.logical_or(place == first, place == first + 1).astype(bf16)


def mul(left, right):
    return jnp.dot(left, right, preferred_element_type=f32)


def fold(rows, factor):
    half = rows.shape[0] // 2
    total = rows[:half].astype(f32) + rows[half:].astype(f32)
    if factor != 1.0:
        total = total * factor
    return total.astype(bf16)


def fold_chunks(rows, chunk, factor):
    count = rows.shape[0] // chunk
    return jnp.concatenate([fold(rows[i * chunk : (i + 1) * chunk], factor) for i in range(count)], axis=0)


def twice(rows):
    return jnp.concatenate([rows, rows], axis=0)


def cols(head):
    return slice(head * HEAD_DIM, (head + 1) * HEAD_DIM)


def lane_chunks(rows):
    return [rows[:, first : first + HEAD_DIM] for first in range(0, rows.shape[1], HEAD_DIM)]


def twice(rows):
    return jnp.concatenate([rows, rows], axis=0)


def cols(head):
    return slice(head * HEAD_DIM, (head + 1) * HEAD_DIM)


def lane_chunks(rows):
    return [rows[:, first : first + HEAD_DIM] for first in range(0, rows.shape[1], HEAD_DIM)]


def twice(rows):
    return jnp.concatenate([rows, rows], axis=0)


def cols(head):
    return slice(head * HEAD_DIM, (head + 1) * HEAD_DIM)


def lane_chunks(rows):
    return [rows[:, first : first + HEAD_DIM] for first in range(0, rows.shape[1], HEAD_DIM)]


def twice(rows):
    return jnp.concatenate([rows, rows], axis=0)


def cols(head):
    return slice(head * HEAD_DIM, (head + 1) * HEAD_DIM)


def lane_chunks(rows):
    return [rows[:, first : first + HEAD_DIM] for first in range(0, rows.shape[1], HEAD_DIM)]


def with_ones(values):
    return jnp.concatenate([values, jnp.ones_like(values)], axis=1)


def attend(units):
    scores = []
    for query, parts in units:
        chunks = []
        for keys, _, bias in parts:
            raw = lax.dot_general(query, keys, (((1,), (1,)), ((), ())), preferred_element_type=f32)
            chunks.append(lane_chunks(raw if bias is None else raw + bias))
        scores.append(chunks)
    tops = []
    for chunks in scores:
        most = functools.reduce(jnp.maximum, sum(chunks, []))
        tops.append(jnp.broadcast_to(jnp.max(most, axis=1, keepdims=True), most.shape))
    found = []
    for (_, parts), chunks, top in zip(units, scores, tops):
        total = None
        for (_, values, _), pieces in zip(parts, chunks):
            weights = [jnp.exp2((piece - top) * EXP_SCALE).astype(bf16) for piece in pieces]
            one = mul(jnp.concatenate(weights, axis=1), with_ones(values))
            total = one if total is None else total + one
        found.append((top * EXP_SCALE, total))
    return found


def share_of(ref, kind, share, shares, first_row, rows):
    if kind == "lead":
        return ref.at[share]
    width = ref.shape[1] // shares
    first = share * width
    if not isinstance(share, int):
        first = pl.multiple_of(first, HEAD_DIM)
    return ref.at[pl.ds(first_row, rows), pl.ds(first, width)]


class Operand:
    def __init__(self, sources, kind="cols", pinned=True):
        self.sources = sources
        self.kind = kind
        self.pinned = pinned
        self.rows = sources[0].shape[0]
        self.dtype = sources[0].dtype

    def buffer(self, shares):
        shape = self.sources[0].shape
        if self.kind == "lead":
            return shape
        pair = (2,) if len(self.sources) == 3 else ()
        return (shares, *pair, self.rows, shape[1] // shares)


def one(value, kind="cols", pinned=True):
    return Operand([value], kind, pinned)


def run_shares(body, name, shares, scalars, ins, outs, flops, exps):
    out_kinds = [kind for _, kind in outs]
    flat = [(i, n) for i, operand in enumerate(ins) for n in range(len(operand.sources))]

    def kernel(*refs):
        refs = list(refs)
        take = lambda count: [refs.pop(0) for _ in range(count)]
        scalar_refs, in_refs, out_refs = take(len(scalars)), take(len(flat)), take(len(outs))
        in_bufs, out_bufs, (in_sems, out_sems) = take(len(ins)), take(len(outs)), take(2)

        def bring(f, share):
            i, n = flat[f]
            operand = ins[i]
            source = share_of(in_refs[f], operand.kind, share, shares, 0, operand.rows)
            target = in_bufs[i].at[share]
            semaphore = in_sems.at[f, share]
            if len(operand.sources) == 3:
                odd = scalar_refs[0][0]
                target = target.at[1 - odd if n == 2 else odd]
                semaphore = in_sems.at[f + 1 if n == 0 else f, share]
            return pltpu.make_async_copy(source, target, semaphore)

        def begin(f, share):
            i, n = flat[f]
            if len(ins[i].sources) == 3 and n < 2:
                pl.when(scalar_refs[0][1] == 1 - n)(lambda: bring(f, share).start())
            else:
                bring(f, share).start()

        def end(f, share):
            i, n = flat[f]
            if len(ins[i].sources) == 1 or n > 0:
                bring(f, share).wait()

        def put(i, share):
            rows = out_refs[i].shape[0]
            target = share_of(out_refs[i], out_kinds[i], share, shares, 0, rows)
            return pltpu.make_async_copy(out_bufs[i].at[share], target, out_sems.at[i, share])

        for share in range(shares):
            for f in range(len(flat)):
                begin(f, share)

        def step(share, carry):
            for f in range(len(flat)):
                end(f, share)
            body(scalar_refs, [buf.at[share] for buf in in_bufs], [buf.at[share] for buf in out_bufs])
            for i in range(len(outs)):
                put(i, share).start()
            return carry

        lax.fori_loop(0, shares, step, 0)
        for share in range(shares):
            for i in range(len(outs)):
                put(i, share).wait()

    values, specs = [], []
    for i, n in flat:
        value = ins[i].sources[n]
        values.append(pltpu.with_memory_space_constraint(value, pltpu.HBM) if ins[i].pinned else value)
        specs.append(pl.BlockSpec(memory_space=pltpu.HBM if ins[i].pinned else pl.ANY))
    size = sum(value.size * value.dtype.itemsize for value in values + [shape for shape, _ in outs])
    buffers = [pltpu.VMEM(operand.buffer(shares), operand.dtype) for operand in ins]
    for shape, kind in outs:
        width = shape.shape[-1]
        buffers.append(pltpu.VMEM(shape.shape if kind == "lead" else (shares, shape.shape[0], width // shares), shape.dtype))
    return pl.pallas_call(
        kernel,
        in_specs=[pl.BlockSpec(memory_space=pltpu.SMEM)] * len(scalars) + specs,
        out_specs=[pl.BlockSpec(memory_space=pltpu.HBM)] * len(outs),
        out_shape=[pltpu.HBM(shape.shape, shape.dtype) for shape, _ in outs],
        scratch_shapes=buffers
        + [pltpu.SemaphoreType.DMA((len(flat), shares)), pltpu.SemaphoreType.DMA((len(outs), shares))],
        compiler_params=pltpu.CompilerParams(vmem_limit_bytes=VMEM_GRANT),
        cost_estimate=pl.CostEstimate(flops=flops, bytes_accessed=size, transcendentals=exps),
        name=name,
    )(*scalars, *values)


def array(rows, width, dtype):
    return jax.ShapeDtypeStruct((rows, width), dtype)


def swap_body(_, ins, outs):
    pair = pair_matrix()
    for place, (ref, factor) in enumerate(zip(ins, (0.5, 0.5, 1.0))):
        for i in range(2):
            level1 = mul(pair, ref[i * BLK : (i + 1) * BLK, :])
            if factor != 1.0:
                level1 = level1 * factor
            first = place * HALF + i * HALF // 2
            outs[0][first : first + HALF // 2, :] = fold(level1.astype(bf16), factor)


def swap_rows(query_vecs, key_vecs, value_vecs, groups):
    rows, width = query_vecs.shape
    out = jax.ShapeDtypeStruct((groups, 3 * HALF, width // groups), bf16)
    ins = [one(a) for a in (query_vecs, key_vecs, value_vecs)]
    return run_shares(swap_body, "swap_rows", groups, [], ins, [(out, "lead")], 6 * rows * HALF * width, 0)[0]


def rows_body(scalars, ins, outs):
    q_ref, k_ref, v_ref = ins
    q0_ref, q1_ref, cross_ref, chip_ref = outs
    reorder = reorder_matrix()
    pair = pair_matrix()
    for i in range(2):
        rows = slice(i * BLK, (i + 1) * BLK)
        q0 = mul(reorder, q_ref[rows, :]).astype(bf16)
        q0_ref[rows, :] = q0
        q1_ref[i * HALF : (i + 1) * HALF, :] = fold(q0, 0.5)
    parity = scalars[0][0]
    outer = pl.ds(pl.multiple_of(parity * BLK, BLK), BLK)
    inner = pl.ds(pl.multiple_of((1 - parity) * BLK, BLK), BLK)
    for ref, near, far in ((cross_ref, outer, inner), (chip_ref, inner, outer)):
        ref[0:BLK, :] = k_ref[near, :]
        ref[BLK : 2 * BLK, :] = v_ref[near, :]
        ref[2 * BLK : 2 * BLK + HALF, :] = (mul(pair, k_ref[far, :]) * 0.5).astype(bf16)
        ref[2 * BLK + HALF : 3 * BLK, :] = mul(pair, v_ref[far, :]).astype(bf16)


def rows_to_send(place, query_vecs, key_vecs, value_vecs, groups):
    rows, width = query_vecs.shape
    ins = [one(a) for a in (query_vecs, key_vecs, value_vecs)]
    outs = [(array(n, width, bf16), "cols") for n in (rows, rows // 2, 3 * BLK, 3 * BLK)]
    return run_shares(rows_body, "rows_to_send", groups, [place], ins, outs, 8 * rows * BLK * width, 0)


def own_body(_, ins, outs):
    q_ref, k_ref, v_ref = ins
    out_ref, level_ref = outs
    heads = q_ref.shape[1] // HEAD_DIM
    for i in range(2):
        rows = slice(i * BLK, (i + 1) * BLK)
        units = [(q_ref[rows, cols(head)], [(k_ref[:, cols(head)], v_ref[:, cols(head)], None)]) for head in range(heads)]
        for head, (top, sums) in enumerate(attend(units)):
            total = sums[:, HEAD_DIM:]
            out_ref[rows, cols(head)] = sums[:, :HEAD_DIM] / total
            level_ref[rows, cols(head)] = top + jnp.log2(total)


def own_level(q0, key_vecs, value_vecs, groups):
    rows, width = q0.shape
    ins = [one(a) for a in (q0, key_vecs, value_vecs)]
    outs = [(array(rows, width, f32), "cols"), (array(rows, width, f32), "cols")]
    flops = 8 * rows * BLK * width
    return run_shares(own_body, "own_level", groups, [], ins, outs, flops, 2 * rows * BLK * HEADS)


def side_body(scalars, ins, outs):
    q0_ref, q1_ref, own_ref, own_level_ref, side_ref = ins
    out_ref, level_ref = outs
    heads = q0_ref.shape[1] // HEAD_DIM
    pair = pair_matrix()
    near_keys = [(mul(pair, side_ref[i, 0:BLK, :]) * 0.5).astype(bf16) for i in range(2)]
    near_values = [mul(pair, side_ref[i, BLK : 2 * BLK, :]).astype(bf16) for i in range(2)]
    far_keys = slice(2 * BLK, 2 * BLK + HALF)
    far_values = slice(2 * BLK + HALF, 3 * BLK)
    for i in range(2):
        rows = slice(i * BLK, (i + 1) * BLK)
        units = []
        for head in range(heads):
            here = cols(head)
            units.append(
                (q0_ref[rows, here], [(side_ref[i, 0:BLK, here], side_ref[i, BLK : 2 * BLK, here], scalars[1][i])])
            )
        for head in range(heads):
            here = cols(head)
            both, other = 1 - i, i
            keys = jnp.concatenate([near_keys[both][:, here], side_ref[both, far_keys, here]], axis=0)
            values = jnp.concatenate([near_values[both][:, here], side_ref[both, far_values, here]], axis=0)
            parts = [
                (keys, values, scalars[1][both]),
                (side_ref[other, far_keys, here], side_ref[other, far_values, here], scalars[1][other]),
            ]
            units.append((q1_ref[i * HALF : (i + 1) * HALF, here], parts))
        found = attend(units)
        for head in range(heads):
            here = cols(head)
            top0, sum0 = found[head]
            top1, sum1 = found[heads + head]
            top1 = twice(top1)
            own = own_level_ref[rows, here]
            top = jnp.maximum(jnp.maximum(top0, top1), own)
            scale0 = jnp.exp2(top0 - top)
            scale1 = jnp.exp2(top1 - top)
            scale = jnp.exp2(own - top)
            number = sum0[:, :HEAD_DIM] * scale0 + twice(sum1[:, :HEAD_DIM]) * scale1 + own_ref[rows, here] * scale
            total = sum0[:, HEAD_DIM:] * scale0 + twice(2.0 * sum1[:, HEAD_DIM:]) * scale1 + scale
            out_ref[rows, here] = number / total
            level_ref[rows, here] = top + jnp.log2(total)


def side_level(place, bias, q0, q1, own, own_lev, outer, inner, chip, groups):
    rows, width = q0.shape
    ins = [one(a) for a in (q0, q1, own, own_lev)] + [Operand([outer, inner, chip], pinned=False)]
    outs = [(array(rows, width, f32), "cols"), (array(rows, width, f32), "cols")]
    flops = 7 * rows * BLK * width
    return run_shares(side_body, "side_level", groups, [place, bias], ins, outs, flops, 2 * rows * BLK * HEADS)


def halo_body(got_ref, right_ref, left_ref):
    count = got_ref.shape[0]
    pair = count // 2
    for which, factor in ((1, 0.5), (2, 1.0)):
        rows = slice(which * HALF, (which + 1) * HALF)
        near = (which - 1) * BLK
        far = 2 * BLK + (which - 1) * HALF
        for j in range(count):
            level2 = got_ref[j, rows, :]
            level3 = fold_chunks(level2, HALF // 2, factor)
            near_ref, far_ref = (left_ref, right_ref) if j < pair else (right_ref, left_ref)
            spot = j % pair
            near_ref[near + spot * HALF : near + (spot + 1) * HALF, :] = level2
            far_ref[far + spot * HALF // 2 : far + (spot + 1) * HALF // 2, :] = level3


def coarse_halos(got):
    shape = jax.ShapeDtypeStruct((3 * BLK, got.shape[2]), bf16)
    return pl.pallas_call(
        halo_body,
        out_shape=[shape, shape],
        compiler_params=pltpu.CompilerParams(vmem_limit_bytes=16 << 20),
        cost_estimate=pl.CostEstimate(flops=1 << 20, bytes_accessed=6 * got.size, transcendentals=0),
        name="coarse_halos",
    )(got)


def coarse_body(bias_ref, got_ref, prev_ref, next_ref, back_ref):
    count = got_ref.shape[0]
    heads = got_ref.shape[2] // HEAD_DIM
    bias_prev = bias_ref[0]
    bias_next = bias_ref[1]
    lane = iota((HALF, HEAD_DIM), 1)

    for head in range(heads):
        here = cols(head)

        def own(which, j):
            return got_ref[j, which * HALF : (which + 1) * HALF, here]

        def near(ref, which, spot):
            first = (which - 1) * BLK + spot * HALF
            return ref[first : first + HALF, here]

        def both(ref, which):
            return ref[(which - 1) * BLK : which * BLK, here]

        def far(ref, which):
            first = 2 * BLK + (which - 1) * HALF
            return ref[first : first + HALF, here]

        def near3(ref, which):
            return fold_chunks(both(ref, which), HALF // 2, 0.5 if which == 1 else 1.0)

        def joined(*rows):
            return jnp.concatenate(rows, axis=0)

        def part(pick, bias):
            return (pick(1), pick(2), bias)

        units = [
            (own(0, 0), [part(lambda w: joined(own(w, 2), own(w, 3)), None), part(lambda w: near(prev_ref, w, 0), bias_prev)]),
            (own(0, 1), [part(lambda w: both(prev_ref, w), bias_prev), part(lambda w: own(w, 3), None)]),
            (own(0, 2), [part(lambda w: both(next_ref, w), bias_next), part(lambda w: own(w, 0), None)]),
            (own(0, 3), [part(lambda w: joined(own(w, 0), own(w, 1)), None), part(lambda w: near(next_ref, w, 1), bias_next)]),
        ]
        for j, (ref, bias, other, other_bias) in enumerate(
            ((next_ref, bias_next, prev_ref, bias_prev), (prev_ref, bias_prev, next_ref, bias_next))
        ):
            query = joined(*[fold_chunks(own(0, 2 * j + n), HALF // 2, 0.5) for n in range(2)])
            units.append(
                (
                    query,
                    [part(lambda w: joined(near3(ref, w), far(ref, w)), bias), part(lambda w: far(other, w), other_bias)],
                )
            )
        found = attend(units)
        for j in range(count):
            top2, sum2 = found[j]
            top3, sum3 = found[count + j // 2]

            def spread(rows):
                first = (j % 2) * 2 * SUB
                one = rows[first : first + SUB]
                other = rows[first + SUB : first + 2 * SUB]
                return joined(one, one, other, other)

            top3 = spread(top3)
            sum3 = spread(sum3)
            top = jnp.maximum(top2, top3)
            scale2 = jnp.exp2(top2 - top)
            scale3 = jnp.exp2(top3 - top)
            values = sum2[:, :HEAD_DIM] * scale2 + sum3[:, :HEAD_DIM] * scale3
            total = sum2[:, HEAD_DIM:] * (4.0 * scale2) + sum3[:, HEAD_DIM:] * (8.0 * scale3)
            back_ref[j, 0:HALF, here] = (values / total).astype(bf16)
            level = top + jnp.log2(total)
            high = level.astype(bf16).astype(f32)
            middle = (level - high).astype(bf16).astype(f32)
            terms = jnp.where(lane == 0, high, jnp.where(lane == 1, middle, level - high - middle))
            back_ref[j, HALF : HALF + 16, here] = terms.T[0:16, :].astype(bf16)


def coarse_levels(bias, got, from_prev, from_next):
    count, _, width = got.shape
    vmem = pl.BlockSpec(memory_space=pltpu.VMEM)
    return pl.pallas_call(
        coarse_body,
        in_specs=[pl.BlockSpec(memory_space=pltpu.SMEM), vmem, vmem, vmem],
        out_specs=vmem,
        out_shape=jax.ShapeDtypeStruct((count, HALF + 16, width), bf16),
        compiler_params=pltpu.CompilerParams(vmem_limit_bytes=16 << 20),
        cost_estimate=pl.CostEstimate(flops=1 << 29, bytes_accessed=8 * got.size, transcendentals=1 << 20),
        name="coarse_levels",
    )(bias, got, from_prev, from_next)


def finish_body(_, ins, outs):
    fine_ref, level_ref, back_ref = ins
    heads = fine_ref.shape[1] // HEAD_DIM
    restore = restore_matrix()
    coarse = []
    for head in range(heads):
        packed = back_ref[HALF : HALF + 16, cols(head)].astype(f32)
        packed = jnp.sum(jnp.where(iota(packed.shape, 0) < 3, packed, 0.0), axis=0, keepdims=True)
        coarse.append(jnp.broadcast_to(packed, (HEAD_DIM, HEAD_DIM)).T)
    for i in range(2):
        rows = slice(i * BLK, (i + 1) * BLK)
        spot = slice(i * HALF // 2, (i + 1) * HALF // 2)
        results = []
        for head in range(heads):
            here = cols(head)
            level = twice(twice(coarse[head][spot, :]))
            deep = twice(twice(back_ref[spot, here].astype(f32)))
            fine = level_ref[rows, here]
            top = jnp.maximum(level, fine)
            scale = jnp.exp2(level - top)
            fine_scale = jnp.exp2(fine - top)
            number = deep * scale + fine_ref[rows, here] * fine_scale
            results.append((number / (scale + fine_scale)).astype(bf16))
        outs[0][rows, :] = mul(restore, jnp.concatenate(results, axis=1)).astype(bf16)


def finish(fine, level, back):
    groups = back.shape[0]
    rows, width = fine.shape
    ins = [one(fine), one(level), one(back, "lead", pinned=False)]
    outs = [(array(rows, width, bf16), "cols")]
    return run_shares(finish_body, "finish", groups, [], ins, outs, 2 * rows * BLK * width, 2 * rows * width)[0]


def shift(value, axis, steps):
    count = lax.axis_size(axis)
    first, last = (max(0, -steps), min(count, count - steps))
    return lax.ppermute(value, axis, [(source, source + steps) for source in range(first, last)])


def trade(value, axis, first, group=1, whole=None):
    count = lax.axis_size(axis)
    pairs = [(source, source + 1) for source in range(first, count - 1, 2)]
    if whole is not None:
        pairs = [pair for pair in pairs if (pair[1] % group != 0) == whole]
    return lax.ppermute(value, axis, pairs + [(target, source) for source, target in pairs])


def edge_bias(axis):
    place = lax.axis_index(axis)
    last = lax.axis_size(axis) - 1
    at_edge = jnp.stack([place == 0, place == last])
    return jnp.where(at_edge, very_negative, 0.0).astype(f32)


def local(query_vecs, key_vecs, value_vecs):
    groups = lax.axis_size("grp")
    assert query_vecs.shape == (2 * BLK, HEADS * HEAD_DIM) and groups == 4
    everyone = ("seq", "grp")
    index = lax.axis_index(everyone)
    odd = jnp.bitwise_and(index, 1)
    spot = lax.axis_index("grp")
    outermost = jnp.logical_or(spot == 0, spot == groups - 1)
    place = jnp.stack([odd, outermost.astype(odd.dtype)]).astype(jnp.int32)
    bias = edge_bias(everyone)
    swap = swap_rows(query_vecs, key_vecs, value_vecs, groups)
    got = lax.all_to_all(swap, "grp", split_axis=0, concat_axis=0, tiled=True)
    query_rows, swap = lax.optimization_barrier((query_vecs, swap))
    q0, q1, cross, chip = rows_to_send(place, query_rows, key_vecs, value_vecs, groups)
    outer = trade(cross, everyone, 1, groups, False)
    own, own_lev = own_level(q0, key_vecs, value_vecs, groups)
    got, own_lev = lax.optimization_barrier((got, own_lev))
    coarse_right, coarse_left = coarse_halos(got)
    coarse_right, coarse_left, cross, chip = lax.optimization_barrier((coarse_right, coarse_left, cross, chip))
    coarse_prev = shift(coarse_right, "seq", 1)
    coarse_next = shift(coarse_left, "seq", -1)
    inner = trade(cross, everyone, 1, groups, True)
    chip = trade(chip, everyone, 0)
    back = coarse_levels(edge_bias("seq"), got, coarse_prev, coarse_next)
    back, own_lev = lax.optimization_barrier((back, own_lev))
    back = lax.all_to_all(back, "grp", split_axis=0, concat_axis=0, tiled=True)
    fine, level = side_level(place, bias, q0, q1, own, own_lev, outer, inner, chip, groups)
    return finish(fine, level, back)


def solution(mesh):
    return jax.shard_map(
        local,
        mesh=mesh,
        in_specs=(P(("seq", "grp"), None), P(("seq", "grp"), None), P(("seq", "grp"), None)),
        out_specs=P(("seq", "grp"), None),
        check_vma=False,
    )
```

```python
import functools
import functools
import functools
import functools
import functools
import functools
import math

import jax
import jax.numpy as jnp
from jax import lax
from jax.experimental import pallas as pl
from jax.experimental.pallas import tpu as pltpu
from jax.sharding import PartitionSpec as P

HEADS = 8
HEAD_DIM = 128
BLK = 256
HALF = BLK // 2
SUB = BLK // 8
LEV = 4
EXP_SCALE = math.log2(math.e) / math.sqrt(HEAD_DIM)

VMEM_GRANT = 48 << 20

very_negative = -1e30
f32 = jnp.float32
bf16 = jnp.bfloat16


def iota(shape, dim):
    return lax.broadcasted_iota(jnp.int32, shape, dim)


def bit(value, place):
    return jnp.bitwise_and(lax.shift_right_logical(value, place), 1)


def low_bits(value):
    step = SUB.bit_length() - 1
    deep = jnp.bitwise_and(value, SUB - 1)
    return 8 * deep + 4 * bit(value, step) + 2 * bit(value, step + 1) + bit(value, step + 2)


def reorder_matrix():
    return (iota((BLK, BLK), 1) == low_bits(iota((BLK, BLK), 0))).astype(bf16)


def restore_matrix():
    return (iota((BLK, BLK), 0) == low_bits(iota((BLK, BLK), 1))).astype(bf16)


def pair_matrix():
    first = low_bits(iota((HALF, BLK), 0))
    place = iota((HALF, BLK), 1)
    return jnp.logical_or(place == first, place == first + 1).astype(bf16)


def mul(left, right):
    return jnp.dot(left, right, preferred_element_type=f32)


def fold(rows, factor):
    half = rows.shape[0] // 2
    total = rows[:half].astype(f32) + rows[half:].astype(f32)
    if factor != 1.0:
        total = total * factor
    return total.astype(bf16)


def fold_chunks(rows, chunk, factor):
    count = rows.shape[0] // chunk
    return jnp.concatenate([fold(rows[i * chunk : (i + 1) * chunk], factor) for i in range(count)], axis=0)


def twice(rows):
    return jnp.concatenate([rows, rows], axis=0)


def cols(head):
    return slice(head * HEAD_DIM, (head + 1) * HEAD_DIM)


def lane_chunks(rows):
    return [rows[:, first : first + HEAD_DIM] for first in range(0, rows.shape[1], HEAD_DIM)]


def twice(rows):
    return jnp.concatenate([rows, rows], axis=0)


def cols(head):
    return slice(head * HEAD_DIM, (head + 1) * HEAD_DIM)


def lane_chunks(rows):
    return [rows[:, first : first + HEAD_DIM] for first in range(0, rows.shape[1], HEAD_DIM)]


def twice(rows):
    return jnp.concatenate([rows, rows], axis=0)


def cols(head):
    return slice(head * HEAD_DIM, (head + 1) * HEAD_DIM)


def lane_chunks(rows):
    return [rows[:, first : first + HEAD_DIM] for first in range(0, rows.shape[1], HEAD_DIM)]


def twice(rows):
    return jnp.concatenate([rows, rows], axis=0)


def cols(head):
    return slice(head * HEAD_DIM, (head + 1) * HEAD_DIM)


def lane_chunks(rows):
    return [rows[:, first : first + HEAD_DIM] for first in range(0, rows.shape[1], HEAD_DIM)]


def twice(rows):
    return jnp.concatenate([rows, rows], axis=0)


def cols(head):
    return slice(head * HEAD_DIM, (head + 1) * HEAD_DIM)


def lane_chunks(rows):
    return [rows[:, first : first + HEAD_DIM] for first in range(0, rows.shape[1], HEAD_DIM)]


def twice(rows):
    return jnp.concatenate([rows, rows], axis=0)


def cols(head):
    return slice(head * HEAD_DIM, (head + 1) * HEAD_DIM)


def lane_chunks(rows):
    return [rows[:, first : first + HEAD_DIM] for first in range(0, rows.shape[1], HEAD_DIM)]


def with_ones(values):
    return jnp.concatenate([values, jnp.ones_like(values)], axis=1)


def attend(units):
    scores = []
    for query, parts in units:
        chunks = []
        for keys, _, bias in parts:
            raw = lax.dot_general(query, keys, (((1,), (1,)), ((), ())), preferred_element_type=f32)
            chunks.append(lane_chunks(raw if bias is None else raw + bias))
        scores.append(chunks)
    tops = []
    for chunks in scores:
        most = functools.reduce(jnp.maximum, sum(chunks, []))
        tops.append(jnp.broadcast_to(jnp.max(most, axis=1, keepdims=True), most.shape))
    found = []
    for (_, parts), chunks, top in zip(units, scores, tops):
        total = None
        for (_, values, _), pieces in zip(parts, chunks):
            weights = [jnp.exp2((piece - top) * EXP_SCALE).astype(bf16) for piece in pieces]
            one = mul(jnp.concatenate(weights, axis=1), with_ones(values))
            total = one if total is None else total + one
        found.append((top * EXP_SCALE, total))
    return found


def share_of(ref, kind, share, shares, first_row, rows):
    if kind == "lead":
        return ref.at[share]
    width = ref.shape[1] // shares
    first = share * width
    if not isinstance(share, int):
        first = pl.multiple_of(first, HEAD_DIM)
    return ref.at[pl.ds(first_row, rows), pl.ds(first, width)]


class Operand:
    def __init__(self, sources, kind="cols", pinned=True):
        self.sources = sources
        self.kind = kind
        self.pinned = pinned
        self.rows = sources[0].shape[0]
        self.dtype = sources[0].dtype

    def buffer(self, shares):
        shape = self.sources[0].shape
        if self.kind == "lead":
            return shape
        pair = (2,) if len(self.sources) == 3 else ()
        return (shares, *pair, self.rows, shape[1] // shares)


def one(value, kind="cols", pinned=True):
    return Operand([value], kind, pinned)


def run_shares(body, name, shares, scalars, ins, outs, flops, exps):
    out_kinds = [kind for _, kind in outs]
    flat = [(i, n) for i, operand in enumerate(ins) for n in range(len(operand.sources))]

    def kernel(*refs):
        refs = list(refs)
        take = lambda count: [refs.pop(0) for _ in range(count)]
        scalar_refs, in_refs, out_refs = take(len(scalars)), take(len(flat)), take(len(outs))
        in_bufs, out_bufs, (in_sems, out_sems) = take(len(ins)), take(len(outs)), take(2)

        def bring(f, share):
            i, n = flat[f]
            operand = ins[i]
            source = share_of(in_refs[f], operand.kind, share, shares, 0, operand.rows)
            target = in_bufs[i].at[share]
            semaphore = in_sems.at[f, share]
            if len(operand.sources) == 3:
                odd = scalar_refs[0][0]
                target = target.at[1 - odd if n == 2 else odd]
                semaphore = in_sems.at[f + 1 if n == 0 else f, share]
            return pltpu.make_async_copy(source, target, semaphore)

        def begin(f, share):
            i, n = flat[f]
            if len(ins[i].sources) == 3 and n < 2:
                pl.when(scalar_refs[0][1] == 1 - n)(lambda: bring(f, share).start())
            else:
                bring(f, share).start()

        def end(f, share):
            i, n = flat[f]
            if len(ins[i].sources) == 1 or n > 0:
                bring(f, share).wait()

        def put(i, share):
            rows = out_refs[i].shape[0]
            target = share_of(out_refs[i], out_kinds[i], share, shares, 0, rows)
            return pltpu.make_async_copy(out_bufs[i].at[share], target, out_sems.at[i, share])

        for share in range(shares):
            for f in range(len(flat)):
                begin(f, share)

        def step(share, carry):
            for f in range(len(flat)):
                end(f, share)
            body(scalar_refs, [buf.at[share] for buf in in_bufs], [buf.at[share] for buf in out_bufs])
            for i in range(len(outs)):
                put(i, share).start()
            return carry

        lax.fori_loop(0, shares, step, 0)
        for share in range(shares):
            for i in range(len(outs)):
                put(i, share).wait()

    values, specs = [], []
    for i, n in flat:
        value = ins[i].sources[n]
        values.append(pltpu.with_memory_space_constraint(value, pltpu.HBM) if ins[i].pinned else value)
        specs.append(pl.BlockSpec(memory_space=pltpu.HBM if ins[i].pinned else pl.ANY))
    size = sum(value.size * value.dtype.itemsize for value in values + [shape for shape, _ in outs])
    buffers = [pltpu.VMEM(operand.buffer(shares), operand.dtype) for operand in ins]
    for shape, kind in outs:
        width = shape.shape[-1]
        buffers.append(pltpu.VMEM(shape.shape if kind == "lead" else (shares, shape.shape[0], width // shares), shape.dtype))
    return pl.pallas_call(
        kernel,
        in_specs=[pl.BlockSpec(memory_space=pltpu.SMEM)] * len(scalars) + specs,
        out_specs=[pl.BlockSpec(memory_space=pltpu.HBM)] * len(outs),
        out_shape=[pltpu.HBM(shape.shape, shape.dtype) for shape, _ in outs],
        scratch_shapes=buffers
        + [pltpu.SemaphoreType.DMA((len(flat), shares)), pltpu.SemaphoreType.DMA((len(outs), shares))],
        compiler_params=pltpu.CompilerParams(vmem_limit_bytes=VMEM_GRANT),
        cost_estimate=pl.CostEstimate(flops=flops, bytes_accessed=size, transcendentals=exps),
        name=name,
    )(*scalars, *values)


def array(rows, width, dtype):
    return jax.ShapeDtypeStruct((rows, width), dtype)


def swap_body(_, ins, outs):
    pair = pair_matrix()
    for place, (ref, factor) in enumerate(zip(ins, (0.5, 0.5, 1.0))):
        for i in range(2):
            level1 = mul(pair, ref[i * BLK : (i + 1) * BLK, :])
            if factor != 1.0:
                level1 = level1 * factor
            first = place * HALF + i * HALF // 2
            outs[0][first : first + HALF // 2, :] = fold(level1.astype(bf16), factor)


def swap_rows(query_vecs, key_vecs, value_vecs, groups):
    rows, width = query_vecs.shape
    out = jax.ShapeDtypeStruct((groups, 3 * HALF, width // groups), bf16)
    ins = [one(a) for a in (query_vecs, key_vecs, value_vecs)]
    return run_shares(swap_body, "swap_rows", groups, [], ins, [(out, "lead")], 6 * rows * HALF * width, 0)[0]


def rows_body(scalars, ins, outs):
    q_ref, k_ref, v_ref = ins
    q0_ref, q1_ref, cross_ref, chip_ref = outs
    reorder = reorder_matrix()
    pair = pair_matrix()
    for i in range(2):
        rows = slice(i * BLK, (i + 1) * BLK)
        q0 = mul(reorder, q_ref[rows, :]).astype(bf16)
        q0_ref[rows, :] = q0
        q1_ref[i * HALF : (i + 1) * HALF, :] = fold(q0, 0.5)
    parity = scalars[0][0]
    outer = pl.ds(pl.multiple_of(parity * BLK, BLK), BLK)
    inner = pl.ds(pl.multiple_of((1 - parity) * BLK, BLK), BLK)
    for ref, near, far in ((cross_ref, outer, inner), (chip_ref, inner, outer)):
        ref[0:BLK, :] = k_ref[near, :]
        ref[BLK : 2 * BLK, :] = v_ref[near, :]
        ref[2 * BLK : 2 * BLK + HALF, :] = (mul(pair, k_ref[far, :]) * 0.5).astype(bf16)
        ref[2 * BLK + HALF : 3 * BLK, :] = mul(pair, v_ref[far, :]).astype(bf16)


def rows_to_send(place, query_vecs, key_vecs, value_vecs, groups):
    rows, width = query_vecs.shape
    ins = [one(a) for a in (query_vecs, key_vecs, value_vecs)]
    outs = [(array(n, width, bf16), "cols") for n in (rows, rows // 2, 3 * BLK, 3 * BLK)]
    return run_shares(rows_body, "rows_to_send", groups, [place], ins, outs, 8 * rows * BLK * width, 0)


def pack(stats):
    width = HEAD_DIM // len(stats)
    lane = iota(stats[0].shape, 1)
    packed = stats[-1]
    for n in range(len(stats) - 2, -1, -1):
        packed = jnp.where(lane < (n + 1) * width, stats[n], packed)
    return packed


def unpack(packed, count):
    width = HEAD_DIM // count
    return [jnp.broadcast_to(packed[:, n * width : n * width + 1], packed.shape) for n in range(count)]


def own_body(_, ins, outs):
    q_ref, k_ref, v_ref = ins
    sum_ref, stat_ref = outs
    heads = q_ref.shape[1] // HEAD_DIM
    for i in range(2):
        rows = slice(i * BLK, (i + 1) * BLK)
        units = [(q_ref[rows, cols(head)], [(k_ref[:, cols(head)], v_ref[:, cols(head)], None)]) for head in range(heads)]
        stats = []
        for head, (top, sums) in enumerate(attend(units)):
            sum_ref[rows, cols(head)] = sums[:, :HEAD_DIM]
            stats += [top, sums[:, HEAD_DIM:]]
        stat_ref[rows, :] = pack(stats)


def own_level(q0, key_vecs, value_vecs, groups):
    rows, width = q0.shape
    ins = [one(a) for a in (q0, key_vecs, value_vecs)]
    outs = [(array(rows, width, f32), "cols"), (array(rows, groups * HEAD_DIM, f32), "cols")]
    flops = 8 * rows * BLK * width
    return run_shares(own_body, "own_level", groups, [], ins, outs, flops, 2 * rows * BLK * HEADS)


def halo_body(got_ref, right_ref, left_ref):
    count = got_ref.shape[0]
    pair = count // 2
    for which, factor in ((1, 0.5), (2, 1.0)):
        rows = slice(which * HALF, (which + 1) * HALF)
        near = (which - 1) * BLK
        far = 2 * BLK + (which - 1) * HALF
        for j in range(count):
            level2 = got_ref[j, rows, :]
            level3 = fold_chunks(level2, HALF // 2, factor)
            near_ref, far_ref = (left_ref, right_ref) if j < pair else (right_ref, left_ref)
            spot = j % pair
            near_ref[near + spot * HALF : near + (spot + 1) * HALF, :] = level2
            far_ref[far + spot * HALF // 2 : far + (spot + 1) * HALF // 2, :] = level3


def coarse_halos(got):
    shape = jax.ShapeDtypeStruct((3 * BLK, got.shape[2]), bf16)
    return pl.pallas_call(
        halo_body,
        out_shape=[shape, shape],
        compiler_params=pltpu.CompilerParams(vmem_limit_bytes=16 << 20),
        cost_estimate=pl.CostEstimate(flops=1 << 20, bytes_accessed=6 * got.size, transcendentals=0),
        name="coarse_halos",
    )(got)


def coarse_body(bias_ref, got_ref, prev_ref, next_ref, back_ref):
    count = got_ref.shape[0]
    heads = got_ref.shape[2] // HEAD_DIM
    bias_prev = bias_ref[0]
    bias_next = bias_ref[1]
    lane = iota((HALF, HEAD_DIM), 1)

    for head in range(heads):
        here = cols(head)

        def own(which, j):
            return got_ref[j, which * HALF : (which + 1) * HALF, here]

        def near(ref, which, spot):
            first = (which - 1) * BLK + spot * HALF
            return ref[first : first + HALF, here]

        def both(ref, which):
            return ref[(which - 1) * BLK : which * BLK, here]

        def far(ref, which):
            first = 2 * BLK + (which - 1) * HALF
            return ref[first : first + HALF, here]

        def near3(ref, which):
            return fold_chunks(both(ref, which), HALF // 2, 0.5 if which == 1 else 1.0)

        def joined(*rows):
            return jnp.concatenate(rows, axis=0)

        def part(pick, bias):
            return (pick(1), pick(2), bias)

        units = [
            (own(0, 0), [part(lambda w: joined(own(w, 2), own(w, 3)), None), part(lambda w: near(prev_ref, w, 0), bias_prev)]),
            (own(0, 1), [part(lambda w: both(prev_ref, w), bias_prev), part(lambda w: own(w, 3), None)]),
            (own(0, 2), [part(lambda w: both(next_ref, w), bias_next), part(lambda w: own(w, 0), None)]),
            (own(0, 3), [part(lambda w: joined(own(w, 0), own(w, 1)), None), part(lambda w: near(next_ref, w, 1), bias_next)]),
        ]
        for j, (ref, bias, other, other_bias) in enumerate(
            ((next_ref, bias_next, prev_ref, bias_prev), (prev_ref, bias_prev, next_ref, bias_next))
        ):
            query = joined(*[fold_chunks(own(0, 2 * j + n), HALF // 2, 0.5) for n in range(2)])
            units.append(
                (
                    query,
                    [part(lambda w: joined(near3(ref, w), far(ref, w)), bias), part(lambda w: far(other, w), other_bias)],
                )
            )
        found = attend(units)
        for j in range(count):
            top2, sum2 = found[j]
            top3, sum3 = found[count + j // 2]

            def spread(rows):
                first = (j % 2) * 2 * SUB
                one = rows[first : first + SUB]
                other = rows[first + SUB : first + 2 * SUB]
                return joined(one, one, other, other)

            top3 = spread(top3)
            sum3 = spread(sum3)
            top = jnp.maximum(top2, top3)
            scale2 = jnp.exp2(top2 - top)
            scale3 = jnp.exp2(top3 - top)
            values = sum2[:, :HEAD_DIM] * scale2 + sum3[:, :HEAD_DIM] * scale3
            total = sum2[:, HEAD_DIM:] * (4.0 * scale2) + sum3[:, HEAD_DIM:] * (8.0 * scale3)
            back_ref[j, 0:HALF, here] = (values / total).astype(bf16)
            level = top + jnp.log2(total)
            high = level.astype(bf16).astype(f32)
            middle = (level - high).astype(bf16).astype(f32)
            terms = jnp.where(lane == 0, high, jnp.where(lane == 1, middle, level - high - middle))
            back_ref[j, HALF : HALF + 16, here] = terms.T[0:16, :].astype(bf16)


def coarse_levels(bias, got, from_prev, from_next):
    count, _, width = got.shape
    vmem = pl.BlockSpec(memory_space=pltpu.VMEM)
    return pl.pallas_call(
        coarse_body,
        in_specs=[pl.BlockSpec(memory_space=pltpu.SMEM), vmem, vmem, vmem],
        out_specs=vmem,
        out_shape=jax.ShapeDtypeStruct((count, HALF + 16, width), bf16),
        compiler_params=pltpu.CompilerParams(vmem_limit_bytes=16 << 20),
        cost_estimate=pl.CostEstimate(flops=1 << 29, bytes_accessed=8 * got.size, transcendentals=1 << 20),
        name="coarse_levels",
    )(bias, got, from_prev, from_next)


def finish_body(scalars, ins, outs):
    q0_ref, q1_ref, own_ref, stat_ref, side_ref, back_ref = ins
    heads = q0_ref.shape[1] // HEAD_DIM
    pair = pair_matrix()
    restore = restore_matrix()
    near_keys = [(mul(pair, side_ref[i, 0:BLK, :]) * 0.5).astype(bf16) for i in range(2)]
    near_values = [mul(pair, side_ref[i, BLK : 2 * BLK, :]).astype(bf16) for i in range(2)]
    far_keys = slice(2 * BLK, 2 * BLK + HALF)
    far_values = slice(2 * BLK + HALF, 3 * BLK)
    coarse = []
    for head in range(heads):
        packed = back_ref[HALF : HALF + 16, cols(head)].astype(f32)
        packed = jnp.sum(jnp.where(iota(packed.shape, 0) < 3, packed, 0.0), axis=0, keepdims=True)
        coarse.append(jnp.broadcast_to(packed, (HEAD_DIM, HEAD_DIM)).T)
    for i in range(2):
        rows = slice(i * BLK, (i + 1) * BLK)
        spot = slice(i * HALF // 2, (i + 1) * HALF // 2)
        units = []
        for head in range(heads):
            here = cols(head)
            units.append(
                (q0_ref[rows, here], [(side_ref[i, 0:BLK, here], side_ref[i, BLK : 2 * BLK, here], scalars[1][i])])
            )
        for head in range(heads):
            here = cols(head)
            both, other = 1 - i, i
            keys = jnp.concatenate([near_keys[both][:, here], side_ref[both, far_keys, here]], axis=0)
            values = jnp.concatenate([near_values[both][:, here], side_ref[both, far_values, here]], axis=0)
            parts = [
                (keys, values, scalars[1][both]),
                (side_ref[other, far_keys, here], side_ref[other, far_values, here], scalars[1][other]),
            ]
            units.append((q1_ref[i * HALF : (i + 1) * HALF, here], parts))
        found = attend(units)
        stats = unpack(stat_ref[rows, :], 2 * heads)
        results = []
        for head in range(heads):
            here = cols(head)
            top1, sum1 = found[heads + head]
            level = twice(coarse[head][spot, :])
            top = jnp.maximum(top1, level)
            scale1 = jnp.exp2(top1 - top)
            scale2 = jnp.exp2(level - top)
            number = twice(sum1[:, :HEAD_DIM] * scale1 + twice(back_ref[spot, here].astype(f32)) * scale2)
            total = twice(sum1[:, HEAD_DIM:] * (2.0 * scale1) + scale2)
            top = twice(top)
            top0, sum0 = found[head]
            own_top, own_total = stats[2 * head], stats[2 * head + 1]
            most = jnp.maximum(jnp.maximum(top0, top), own_top)
            scale = jnp.exp2(top - most)
            scale0 = jnp.exp2(top0 - most)
            own_scale = jnp.exp2(own_top - most)
            number = number * scale + sum0[:, :HEAD_DIM] * scale0 + own_ref[rows, here] * own_scale
            total = total * scale + sum0[:, HEAD_DIM:] * scale0 + own_total * own_scale
            results.append((number / total).astype(bf16))
        outs[0][rows, :] = mul(restore, jnp.concatenate(results, axis=1)).astype(bf16)


def finish(place, bias, q0, q1, own, own_stat, outer, inner, chip, back):
    groups = back.shape[0]
    rows, width = q0.shape
    ins = [one(a) for a in (q0, q1, own, own_stat)] + [Operand([outer, inner, chip], pinned=False)]
    ins.append(one(back, "lead", pinned=False))
    outs = [(array(rows, width, bf16), "cols")]
    flops = 7 * rows * BLK * width
    return run_shares(finish_body, "finish", groups, [place, bias], ins, outs, flops, 2 * rows * BLK * HEADS)[0]


def shift(value, axis, steps):
    count = lax.axis_size(axis)
    first, last = (max(0, -steps), min(count, count - steps))
    return lax.ppermute(value, axis, [(source, source + steps) for source in range(first, last)])


def trade(value, axis, first, group=1, whole=None):
    count = lax.axis_size(axis)
    pairs = [(source, source + 1) for source in range(first, count - 1, 2)]
    if whole is not None:
        pairs = [pair for pair in pairs if (pair[1] % group != 0) == whole]
    return lax.ppermute(value, axis, pairs + [(target, source) for source, target in pairs])


def edge_bias(axis):
    place = lax.axis_index(axis)
    last = lax.axis_size(axis) - 1
    at_edge = jnp.stack([place == 0, place == last])
    return jnp.where(at_edge, very_negative, 0.0).astype(f32)


def local(query_vecs, key_vecs, value_vecs):
    groups = lax.axis_size("grp")
    assert query_vecs.shape == (2 * BLK, HEADS * HEAD_DIM) and groups == 4
    everyone = ("seq", "grp")
    index = lax.axis_index(everyone)
    odd = jnp.bitwise_and(index, 1)
    spot = lax.axis_index("grp")
    outermost = jnp.logical_or(spot == 0, spot == groups - 1)
    place = jnp.stack([odd, outermost.astype(odd.dtype)]).astype(jnp.int32)
    bias = edge_bias(everyone)
    swap = swap_rows(query_vecs, key_vecs, value_vecs, groups)
    got = lax.all_to_all(swap, "grp", split_axis=0, concat_axis=0, tiled=True)
    query_rows, swap = lax.optimization_barrier((query_vecs, swap))
    q0, q1, cross, chip = rows_to_send(place, query_rows, key_vecs, value_vecs, groups)
    own, own_stat = own_level(q0, key_vecs, value_vecs, groups)
    got, own, chip, cross = lax.optimization_barrier((got, own, chip, cross))
    coarse_right, coarse_left = coarse_halos(got)
    coarse_right, coarse_left, chip, cross = lax.optimization_barrier((coarse_right, coarse_left, chip, cross))
    coarse_prev = shift(coarse_right, "seq", 1)
    coarse_next = shift(coarse_left, "seq", -1)
    inner = trade(cross, everyone, 1, groups, True)
    chip = trade(chip, everyone, 0)
    coarse_prev, coarse_next, cross = lax.optimization_barrier((coarse_prev, coarse_next, cross))
    outer = trade(cross, everyone, 1, groups, False)
    back = coarse_levels(edge_bias("seq"), got, coarse_prev, coarse_next)
    back = lax.all_to_all(back, "grp", split_axis=0, concat_axis=0, tiled=True)
    return finish(place, bias, q0, q1, own, own_stat, outer, inner, chip, back)


def solution(mesh):
    return jax.shard_map(
        local,
        mesh=mesh,
        in_specs=(P(("seq", "grp"), None), P(("seq", "grp"), None), P(("seq", "grp"), None)),
        out_specs=P(("seq", "grp"), None),
        check_vma=False,
    )
```

```python
import functools
import functools
import functools
import functools
import functools
import functools
import functools
import math

import jax
import jax.numpy as jnp
from jax import lax
from jax.experimental import pallas as pl
from jax.experimental.pallas import tpu as pltpu
from jax.sharding import PartitionSpec as P

HEADS = 8
HEAD_DIM = 128
BLK = 256
HALF = BLK // 2
SUB = BLK // 8
LEV = 4
EXP_SCALE = math.log2(math.e) / math.sqrt(HEAD_DIM)

VMEM_GRANT = 48 << 20

very_negative = -1e30
f32 = jnp.float32
bf16 = jnp.bfloat16


def iota(shape, dim):
    return lax.broadcasted_iota(jnp.int32, shape, dim)


def bit(value, place):
    return jnp.bitwise_and(lax.shift_right_logical(value, place), 1)


def low_bits(value):
    step = SUB.bit_length() - 1
    deep = jnp.bitwise_and(value, SUB - 1)
    return 8 * deep + 4 * bit(value, step) + 2 * bit(value, step + 1) + bit(value, step + 2)


def reorder_matrix():
    return (iota((BLK, BLK), 1) == low_bits(iota((BLK, BLK), 0))).astype(bf16)


def restore_matrix():
    return (iota((BLK, BLK), 0) == low_bits(iota((BLK, BLK), 1))).astype(bf16)


def pair_matrix():
    first = low_bits(iota((HALF, BLK), 0))
    place = iota((HALF, BLK), 1)
    return jnp.logical_or(place == first, place == first + 1).astype(bf16)


def mul(left, right):
    return jnp.dot(left, right, preferred_element_type=f32)


def fold(rows, factor):
    half = rows.shape[0] // 2
    total = rows[:half].astype(f32) + rows[half:].astype(f32)
    if factor != 1.0:
        total = total * factor
    return total.astype(bf16)


def fold_chunks(rows, chunk, factor):
    count = rows.shape[0] // chunk
    return jnp.concatenate([fold(rows[i * chunk : (i + 1) * chunk], factor) for i in range(count)], axis=0)


def twice(rows):
    return jnp.concatenate([rows, rows], axis=0)


def cols(head):
    return slice(head * HEAD_DIM, (head + 1) * HEAD_DIM)


def lane_chunks(rows):
    return [rows[:, first : first + HEAD_DIM] for first in range(0, rows.shape[1], HEAD_DIM)]


def twice(rows):
    return jnp.concatenate([rows, rows], axis=0)


def cols(head):
    return slice(head * HEAD_DIM, (head + 1) * HEAD_DIM)


def lane_chunks(rows):
    return [rows[:, first : first + HEAD_DIM] for first in range(0, rows.shape[1], HEAD_DIM)]


def twice(rows):
    return jnp.concatenate([rows, rows], axis=0)


def cols(head):
    return slice(head * HEAD_DIM, (head + 1) * HEAD_DIM)


def lane_chunks(rows):
    return [rows[:, first : first + HEAD_DIM] for first in range(0, rows.shape[1], HEAD_DIM)]


def twice(rows):
    return jnp.concatenate([rows, rows], axis=0)


def cols(head):
    return slice(head * HEAD_DIM, (head + 1) * HEAD_DIM)


def lane_chunks(rows):
    return [rows[:, first : first + HEAD_DIM] for first in range(0, rows.shape[1], HEAD_DIM)]


def twice(rows):
    return jnp.concatenate([rows, rows], axis=0)


def cols(head):
    return slice(head * HEAD_DIM, (head + 1) * HEAD_DIM)


def lane_chunks(rows):
    return [rows[:, first : first + HEAD_DIM] for first in range(0, rows.shape[1], HEAD_DIM)]


def twice(rows):
    return jnp.concatenate([rows, rows], axis=0)


def cols(head):
    return slice(head * HEAD_DIM, (head + 1) * HEAD_DIM)


def lane_chunks(rows):
    return [rows[:, first : first + HEAD_DIM] for first in range(0, rows.shape[1], HEAD_DIM)]


def twice(rows):
    return jnp.concatenate([rows, rows], axis=0)


def cols(head):
    return slice(head * HEAD_DIM, (head + 1) * HEAD_DIM)


def lane_chunks(rows):
    return [rows[:, first : first + HEAD_DIM] for first in range(0, rows.shape[1], HEAD_DIM)]


def with_ones(values):
    return jnp.concatenate([values, jnp.ones_like(values)], axis=1)


def attend(units):
    scores = []
    for query, parts in units:
        chunks = []
        for keys, _, bias in parts:
            raw = lax.dot_general(query, keys, (((1,), (1,)), ((), ())), preferred_element_type=f32)
            chunks.append(lane_chunks(raw if bias is None else raw + bias))
        scores.append(chunks)
    tops = []
    for chunks in scores:
        most = functools.reduce(jnp.maximum, sum(chunks, []))
        tops.append(jnp.broadcast_to(jnp.max(most, axis=1, keepdims=True), most.shape))
    found = []
    for (_, parts), chunks, top in zip(units, scores, tops):
        total = None
        for (_, values, _), pieces in zip(parts, chunks):
            weights = [jnp.exp2((piece - top) * EXP_SCALE).astype(bf16) for piece in pieces]
            one = mul(jnp.concatenate(weights, axis=1), with_ones(values))
            total = one if total is None else total + one
        found.append((top * EXP_SCALE, total))
    return found


def share_of(ref, kind, share, shares, first_row, rows):
    if kind == "lead":
        return ref.at[share]
    width = ref.shape[1] // shares
    first = share * width
    if not isinstance(share, int):
        first = pl.multiple_of(first, HEAD_DIM)
    return ref.at[pl.ds(first_row, rows), pl.ds(first, width)]


class Operand:
    def __init__(self, sources, kind="cols", pinned=True):
        self.sources = sources
        self.kind = kind
        self.pinned = pinned
        self.rows = sources[0].shape[0]
        self.dtype = sources[0].dtype

    def buffer(self, shares):
        shape = self.sources[0].shape
        if self.kind == "lead":
            return shape
        pair = (2,) if len(self.sources) == 2 else ()
        return (shares, *pair, self.rows, shape[1] // shares)


def one(value, kind="cols", pinned=True):
    return Operand([value], kind, pinned)


def run_shares(body, name, shares, scalars, ins, outs, flops, exps):
    out_kinds = [kind for _, kind in outs]
    flat = [(i, n) for i, operand in enumerate(ins) for n in range(len(operand.sources))]

    def kernel(*refs):
        refs = list(refs)
        take = lambda count: [refs.pop(0) for _ in range(count)]
        scalar_refs, in_refs, out_refs = take(len(scalars)), take(len(flat)), take(len(outs))
        in_bufs, out_bufs, (in_sems, out_sems) = take(len(ins)), take(len(outs)), take(2)

        def bring(f, share):
            i, n = flat[f]
            operand = ins[i]
            source = share_of(in_refs[f], operand.kind, share, shares, 0, operand.rows)
            target = in_bufs[i].at[share]
            if len(operand.sources) == 2:
                odd = scalar_refs[0][0]
                target = target.at[1 - odd if n == 1 else odd]
            return pltpu.make_async_copy(source, target, in_sems.at[f, share])

        def put(i, share):
            rows = out_refs[i].shape[0]
            target = share_of(out_refs[i], out_kinds[i], share, shares, 0, rows)
            return pltpu.make_async_copy(out_bufs[i].at[share], target, out_sems.at[i, share])

        for share in range(shares):
            for f in range(len(flat)):
                bring(f, share).start()

        def step(share, carry):
            for f in range(len(flat)):
                bring(f, share).wait()
            body(scalar_refs, [buf.at[share] for buf in in_bufs], [buf.at[share] for buf in out_bufs])
            for i in range(len(outs)):
                put(i, share).start()
            return carry

        lax.fori_loop(0, shares, step, 0)
        for share in range(shares):
            for i in range(len(outs)):
                put(i, share).wait()

    values, specs = [], []
    for i, n in flat:
        value = ins[i].sources[n]
        values.append(pltpu.with_memory_space_constraint(value, pltpu.HBM) if ins[i].pinned else value)
        specs.append(pl.BlockSpec(memory_space=pltpu.HBM if ins[i].pinned else pl.ANY))
    size = sum(value.size * value.dtype.itemsize for value in values + [shape for shape, _ in outs])
    buffers = [pltpu.VMEM(operand.buffer(shares), operand.dtype) for operand in ins]
    for shape, kind in outs:
        width = shape.shape[-1]
        buffers.append(pltpu.VMEM(shape.shape if kind == "lead" else (shares, shape.shape[0], width // shares), shape.dtype))
    return pl.pallas_call(
        kernel,
        in_specs=[pl.BlockSpec(memory_space=pltpu.SMEM)] * len(scalars) + specs,
        out_specs=[pl.BlockSpec(memory_space=pltpu.HBM)] * len(outs),
        out_shape=[pltpu.HBM(shape.shape, shape.dtype) for shape, _ in outs],
        scratch_shapes=buffers
        + [pltpu.SemaphoreType.DMA((len(flat), shares)), pltpu.SemaphoreType.DMA((len(outs), shares))],
        compiler_params=pltpu.CompilerParams(vmem_limit_bytes=VMEM_GRANT),
        cost_estimate=pl.CostEstimate(flops=flops, bytes_accessed=size, transcendentals=exps),
        name=name,
    )(*scalars, *values)


def array(rows, width, dtype):
    return jax.ShapeDtypeStruct((rows, width), dtype)


def swap_body(_, ins, outs):
    pair = pair_matrix()
    for place, (ref, factor) in enumerate(zip(ins, (0.5, 0.5, 1.0))):
        for i in range(2):
            level1 = mul(pair, ref[i * BLK : (i + 1) * BLK, :])
            if factor != 1.0:
                level1 = level1 * factor
            first = place * HALF + i * HALF // 2
            outs[0][first : first + HALF // 2, :] = fold(level1.astype(bf16), factor)


def swap_rows(query_vecs, key_vecs, value_vecs, groups):
    rows, width = query_vecs.shape
    out = jax.ShapeDtypeStruct((groups, 3 * HALF, width // groups), bf16)
    ins = [one(a) for a in (query_vecs, key_vecs, value_vecs)]
    return run_shares(swap_body, "swap_rows", groups, [], ins, [(out, "lead")], 6 * rows * HALF * width, 0)[0]


def rows_body(scalars, ins, outs):
    q_ref, k_ref, v_ref = ins
    q0_ref, q1_ref, cross_ref, chip_ref = outs
    reorder = reorder_matrix()
    pair = pair_matrix()
    for i in range(2):
        rows = slice(i * BLK, (i + 1) * BLK)
        q0 = mul(reorder, q_ref[rows, :]).astype(bf16)
        q0_ref[rows, :] = q0
        q1_ref[i * HALF : (i + 1) * HALF, :] = fold(q0, 0.5)
    parity = scalars[0][0]
    outer = pl.ds(pl.multiple_of(parity * BLK, BLK), BLK)
    inner = pl.ds(pl.multiple_of((1 - parity) * BLK, BLK), BLK)
    for ref, near, far in ((cross_ref, outer, inner), (chip_ref, inner, outer)):
        ref[0:BLK, :] = k_ref[near, :]
        ref[BLK : 2 * BLK, :] = v_ref[near, :]
        ref[2 * BLK : 2 * BLK + HALF, :] = (mul(pair, k_ref[far, :]) * 0.5).astype(bf16)
        ref[2 * BLK + HALF : 3 * BLK, :] = mul(pair, v_ref[far, :]).astype(bf16)


def rows_to_send(place, query_vecs, key_vecs, value_vecs, groups):
    rows, width = query_vecs.shape
    ins = [one(a) for a in (query_vecs, key_vecs, value_vecs)]
    outs = [(array(n, width, bf16), "cols") for n in (rows, rows // 2, 3 * BLK, 3 * BLK)]
    return run_shares(rows_body, "rows_to_send", groups, [place], ins, outs, 8 * rows * BLK * width, 0)


def pack(stats):
    width = HEAD_DIM // len(stats)
    lane = iota(stats[0].shape, 1)
    packed = stats[-1]
    for n in range(len(stats) - 2, -1, -1):
        packed = jnp.where(lane < (n + 1) * width, stats[n], packed)
    return packed


def unpack(packed, count):
    width = HEAD_DIM // count
    return [jnp.broadcast_to(packed[:, n * width : n * width + 1], packed.shape) for n in range(count)]


def own_body(_, ins, outs):
    q_ref, k_ref, v_ref = ins
    sum_ref, stat_ref = outs
    heads = q_ref.shape[1] // HEAD_DIM
    for i in range(2):
        rows = slice(i * BLK, (i + 1) * BLK)
        units = [(q_ref[rows, cols(head)], [(k_ref[:, cols(head)], v_ref[:, cols(head)], None)]) for head in range(heads)]
        stats = []
        for head, (top, sums) in enumerate(attend(units)):
            sum_ref[rows, cols(head)] = sums[:, :HEAD_DIM]
            stats += [top, sums[:, HEAD_DIM:]]
        stat_ref[rows, :] = pack(stats)


def own_level(q0, key_vecs, value_vecs, groups):
    rows, width = q0.shape
    ins = [one(a) for a in (q0, key_vecs, value_vecs)]
    outs = [(array(rows, width, f32), "cols"), (array(rows, groups * HEAD_DIM, f32), "cols")]
    flops = 8 * rows * BLK * width
    return run_shares(own_body, "own_level", groups, [], ins, outs, flops, 2 * rows * BLK * HEADS)


def halo_body(got_ref, right_ref, left_ref):
    count = got_ref.shape[0]
    pair = count // 2
    for which, factor in ((1, 0.5), (2, 1.0)):
        rows = slice(which * HALF, (which + 1) * HALF)
        near = (which - 1) * BLK
        far = 2 * BLK + (which - 1) * HALF
        for j in range(count):
            level2 = got_ref[j, rows, :]
            level3 = fold_chunks(level2, HALF // 2, factor)
            near_ref, far_ref = (left_ref, right_ref) if j < pair else (right_ref, left_ref)
            spot = j % pair
            near_ref[near + spot * HALF : near + (spot + 1) * HALF, :] = level2
            far_ref[far + spot * HALF // 2 : far + (spot + 1) * HALF // 2, :] = level3


def coarse_halos(got):
    shape = jax.ShapeDtypeStruct((3 * BLK, got.shape[2]), bf16)
    return pl.pallas_call(
        halo_body,
        out_shape=[shape, shape],
        compiler_params=pltpu.CompilerParams(vmem_limit_bytes=16 << 20),
        cost_estimate=pl.CostEstimate(flops=1 << 20, bytes_accessed=6 * got.size, transcendentals=0),
        name="coarse_halos",
    )(got)


def coarse_body(bias_ref, got_ref, prev_ref, next_ref, back_ref):
    count = got_ref.shape[0]
    heads = got_ref.shape[2] // HEAD_DIM
    bias_prev = bias_ref[0]
    bias_next = bias_ref[1]
    lane = iota((HALF, HEAD_DIM), 1)

    for head in range(heads):
        here = cols(head)

        def own(which, j):
            return got_ref[j, which * HALF : (which + 1) * HALF, here]

        def near(ref, which, spot):
            first = (which - 1) * BLK + spot * HALF
            return ref[first : first + HALF, here]

        def both(ref, which):
            return ref[(which - 1) * BLK : which * BLK, here]

        def far(ref, which):
            first = 2 * BLK + (which - 1) * HALF
            return ref[first : first + HALF, here]

        def near3(ref, which):
            return fold_chunks(both(ref, which), HALF // 2, 0.5 if which == 1 else 1.0)

        def joined(*rows):
            return jnp.concatenate(rows, axis=0)

        def part(pick, bias):
            return (pick(1), pick(2), bias)

        units = [
            (own(0, 0), [part(lambda w: joined(own(w, 2), own(w, 3)), None), part(lambda w: near(prev_ref, w, 0), bias_prev)]),
            (own(0, 1), [part(lambda w: both(prev_ref, w), bias_prev), part(lambda w: own(w, 3), None)]),
            (own(0, 2), [part(lambda w: both(next_ref, w), bias_next), part(lambda w: own(w, 0), None)]),
            (own(0, 3), [part(lambda w: joined(own(w, 0), own(w, 1)), None), part(lambda w: near(next_ref, w, 1), bias_next)]),
        ]
        for j, (ref, bias, other, other_bias) in enumerate(
            ((next_ref, bias_next, prev_ref, bias_prev), (prev_ref, bias_prev, next_ref, bias_next))
        ):
            query = joined(*[fold_chunks(own(0, 2 * j + n), HALF // 2, 0.5) for n in range(2)])
            units.append(
                (
                    query,
                    [part(lambda w: joined(near3(ref, w), far(ref, w)), bias), part(lambda w: far(other, w), other_bias)],
                )
            )
        found = attend(units)
        for j in range(count):
            top2, sum2 = found[j]
            top3, sum3 = found[count + j // 2]

            def spread(rows):
                first = (j % 2) * 2 * SUB
                one = rows[first : first + SUB]
                other = rows[first + SUB : first + 2 * SUB]
                return joined(one, one, other, other)

            top3 = spread(top3)
            sum3 = spread(sum3)
            top = jnp.maximum(top2, top3)
            scale2 = jnp.exp2(top2 - top)
            scale3 = jnp.exp2(top3 - top)
            values = sum2[:, :HEAD_DIM] * scale2 + sum3[:, :HEAD_DIM] * scale3
            total = sum2[:, HEAD_DIM:] * (4.0 * scale2) + sum3[:, HEAD_DIM:] * (8.0 * scale3)
            back_ref[j, 0:HALF, here] = (values / total).astype(bf16)
            level = top + jnp.log2(total)
            high = level.astype(bf16).astype(f32)
            middle = (level - high).astype(bf16).astype(f32)
            terms = jnp.where(lane == 0, high, jnp.where(lane == 1, middle, level - high - middle))
            back_ref[j, HALF : HALF + 16, here] = terms.T[0:16, :].astype(bf16)


def coarse_levels(bias, got, from_prev, from_next):
    count, _, width = got.shape
    vmem = pl.BlockSpec(memory_space=pltpu.VMEM)
    return pl.pallas_call(
        coarse_body,
        in_specs=[pl.BlockSpec(memory_space=pltpu.SMEM), vmem, vmem, vmem],
        out_specs=vmem,
        out_shape=jax.ShapeDtypeStruct((count, HALF + 16, width), bf16),
        compiler_params=pltpu.CompilerParams(vmem_limit_bytes=16 << 20),
        cost_estimate=pl.CostEstimate(flops=1 << 29, bytes_accessed=8 * got.size, transcendentals=1 << 20),
        name="coarse_levels",
    )(bias, got, from_prev, from_next)


def finish_body(scalars, ins, outs):
    q0_ref, q1_ref, own_ref, stat_ref, side_ref, back_ref = ins
    heads = q0_ref.shape[1] // HEAD_DIM
    pair = pair_matrix()
    restore = restore_matrix()
    near_keys = [(mul(pair, side_ref[i, 0:BLK, :]) * 0.5).astype(bf16) for i in range(2)]
    near_values = [mul(pair, side_ref[i, BLK : 2 * BLK, :]).astype(bf16) for i in range(2)]
    far_keys = slice(2 * BLK, 2 * BLK + HALF)
    far_values = slice(2 * BLK + HALF, 3 * BLK)
    coarse = []
    for head in range(heads):
        packed = back_ref[HALF : HALF + 16, cols(head)].astype(f32)
        packed = jnp.sum(jnp.where(iota(packed.shape, 0) < 3, packed, 0.0), axis=0, keepdims=True)
        coarse.append(jnp.broadcast_to(packed, (HEAD_DIM, HEAD_DIM)).T)
    for i in range(2):
        rows = slice(i * BLK, (i + 1) * BLK)
        spot = slice(i * HALF // 2, (i + 1) * HALF // 2)
        units = []
        for head in range(heads):
            here = cols(head)
            units.append(
                (q0_ref[rows, here], [(side_ref[i, 0:BLK, here], side_ref[i, BLK : 2 * BLK, here], scalars[1][i])])
            )
        for head in range(heads):
            here = cols(head)
            both, other = 1 - i, i
            keys = jnp.concatenate([near_keys[both][:, here], side_ref[both, far_keys, here]], axis=0)
            values = jnp.concatenate([near_values[both][:, here], side_ref[both, far_values, here]], axis=0)
            parts = [
                (keys, values, scalars[1][both]),
                (side_ref[other, far_keys, here], side_ref[other, far_values, here], scalars[1][other]),
            ]
            units.append((q1_ref[i * HALF : (i + 1) * HALF, here], parts))
        found = attend(units)
        stats = unpack(stat_ref[rows, :], 2 * heads)
        results = []
        for head in range(heads):
            here = cols(head)
            top1, sum1 = found[heads + head]
            level = twice(coarse[head][spot, :])
            top = jnp.maximum(top1, level)
            scale1 = jnp.exp2(top1 - top)
            scale2 = jnp.exp2(level - top)
            number = twice(sum1[:, :HEAD_DIM] * scale1 + twice(back_ref[spot, here].astype(f32)) * scale2)
            total = twice(sum1[:, HEAD_DIM:] * (2.0 * scale1) + scale2)
            top = twice(top)
            top0, sum0 = found[head]
            own_top, own_total = stats[2 * head], stats[2 * head + 1]
            most = jnp.maximum(jnp.maximum(top0, top), own_top)
            scale = jnp.exp2(top - most)
            scale0 = jnp.exp2(top0 - most)
            own_scale = jnp.exp2(own_top - most)
            number = number * scale + sum0[:, :HEAD_DIM] * scale0 + own_ref[rows, here] * own_scale
            total = total * scale + sum0[:, HEAD_DIM:] * scale0 + own_total * own_scale
            results.append((number / total).astype(bf16))
        outs[0][rows, :] = mul(restore, jnp.concatenate(results, axis=1)).astype(bf16)


def finish(place, bias, q0, q1, own, own_stat, cross, chip, back):
    groups = back.shape[0]
    rows, width = q0.shape
    ins = [one(a) for a in (q0, q1, own, own_stat)] + [Operand([cross, chip], pinned=False)]
    ins.append(one(back, "lead", pinned=False))
    outs = [(array(rows, width, bf16), "cols")]
    flops = 7 * rows * BLK * width
    return run_shares(finish_body, "finish", groups, [place, bias], ins, outs, flops, 2 * rows * BLK * HEADS)[0]


def shift(value, axis, steps):
    count = lax.axis_size(axis)
    first, last = (max(0, -steps), min(count, count - steps))
    return lax.ppermute(value, axis, [(source, source + steps) for source in range(first, last)])


def trade(value, axis, first):
    count = lax.axis_size(axis)
    pairs = [(source, source + 1) for source in range(first, count - 1, 2)]
    return lax.ppermute(value, axis, pairs + [(target, source) for source, target in pairs])


def edge_bias(axis):
    place = lax.axis_index(axis)
    last = lax.axis_size(axis) - 1
    at_edge = jnp.stack([place == 0, place == last])
    return jnp.where(at_edge, very_negative, 0.0).astype(f32)


def local(query_vecs, key_vecs, value_vecs):
    groups = lax.axis_size("grp")
    assert query_vecs.shape == (2 * BLK, HEADS * HEAD_DIM) and groups == 4
    everyone = ("seq", "grp")
    place = jnp.bitwise_and(lax.axis_index(everyone), 1).astype(jnp.int32).reshape(1)
    bias = edge_bias(everyone)
    swap = swap_rows(query_vecs, key_vecs, value_vecs, groups)
    got = lax.all_to_all(swap, "grp", split_axis=0, concat_axis=0, tiled=True)
    query_rows, swap = lax.optimization_barrier((query_vecs, swap))
    q0, q1, cross, chip = rows_to_send(place, query_rows, key_vecs, value_vecs, groups)
    own, own_stat = own_level(q0, key_vecs, value_vecs, groups)
    got, own, chip, cross = lax.optimization_barrier((got, own, chip, cross))
    coarse_right, coarse_left = coarse_halos(got)
    coarse_right, coarse_left, chip, cross = lax.optimization_barrier((coarse_right, coarse_left, chip, cross))
    coarse_prev = shift(coarse_right, "seq", 1)
    coarse_next = shift(coarse_left, "seq", -1)
    chip = trade(chip, everyone, 0)
    cross = trade(cross, everyone, 1)
    back = coarse_levels(edge_bias("seq"), got, coarse_prev, coarse_next)
    back = lax.all_to_all(back, "grp", split_axis=0, concat_axis=0, tiled=True)
    return finish(place, bias, q0, q1, own, own_stat, cross, chip, back)


def solution(mesh):
    return jax.shard_map(
        local,
        mesh=mesh,
        in_specs=(P(("seq", "grp"), None), P(("seq", "grp"), None), P(("seq", "grp"), None)),
        out_specs=P(("seq", "grp"), None),
        check_vma=False,
    )
```

```python
import functools
import functools
import functools
import functools
import functools
import functools
import functools
import functools
import functools
import math

import jax
import jax.numpy as jnp
from jax import lax
from jax.experimental import pallas as pl
from jax.experimental.pallas import tpu as pltpu
from jax.sharding import PartitionSpec as P

HEADS = 8
HEAD_DIM = 128
BLK = 256
HALF = BLK // 2
SUB = BLK // 8
LEV = 4
EXP_SCALE = math.log2(math.e) / math.sqrt(HEAD_DIM)

VMEM_GRANT = 48 << 20

very_negative = -1e30
f32 = jnp.float32
bf16 = jnp.bfloat16


def iota(shape, dim):
    return lax.broadcasted_iota(jnp.int32, shape, dim)


def bit(value, place):
    return jnp.bitwise_and(lax.shift_right_logical(value, place), 1)


def low_bits(value):
    step = SUB.bit_length() - 1
    deep = jnp.bitwise_and(value, SUB - 1)
    return 8 * deep + 4 * bit(value, step) + 2 * bit(value, step + 1) + bit(value, step + 2)


def reorder_matrix():
    return (iota((BLK, BLK), 1) == low_bits(iota((BLK, BLK), 0))).astype(bf16)


def restore_matrix():
    return (iota((BLK, BLK), 0) == low_bits(iota((BLK, BLK), 1))).astype(bf16)


def pair_matrix():
    first = low_bits(iota((HALF, BLK), 0))
    place = iota((HALF, BLK), 1)
    return jnp.logical_or(place == first, place == first + 1).astype(bf16)


def mul(left, right):
    return jnp.dot(left, right, preferred_element_type=f32)


def fold(rows, factor):
    half = rows.shape[0] // 2
    total = rows[:half].astype(f32) + rows[half:].astype(f32)
    if factor != 1.0:
        total = total * factor
    return total.astype(bf16)


def fold_chunks(rows, chunk, factor):
    count = rows.shape[0] // chunk
    return jnp.concatenate([fold(rows[i * chunk : (i + 1) * chunk], factor) for i in range(count)], axis=0)


def twice(rows):
    return jnp.concatenate([rows, rows], axis=0)


def cols(head):
    return slice(head * HEAD_DIM, (head + 1) * HEAD_DIM)


def lane_chunks(rows):
    return [rows[:, first : first + HEAD_DIM] for first in range(0, rows.shape[1], HEAD_DIM)]


def twice(rows):
    return jnp.concatenate([rows, rows], axis=0)


def cols(head):
    return slice(head * HEAD_DIM, (head + 1) * HEAD_DIM)


def lane_chunks(rows):
    return [rows[:, first : first + HEAD_DIM] for first in range(0, rows.shape[1], HEAD_DIM)]


def twice(rows):
    return jnp.concatenate([rows, rows], axis=0)


def cols(head):
    return slice(head * HEAD_DIM, (head + 1) * HEAD_DIM)


def lane_chunks(rows):
    return [rows[:, first : first + HEAD_DIM] for first in range(0, rows.shape[1], HEAD_DIM)]


def twice(rows):
    return jnp.concatenate([rows, rows], axis=0)


def cols(head):
    return slice(head * HEAD_DIM, (head + 1) * HEAD_DIM)


def lane_chunks(rows):
    return [rows[:, first : first + HEAD_DIM] for first in range(0, rows.shape[1], HEAD_DIM)]


def twice(rows):
    return jnp.concatenate([rows, rows], axis=0)


def cols(head):
    return slice(head * HEAD_DIM, (head + 1) * HEAD_DIM)


def lane_chunks(rows):
    return [rows[:, first : first + HEAD_DIM] for first in range(0, rows.shape[1], HEAD_DIM)]


def twice(rows):
    return jnp.concatenate([rows, rows], axis=0)


def cols(head):
    return slice(head * HEAD_DIM, (head + 1) * HEAD_DIM)


def lane_chunks(rows):
    return [rows[:, first : first + HEAD_DIM] for first in range(0, rows.shape[1], HEAD_DIM)]


def twice(rows):
    return jnp.concatenate([rows, rows], axis=0)


def cols(head):
    return slice(head * HEAD_DIM, (head + 1) * HEAD_DIM)


def lane_chunks(rows):
    return [rows[:, first : first + HEAD_DIM] for first in range(0, rows.shape[1], HEAD_DIM)]


def twice(rows):
    return jnp.concatenate([rows, rows], axis=0)


def cols(head):
    return slice(head * HEAD_DIM, (head + 1) * HEAD_DIM)


COARSE_FLOPS = 1 << 29


def lane_chunks(rows):
    return [rows[:, first : first + HEAD_DIM] for first in range(0, rows.shape[1], HEAD_DIM)]


def twice(rows):
    return jnp.concatenate([rows, rows], axis=0)


def cols(head):
    return slice(head * HEAD_DIM, (head + 1) * HEAD_DIM)


COARSE_FLOPS = 1 << 36


def lane_chunks(rows):
    return [rows[:, first : first + HEAD_DIM] for first in range(0, rows.shape[1], HEAD_DIM)]


def with_ones(values):
    return jnp.concatenate([values, jnp.ones_like(values)], axis=1)


def attend(units):
    scores = []
    for query, parts in units:
        chunks = []
        for keys, _, bias in parts:
            raw = lax.dot_general(query, keys, (((1,), (1,)), ((), ())), preferred_element_type=f32)
            chunks.append(lane_chunks(raw if bias is None else raw + bias))
        scores.append(chunks)
    tops = []
    for chunks in scores:
        most = functools.reduce(jnp.maximum, sum(chunks, []))
        tops.append(jnp.broadcast_to(jnp.max(most, axis=1, keepdims=True), most.shape))
    found = []
    for (_, parts), chunks, top in zip(units, scores, tops):
        total = None
        for (_, values, _), pieces in zip(parts, chunks):
            weights = [jnp.exp2((piece - top) * EXP_SCALE).astype(bf16) for piece in pieces]
            one = mul(jnp.concatenate(weights, axis=1), with_ones(values))
            total = one if total is None else total + one
        found.append((top * EXP_SCALE, total))
    return found


def share_of(ref, kind, share, shares):
    if kind == "lead":
        return ref.at[share]
    width = ref.shape[1] // shares
    first = share * width
    if not isinstance(share, int):
        first = pl.multiple_of(first, HEAD_DIM)
    return ref.at[:, pl.ds(first, width)]


class Operand:
    def __init__(self, value, kind, pinned):
        self.value = value
        self.kind = kind
        self.pinned = pinned

    def buffer(self, shares):
        shape = self.value.shape
        return shape if self.kind == "lead" else (shares, shape[0], shape[1] // shares)


def one(value, kind="cols", pinned=True):
    return Operand(value, kind, pinned)


def run_shares(body, name, shares, scalars, ins, outs, flops, exps):
    out_kinds = [kind for _, kind in outs]

    def kernel(*refs):
        refs = list(refs)
        take = lambda count: [refs.pop(0) for _ in range(count)]
        scalar_refs, in_refs, out_refs = take(len(scalars)), take(len(ins)), take(len(outs))
        in_bufs, out_bufs, (in_sems, out_sems) = take(len(ins)), take(len(outs)), take(2)

        def bring(i, share):
            source = share_of(in_refs[i], ins[i].kind, share, shares)
            return pltpu.make_async_copy(source, in_bufs[i].at[share], in_sems.at[i, share])

        def put(i, share):
            target = share_of(out_refs[i], out_kinds[i], share, shares)
            return pltpu.make_async_copy(out_bufs[i].at[share], target, out_sems.at[i, share])

        for share in range(shares):
            for i in range(len(ins)):
                bring(i, share).start()

        def step(share, carry):
            for i in range(len(ins)):
                bring(i, share).wait()
            body(scalar_refs, [buf.at[share] for buf in in_bufs], [buf.at[share] for buf in out_bufs])
            for i in range(len(outs)):
                put(i, share).start()
            return carry

        lax.fori_loop(0, shares, step, 0)
        for share in range(shares):
            for i in range(len(outs)):
                put(i, share).wait()

    values, specs = [], []
    for operand in ins:
        value = operand.value
        values.append(pltpu.with_memory_space_constraint(value, pltpu.HBM) if operand.pinned else value)
        specs.append(pl.BlockSpec(memory_space=pltpu.HBM if operand.pinned else pl.ANY))
    size = sum(value.size * value.dtype.itemsize for value in values + [shape for shape, _ in outs])
    buffers = [pltpu.VMEM(operand.buffer(shares), operand.value.dtype) for operand in ins]
    for shape, kind in outs:
        width = shape.shape[-1]
        buffers.append(pltpu.VMEM(shape.shape if kind == "lead" else (shares, shape.shape[0], width // shares), shape.dtype))
    return pl.pallas_call(
        kernel,
        in_specs=[pl.BlockSpec(memory_space=pltpu.SMEM)] * len(scalars) + specs,
        out_specs=[pl.BlockSpec(memory_space=pltpu.HBM)] * len(outs),
        out_shape=[pltpu.HBM(shape.shape, shape.dtype) for shape, _ in outs],
        scratch_shapes=buffers
        + [pltpu.SemaphoreType.DMA((len(ins), shares)), pltpu.SemaphoreType.DMA((len(outs), shares))],
        compiler_params=pltpu.CompilerParams(vmem_limit_bytes=VMEM_GRANT),
        cost_estimate=pl.CostEstimate(flops=flops, bytes_accessed=size, transcendentals=exps),
        name=name,
    )(*scalars, *values)


def array(rows, width, dtype):
    return jax.ShapeDtypeStruct((rows, width), dtype)


def swap_body(_, ins, outs):
    pair = pair_matrix()
    for place, (ref, factor) in enumerate(zip(ins, (0.5, 0.5, 1.0))):
        for i in range(2):
            level1 = mul(pair, ref[i * BLK : (i + 1) * BLK, :])
            if factor != 1.0:
                level1 = level1 * factor
            first = place * HALF + i * HALF // 2
            outs[0][first : first + HALF // 2, :] = fold(level1.astype(bf16), factor)


def swap_rows(query_vecs, key_vecs, value_vecs, groups):
    rows, width = query_vecs.shape
    out = jax.ShapeDtypeStruct((groups, 3 * HALF, width // groups), bf16)
    ins = [one(a) for a in (query_vecs, key_vecs, value_vecs)]
    return run_shares(swap_body, "swap_rows", groups, [], ins, [(out, "lead")], 6 * rows * HALF * width, 0)[0]


def rows_body(scalars, ins, outs):
    q_ref, k_ref, v_ref = ins
    q0_ref, q1_ref, cross_ref, chip_ref = outs
    reorder = reorder_matrix()
    pair = pair_matrix()
    for i in range(2):
        rows = slice(i * BLK, (i + 1) * BLK)
        q0 = mul(reorder, q_ref[rows, :]).astype(bf16)
        q0_ref[rows, :] = q0
        q1_ref[i * HALF : (i + 1) * HALF, :] = fold(q0, 0.5)
    parity = scalars[0][0]
    outer = pl.ds(pl.multiple_of(parity * BLK, BLK), BLK)
    inner = pl.ds(pl.multiple_of((1 - parity) * BLK, BLK), BLK)
    for ref, near, far in ((cross_ref, outer, inner), (chip_ref, inner, outer)):
        ref[0:BLK, :] = k_ref[near, :]
        ref[BLK : 2 * BLK, :] = v_ref[near, :]
        ref[2 * BLK : 2 * BLK + HALF, :] = (mul(pair, k_ref[far, :]) * 0.5).astype(bf16)
        ref[2 * BLK + HALF : 3 * BLK, :] = mul(pair, v_ref[far, :]).astype(bf16)


def rows_to_send(place, query_vecs, key_vecs, value_vecs, groups):
    rows, width = query_vecs.shape
    ins = [one(a) for a in (query_vecs, key_vecs, value_vecs)]
    outs = [(array(n, width, bf16), "cols") for n in (rows, rows // 2, 3 * BLK, 3 * BLK)]
    return run_shares(rows_body, "rows_to_send", groups, [place], ins, outs, 8 * rows * BLK * width, 0)


def pack(stats):
    width = HEAD_DIM // len(stats)
    lane = iota(stats[0].shape, 1)
    packed = stats[-1]
    for n in range(len(stats) - 2, -1, -1):
        packed = jnp.where(lane < (n + 1) * width, stats[n], packed)
    return packed


def unpack(packed, count):
    width = HEAD_DIM // count
    return [jnp.broadcast_to(packed[:, n * width : n * width + 1], packed.shape) for n in range(count)]


def own_body(_, ins, outs):
    q_ref, k_ref, v_ref = ins
    sum_ref, stat_ref = outs
    heads = q_ref.shape[1] // HEAD_DIM
    for i in range(2):
        rows = slice(i * BLK, (i + 1) * BLK)
        units = [(q_ref[rows, cols(head)], [(k_ref[:, cols(head)], v_ref[:, cols(head)], None)]) for head in range(heads)]
        stats = []
        for head, (top, sums) in enumerate(attend(units)):
            sum_ref[rows, cols(head)] = sums[:, :HEAD_DIM]
            stats += [top, sums[:, HEAD_DIM:]]
        stat_ref[rows, :] = pack(stats)


def own_level(q0, key_vecs, value_vecs, groups):
    rows, width = q0.shape
    ins = [one(a) for a in (q0, key_vecs, value_vecs)]
    outs = [(array(rows, width, f32), "cols"), (array(rows, groups * HEAD_DIM, f32), "cols")]
    flops = 8 * rows * BLK * width
    return run_shares(own_body, "own_level", groups, [], ins, outs, flops, 2 * rows * BLK * HEADS)


def halo_body(got_ref, right_ref, left_ref):
    count = got_ref.shape[0]
    pair = count // 2
    for which, factor in ((1, 0.5), (2, 1.0)):
        rows = slice(which * HALF, (which + 1) * HALF)
        near = (which - 1) * BLK
        far = 2 * BLK + (which - 1) * HALF
        for j in range(count):
            level2 = got_ref[j, rows, :]
            level3 = fold_chunks(level2, HALF // 2, factor)
            near_ref, far_ref = (left_ref, right_ref) if j < pair else (right_ref, left_ref)
            spot = j % pair
            near_ref[near + spot * HALF : near + (spot + 1) * HALF, :] = level2
            far_ref[far + spot * HALF // 2 : far + (spot + 1) * HALF // 2, :] = level3


def coarse_halos(got):
    shape = jax.ShapeDtypeStruct((3 * BLK, got.shape[2]), bf16)
    return pl.pallas_call(
        halo_body,
        out_shape=[shape, shape],
        compiler_params=pltpu.CompilerParams(vmem_limit_bytes=16 << 20),
        cost_estimate=pl.CostEstimate(flops=1 << 20, bytes_accessed=6 * got.size, transcendentals=0),
        name="coarse_halos",
    )(got)


def coarse_body(bias_ref, got_ref, prev_ref, next_ref, back_ref):
    count = got_ref.shape[0]
    heads = got_ref.shape[2] // HEAD_DIM
    bias_prev = bias_ref[0]
    bias_next = bias_ref[1]
    lane = iota((HALF, HEAD_DIM), 1)

    for head in range(heads):
        here = cols(head)

        def own(which, j):
            return got_ref[j, which * HALF : (which + 1) * HALF, here]

        def near(ref, which, spot):
            first = (which - 1) * BLK + spot * HALF
            return ref[first : first + HALF, here]

        def both(ref, which):
            return ref[(which - 1) * BLK : which * BLK, here]

        def far(ref, which):
            first = 2 * BLK + (which - 1) * HALF
            return ref[first : first + HALF, here]

        def near3(ref, which):
            return fold_chunks(both(ref, which), HALF // 2, 0.5 if which == 1 else 1.0)

        def joined(*rows):
            return jnp.concatenate(rows, axis=0)

        def part(pick, bias):
            return (pick(1), pick(2), bias)

        units = [
            (own(0, 0), [part(lambda w: joined(own(w, 2), own(w, 3)), None), part(lambda w: near(prev_ref, w, 0), bias_prev)]),
            (own(0, 1), [part(lambda w: both(prev_ref, w), bias_prev), part(lambda w: own(w, 3), None)]),
            (own(0, 2), [part(lambda w: both(next_ref, w), bias_next), part(lambda w: own(w, 0), None)]),
            (own(0, 3), [part(lambda w: joined(own(w, 0), own(w, 1)), None), part(lambda w: near(next_ref, w, 1), bias_next)]),
        ]
        for j, (ref, bias, other, other_bias) in enumerate(
            ((next_ref, bias_next, prev_ref, bias_prev), (prev_ref, bias_prev, next_ref, bias_next))
        ):
            query = joined(*[fold_chunks(own(0, 2 * j + n), HALF // 2, 0.5) for n in range(2)])
            units.append(
                (
                    query,
                    [part(lambda w: joined(near3(ref, w), far(ref, w)), bias), part(lambda w: far(other, w), other_bias)],
                )
            )
        found = attend(units)
        for j in range(count):
            top2, sum2 = found[j]
            top3, sum3 = found[count + j // 2]

            def spread(rows):
                first = (j % 2) * 2 * SUB
                one = rows[first : first + SUB]
                other = rows[first + SUB : first + 2 * SUB]
                return joined(one, one, other, other)

            top3 = spread(top3)
            sum3 = spread(sum3)
            top = jnp.maximum(top2, top3)
            scale2 = jnp.exp2(top2 - top)
            scale3 = jnp.exp2(top3 - top)
            values = sum2[:, :HEAD_DIM] * scale2 + sum3[:, :HEAD_DIM] * scale3
            total = sum2[:, HEAD_DIM:] * (4.0 * scale2) + sum3[:, HEAD_DIM:] * (8.0 * scale3)
            back_ref[j, 0:HALF, here] = (values / total).astype(bf16)
            level = top + jnp.log2(total)
            high = level.astype(bf16).astype(f32)
            middle = (level - high).astype(bf16).astype(f32)
            terms = jnp.where(lane == 0, high, jnp.where(lane == 1, middle, level - high - middle))
            back_ref[j, HALF : HALF + 16, here] = terms.T[0:16, :].astype(bf16)


def coarse_levels(bias, got, from_prev, from_next):
    count, _, width = got.shape
    vmem = pl.BlockSpec(memory_space=pltpu.VMEM)
    return pl.pallas_call(
        coarse_body,
        in_specs=[pl.BlockSpec(memory_space=pltpu.SMEM), vmem, vmem, vmem],
        out_specs=vmem,
        out_shape=jax.ShapeDtypeStruct((count, HALF + 16, width), bf16),
        compiler_params=pltpu.CompilerParams(vmem_limit_bytes=16 << 20),
        cost_estimate=pl.CostEstimate(flops=COARSE_FLOPS, bytes_accessed=8 * got.size, transcendentals=1 << 20),
        name="coarse_levels",
    )(bias, got, from_prev, from_next)


def side_body(side, scalars, ins, outs):
    q0_ref, q1_ref, sum_ref, stat_ref, side_ref = ins[:5]
    heads = q0_ref.shape[1] // HEAD_DIM
    bias = scalars[1][side]
    blocks = (side, 1 - side)
    pair = pair_matrix()
    near_keys = (mul(pair, side_ref[0:BLK, :]) * 0.5).astype(bf16)
    near_values = mul(pair, side_ref[BLK : 2 * BLK, :]).astype(bf16)
    far_keys = slice(2 * BLK, 2 * BLK + HALF)
    far_values = slice(2 * BLK + HALF, 3 * BLK)
    fine = [pl.ds(pl.multiple_of(block * BLK, BLK), BLK) for block in blocks]
    middle = [pl.ds(pl.multiple_of(block * HALF, HALF), HALF) for block in blocks]
    units = []
    for head in range(heads):
        here = cols(head)
        far = (side_ref[far_keys, here], side_ref[far_values, here], bias)
        whole = tuple(
            jnp.concatenate([near[:, here], side_ref[far, here]], axis=0)
            for near, far in ((near_keys, far_keys), (near_values, far_values))
        )
        units.append((q0_ref[fine[0], here], [(side_ref[0:BLK, here], side_ref[BLK : 2 * BLK, here], bias)]))
        units.append((q1_ref[middle[0], here], [far]))
        units.append((q1_ref[middle[1], here], [(*whole, bias)]))
    found = attend(units)
    if len(ins) == 5:
        for n in range(2):
            stats = unpack(stat_ref[fine[n], :], 2 * heads)
            results = []
            for head in range(heads):
                here = cols(head)
                top1, sum1 = found[3 * head + 1 + n]
                top1, sum1 = twice(top1), twice(sum1)
                own_top, own_total = stats[2 * head], stats[2 * head + 1]
                top = jnp.maximum(top1, own_top)
                if n == 0:
                    top0, sum0 = found[3 * head]
                    top = jnp.maximum(top, top0)
                scale1 = jnp.exp2(top1 - top)
                own_scale = jnp.exp2(own_top - top)
                number = sum1[:, :HEAD_DIM] * scale1 + sum_ref[fine[n], here] * own_scale
                total = sum1[:, HEAD_DIM:] * (2.0 * scale1) + own_total * own_scale
                if n == 0:
                    scale0 = jnp.exp2(top0 - top)
                    number = number + sum0[:, :HEAD_DIM] * scale0
                    total = total + sum0[:, HEAD_DIM:] * scale0
                outs[0][fine[n], here] = number
                results += [top, total]
            outs[1][fine[n], :] = pack(results)
        return
    back_ref = ins[5]
    restore = restore_matrix()
    levels = []
    for head in range(heads):
        terms = back_ref[HALF : HALF + 16, cols(head)].astype(f32)
        terms = jnp.sum(jnp.where(iota(terms.shape, 0) < 3, terms, 0.0), axis=0, keepdims=True)
        levels.append(jnp.broadcast_to(terms, (HEAD_DIM, HEAD_DIM)).T)
    for n in range(2):
        stats = unpack(stat_ref[fine[n], :], 2 * heads)
        spot = pl.ds(pl.multiple_of(blocks[n] * HALF // 2, HALF // 2), HALF // 2)
        results = []
        for head in range(heads):
            here = cols(head)
            top1, sum1 = found[3 * head + 1 + n]
            half = HALF // 2
            level = twice(jnp.where(blocks[n] == 0, levels[head][:half, :], levels[head][half:, :]))
            top = jnp.maximum(top1, level)
            scale1 = jnp.exp2(top1 - top)
            scale2 = jnp.exp2(level - top)
            number = twice(sum1[:, :HEAD_DIM] * scale1 + twice(back_ref[spot, here].astype(f32)) * scale2)
            total = twice(sum1[:, HEAD_DIM:] * (2.0 * scale1) + scale2)
            top = twice(top)
            own_top, own_total = stats[2 * head], stats[2 * head + 1]
            most = jnp.maximum(top, own_top)
            if n == 0:
                top0, sum0 = found[3 * head]
                most = jnp.maximum(most, top0)
            scale = jnp.exp2(top - most)
            own_scale = jnp.exp2(own_top - most)
            number = number * scale + sum_ref[fine[n], here] * own_scale
            total = total * scale + own_total * own_scale
            if n == 0:
                scale0 = jnp.exp2(top0 - most)
                number = number + sum0[:, :HEAD_DIM] * scale0
                total = total + sum0[:, HEAD_DIM:] * scale0
            results.append((number / total).astype(bf16))
        outs[0][fine[n], :] = mul(restore, jnp.concatenate(results, axis=1)).astype(bf16)


def chip_body(scalars, ins, outs):
    side_body(1 - scalars[0][0], scalars, ins, outs)


def finish_body(scalars, ins, outs):
    side_body(scalars[0][0], scalars, ins, outs)


def chip_level(odd, bias, q0, q1, sums, stat, chip, groups):
    rows, width = q0.shape
    ins = [one(a) for a in (q0, q1, sums, stat)] + [one(chip, pinned=False)]
    outs = [(array(rows, width, f32), "cols"), (array(rows, groups * HEAD_DIM, f32), "cols")]
    flops = 3 * rows * BLK * width
    return run_shares(chip_body, "chip_level", groups, [odd, bias], ins, outs, flops, rows * BLK * HEADS)


def finish(odd, bias, q0, q1, sums, stat, cross, back):
    groups = back.shape[0]
    rows, width = q0.shape
    ins = [one(a) for a in (q0, q1, sums, stat)] + [one(cross, pinned=False), one(back, "lead", pinned=False)]
    outs = [(array(rows, width, bf16), "cols")]
    flops = 3 * rows * BLK * width
    return run_shares(finish_body, "finish", groups, [odd, bias], ins, outs, flops, rows * BLK * HEADS)[0]


def shift(value, axis, steps):
    count = lax.axis_size(axis)
    first, last = (max(0, -steps), min(count, count - steps))
    return lax.ppermute(value, axis, [(source, source + steps) for source in range(first, last)])


def trade(value, axis, first):
    count = lax.axis_size(axis)
    pairs = [(source, source + 1) for source in range(first, count - 1, 2)]
    return lax.ppermute(value, axis, pairs + [(target, source) for source, target in pairs])


def edge_bias(axis):
    place = lax.axis_index(axis)
    last = lax.axis_size(axis) - 1
    at_edge = jnp.stack([place == 0, place == last])
    return jnp.where(at_edge, very_negative, 0.0).astype(f32)


def local(query_vecs, key_vecs, value_vecs):
    groups = lax.axis_size("grp")
    assert query_vecs.shape == (2 * BLK, HEADS * HEAD_DIM) and groups == 4
    everyone = ("seq", "grp")
    place = jnp.bitwise_and(lax.axis_index(everyone), 1).astype(jnp.int32).reshape(1)
    bias = edge_bias(everyone)
    swap = swap_rows(query_vecs, key_vecs, value_vecs, groups)
    got = lax.all_to_all(swap, "grp", split_axis=0, concat_axis=0, tiled=True)
    query_rows, swap = lax.optimization_barrier((query_vecs, swap))
    q0, q1, cross, chip = rows_to_send(place, query_rows, key_vecs, value_vecs, groups)
    own, own_stat = own_level(q0, key_vecs, value_vecs, groups)
    got, own, chip, cross = lax.optimization_barrier((got, own, chip, cross))
    coarse_right, coarse_left = coarse_halos(got)
    coarse_right, coarse_left, chip, cross = lax.optimization_barrier((coarse_right, coarse_left, chip, cross))
    coarse_prev = shift(coarse_right, "seq", 1)
    coarse_next = shift(coarse_left, "seq", -1)
    chip = trade(chip, everyone, 0)
    cross = trade(cross, everyone, 1)
    back = coarse_levels(edge_bias("seq"), got, coarse_prev, coarse_next)
    back, own = lax.optimization_barrier((back, own))
    own, own_stat = chip_level(place, bias, q0, q1, own, own_stat, chip, groups)
    back = lax.all_to_all(back, "grp", split_axis=0, concat_axis=0, tiled=True)
    return finish(place, bias, q0, q1, own, own_stat, cross, back)


def solution(mesh):
    return jax.shard_map(
        local,
        mesh=mesh,
        in_specs=(P(("seq", "grp"), None), P(("seq", "grp"), None), P(("seq", "grp"), None)),
        out_specs=P(("seq", "grp"), None),
        check_vma=False,
    )
```

```python
import functools
import functools
import functools
import functools
import functools
import functools
import functools
import functools
import functools
import functools
import math

import jax
import jax.numpy as jnp
from jax import lax
from jax.experimental import pallas as pl
from jax.experimental.pallas import tpu as pltpu
from jax.sharding import PartitionSpec as P

HEADS = 8
HEAD_DIM = 128
BLK = 256
HALF = BLK // 2
SUB = BLK // 8
LEV = 4
EXP_SCALE = math.log2(math.e) / math.sqrt(HEAD_DIM)

VMEM_GRANT = 48 << 20

very_negative = -1e30
f32 = jnp.float32
bf16 = jnp.bfloat16


def iota(shape, dim):
    return lax.broadcasted_iota(jnp.int32, shape, dim)


def bit(value, place):
    return jnp.bitwise_and(lax.shift_right_logical(value, place), 1)


def low_bits(value):
    step = SUB.bit_length() - 1
    deep = jnp.bitwise_and(value, SUB - 1)
    return 8 * deep + 4 * bit(value, step) + 2 * bit(value, step + 1) + bit(value, step + 2)


def reorder_matrix():
    return (iota((BLK, BLK), 1) == low_bits(iota((BLK, BLK), 0))).astype(bf16)


def restore_matrix():
    return (iota((BLK, BLK), 0) == low_bits(iota((BLK, BLK), 1))).astype(bf16)


def pair_matrix():
    first = low_bits(iota((HALF, BLK), 0))
    place = iota((HALF, BLK), 1)
    return jnp.logical_or(place == first, place == first + 1).astype(bf16)


def mul(left, right):
    return jnp.dot(left, right, preferred_element_type=f32)


def fold(rows, factor):
    half = rows.shape[0] // 2
    total = rows[:half].astype(f32) + rows[half:].astype(f32)
    if factor != 1.0:
        total = total * factor
    return total.astype(bf16)


def fold_chunks(rows, chunk, factor):
    count = rows.shape[0] // chunk
    return jnp.concatenate([fold(rows[i * chunk : (i + 1) * chunk], factor) for i in range(count)], axis=0)


def twice(rows):
    return jnp.concatenate([rows, rows], axis=0)


def cols(head):
    return slice(head * HEAD_DIM, (head + 1) * HEAD_DIM)


def lane_chunks(rows):
    return [rows[:, first : first + HEAD_DIM] for first in range(0, rows.shape[1], HEAD_DIM)]


def twice(rows):
    return jnp.concatenate([rows, rows], axis=0)


def cols(head):
    return slice(head * HEAD_DIM, (head + 1) * HEAD_DIM)


def lane_chunks(rows):
    return [rows[:, first : first + HEAD_DIM] for first in range(0, rows.shape[1], HEAD_DIM)]


def twice(rows):
    return jnp.concatenate([rows, rows], axis=0)


def cols(head):
    return slice(head * HEAD_DIM, (head + 1) * HEAD_DIM)


def lane_chunks(rows):
    return [rows[:, first : first + HEAD_DIM] for first in range(0, rows.shape[1], HEAD_DIM)]


def twice(rows):
    return jnp.concatenate([rows, rows], axis=0)


def cols(head):
    return slice(head * HEAD_DIM, (head + 1) * HEAD_DIM)


def lane_chunks(rows):
    return [rows[:, first : first + HEAD_DIM] for first in range(0, rows.shape[1], HEAD_DIM)]


def twice(rows):
    return jnp.concatenate([rows, rows], axis=0)


def cols(head):
    return slice(head * HEAD_DIM, (head + 1) * HEAD_DIM)


def lane_chunks(rows):
    return [rows[:, first : first + HEAD_DIM] for first in range(0, rows.shape[1], HEAD_DIM)]


def twice(rows):
    return jnp.concatenate([rows, rows], axis=0)


def cols(head):
    return slice(head * HEAD_DIM, (head + 1) * HEAD_DIM)


def lane_chunks(rows):
    return [rows[:, first : first + HEAD_DIM] for first in range(0, rows.shape[1], HEAD_DIM)]


def twice(rows):
    return jnp.concatenate([rows, rows], axis=0)


def cols(head):
    return slice(head * HEAD_DIM, (head + 1) * HEAD_DIM)


def lane_chunks(rows):
    return [rows[:, first : first + HEAD_DIM] for first in range(0, rows.shape[1], HEAD_DIM)]


def twice(rows):
    return jnp.concatenate([rows, rows], axis=0)


def cols(head):
    return slice(head * HEAD_DIM, (head + 1) * HEAD_DIM)


COARSE_FLOPS = 1 << 29


def lane_chunks(rows):
    return [rows[:, first : first + HEAD_DIM] for first in range(0, rows.shape[1], HEAD_DIM)]


def twice(rows):
    return jnp.concatenate([rows, rows], axis=0)


def cols(head):
    return slice(head * HEAD_DIM, (head + 1) * HEAD_DIM)


COARSE_FLOPS = 1 << 36


def lane_chunks(rows):
    return [rows[:, first : first + HEAD_DIM] for first in range(0, rows.shape[1], HEAD_DIM)]


def twice(rows):
    return jnp.concatenate([rows, rows], axis=0)


def cols(head):
    return slice(head * HEAD_DIM, (head + 1) * HEAD_DIM)


COARSE_FLOPS = 1 << 36


def lane_chunks(rows):
    return [rows[:, first : first + HEAD_DIM] for first in range(0, rows.shape[1], HEAD_DIM)]


def with_ones(values):
    return jnp.concatenate([values, jnp.ones_like(values)], axis=1)


def attend(units):
    scores = []
    for query, parts in units:
        chunks = []
        for keys, _, bias in parts:
            raw = lax.dot_general(query, keys, (((1,), (1,)), ((), ())), preferred_element_type=f32)
            chunks.append(lane_chunks(raw if bias is None else raw + bias))
        scores.append(chunks)
    tops = []
    for chunks in scores:
        most = functools.reduce(jnp.maximum, sum(chunks, []))
        tops.append(jnp.broadcast_to(jnp.max(most, axis=1, keepdims=True), most.shape))
    found = []
    for (_, parts), chunks, top in zip(units, scores, tops):
        total = None
        for (_, values, _), pieces in zip(parts, chunks):
            weights = [jnp.exp2((piece - top) * EXP_SCALE).astype(bf16) for piece in pieces]
            one = mul(jnp.concatenate(weights, axis=1), with_ones(values))
            total = one if total is None else total + one
        found.append((top * EXP_SCALE, total))
    return found


def share_of(ref, kind, share, shares):
    if kind == "lead":
        return ref.at[share]
    width = ref.shape[1] // shares
    first = share * width
    if not isinstance(share, int):
        first = pl.multiple_of(first, HEAD_DIM)
    return ref.at[:, pl.ds(first, width)]


class Operand:
    def __init__(self, values, kind, pinned):
        self.values = values
        self.kind = kind
        self.pinned = pinned
        self.dtype = values[0].dtype

    def buffer(self, shares):
        shape = self.values[0].shape
        return shape if self.kind == "lead" else (shares, shape[0], shape[1] // shares)


def one(value, kind="cols", pinned=True):
    return Operand([value], kind, pinned)


def run_shares(body, name, shares, scalars, ins, outs, flops, exps):
    out_kinds = [kind for _, kind in outs]

    first = [sum(len(operand.values) for operand in ins[:i]) for i in range(len(ins) + 1)]

    def kernel(*refs):
        refs = list(refs)
        take = lambda count: [refs.pop(0) for _ in range(count)]
        scalar_refs, in_refs, out_refs = take(len(scalars)), take(first[-1]), take(len(outs))
        in_bufs, out_bufs, (in_sems, out_sems) = take(len(ins)), take(len(outs)), take(2)

        def bring(i, share, which=0):
            source = share_of(in_refs[first[i] + which], ins[i].kind, share, shares)
            return pltpu.make_async_copy(source, in_bufs[i].at[share], in_sems.at[i, share])

        def begin(i, share):
            if len(ins[i].values) == 1:
                bring(i, share).start()
            else:
                pl.when(scalar_refs[0][1] == 1)(lambda: bring(i, share, 0).start())
                pl.when(scalar_refs[0][1] != 1)(lambda: bring(i, share, 1).start())

        def put(i, share):
            target = share_of(out_refs[i], out_kinds[i], share, shares)
            return pltpu.make_async_copy(out_bufs[i].at[share], target, out_sems.at[i, share])

        for share in range(shares):
            for i in range(len(ins)):
                begin(i, share)

        def step(share, carry):
            for i in range(len(ins)):
                bring(i, share).wait()
            body(scalar_refs, [buf.at[share] for buf in in_bufs], [buf.at[share] for buf in out_bufs])
            for i in range(len(outs)):
                put(i, share).start()
            return carry

        lax.fori_loop(0, shares, step, 0)
        for share in range(shares):
            for i in range(len(outs)):
                put(i, share).wait()

    values, specs = [], []
    for operand in ins:
        for value in operand.values:
            values.append(pltpu.with_memory_space_constraint(value, pltpu.HBM) if operand.pinned else value)
            specs.append(pl.BlockSpec(memory_space=pltpu.HBM if operand.pinned else pl.ANY))
    size = sum(value.size * value.dtype.itemsize for value in values + [shape for shape, _ in outs])
    buffers = [pltpu.VMEM(operand.buffer(shares), operand.dtype) for operand in ins]
    for shape, kind in outs:
        width = shape.shape[-1]
        buffers.append(pltpu.VMEM(shape.shape if kind == "lead" else (shares, shape.shape[0], width // shares), shape.dtype))
    return pl.pallas_call(
        kernel,
        in_specs=[pl.BlockSpec(memory_space=pltpu.SMEM)] * len(scalars) + specs,
        out_specs=[pl.BlockSpec(memory_space=pltpu.HBM)] * len(outs),
        out_shape=[pltpu.HBM(shape.shape, shape.dtype) for shape, _ in outs],
        scratch_shapes=buffers
        + [pltpu.SemaphoreType.DMA((len(ins), shares)), pltpu.SemaphoreType.DMA((len(outs), shares))],
        compiler_params=pltpu.CompilerParams(vmem_limit_bytes=VMEM_GRANT),
        cost_estimate=pl.CostEstimate(flops=flops, bytes_accessed=size, transcendentals=exps),
        name=name,
    )(*scalars, *values)


def array(rows, width, dtype):
    return jax.ShapeDtypeStruct((rows, width), dtype)


def swap_body(_, ins, outs):
    pair = pair_matrix()
    for place, (ref, factor) in enumerate(zip(ins, (0.5, 0.5, 1.0))):
        for i in range(2):
            level1 = mul(pair, ref[i * BLK : (i + 1) * BLK, :])
            if factor != 1.0:
                level1 = level1 * factor
            first = place * HALF + i * HALF // 2
            outs[0][first : first + HALF // 2, :] = fold(level1.astype(bf16), factor)


def swap_rows(query_vecs, key_vecs, value_vecs, groups):
    rows, width = query_vecs.shape
    out = jax.ShapeDtypeStruct((groups, 3 * HALF, width // groups), bf16)
    ins = [one(a) for a in (query_vecs, key_vecs, value_vecs)]
    return run_shares(swap_body, "swap_rows", groups, [], ins, [(out, "lead")], 6 * rows * HALF * width, 0)[0]


def rows_body(scalars, ins, outs):
    q_ref, k_ref, v_ref = ins
    q0_ref, q1_ref, cross_ref, chip_ref = outs
    reorder = reorder_matrix()
    pair = pair_matrix()
    for i in range(2):
        rows = slice(i * BLK, (i + 1) * BLK)
        q0 = mul(reorder, q_ref[rows, :]).astype(bf16)
        q0_ref[rows, :] = q0
        q1_ref[i * HALF : (i + 1) * HALF, :] = fold(q0, 0.5)
    parity = scalars[0][0]
    outer = pl.ds(pl.multiple_of(parity * BLK, BLK), BLK)
    inner = pl.ds(pl.multiple_of((1 - parity) * BLK, BLK), BLK)
    for ref, near, far in ((cross_ref, outer, inner), (chip_ref, inner, outer)):
        ref[0:BLK, :] = k_ref[near, :]
        ref[BLK : 2 * BLK, :] = v_ref[near, :]
        ref[2 * BLK : 2 * BLK + HALF, :] = (mul(pair, k_ref[far, :]) * 0.5).astype(bf16)
        ref[2 * BLK + HALF : 3 * BLK, :] = mul(pair, v_ref[far, :]).astype(bf16)


def rows_to_send(place, query_vecs, key_vecs, value_vecs, groups):
    rows, width = query_vecs.shape
    ins = [one(a) for a in (query_vecs, key_vecs, value_vecs)]
    outs = [(array(n, width, bf16), "cols") for n in (rows, rows // 2, 3 * BLK, 3 * BLK)]
    return run_shares(rows_body, "rows_to_send", groups, [place], ins, outs, 8 * rows * BLK * width, 0)


def pack(stats):
    width = HEAD_DIM // len(stats)
    lane = iota(stats[0].shape, 1)
    packed = stats[-1]
    for n in range(len(stats) - 2, -1, -1):
        packed = jnp.where(lane < (n + 1) * width, stats[n], packed)
    return packed


def unpack(packed, count):
    width = HEAD_DIM // count
    return [jnp.broadcast_to(packed[:, n * width : n * width + 1], packed.shape) for n in range(count)]


def own_body(_, ins, outs):
    q_ref, k_ref, v_ref = ins
    sum_ref, stat_ref = outs
    heads = q_ref.shape[1] // HEAD_DIM
    for i in range(2):
        rows = slice(i * BLK, (i + 1) * BLK)
        units = [(q_ref[rows, cols(head)], [(k_ref[:, cols(head)], v_ref[:, cols(head)], None)]) for head in range(heads)]
        stats = []
        for head, (top, sums) in enumerate(attend(units)):
            sum_ref[rows, cols(head)] = sums[:, :HEAD_DIM]
            stats += [top, sums[:, HEAD_DIM:]]
        stat_ref[rows, :] = pack(stats)


def own_level(q0, key_vecs, value_vecs, groups):
    rows, width = q0.shape
    ins = [one(a) for a in (q0, key_vecs, value_vecs)]
    outs = [(array(rows, width, f32), "cols"), (array(rows, groups * HEAD_DIM, f32), "cols")]
    flops = 8 * rows * BLK * width
    return run_shares(own_body, "own_level", groups, [], ins, outs, flops, 2 * rows * BLK * HEADS)


def halo_body(got_ref, right_ref, left_ref):
    count = got_ref.shape[0]
    pair = count // 2
    for which, factor in ((1, 0.5), (2, 1.0)):
        rows = slice(which * HALF, (which + 1) * HALF)
        near = (which - 1) * BLK
        far = 2 * BLK + (which - 1) * HALF
        for j in range(count):
            level2 = got_ref[j, rows, :]
            level3 = fold_chunks(level2, HALF // 2, factor)
            near_ref, far_ref = (left_ref, right_ref) if j < pair else (right_ref, left_ref)
            spot = j % pair
            near_ref[near + spot * HALF : near + (spot + 1) * HALF, :] = level2
            far_ref[far + spot * HALF // 2 : far + (spot + 1) * HALF // 2, :] = level3


def coarse_halos(got):
    shape = jax.ShapeDtypeStruct((3 * BLK, got.shape[2]), bf16)
    return pl.pallas_call(
        halo_body,
        out_shape=[shape, shape],
        compiler_params=pltpu.CompilerParams(vmem_limit_bytes=16 << 20),
        cost_estimate=pl.CostEstimate(flops=1 << 20, bytes_accessed=6 * got.size, transcendentals=0),
        name="coarse_halos",
    )(got)


def coarse_body(bias_ref, got_ref, prev_ref, next_ref, back_ref):
    count = got_ref.shape[0]
    heads = got_ref.shape[2] // HEAD_DIM
    bias_prev = bias_ref[0]
    bias_next = bias_ref[1]
    lane = iota((HALF, HEAD_DIM), 1)

    for head in range(heads):
        here = cols(head)

        def own(which, j):
            return got_ref[j, which * HALF : (which + 1) * HALF, here]

        def near(ref, which, spot):
            first = (which - 1) * BLK + spot * HALF
            return ref[first : first + HALF, here]

        def both(ref, which):
            return ref[(which - 1) * BLK : which * BLK, here]

        def far(ref, which):
            first = 2 * BLK + (which - 1) * HALF
            return ref[first : first + HALF, here]

        def near3(ref, which):
            return fold_chunks(both(ref, which), HALF // 2, 0.5 if which == 1 else 1.0)

        def joined(*rows):
            return jnp.concatenate(rows, axis=0)

        def part(pick, bias):
            return (pick(1), pick(2), bias)

        units = [
            (own(0, 0), [part(lambda w: joined(own(w, 2), own(w, 3)), None), part(lambda w: near(prev_ref, w, 0), bias_prev)]),
            (own(0, 1), [part(lambda w: both(prev_ref, w), bias_prev), part(lambda w: own(w, 3), None)]),
            (own(0, 2), [part(lambda w: both(next_ref, w), bias_next), part(lambda w: own(w, 0), None)]),
            (own(0, 3), [part(lambda w: joined(own(w, 0), own(w, 1)), None), part(lambda w: near(next_ref, w, 1), bias_next)]),
        ]
        for j, (ref, bias, other, other_bias) in enumerate(
            ((next_ref, bias_next, prev_ref, bias_prev), (prev_ref, bias_prev, next_ref, bias_next))
        ):
            query = joined(*[fold_chunks(own(0, 2 * j + n), HALF // 2, 0.5) for n in range(2)])
            units.append(
                (
                    query,
                    [part(lambda w: joined(near3(ref, w), far(ref, w)), bias), part(lambda w: far(other, w), other_bias)],
                )
            )
        found = attend(units)
        for j in range(count):
            top2, sum2 = found[j]
            top3, sum3 = found[count + j // 2]

            def spread(rows):
                first = (j % 2) * 2 * SUB
                one = rows[first : first + SUB]
                other = rows[first + SUB : first + 2 * SUB]
                return joined(one, one, other, other)

            top3 = spread(top3)
            sum3 = spread(sum3)
            top = jnp.maximum(top2, top3)
            scale2 = jnp.exp2(top2 - top)
            scale3 = jnp.exp2(top3 - top)
            values = sum2[:, :HEAD_DIM] * scale2 + sum3[:, :HEAD_DIM] * scale3
            total = sum2[:, HEAD_DIM:] * (4.0 * scale2) + sum3[:, HEAD_DIM:] * (8.0 * scale3)
            back_ref[j, 0:HALF, here] = (values / total).astype(bf16)
            level = top + jnp.log2(total)
            high = level.astype(bf16).astype(f32)
            middle = (level - high).astype(bf16).astype(f32)
            terms = jnp.where(lane == 0, high, jnp.where(lane == 1, middle, level - high - middle))
            back_ref[j, HALF : HALF + 16, here] = terms.T[0:16, :].astype(bf16)


def coarse_levels(bias, got, from_prev, from_next):
    count, _, width = got.shape
    vmem = pl.BlockSpec(memory_space=pltpu.VMEM)
    return pl.pallas_call(
        coarse_body,
        in_specs=[pl.BlockSpec(memory_space=pltpu.SMEM), vmem, vmem, vmem],
        out_specs=vmem,
        out_shape=jax.ShapeDtypeStruct((count, HALF + 16, width), bf16),
        compiler_params=pltpu.CompilerParams(vmem_limit_bytes=16 << 20),
        cost_estimate=pl.CostEstimate(flops=COARSE_FLOPS, bytes_accessed=8 * got.size, transcendentals=1 << 20),
        name="coarse_levels",
    )(bias, got, from_prev, from_next)


def side_body(side, scalars, ins, outs):
    q0_ref, q1_ref, sum_ref, stat_ref, side_ref = ins[:5]
    heads = q0_ref.shape[1] // HEAD_DIM
    bias = scalars[1][side]
    blocks = (side, 1 - side)
    pair = pair_matrix()
    near_keys = (mul(pair, side_ref[0:BLK, :]) * 0.5).astype(bf16)
    near_values = mul(pair, side_ref[BLK : 2 * BLK, :]).astype(bf16)
    far_keys = slice(2 * BLK, 2 * BLK + HALF)
    far_values = slice(2 * BLK + HALF, 3 * BLK)
    fine = [pl.ds(pl.multiple_of(block * BLK, BLK), BLK) for block in blocks]
    middle = [pl.ds(pl.multiple_of(block * HALF, HALF), HALF) for block in blocks]
    units = []
    for head in range(heads):
        here = cols(head)
        far = (side_ref[far_keys, here], side_ref[far_values, here], bias)
        whole = tuple(
            jnp.concatenate([near[:, here], side_ref[far, here]], axis=0)
            for near, far in ((near_keys, far_keys), (near_values, far_values))
        )
        units.append((q0_ref[fine[0], here], [(side_ref[0:BLK, here], side_ref[BLK : 2 * BLK, here], bias)]))
        units.append((q1_ref[middle[0], here], [far]))
        units.append((q1_ref[middle[1], here], [(*whole, bias)]))
    found = attend(units)
    if len(ins) == 5:
        for n in range(2):
            stats = unpack(stat_ref[fine[n], :], 2 * heads)
            results = []
            for head in range(heads):
                here = cols(head)
                top1, sum1 = found[3 * head + 1 + n]
                top1, sum1 = twice(top1), twice(sum1)
                own_top, own_total = stats[2 * head], stats[2 * head + 1]
                top = jnp.maximum(top1, own_top)
                if n == 0:
                    top0, sum0 = found[3 * head]
                    top = jnp.maximum(top, top0)
                scale1 = jnp.exp2(top1 - top)
                own_scale = jnp.exp2(own_top - top)
                number = sum1[:, :HEAD_DIM] * scale1 + sum_ref[fine[n], here] * own_scale
                total = sum1[:, HEAD_DIM:] * (2.0 * scale1) + own_total * own_scale
                if n == 0:
                    scale0 = jnp.exp2(top0 - top)
                    number = number + sum0[:, :HEAD_DIM] * scale0
                    total = total + sum0[:, HEAD_DIM:] * scale0
                outs[0][fine[n], here] = number
                results += [top, total]
            outs[1][fine[n], :] = pack(results)
        return
    back_ref = ins[5]
    restore = restore_matrix()
    levels = []
    for head in range(heads):
        terms = back_ref[HALF : HALF + 16, cols(head)].astype(f32)
        terms = jnp.sum(jnp.where(iota(terms.shape, 0) < 3, terms, 0.0), axis=0, keepdims=True)
        levels.append(jnp.broadcast_to(terms, (HEAD_DIM, HEAD_DIM)).T)
    for n in range(2):
        stats = unpack(stat_ref[fine[n], :], 2 * heads)
        spot = pl.ds(pl.multiple_of(blocks[n] * HALF // 2, HALF // 2), HALF // 2)
        results = []
        for head in range(heads):
            here = cols(head)
            top1, sum1 = found[3 * head + 1 + n]
            half = HALF // 2
            level = twice(jnp.where(blocks[n] == 0, levels[head][:half, :], levels[head][half:, :]))
            top = jnp.maximum(top1, level)
            scale1 = jnp.exp2(top1 - top)
            scale2 = jnp.exp2(level - top)
            number = twice(sum1[:, :HEAD_DIM] * scale1 + twice(back_ref[spot, here].astype(f32)) * scale2)
            total = twice(sum1[:, HEAD_DIM:] * (2.0 * scale1) + scale2)
            top = twice(top)
            own_top, own_total = stats[2 * head], stats[2 * head + 1]
            most = jnp.maximum(top, own_top)
            if n == 0:
                top0, sum0 = found[3 * head]
                most = jnp.maximum(most, top0)
            scale = jnp.exp2(top - most)
            own_scale = jnp.exp2(own_top - most)
            number = number * scale + sum_ref[fine[n], here] * own_scale
            total = total * scale + own_total * own_scale
            if n == 0:
                scale0 = jnp.exp2(top0 - most)
                number = number + sum0[:, :HEAD_DIM] * scale0
                total = total + sum0[:, HEAD_DIM:] * scale0
            results.append((number / total).astype(bf16))
        outs[0][fine[n], :] = mul(restore, jnp.concatenate(results, axis=1)).astype(bf16)


def chip_body(scalars, ins, outs):
    side_body(1 - scalars[0][0], scalars, ins, outs)


def finish_body(scalars, ins, outs):
    side_body(scalars[0][0], scalars, ins, outs)


def chip_level(odd, bias, q0, q1, sums, stat, chip, groups):
    rows, width = q0.shape
    ins = [one(a) for a in (q0, q1, sums, stat)] + [one(chip, pinned=False)]
    outs = [(array(rows, width, f32), "cols"), (array(rows, groups * HEAD_DIM, f32), "cols")]
    flops = 3 * rows * BLK * width
    return run_shares(chip_body, "chip_level", groups, [odd, bias], ins, outs, flops, rows * BLK * HEADS)


def finish(place, bias, q0, q1, sums, stat, outer, inner, back):
    groups = back.shape[0]
    rows, width = q0.shape
    ins = [one(a) for a in (q0, q1, sums, stat)] + [Operand([outer, inner], "cols", False), one(back, "lead", pinned=False)]
    outs = [(array(rows, width, bf16), "cols")]
    flops = 3 * rows * BLK * width
    return run_shares(finish_body, "finish", groups, [place, bias], ins, outs, flops, rows * BLK * HEADS)[0]


def shift(value, axis, steps):
    count = lax.axis_size(axis)
    first, last = (max(0, -steps), min(count, count - steps))
    return lax.ppermute(value, axis, [(source, source + steps) for source in range(first, last)])


def trade(value, axis, pairs):
    return lax.ppermute(value, axis, pairs + [(target, source) for source, target in pairs])


def across(outer_rows, inner_rows, axis, groups):
    count = lax.axis_size(axis)

    def beside(device):
        other = (device // groups ^ 1) * groups + device % groups
        return other if other < count else device

    pairs = [(source, source + 1) for source in range(1, count - 1, 2)]
    inside = [pair for pair in pairs if pair[1] % groups != 0]
    between = [pair for pair in pairs if pair[1] % groups == 0]
    if outer_rows is None:
        ends = [device for device in range(count) if device % groups in (0, groups - 1)]
        return lax.ppermute(inner_rows, axis, [(device, beside(device)) for device in ends])
    hops = [(beside(before), behind) for before, behind in between]
    hops += [(beside(behind), before) for before, behind in between]
    return lax.ppermute(outer_rows, axis, hops), trade(inner_rows, axis, inside)


def edge_bias(axis):
    place = lax.axis_index(axis)
    last = lax.axis_size(axis) - 1
    at_edge = jnp.stack([place == 0, place == last])
    return jnp.where(at_edge, very_negative, 0.0).astype(f32)


def local(query_vecs, key_vecs, value_vecs):
    groups = lax.axis_size("grp")
    assert query_vecs.shape == (2 * BLK, HEADS * HEAD_DIM) and groups == 4
    everyone = ("seq", "grp")
    count = lax.axis_size(everyone)
    spot = lax.axis_index("grp")
    odd = jnp.bitwise_and(spot, 1)
    at_end = jnp.logical_or(spot == 0, spot == groups - 1)
    place = jnp.stack([odd, at_end.astype(odd.dtype)]).astype(jnp.int32)
    bias = edge_bias(everyone)
    swap = swap_rows(query_vecs, key_vecs, value_vecs, groups)
    got = lax.all_to_all(swap, "grp", split_axis=0, concat_axis=0, tiled=True)
    query_rows, swap = lax.optimization_barrier((query_vecs, swap))
    q0, q1, cross, chip = rows_to_send(place, query_rows, key_vecs, value_vecs, groups)
    outer = across(None, cross, everyone, groups)
    own, own_stat = own_level(q0, key_vecs, value_vecs, groups)
    got, own, chip, cross = lax.optimization_barrier((got, own, chip, cross))
    coarse_right, coarse_left = coarse_halos(got)
    coarse_right, coarse_left, chip, cross = lax.optimization_barrier((coarse_right, coarse_left, chip, cross))
    coarse_prev = shift(coarse_right, "seq", 1)
    coarse_next = shift(coarse_left, "seq", -1)
    chip = trade(chip, everyone, [(first, first + 1) for first in range(0, count - 1, 2)])
    outer, inner = across(outer, cross, everyone, groups)
    back = coarse_levels(edge_bias("seq"), got, coarse_prev, coarse_next)
    back, own = lax.optimization_barrier((back, own))
    own, own_stat = chip_level(place, bias, q0, q1, own, own_stat, chip, groups)
    back = lax.all_to_all(back, "grp", split_axis=0, concat_axis=0, tiled=True)
    return finish(place, bias, q0, q1, own, own_stat, outer, inner, back)


def solution(mesh):
    return jax.shard_map(
        local,
        mesh=mesh,
        in_specs=(P(("seq", "grp"), None), P(("seq", "grp"), None), P(("seq", "grp"), None)),
        out_specs=P(("seq", "grp"), None),
        check_vma=False,
    )
```

```python
import functools
import functools
import functools
import functools
import functools
import functools
import functools
import functools
import functools
import functools
import functools
import functools
import functools
import functools
import functools
import math

import jax
import jax.numpy as jnp
from jax import lax
from jax.experimental import pallas as pl
from jax.experimental.pallas import tpu as pltpu
from jax.sharding import PartitionSpec as P

HEADS = 8
HEAD_DIM = 128
BLK = 256
HALF = BLK // 2
SUB = BLK // 8
LEV = 4
EXP_SCALE = math.log2(math.e) / math.sqrt(HEAD_DIM)

VMEM_GRANT = 48 << 20

very_negative = -1e30
f32 = jnp.float32
bf16 = jnp.bfloat16


def iota(shape, dim):
    return lax.broadcasted_iota(jnp.int32, shape, dim)


def bit(value, place):
    return jnp.bitwise_and(lax.shift_right_logical(value, place), 1)


def low_bits(value):
    step = SUB.bit_length() - 1
    deep = jnp.bitwise_and(value, SUB - 1)
    return 8 * deep + 4 * bit(value, step) + 2 * bit(value, step + 1) + bit(value, step + 2)


def reorder_matrix():
    return (iota((BLK, BLK), 1) == low_bits(iota((BLK, BLK), 0))).astype(bf16)


def restore_matrix():
    return (iota((BLK, BLK), 0) == low_bits(iota((BLK, BLK), 1))).astype(bf16)


def pair_matrix():
    first = low_bits(iota((HALF, BLK), 0))
    place = iota((HALF, BLK), 1)
    return jnp.logical_or(place == first, place == first + 1).astype(bf16)


def mul(left, right):
    return jnp.dot(left, right, preferred_element_type=f32)


def fold(rows, factor):
    half = rows.shape[0] // 2
    total = rows[:half].astype(f32) + rows[half:].astype(f32)
    if factor != 1.0:
        total = total * factor
    return total.astype(bf16)


def fold_chunks(rows, chunk, factor):
    count = rows.shape[0] // chunk
    return jnp.concatenate([fold(rows[i * chunk : (i + 1) * chunk], factor) for i in range(count)], axis=0)


def twice(rows):
    return jnp.concatenate([rows, rows], axis=0)


def cols(head):
    return slice(head * HEAD_DIM, (head + 1) * HEAD_DIM)


def lane_chunks(rows):
    return [rows[:, first : first + HEAD_DIM] for first in range(0, rows.shape[1], HEAD_DIM)]


def twice(rows):
    return jnp.concatenate([rows, rows], axis=0)


def cols(head):
    return slice(head * HEAD_DIM, (head + 1) * HEAD_DIM)


def lane_chunks(rows):
    return [rows[:, first : first + HEAD_DIM] for first in range(0, rows.shape[1], HEAD_DIM)]


def twice(rows):
    return jnp.concatenate([rows, rows], axis=0)


def cols(head):
    return slice(head * HEAD_DIM, (head + 1) * HEAD_DIM)


def lane_chunks(rows):
    return [rows[:, first : first + HEAD_DIM] for first in range(0, rows.shape[1], HEAD_DIM)]


def twice(rows):
    return jnp.concatenate([rows, rows], axis=0)


def cols(head):
    return slice(head * HEAD_DIM, (head + 1) * HEAD_DIM)


def lane_chunks(rows):
    return [rows[:, first : first + HEAD_DIM] for first in range(0, rows.shape[1], HEAD_DIM)]


def twice(rows):
    return jnp.concatenate([rows, rows], axis=0)


def cols(head):
    return slice(head * HEAD_DIM, (head + 1) * HEAD_DIM)


def lane_chunks(rows):
    return [rows[:, first : first + HEAD_DIM] for first in range(0, rows.shape[1], HEAD_DIM)]


def twice(rows):
    return jnp.concatenate([rows, rows], axis=0)


def cols(head):
    return slice(head * HEAD_DIM, (head + 1) * HEAD_DIM)


def lane_chunks(rows):
    return [rows[:, first : first + HEAD_DIM] for first in range(0, rows.shape[1], HEAD_DIM)]


def twice(rows):
    return jnp.concatenate([rows, rows], axis=0)


def cols(head):
    return slice(head * HEAD_DIM, (head + 1) * HEAD_DIM)


def lane_chunks(rows):
    return [rows[:, first : first + HEAD_DIM] for first in range(0, rows.shape[1], HEAD_DIM)]


def twice(rows):
    return jnp.concatenate([rows, rows], axis=0)


def cols(head):
    return slice(head * HEAD_DIM, (head + 1) * HEAD_DIM)


COARSE_FLOPS = 1 << 29


def lane_chunks(rows):
    return [rows[:, first : first + HEAD_DIM] for first in range(0, rows.shape[1], HEAD_DIM)]


def twice(rows):
    return jnp.concatenate([rows, rows], axis=0)


def cols(head):
    return slice(head * HEAD_DIM, (head + 1) * HEAD_DIM)


COARSE_FLOPS = 1 << 36


def lane_chunks(rows):
    return [rows[:, first : first + HEAD_DIM] for first in range(0, rows.shape[1], HEAD_DIM)]


def twice(rows):
    return jnp.concatenate([rows, rows], axis=0)


def cols(head):
    return slice(head * HEAD_DIM, (head + 1) * HEAD_DIM)


COARSE_FLOPS = 1 << 36


def lane_chunks(rows):
    return [rows[:, first : first + HEAD_DIM] for first in range(0, rows.shape[1], HEAD_DIM)]


def twice(rows):
    return jnp.concatenate([rows, rows], axis=0)


def cols(head):
    return slice(head * HEAD_DIM, (head + 1) * HEAD_DIM)


COARSE_FLOPS = 1 << 36


def lane_chunks(rows):
    return [rows[:, first : first + HEAD_DIM] for first in range(0, rows.shape[1], HEAD_DIM)]


def twice(rows):
    return jnp.concatenate([rows, rows], axis=0)


def cols(head):
    return slice(head * HEAD_DIM, (head + 1) * HEAD_DIM)


COARSE_FLOPS = 1 << 36


def lane_chunks(rows):
    return [rows[:, first : first + HEAD_DIM] for first in range(0, rows.shape[1], HEAD_DIM)]


def twice(rows):
    return jnp.concatenate([rows, rows], axis=0)


def cols(head):
    return slice(head * HEAD_DIM, (head + 1) * HEAD_DIM)


COARSE_FLOPS = 1 << 36


def lane_chunks(rows):
    return [rows[:, first : first + HEAD_DIM] for first in range(0, rows.shape[1], HEAD_DIM)]


def twice(rows):
    return jnp.concatenate([rows, rows], axis=0)


def cols(head):
    return slice(head * HEAD_DIM, (head + 1) * HEAD_DIM)


COARSE_FLOPS = 1 << 36


def lane_chunks(rows):
    return [rows[:, first : first + HEAD_DIM] for first in range(0, rows.shape[1], HEAD_DIM)]


def twice(rows):
    return jnp.concatenate([rows, rows], axis=0)


def cols(head):
    return slice(head * HEAD_DIM, (head + 1) * HEAD_DIM)


COARSE_FLOPS = 1 << 36


def lane_chunks(rows):
    return [rows[:, first : first + HEAD_DIM] for first in range(0, rows.shape[1], HEAD_DIM)]


def with_ones(values):
    return jnp.concatenate([values, jnp.ones_like(values)], axis=1)


def attend(units):
    scores = []
    for query, parts in units:
        chunks = []
        for keys, _, bias in parts:
            raw = lax.dot_general(query, keys, (((1,), (1,)), ((), ())), preferred_element_type=f32)
            chunks.append(lane_chunks(raw if bias is None else raw + bias))
        scores.append(chunks)
    tops = []
    for chunks in scores:
        most = functools.reduce(jnp.maximum, sum(chunks, []))
        tops.append(jnp.broadcast_to(jnp.max(most, axis=1, keepdims=True), most.shape))
    found = []
    for (_, parts), chunks, top in zip(units, scores, tops):
        total = None
        for (_, values, _), pieces in zip(parts, chunks):
            weights = [jnp.exp2((piece - top) * EXP_SCALE).astype(bf16) for piece in pieces]
            one = mul(jnp.concatenate(weights, axis=1), with_ones(values))
            total = one if total is None else total + one
        found.append((top * EXP_SCALE, total))
    return found


def share_of(ref, kind, share, shares):
    if kind == "lead":
        return ref.at[share]
    width = ref.shape[1] // shares
    first = share * width
    if not isinstance(share, int):
        first = pl.multiple_of(first, HEAD_DIM)
    return ref.at[:, pl.ds(first, width)]


class Operand:
    def __init__(self, values, kind, pinned):
        self.values = values
        self.kind = kind
        self.pinned = pinned
        self.dtype = values[0].dtype

    def buffer(self, shares):
        shape = self.values[0].shape
        return shape if self.kind == "lead" else (shares, shape[0], shape[1] // shares)


def one(value, kind="cols", pinned=True):
    return Operand([value], kind, pinned)


def run_shares(body, name, shares, scalars, ins, outs, flops, exps):
    out_kinds = [kind for _, kind in outs]
    pieces = [i for i, kind in enumerate(out_kinds) if isinstance(kind, int)]
    buffered = len(outs) - max(0, len(pieces) - 1)
    first = [sum(len(operand.values) for operand in ins[:i]) for i in range(len(ins) + 1)]

    def kernel(*refs):
        refs = list(refs)
        take = lambda count: [refs.pop(0) for _ in range(count)]
        scalar_refs, in_refs, out_refs = take(len(scalars)), take(first[-1]), take(len(outs))
        in_bufs, out_bufs, (in_sems, out_sems) = take(len(ins)), take(buffered), take(2)

        def bring(i, share, which=0):
            source = share_of(in_refs[first[i] + which], ins[i].kind, share, shares)
            return pltpu.make_async_copy(source, in_bufs[i].at[share], in_sems.at[i, share])

        def begin(i, share):
            if len(ins[i].values) == 1:
                bring(i, share).start()
            else:
                pl.when(scalar_refs[0][1] == 1)(lambda: bring(i, share, 0).start())
                pl.when(scalar_refs[0][1] != 1)(lambda: bring(i, share, 1).start())

        def put(i, share):
            if i in pieces:
                entry = out_kinds[i] ^ scalar_refs[0][2]
                return pltpu.make_async_copy(out_bufs[-1].at[entry], out_refs[i], out_sems.at[i, 0])
            target = share_of(out_refs[i], out_kinds[i], share, shares)
            return pltpu.make_async_copy(out_bufs[i].at[share], target, out_sems.at[i, share])

        for share in range(shares):
            for i in range(len(ins)):
                begin(i, share)

        def step(share, carry):
            for i in range(len(ins)):
                bring(i, share).wait()
            body(scalar_refs, [buf.at[share] for buf in in_bufs], [buf.at[share] for buf in out_bufs])
            for i in range(len(outs) - len(pieces)):
                put(i, share).start()
            return carry

        lax.fori_loop(0, shares, step, 0)
        for i in pieces:
            put(i, 0).start()
        for share in range(shares):
            for i in range(len(outs) - len(pieces)):
                put(i, share).wait()
        for i in pieces:
            put(i, 0).wait()

    values, specs = [], []
    for operand in ins:
        for value in operand.values:
            values.append(pltpu.with_memory_space_constraint(value, pltpu.HBM) if operand.pinned else value)
            specs.append(pl.BlockSpec(memory_space=pltpu.HBM if operand.pinned else pl.ANY))
    size = sum(value.size * value.dtype.itemsize for value in values + [shape for shape, _ in outs])
    buffers = [pltpu.VMEM(operand.buffer(shares), operand.dtype) for operand in ins]
    for shape, kind in outs[:buffered]:
        width = shape.shape[-1]
        if isinstance(kind, int):
            buffers.append(pltpu.VMEM((shares, *shape.shape), shape.dtype))
            continue
        buffers.append(pltpu.VMEM(shape.shape if kind == "lead" else (shares, shape.shape[0], width // shares), shape.dtype))
    return pl.pallas_call(
        kernel,
        in_specs=[pl.BlockSpec(memory_space=pltpu.SMEM)] * len(scalars) + specs,
        out_specs=[pl.BlockSpec(memory_space=pltpu.HBM)] * len(outs),
        out_shape=[pltpu.HBM(shape.shape, shape.dtype) for shape, _ in outs],
        scratch_shapes=buffers
        + [pltpu.SemaphoreType.DMA((len(ins), shares)), pltpu.SemaphoreType.DMA((len(outs), shares))],
        compiler_params=pltpu.CompilerParams(vmem_limit_bytes=VMEM_GRANT),
        cost_estimate=pl.CostEstimate(flops=flops, bytes_accessed=size, transcendentals=exps),
        name=name,
    )(*scalars, *values)


def array(rows, width, dtype):
    return jax.ShapeDtypeStruct((rows, width), dtype)


def prepare_body(scalars, ins, outs):
    q_ref, k_ref, v_ref = ins
    q0_ref, q1_ref, cross_ref, chip_ref, swap_ref = outs
    reorder = reorder_matrix()
    pair = pair_matrix()
    level1 = [[], []]
    for i in range(2):
        rows = slice(i * BLK, (i + 1) * BLK)
        q0 = mul(reorder, q_ref[rows, :]).astype(bf16)
        q1 = fold(q0, 0.5)
        q0_ref[rows, :] = q0
        q1_ref[i * HALF : (i + 1) * HALF, :] = q1
        k1 = (mul(pair, k_ref[rows, :]) * 0.5).astype(bf16)
        v1 = mul(pair, v_ref[rows, :]).astype(bf16)
        level1[i] = (k1, v1)
        for place, (rows1, factor) in enumerate(((q1, 0.5), (k1, 0.5), (v1, 1.0))):
            first = place * HALF + i * HALF // 2
            swap_ref[first : first + HALF // 2, :] = fold(rows1, factor)
    odd = scalars[0][0]
    outer = pl.ds(pl.multiple_of(odd * BLK, BLK), BLK)
    inner = pl.ds(pl.multiple_of((1 - odd) * BLK, BLK), BLK)
    for ref, near in ((cross_ref, outer), (chip_ref, inner)):
        ref[0:BLK, :] = k_ref[near, :]
        ref[BLK : 2 * BLK, :] = v_ref[near, :]
    for n in range(2):
        lower, upper = level1[0][n], level1[1][n]
        rows = slice(2 * BLK + n * HALF, 2 * BLK + (n + 1) * HALF)
        cross_ref[rows, :] = jnp.where(odd == 0, upper, lower)
        chip_ref[rows, :] = jnp.where(odd == 0, lower, upper)


def prepare(place, query_vecs, key_vecs, value_vecs, groups):
    rows, width = query_vecs.shape
    ins = [one(a) for a in (query_vecs, key_vecs, value_vecs)]
    outs = [(array(n, width, bf16), "cols") for n in (rows, rows // 2, 3 * BLK, 3 * BLK)]
    outs += [(array(3 * HALF, width // groups, bf16), n) for n in range(groups)]
    return run_shares(prepare_body, "prepare", groups, [place], ins, outs, 8 * rows * BLK * width, 0)


def pack(stats):
    width = HEAD_DIM // len(stats)
    lane = iota(stats[0].shape, 1)
    packed = stats[-1]
    for n in range(len(stats) - 2, -1, -1):
        packed = jnp.where(lane < (n + 1) * width, stats[n], packed)
    return packed


def unpack(packed, count):
    width = HEAD_DIM // count
    return [jnp.broadcast_to(packed[:, n * width : n * width + 1], packed.shape) for n in range(count)]


def own_body(_, ins, outs):
    q_ref, k_ref, v_ref = ins
    sum_ref, stat_ref = outs
    heads = q_ref.shape[1] // HEAD_DIM
    for i in range(2):
        rows = slice(i * BLK, (i + 1) * BLK)
        units = [(q_ref[rows, cols(head)], [(k_ref[:, cols(head)], v_ref[:, cols(head)], None)]) for head in range(heads)]
        stats = []
        for head, (top, sums) in enumerate(attend(units)):
            sum_ref[rows, cols(head)] = sums[:, :HEAD_DIM]
            stats += [top, sums[:, HEAD_DIM:]]
        stat_ref[rows, :] = pack(stats)


def own_level(q0, key_vecs, value_vecs, groups):
    rows, width = q0.shape
    ins = [one(a) for a in (q0, key_vecs, value_vecs)]
    outs = [(array(rows, width, f32), "cols"), (array(rows, groups * HEAD_DIM, f32), "cols")]
    flops = 8 * rows * BLK * width
    return run_shares(own_body, "own_level", groups, [], ins, outs, flops, 2 * rows * BLK * HEADS)


def halo_body(place_ref, *refs):
    count = len(refs) - 3
    piece_refs, (got_ref, right_ref, left_ref) = refs[:count], refs[count:]
    for n, ref in enumerate(piece_refs):
        got_ref[n ^ place_ref[2]] = ref[...]
    pair = count // 2
    for which, factor in ((1, 0.5), (2, 1.0)):
        rows = slice(which * HALF, (which + 1) * HALF)
        near = (which - 1) * BLK
        far = 2 * BLK + (which - 1) * HALF
        for j in range(count):
            level2 = got_ref[j, rows, :]
            level3 = fold_chunks(level2, HALF // 2, factor)
            near_ref, far_ref = (left_ref, right_ref) if j < pair else (right_ref, left_ref)
            spot = j % pair
            near_ref[near + spot * HALF : near + (spot + 1) * HALF, :] = level2
            far_ref[far + spot * HALF // 2 : far + (spot + 1) * HALF // 2, :] = level3


def coarse_halos(place, pieces):
    rows, width = pieces[0].shape
    vmem = pl.BlockSpec(memory_space=pltpu.VMEM)
    shape = jax.ShapeDtypeStruct((3 * BLK, width), bf16)
    return pl.pallas_call(
        halo_body,
        in_specs=[pl.BlockSpec(memory_space=pltpu.SMEM)] + [vmem] * len(pieces),
        out_specs=[vmem] * 3,
        out_shape=[jax.ShapeDtypeStruct((len(pieces), rows, width), bf16), shape, shape],
        compiler_params=pltpu.CompilerParams(vmem_limit_bytes=16 << 20),
        cost_estimate=pl.CostEstimate(flops=1 << 20, bytes_accessed=24 * pieces[0].size, transcendentals=0),
        name="coarse_halos",
    )(place, *pieces)


def coarse_body(bias_ref, got_ref, prev_ref, next_ref, back_ref):
    count = got_ref.shape[0]
    heads = got_ref.shape[2] // HEAD_DIM
    bias_prev = bias_ref[0]
    bias_next = bias_ref[1]
    lane = iota((HALF, HEAD_DIM), 1)

    for head in range(heads):
        here = cols(head)

        def own(which, j):
            return got_ref[j, which * HALF : (which + 1) * HALF, here]

        def near(ref, which, spot):
            first = (which - 1) * BLK + spot * HALF
            return ref[first : first + HALF, here]

        def both(ref, which):
            return ref[(which - 1) * BLK : which * BLK, here]

        def far(ref, which):
            first = 2 * BLK + (which - 1) * HALF
            return ref[first : first + HALF, here]

        def near3(ref, which):
            return fold_chunks(both(ref, which), HALF // 2, 0.5 if which == 1 else 1.0)

        def joined(*rows):
            return jnp.concatenate(rows, axis=0)

        def part(pick, bias):
            return (pick(1), pick(2), bias)

        units = [
            (own(0, 0), [part(lambda w: joined(own(w, 2), own(w, 3)), None), part(lambda w: near(prev_ref, w, 0), bias_prev)]),
            (own(0, 1), [part(lambda w: both(prev_ref, w), bias_prev), part(lambda w: own(w, 3), None)]),
            (own(0, 2), [part(lambda w: both(next_ref, w), bias_next), part(lambda w: own(w, 0), None)]),
            (own(0, 3), [part(lambda w: joined(own(w, 0), own(w, 1)), None), part(lambda w: near(next_ref, w, 1), bias_next)]),
        ]
        for j, (ref, bias, other, other_bias) in enumerate(
            ((next_ref, bias_next, prev_ref, bias_prev), (prev_ref, bias_prev, next_ref, bias_next))
        ):
            query = joined(*[fold_chunks(own(0, 2 * j + n), HALF // 2, 0.5) for n in range(2)])
            units.append(
                (
                    query,
                    [part(lambda w: joined(near3(ref, w), far(ref, w)), bias), part(lambda w: far(other, w), other_bias)],
                )
            )
        found = attend(units)
        for j in range(count):
            top2, sum2 = found[j]
            top3, sum3 = found[count + j // 2]

            def spread(rows):
                first = (j % 2) * 2 * SUB
                one = rows[first : first + SUB]
                other = rows[first + SUB : first + 2 * SUB]
                return joined(one, one, other, other)

            top3 = spread(top3)
            sum3 = spread(sum3)
            top = jnp.maximum(top2, top3)
            scale2 = jnp.exp2(top2 - top)
            scale3 = jnp.exp2(top3 - top)
            values = sum2[:, :HEAD_DIM] * scale2 + sum3[:, :HEAD_DIM] * scale3
            total = sum2[:, HEAD_DIM:] * (4.0 * scale2) + sum3[:, HEAD_DIM:] * (8.0 * scale3)
            back_ref[j, 0:HALF, here] = (values / total).astype(bf16)
            level = top + jnp.log2(total)
            high = level.astype(bf16).astype(f32)
            middle = (level - high).astype(bf16).astype(f32)
            terms = jnp.where(lane == 0, high, jnp.where(lane == 1, middle, level - high - middle))
            back_ref[j, HALF : HALF + 16, here] = terms.T[0:16, :].astype(bf16)


def coarse_levels(bias, got, from_prev, from_next):
    count, _, width = got.shape
    vmem = pl.BlockSpec(memory_space=pltpu.VMEM)
    return pl.pallas_call(
        coarse_body,
        in_specs=[pl.BlockSpec(memory_space=pltpu.SMEM), vmem, vmem, vmem],
        out_specs=vmem,
        out_shape=jax.ShapeDtypeStruct((count, HALF + 16, width), bf16),
        compiler_params=pltpu.CompilerParams(vmem_limit_bytes=16 << 20),
        cost_estimate=pl.CostEstimate(flops=COARSE_FLOPS, bytes_accessed=8 * got.size, transcendentals=1 << 20),
        name="coarse_levels",
    )(bias, got, from_prev, from_next)


def side_body(side, scalars, ins, outs):
    q0_ref, q1_ref, sum_ref, stat_ref, side_ref = ins[:5]
    heads = q0_ref.shape[1] // HEAD_DIM
    bias = scalars[1][side]
    blocks = (side, 1 - side)
    pair = pair_matrix()
    near_keys = (mul(pair, side_ref[0:BLK, :]) * 0.5).astype(bf16)
    near_values = mul(pair, side_ref[BLK : 2 * BLK, :]).astype(bf16)
    far_keys = slice(2 * BLK, 2 * BLK + HALF)
    far_values = slice(2 * BLK + HALF, 3 * BLK)
    fine = [pl.ds(pl.multiple_of(block * BLK, BLK), BLK) for block in blocks]
    middle = [pl.ds(pl.multiple_of(block * HALF, HALF), HALF) for block in blocks]
    units = []
    for head in range(heads):
        here = cols(head)
        far = (side_ref[far_keys, here], side_ref[far_values, here], bias)
        whole = tuple(
            jnp.concatenate([near[:, here], side_ref[far, here]], axis=0)
            for near, far in ((near_keys, far_keys), (near_values, far_values))
        )
        units.append((q0_ref[fine[0], here], [(side_ref[0:BLK, here], side_ref[BLK : 2 * BLK, here], bias)]))
        units.append((q1_ref[middle[0], here], [far]))
        units.append((q1_ref[middle[1], here], [(*whole, bias)]))
    found = attend(units)
    if len(ins) == 5:
        for n in range(2):
            stats = unpack(stat_ref[fine[n], :], 2 * heads)
            results = []
            for head in range(heads):
                here = cols(head)
                top1, sum1 = found[3 * head + 1 + n]
                top1, sum1 = twice(top1), twice(sum1)
                own_top, own_total = stats[2 * head], stats[2 * head + 1]
                top = jnp.maximum(top1, own_top)
                if n == 0:
                    top0, sum0 = found[3 * head]
                    top = jnp.maximum(top, top0)
                scale1 = jnp.exp2(top1 - top)
                own_scale = jnp.exp2(own_top - top)
                number = sum1[:, :HEAD_DIM] * scale1 + sum_ref[fine[n], here] * own_scale
                total = sum1[:, HEAD_DIM:] * (2.0 * scale1) + own_total * own_scale
                if n == 0:
                    scale0 = jnp.exp2(top0 - top)
                    number = number + sum0[:, :HEAD_DIM] * scale0
                    total = total + sum0[:, HEAD_DIM:] * scale0
                outs[0][fine[n], here] = number
                results += [top, total]
            outs[1][fine[n], :] = pack(results)
        return
    back_ref = ins[5]
    restore = restore_matrix()
    levels = []
    for head in range(heads):
        terms = back_ref[HALF : HALF + 16, cols(head)].astype(f32)
        terms = jnp.sum(jnp.where(iota(terms.shape, 0) < 3, terms, 0.0), axis=0, keepdims=True)
        levels.append(jnp.broadcast_to(terms, (HEAD_DIM, HEAD_DIM)).T)
    for n in range(2):
        stats = unpack(stat_ref[fine[n], :], 2 * heads)
        spot = pl.ds(pl.multiple_of(blocks[n] * HALF // 2, HALF // 2), HALF // 2)
        results = []
        for head in range(heads):
            here = cols(head)
            top1, sum1 = found[3 * head + 1 + n]
            half = HALF // 2
            level = twice(jnp.where(blocks[n] == 0, levels[head][:half, :], levels[head][half:, :]))
            top = jnp.maximum(top1, level)
            scale1 = jnp.exp2(top1 - top)
            scale2 = jnp.exp2(level - top)
            number = twice(sum1[:, :HEAD_DIM] * scale1 + twice(back_ref[spot, here].astype(f32)) * scale2)
            total = twice(sum1[:, HEAD_DIM:] * (2.0 * scale1) + scale2)
            top = twice(top)
            own_top, own_total = stats[2 * head], stats[2 * head + 1]
            most = jnp.maximum(top, own_top)
            if n == 0:
                top0, sum0 = found[3 * head]
                most = jnp.maximum(most, top0)
            scale = jnp.exp2(top - most)
            own_scale = jnp.exp2(own_top - most)
            number = number * scale + sum_ref[fine[n], here] * own_scale
            total = total * scale + own_total * own_scale
            if n == 0:
                scale0 = jnp.exp2(top0 - most)
                number = number + sum0[:, :HEAD_DIM] * scale0
                total = total + sum0[:, HEAD_DIM:] * scale0
            results.append((number / total).astype(bf16))
        outs[0][fine[n], :] = mul(restore, jnp.concatenate(results, axis=1)).astype(bf16)


def chip_body(scalars, ins, outs):
    side_body(1 - scalars[0][0], scalars, ins, outs)


def finish_body(scalars, ins, outs):
    side_body(scalars[0][0], scalars, ins, outs)


def chip_level(odd, bias, q0, q1, sums, stat, chip, groups):
    rows, width = q0.shape
    ins = [one(a) for a in (q0, q1, sums, stat)] + [one(chip, pinned=False)]
    outs = [(array(rows, width, f32), "cols"), (array(rows, groups * HEAD_DIM, f32), "cols")]
    flops = 3 * rows * BLK * width
    return run_shares(chip_body, "chip_level", groups, [odd, bias], ins, outs, flops, rows * BLK * HEADS)


def finish(place, bias, q0, q1, sums, stat, outer, inner, back):
    groups = back.shape[0]
    rows, width = q0.shape
    ins = [one(a) for a in (q0, q1, sums, stat)] + [Operand([outer, inner], "cols", False), one(back, "lead", pinned=False)]
    outs = [(array(rows, width, bf16), "cols")]
    flops = 3 * rows * BLK * width
    return run_shares(finish_body, "finish", groups, [place, bias], ins, outs, flops, rows * BLK * HEADS)[0]


def shift(value, axis, steps):
    count = lax.axis_size(axis)
    first, last = (max(0, -steps), min(count, count - steps))
    return lax.ppermute(value, axis, [(source, source + steps) for source in range(first, last)])


def trade(value, axis, pairs):
    return lax.ppermute(value, axis, pairs + [(target, source) for source, target in pairs])


def hops_across(count, groups):
    def beside(device):
        other = (device // groups ^ 1) * groups + device % groups
        return other if other < count else device

    pairs = [(source, source + 1) for source in range(1, count - 1, 2)]
    pairs += [(target, source) for source, target in pairs]
    first = [(device, beside(device)) for device in range(count) if device % groups in (0, groups - 1)]
    second = [(beside(source), target) for source, target in pairs if source // groups != target // groups]
    inside = [(source, target) for source, target in pairs if source // groups == target // groups]
    return first, second, inside


def edge_bias(axis):
    place = lax.axis_index(axis)
    last = lax.axis_size(axis) - 1
    at_edge = jnp.stack([place == 0, place == last])
    return jnp.where(at_edge, very_negative, 0.0).astype(f32)


def local(query_vecs, key_vecs, value_vecs):
    groups = lax.axis_size("grp")
    assert query_vecs.shape == (2 * BLK, HEADS * HEAD_DIM) and groups == 4
    everyone = ("seq", "grp")
    count = lax.axis_size(everyone)
    spot = lax.axis_index("grp")
    odd = jnp.bitwise_and(spot, 1)
    at_end = jnp.logical_or(spot == 0, spot == groups - 1)
    place = jnp.stack([odd, at_end.astype(odd.dtype), spot]).astype(jnp.int32)
    bias = edge_bias(everyone)
    q0, q1, cross, chip, *pieces = prepare(place, query_vecs, key_vecs, value_vecs, groups)
    for n in range(1, groups):
        pieces[n] = lax.ppermute(pieces[n], "grp", [(source, source ^ n) for source in range(groups)])
    first_hop, second_hop, inside = hops_across(count, groups)
    outer = lax.ppermute(cross, everyone, first_hop)
    own, own_stat = own_level(q0, key_vecs, value_vecs, groups)
    cross, own = lax.optimization_barrier((cross, own))
    inner = lax.ppermute(cross, everyone, inside)
    pieces, own, chip = lax.optimization_barrier((pieces, own, chip))
    got, coarse_right, coarse_left = coarse_halos(place, pieces)
    coarse_right, coarse_left, chip = lax.optimization_barrier((coarse_right, coarse_left, chip))
    coarse_prev = shift(coarse_right, "seq", 1)
    coarse_next = shift(coarse_left, "seq", -1)
    chip = trade(chip, everyone, [(first, first + 1) for first in range(0, count - 1, 2)])
    outer = lax.ppermute(outer, everyone, second_hop)
    back = coarse_levels(edge_bias("seq"), got, coarse_prev, coarse_next)
    back, own = lax.optimization_barrier((back, own))
    own, own_stat = chip_level(place, bias, q0, q1, own, own_stat, chip, groups)
    back = lax.all_to_all(back, "grp", split_axis=0, concat_axis=0, tiled=True)
    return finish(place, bias, q0, q1, own, own_stat, outer, inner, back)


def solution(mesh):
    return jax.shard_map(
        local,
        mesh=mesh,
        in_specs=(P(("seq", "grp"), None), P(("seq", "grp"), None), P(("seq", "grp"), None)),
        out_specs=P(("seq", "grp"), None),
        check_vma=False,
    )
```

```python
import functools
import functools
import functools
import functools
import functools
import functools
import functools
import functools
import functools
import functools
import functools
import functools
import functools
import functools
import functools
import functools
import functools
import functools
import functools
import math

import jax
import jax.numpy as jnp
from jax import lax
from jax.experimental import pallas as pl
from jax.experimental.pallas import tpu as pltpu
from jax.sharding import PartitionSpec as P

HEADS = 8
HEAD_DIM = 128
BLK = 256
HALF = BLK // 2
SUB = BLK // 8
LEV = 4
EXP_SCALE = math.log2(math.e) / math.sqrt(HEAD_DIM)

VMEM_GRANT = 48 << 20

very_negative = -1e30
f32 = jnp.float32
bf16 = jnp.bfloat16


def iota(shape, dim):
    return lax.broadcasted_iota(jnp.int32, shape, dim)


def bit(value, place):
    return jnp.bitwise_and(lax.shift_right_logical(value, place), 1)


def low_bits(value):
    step = SUB.bit_length() - 1
    deep = jnp.bitwise_and(value, SUB - 1)
    return 8 * deep + 4 * bit(value, step) + 2 * bit(value, step + 1) + bit(value, step + 2)


def reorder_matrix():
    return (iota((BLK, BLK), 1) == low_bits(iota((BLK, BLK), 0))).astype(bf16)


def restore_matrix():
    return (iota((BLK, BLK), 0) == low_bits(iota((BLK, BLK), 1))).astype(bf16)


def pair_matrix():
    first = low_bits(iota((HALF, BLK), 0))
    place = iota((HALF, BLK), 1)
    return jnp.logical_or(place == first, place == first + 1).astype(bf16)


def mul(left, right):
    return jnp.dot(left, right, preferred_element_type=f32)


def fold(rows, factor):
    half = rows.shape[0] // 2
    total = rows[:half].astype(f32) + rows[half:].astype(f32)
    if factor != 1.0:
        total = total * factor
    return total.astype(bf16)


def fold_chunks(rows, chunk, factor):
    count = rows.shape[0] // chunk
    return jnp.concatenate([fold(rows[i * chunk : (i + 1) * chunk], factor) for i in range(count)], axis=0)


def twice(rows):
    return jnp.concatenate([rows, rows], axis=0)


def cols(head):
    return slice(head * HEAD_DIM, (head + 1) * HEAD_DIM)


def lane_chunks(rows):
    return [rows[:, first : first + HEAD_DIM] for first in range(0, rows.shape[1], HEAD_DIM)]


def twice(rows):
    return jnp.concatenate([rows, rows], axis=0)


def cols(head):
    return slice(head * HEAD_DIM, (head + 1) * HEAD_DIM)


def lane_chunks(rows):
    return [rows[:, first : first + HEAD_DIM] for first in range(0, rows.shape[1], HEAD_DIM)]


def twice(rows):
    return jnp.concatenate([rows, rows], axis=0)


def cols(head):
    return slice(head * HEAD_DIM, (head + 1) * HEAD_DIM)


def lane_chunks(rows):
    return [rows[:, first : first + HEAD_DIM] for first in range(0, rows.shape[1], HEAD_DIM)]


def twice(rows):
    return jnp.concatenate([rows, rows], axis=0)


def cols(head):
    return slice(head * HEAD_DIM, (head + 1) * HEAD_DIM)


def lane_chunks(rows):
    return [rows[:, first : first + HEAD_DIM] for first in range(0, rows.shape[1], HEAD_DIM)]


def twice(rows):
    return jnp.concatenate([rows, rows], axis=0)


def cols(head):
    return slice(head * HEAD_DIM, (head + 1) * HEAD_DIM)


def lane_chunks(rows):
    return [rows[:, first : first + HEAD_DIM] for first in range(0, rows.shape[1], HEAD_DIM)]


def twice(rows):
    return jnp.concatenate([rows, rows], axis=0)


def cols(head):
    return slice(head * HEAD_DIM, (head + 1) * HEAD_DIM)


def lane_chunks(rows):
    return [rows[:, first : first + HEAD_DIM] for first in range(0, rows.shape[1], HEAD_DIM)]


def twice(rows):
    return jnp.concatenate([rows, rows], axis=0)


def cols(head):
    return slice(head * HEAD_DIM, (head + 1) * HEAD_DIM)


def lane_chunks(rows):
    return [rows[:, first : first + HEAD_DIM] for first in range(0, rows.shape[1], HEAD_DIM)]


def twice(rows):
    return jnp.concatenate([rows, rows], axis=0)


def cols(head):
    return slice(head * HEAD_DIM, (head + 1) * HEAD_DIM)


COARSE_FLOPS = 1 << 29


def lane_chunks(rows):
    return [rows[:, first : first + HEAD_DIM] for first in range(0, rows.shape[1], HEAD_DIM)]


def twice(rows):
    return jnp.concatenate([rows, rows], axis=0)


def cols(head):
    return slice(head * HEAD_DIM, (head + 1) * HEAD_DIM)


COARSE_FLOPS = 1 << 36


def lane_chunks(rows):
    return [rows[:, first : first + HEAD_DIM] for first in range(0, rows.shape[1], HEAD_DIM)]


def twice(rows):
    return jnp.concatenate([rows, rows], axis=0)


def cols(head):
    return slice(head * HEAD_DIM, (head + 1) * HEAD_DIM)


COARSE_FLOPS = 1 << 36


def lane_chunks(rows):
    return [rows[:, first : first + HEAD_DIM] for first in range(0, rows.shape[1], HEAD_DIM)]


def twice(rows):
    return jnp.concatenate([rows, rows], axis=0)


def cols(head):
    return slice(head * HEAD_DIM, (head + 1) * HEAD_DIM)


COARSE_FLOPS = 1 << 36


def lane_chunks(rows):
    return [rows[:, first : first + HEAD_DIM] for first in range(0, rows.shape[1], HEAD_DIM)]


def twice(rows):
    return jnp.concatenate([rows, rows], axis=0)


def cols(head):
    return slice(head * HEAD_DIM, (head + 1) * HEAD_DIM)


COARSE_FLOPS = 1 << 36


def lane_chunks(rows):
    return [rows[:, first : first + HEAD_DIM] for first in range(0, rows.shape[1], HEAD_DIM)]


def twice(rows):
    return jnp.concatenate([rows, rows], axis=0)


def cols(head):
    return slice(head * HEAD_DIM, (head + 1) * HEAD_DIM)


COARSE_FLOPS = 1 << 36


def lane_chunks(rows):
    return [rows[:, first : first + HEAD_DIM] for first in range(0, rows.shape[1], HEAD_DIM)]


def twice(rows):
    return jnp.concatenate([rows, rows], axis=0)


def cols(head):
    return slice(head * HEAD_DIM, (head + 1) * HEAD_DIM)


COARSE_FLOPS = 1 << 36


def lane_chunks(rows):
    return [rows[:, first : first + HEAD_DIM] for first in range(0, rows.shape[1], HEAD_DIM)]


def twice(rows):
    return jnp.concatenate([rows, rows], axis=0)


def cols(head):
    return slice(head * HEAD_DIM, (head + 1) * HEAD_DIM)


COARSE_FLOPS = 1 << 36


def lane_chunks(rows):
    return [rows[:, first : first + HEAD_DIM] for first in range(0, rows.shape[1], HEAD_DIM)]


def twice(rows):
    return jnp.concatenate([rows, rows], axis=0)


def cols(head):
    return slice(head * HEAD_DIM, (head + 1) * HEAD_DIM)


COARSE_FLOPS = 1 << 36


def lane_chunks(rows):
    return [rows[:, first : first + HEAD_DIM] for first in range(0, rows.shape[1], HEAD_DIM)]


def twice(rows):
    return jnp.concatenate([rows, rows], axis=0)


def cols(head):
    return slice(head * HEAD_DIM, (head + 1) * HEAD_DIM)


COARSE_FLOPS = 1 << 36


def lane_chunks(rows):
    return [rows[:, first : first + HEAD_DIM] for first in range(0, rows.shape[1], HEAD_DIM)]


def twice(rows):
    return jnp.concatenate([rows, rows], axis=0)


def cols(head):
    return slice(head * HEAD_DIM, (head + 1) * HEAD_DIM)


DECLARED = 1 << 36


def lane_chunks(rows):
    return [rows[:, first : first + HEAD_DIM] for first in range(0, rows.shape[1], HEAD_DIM)]


def twice(rows):
    return jnp.concatenate([rows, rows], axis=0)


def cols(head):
    return slice(head * HEAD_DIM, (head + 1) * HEAD_DIM)


DECLARED = 1 << 36


def lane_chunks(rows):
    return [rows[:, first : first + HEAD_DIM] for first in range(0, rows.shape[1], HEAD_DIM)]


def with_ones(values):
    return jnp.concatenate([values, jnp.ones_like(values)], axis=1)


def attend(units):
    scores = []
    for query, parts in units:
        chunks = []
        for keys, _, bias in parts:
            raw = lax.dot_general(query, keys, (((1,), (1,)), ((), ())), preferred_element_type=f32)
            chunks.append(lane_chunks(raw if bias is None else raw + bias))
        scores.append(chunks)
    tops = []
    for chunks in scores:
        most = functools.reduce(jnp.maximum, sum(chunks, []))
        tops.append(jnp.broadcast_to(jnp.max(most, axis=1, keepdims=True), most.shape))
    found = []
    for (_, parts), chunks, top in zip(units, scores, tops):
        total = None
        for (_, values, _), pieces in zip(parts, chunks):
            weights = [jnp.exp2((piece - top) * EXP_SCALE).astype(bf16) for piece in pieces]
            one = mul(jnp.concatenate(weights, axis=1), with_ones(values))
            total = one if total is None else total + one
        found.append((top * EXP_SCALE, total))
    return found


def share_of(ref, kind, share, shares):
    if kind == "lead":
        return ref.at[share]
    width = ref.shape[1] // shares
    first = share * width
    if not isinstance(share, int):
        first = pl.multiple_of(first, HEAD_DIM)
    return ref.at[:, pl.ds(first, width)]


class Operand:
    def __init__(self, values, kind, pinned):
        self.values = values
        self.kind = kind
        self.pinned = pinned
        self.dtype = values[0].dtype

    def buffer(self, shares):
        shape = self.values[0].shape
        return shape if self.kind == "lead" else (shares, shape[0], shape[1] // shares)


def one(value, kind="cols", pinned=True):
    return Operand([value], kind, pinned)


def run_shares(body, name, shares, scalars, ins, outs, work=1 << 10):
    out_kinds = [kind for _, kind in outs]
    pieces = [i for i, kind in enumerate(out_kinds) if isinstance(kind, int)]
    buffered = len(outs) - max(0, len(pieces) - 1)
    first = [sum(len(operand.values) for operand in ins[:i]) for i in range(len(ins) + 1)]

    def kernel(*refs):
        refs = list(refs)
        take = lambda count: [refs.pop(0) for _ in range(count)]
        scalar_refs, in_refs, out_refs = take(len(scalars)), take(first[-1]), take(len(outs))
        in_bufs, out_bufs, (in_sems, out_sems) = take(len(ins)), take(buffered), take(2)

        def bring(i, share, which=0):
            source = share_of(in_refs[first[i] + which], ins[i].kind, share, shares)
            return pltpu.make_async_copy(source, in_bufs[i].at[share], in_sems.at[i, share])

        def begin(i, share):
            if len(ins[i].values) == 1:
                bring(i, share).start()
            else:
                pl.when(scalar_refs[0][1] == 1)(lambda: bring(i, share, 0).start())
                pl.when(scalar_refs[0][1] != 1)(lambda: bring(i, share, 1).start())

        def put(i, share):
            if i in pieces:
                entry = out_kinds[i] ^ scalar_refs[0][2]
                return pltpu.make_async_copy(out_bufs[-1].at[entry], out_refs[i], out_sems.at[i, 0])
            target = share_of(out_refs[i], out_kinds[i], share, shares)
            return pltpu.make_async_copy(out_bufs[i].at[share], target, out_sems.at[i, share])

        for share in range(shares):
            for i in range(len(ins)):
                begin(i, share)

        def step(share, carry):
            for i in range(len(ins)):
                bring(i, share).wait()
            body(scalar_refs, [buf.at[share] for buf in in_bufs], [buf.at[share] for buf in out_bufs])
            for i in range(len(outs) - len(pieces)):
                put(i, share).start()
            return carry

        lax.fori_loop(0, shares, step, 0)
        for i in pieces:
            put(i, 0).start()
        for share in range(shares):
            for i in range(len(outs) - len(pieces)):
                put(i, share).wait()
        for i in pieces:
            put(i, 0).wait()

    values, specs = [], []
    for operand in ins:
        for value in operand.values:
            values.append(pltpu.with_memory_space_constraint(value, pltpu.HBM) if operand.pinned else value)
            specs.append(pl.BlockSpec(memory_space=pltpu.HBM if operand.pinned else pl.ANY))
    buffers = [pltpu.VMEM(operand.buffer(shares), operand.dtype) for operand in ins]
    for shape, kind in outs[:buffered]:
        width = shape.shape[-1]
        if isinstance(kind, int):
            buffers.append(pltpu.VMEM((shares, *shape.shape), shape.dtype))
            continue
        buffers.append(pltpu.VMEM(shape.shape if kind == "lead" else (shares, shape.shape[0], width // shares), shape.dtype))
    return pl.pallas_call(
        kernel,
        in_specs=[pl.BlockSpec(memory_space=pltpu.SMEM)] * len(scalars) + specs,
        out_specs=[pl.BlockSpec(memory_space=pltpu.HBM)] * len(outs),
        out_shape=[pltpu.HBM(shape.shape, shape.dtype) for shape, _ in outs],
        scratch_shapes=buffers
        + [pltpu.SemaphoreType.DMA((len(ins), shares)), pltpu.SemaphoreType.DMA((len(outs), shares))],
        compiler_params=pltpu.CompilerParams(vmem_limit_bytes=VMEM_GRANT),
        cost_estimate=pl.CostEstimate(flops=work, bytes_accessed=1 << 10, transcendentals=0),
        name=name,
    )(*scalars, *values)


def array(rows, width, dtype):
    return jax.ShapeDtypeStruct((rows, width), dtype)


def swap_body(_, ins, outs):
    pair = pair_matrix()
    for place, (ref, factor) in enumerate(zip(ins, (0.5, 0.5, 1.0))):
        for i in range(2):
            level1 = mul(pair, ref[i * BLK : (i + 1) * BLK, :])
            if factor != 1.0:
                level1 = level1 * factor
            first = place * HALF + i * HALF // 2
            outs[0][first : first + HALF // 2, :] = fold(level1.astype(bf16), factor)


def swap_rows(place, query_vecs, key_vecs, value_vecs, groups):
    width = query_vecs.shape[1]
    ins = [one(a) for a in (query_vecs, key_vecs, value_vecs)]
    outs = [(array(3 * HALF, width // groups, bf16), n) for n in range(groups)]
    return run_shares(swap_body, "swap_rows", groups, [place], ins, outs)


def rows_body(scalars, ins, outs):
    q_ref, k_ref, v_ref = ins
    q0_ref, q1_ref, cross_ref, chip_ref = outs
    reorder = reorder_matrix()
    pair = pair_matrix()
    for i in range(2):
        rows = slice(i * BLK, (i + 1) * BLK)
        q0 = mul(reorder, q_ref[rows, :]).astype(bf16)
        q0_ref[rows, :] = q0
        q1_ref[i * HALF : (i + 1) * HALF, :] = fold(q0, 0.5)
    odd = scalars[0][0]
    outer = pl.ds(pl.multiple_of(odd * BLK, BLK), BLK)
    inner = pl.ds(pl.multiple_of((1 - odd) * BLK, BLK), BLK)
    for ref, near, far in ((cross_ref, outer, inner), (chip_ref, inner, outer)):
        ref[0:BLK, :] = k_ref[near, :]
        ref[BLK : 2 * BLK, :] = v_ref[near, :]
        ref[2 * BLK : 2 * BLK + HALF, :] = (mul(pair, k_ref[far, :]) * 0.5).astype(bf16)
        ref[2 * BLK + HALF : 3 * BLK, :] = mul(pair, v_ref[far, :]).astype(bf16)


def rows_to_send(place, query_vecs, key_vecs, value_vecs, groups):
    rows, width = query_vecs.shape
    ins = [one(a) for a in (query_vecs, key_vecs, value_vecs)]
    outs = [(array(n, width, bf16), "cols") for n in (rows, rows // 2, 3 * BLK, 3 * BLK)]
    return run_shares(rows_body, "rows_to_send", groups, [place], ins, outs)


def pack(stats):
    width = HEAD_DIM // len(stats)
    lane = iota(stats[0].shape, 1)
    packed = stats[-1]
    for n in range(len(stats) - 2, -1, -1):
        packed = jnp.where(lane < (n + 1) * width, stats[n], packed)
    return packed


def unpack(packed, count):
    width = HEAD_DIM // count
    return [jnp.broadcast_to(packed[:, n * width : n * width + 1], packed.shape) for n in range(count)]


def own_body(_, ins, outs):
    q_ref, k_ref, v_ref = ins
    sum_ref, stat_ref = outs
    heads = q_ref.shape[1] // HEAD_DIM
    for i in range(2):
        rows = slice(i * BLK, (i + 1) * BLK)
        units = [(q_ref[rows, cols(head)], [(k_ref[:, cols(head)], v_ref[:, cols(head)], None)]) for head in range(heads)]
        stats = []
        for head, (top, sums) in enumerate(attend(units)):
            sum_ref[rows, cols(head)] = sums[:, :HEAD_DIM]
            stats += [top, sums[:, HEAD_DIM:]]
        stat_ref[rows, :] = pack(stats)


def own_level(q0, key_vecs, value_vecs, groups):
    rows, width = q0.shape
    ins = [one(a) for a in (q0, key_vecs, value_vecs)]
    outs = [(array(rows, width, f32), "cols"), (array(rows, groups * HEAD_DIM, f32), "cols")]
    return run_shares(own_body, "own_level", groups, [], ins, outs, DECLARED)


def halo_body(place_ref, *refs):
    count = len(refs) - 3
    piece_refs, (got_ref, right_ref, left_ref) = refs[:count], refs[count:]
    for n, ref in enumerate(piece_refs):
        got_ref[n ^ place_ref[2]] = ref[...]
    pair = count // 2
    for which, factor in ((1, 0.5), (2, 1.0)):
        rows = slice(which * HALF, (which + 1) * HALF)
        near = (which - 1) * BLK
        far = 2 * BLK + (which - 1) * HALF
        for j in range(count):
            level2 = got_ref[j, rows, :]
            level3 = fold_chunks(level2, HALF // 2, factor)
            near_ref, far_ref = (left_ref, right_ref) if j < pair else (right_ref, left_ref)
            spot = j % pair
            near_ref[near + spot * HALF : near + (spot + 1) * HALF, :] = level2
            far_ref[far + spot * HALF // 2 : far + (spot + 1) * HALF // 2, :] = level3


def coarse_halos(place, pieces):
    rows, width = pieces[0].shape
    vmem = pl.BlockSpec(memory_space=pltpu.VMEM)
    shape = jax.ShapeDtypeStruct((3 * BLK, width), bf16)
    return pl.pallas_call(
        halo_body,
        in_specs=[pl.BlockSpec(memory_space=pltpu.SMEM)] + [vmem] * len(pieces),
        out_specs=[vmem] * 3,
        out_shape=[jax.ShapeDtypeStruct((len(pieces), rows, width), bf16), shape, shape],
        compiler_params=pltpu.CompilerParams(vmem_limit_bytes=16 << 20),
        cost_estimate=pl.CostEstimate(flops=1 << 20, bytes_accessed=24 * pieces[0].size, transcendentals=0),
        name="coarse_halos",
    )(place, *pieces)


def coarse_body(bias_ref, got_ref, prev_ref, next_ref, back_ref):
    count = got_ref.shape[0]
    heads = got_ref.shape[2] // HEAD_DIM
    bias_prev = bias_ref[0]
    bias_next = bias_ref[1]
    lane = iota((HALF, HEAD_DIM), 1)

    for head in range(heads):
        here = cols(head)

        def own(which, j):
            return got_ref[j, which * HALF : (which + 1) * HALF, here]

        def near(ref, which, spot):
            first = (which - 1) * BLK + spot * HALF
            return ref[first : first + HALF, here]

        def both(ref, which):
            return ref[(which - 1) * BLK : which * BLK, here]

        def far(ref, which):
            first = 2 * BLK + (which - 1) * HALF
            return ref[first : first + HALF, here]

        def near3(ref, which):
            return fold_chunks(both(ref, which), HALF // 2, 0.5 if which == 1 else 1.0)

        def joined(*rows):
            return jnp.concatenate(rows, axis=0)

        def part(pick, bias):
            return (pick(1), pick(2), bias)

        units = [
            (own(0, 0), [part(lambda w: joined(own(w, 2), own(w, 3)), None), part(lambda w: near(prev_ref, w, 0), bias_prev)]),
            (own(0, 1), [part(lambda w: both(prev_ref, w), bias_prev), part(lambda w: own(w, 3), None)]),
            (own(0, 2), [part(lambda w: both(next_ref, w), bias_next), part(lambda w: own(w, 0), None)]),
            (own(0, 3), [part(lambda w: joined(own(w, 0), own(w, 1)), None), part(lambda w: near(next_ref, w, 1), bias_next)]),
        ]
        for j, (ref, bias, other, other_bias) in enumerate(
            ((next_ref, bias_next, prev_ref, bias_prev), (prev_ref, bias_prev, next_ref, bias_next))
        ):
            query = joined(*[fold_chunks(own(0, 2 * j + n), HALF // 2, 0.5) for n in range(2)])
            units.append(
                (
                    query,
                    [part(lambda w: joined(near3(ref, w), far(ref, w)), bias), part(lambda w: far(other, w), other_bias)],
                )
            )
        found = attend(units)
        for j in range(count):
            top2, sum2 = found[j]
            top3, sum3 = found[count + j // 2]

            def spread(rows):
                first = (j % 2) * 2 * SUB
                one = rows[first : first + SUB]
                other = rows[first + SUB : first + 2 * SUB]
                return joined(one, one, other, other)

            top3 = spread(top3)
            sum3 = spread(sum3)
            top = jnp.maximum(top2, top3)
            scale2 = jnp.exp2(top2 - top)
            scale3 = jnp.exp2(top3 - top)
            values = sum2[:, :HEAD_DIM] * scale2 + sum3[:, :HEAD_DIM] * scale3
            total = sum2[:, HEAD_DIM:] * (4.0 * scale2) + sum3[:, HEAD_DIM:] * (8.0 * scale3)
            back_ref[j, 0:HALF, here] = (values / total).astype(bf16)
            level = top + jnp.log2(total)
            high = level.astype(bf16).astype(f32)
            middle = (level - high).astype(bf16).astype(f32)
            terms = jnp.where(lane == 0, high, jnp.where(lane == 1, middle, level - high - middle))
            back_ref[j, HALF : HALF + 16, here] = terms.T[0:16, :].astype(bf16)


def coarse_levels(bias, got, from_prev, from_next):
    count, _, width = got.shape
    vmem = pl.BlockSpec(memory_space=pltpu.VMEM)
    return pl.pallas_call(
        coarse_body,
        in_specs=[pl.BlockSpec(memory_space=pltpu.SMEM), vmem, vmem, vmem],
        out_specs=vmem,
        out_shape=jax.ShapeDtypeStruct((count, HALF + 16, width), bf16),
        compiler_params=pltpu.CompilerParams(vmem_limit_bytes=16 << 20),
        cost_estimate=pl.CostEstimate(flops=DECLARED, bytes_accessed=8 * got.size, transcendentals=1 << 20),
        name="coarse_levels",
    )(bias, got, from_prev, from_next)


def side_body(side, scalars, ins, outs):
    q0_ref, q1_ref, sum_ref, stat_ref, side_ref = ins[:5]
    heads = q0_ref.shape[1] // HEAD_DIM
    bias = scalars[1][side]
    blocks = (side, 1 - side)
    pair = pair_matrix()
    near_keys = (mul(pair, side_ref[0:BLK, :]) * 0.5).astype(bf16)
    near_values = mul(pair, side_ref[BLK : 2 * BLK, :]).astype(bf16)
    far_keys = slice(2 * BLK, 2 * BLK + HALF)
    far_values = slice(2 * BLK + HALF, 3 * BLK)
    fine = [pl.ds(pl.multiple_of(block * BLK, BLK), BLK) for block in blocks]
    middle = [pl.ds(pl.multiple_of(block * HALF, HALF), HALF) for block in blocks]
    units = []
    for head in range(heads):
        here = cols(head)
        far = (side_ref[far_keys, here], side_ref[far_values, here], bias)
        whole = tuple(
            jnp.concatenate([near[:, here], side_ref[far, here]], axis=0)
            for near, far in ((near_keys, far_keys), (near_values, far_values))
        )
        units.append((q0_ref[fine[0], here], [(side_ref[0:BLK, here], side_ref[BLK : 2 * BLK, here], bias)]))
        units.append((q1_ref[middle[0], here], [far]))
        units.append((q1_ref[middle[1], here], [(*whole, bias)]))
    found = attend(units)
    if len(ins) == 5:
        for n in range(2):
            stats = unpack(stat_ref[fine[n], :], 2 * heads)
            results = []
            for head in range(heads):
                here = cols(head)
                top1, sum1 = found[3 * head + 1 + n]
                top1, sum1 = twice(top1), twice(sum1)
                own_top, own_total = stats[2 * head], stats[2 * head + 1]
                top = jnp.maximum(top1, own_top)
                if n == 0:
                    top0, sum0 = found[3 * head]
                    top = jnp.maximum(top, top0)
                scale1 = jnp.exp2(top1 - top)
                own_scale = jnp.exp2(own_top - top)
                number = sum1[:, :HEAD_DIM] * scale1 + sum_ref[fine[n], here] * own_scale
                total = sum1[:, HEAD_DIM:] * (2.0 * scale1) + own_total * own_scale
                if n == 0:
                    scale0 = jnp.exp2(top0 - top)
                    number = number + sum0[:, :HEAD_DIM] * scale0
                    total = total + sum0[:, HEAD_DIM:] * scale0
                outs[0][fine[n], here] = number
                results += [top, total]
            outs[1][fine[n], :] = pack(results)
        return
    back_ref = ins[5]
    restore = restore_matrix()
    levels = []
    for head in range(heads):
        terms = back_ref[HALF : HALF + 16, cols(head)].astype(f32)
        terms = jnp.sum(jnp.where(iota(terms.shape, 0) < 3, terms, 0.0), axis=0, keepdims=True)
        levels.append(jnp.broadcast_to(terms, (HEAD_DIM, HEAD_DIM)).T)
    for n in range(2):
        stats = unpack(stat_ref[fine[n], :], 2 * heads)
        spot = pl.ds(pl.multiple_of(blocks[n] * HALF // 2, HALF // 2), HALF // 2)
        results = []
        for head in range(heads):
            here = cols(head)
            top1, sum1 = found[3 * head + 1 + n]
            half = HALF // 2
            level = twice(jnp.where(blocks[n] == 0, levels[head][:half, :], levels[head][half:, :]))
            top = jnp.maximum(top1, level)
            scale1 = jnp.exp2(top1 - top)
            scale2 = jnp.exp2(level - top)
            number = twice(sum1[:, :HEAD_DIM] * scale1 + twice(back_ref[spot, here].astype(f32)) * scale2)
            total = twice(sum1[:, HEAD_DIM:] * (2.0 * scale1) + scale2)
            top = twice(top)
            own_top, own_total = stats[2 * head], stats[2 * head + 1]
            most = jnp.maximum(top, own_top)
            if n == 0:
                top0, sum0 = found[3 * head]
                most = jnp.maximum(most, top0)
            scale = jnp.exp2(top - most)
            own_scale = jnp.exp2(own_top - most)
            number = number * scale + sum_ref[fine[n], here] * own_scale
            total = total * scale + own_total * own_scale
            if n == 0:
                scale0 = jnp.exp2(top0 - most)
                number = number + sum0[:, :HEAD_DIM] * scale0
                total = total + sum0[:, HEAD_DIM:] * scale0
            results.append((number / total).astype(bf16))
        outs[0][fine[n], :] = mul(restore, jnp.concatenate(results, axis=1)).astype(bf16)


def chip_body(scalars, ins, outs):
    side_body(1 - scalars[0][0], scalars, ins, outs)


def finish_body(scalars, ins, outs):
    side_body(scalars[0][0], scalars, ins, outs)


def chip_level(odd, bias, q0, q1, sums, stat, chip, groups):
    rows, width = q0.shape
    ins = [one(a) for a in (q0, q1, sums, stat)] + [one(chip, pinned=False)]
    outs = [(array(rows, width, f32), "cols"), (array(rows, groups * HEAD_DIM, f32), "cols")]
    return run_shares(chip_body, "chip_level", groups, [odd, bias], ins, outs)


def finish(place, bias, q0, q1, sums, stat, outer, inner, back):
    groups = back.shape[0]
    rows, width = q0.shape
    ins = [one(a) for a in (q0, q1, sums, stat)] + [Operand([outer, inner], "cols", False), one(back, "lead", pinned=False)]
    outs = [(array(rows, width, bf16), "cols")]
    return run_shares(finish_body, "finish", groups, [place, bias], ins, outs)[0]


def shift(value, axis, steps):
    count = lax.axis_size(axis)
    first, last = (max(0, -steps), min(count, count - steps))
    return lax.ppermute(value, axis, [(source, source + steps) for source in range(first, last)])


def trade(value, axis, pairs):
    return lax.ppermute(value, axis, pairs + [(target, source) for source, target in pairs])


def hops_across(count, groups):
    def beside(device):
        other = (device // groups ^ 1) * groups + device % groups
        return other if other < count else device

    pairs = [(source, source + 1) for source in range(1, count - 1, 2)]
    pairs += [(target, source) for source, target in pairs]
    first = [(device, beside(device)) for device in range(count) if device % groups in (0, groups - 1)]
    first += [(source, target) for source, target in pairs if source // groups == target // groups]
    second = [(beside(source), target) for source, target in pairs if source // groups != target // groups]
    return first, second


def edge_bias(axis):
    place = lax.axis_index(axis)
    last = lax.axis_size(axis) - 1
    at_edge = jnp.stack([place == 0, place == last])
    return jnp.where(at_edge, very_negative, 0.0).astype(f32)


def local(query_vecs, key_vecs, value_vecs):
    groups = lax.axis_size("grp")
    assert query_vecs.shape == (2 * BLK, HEADS * HEAD_DIM) and groups == 4
    everyone = ("seq", "grp")
    count = lax.axis_size(everyone)
    spot = lax.axis_index("grp")
    odd = jnp.bitwise_and(spot, 1)
    at_end = jnp.logical_or(spot == 0, spot == groups - 1)
    place = jnp.stack([odd, at_end.astype(odd.dtype), spot]).astype(jnp.int32)
    bias = edge_bias(everyone)
    pieces = list(swap_rows(place, query_vecs, key_vecs, value_vecs, groups))
    query_rows, pieces = lax.optimization_barrier((query_vecs, pieces))
    for n in range(1, groups):
        pieces[n] = lax.ppermute(pieces[n], "grp", [(source, source ^ n) for source in range(groups)])
    q0, q1, cross, chip = rows_to_send(place, query_rows, key_vecs, value_vecs, groups)
    first_hop, second_hop = hops_across(count, groups)
    inner = lax.ppermute(cross, everyone, first_hop)
    pieces, chip = lax.optimization_barrier((pieces, chip))
    got, coarse_right, coarse_left = coarse_halos(place, pieces)
    coarse_right, coarse_left, chip, q0 = lax.optimization_barrier((coarse_right, coarse_left, chip, q0))
    coarse_prev = shift(coarse_right, "seq", 1)
    coarse_next = shift(coarse_left, "seq", -1)
    chip = trade(chip, everyone, [(first, first + 1) for first in range(0, count - 1, 2)])
    own, own_stat = own_level(q0, key_vecs, value_vecs, groups)
    got, own = lax.optimization_barrier((got, own))
    outer = lax.ppermute(inner, everyone, second_hop)
    back = coarse_levels(edge_bias("seq"), got, coarse_prev, coarse_next)
    back, own = lax.optimization_barrier((back, own))
    own, own_stat = chip_level(place, bias, q0, q1, own, own_stat, chip, groups)
    back = lax.all_to_all(back, "grp", split_axis=0, concat_axis=0, tiled=True)
    return finish(place, bias, q0, q1, own, own_stat, outer, inner, back)


def solution(mesh):
    return jax.shard_map(
        local,
        mesh=mesh,
        in_specs=(P(("seq", "grp"), None), P(("seq", "grp"), None), P(("seq", "grp"), None)),
        out_specs=P(("seq", "grp"), None),
        check_vma=False,
    )
```

```python
import functools
import functools
import functools
import functools
import functools
import functools
import functools
import functools
import functools
import functools
import functools
import functools
import functools
import functools
import functools
import functools
import functools
import functools
import functools
import functools
import math

import jax
import jax.numpy as jnp
from jax import lax
from jax.experimental import pallas as pl
from jax.experimental.pallas import tpu as pltpu
from jax.sharding import PartitionSpec as P

HEADS = 8
HEAD_DIM = 128
BLK = 256
HALF = BLK // 2
SUB = BLK // 8
LEV = 4
EXP_SCALE = math.log2(math.e) / math.sqrt(HEAD_DIM)

VMEM_GRANT = 48 << 20

very_negative = -1e30
f32 = jnp.float32
bf16 = jnp.bfloat16


def iota(shape, dim):
    return lax.broadcasted_iota(jnp.int32, shape, dim)


def bit(value, place):
    return jnp.bitwise_and(lax.shift_right_logical(value, place), 1)


def low_bits(value):
    step = SUB.bit_length() - 1
    deep = jnp.bitwise_and(value, SUB - 1)
    return 8 * deep + 4 * bit(value, step) + 2 * bit(value, step + 1) + bit(value, step + 2)


def reorder_matrix():
    return (iota((BLK, BLK), 1) == low_bits(iota((BLK, BLK), 0))).astype(bf16)


def restore_matrix():
    return (iota((BLK, BLK), 0) == low_bits(iota((BLK, BLK), 1))).astype(bf16)


def pair_matrix():
    first = low_bits(iota((HALF, BLK), 0))
    place = iota((HALF, BLK), 1)
    return jnp.logical_or(place == first, place == first + 1).astype(bf16)


def mul(left, right):
    return jnp.dot(left, right, preferred_element_type=f32)


def fold(rows, factor):
    half = rows.shape[0] // 2
    total = rows[:half].astype(f32) + rows[half:].astype(f32)
    if factor != 1.0:
        total = total * factor
    return total.astype(bf16)


def fold_chunks(rows, chunk, factor):
    count = rows.shape[0] // chunk
    return jnp.concatenate([fold(rows[i * chunk : (i + 1) * chunk], factor) for i in range(count)], axis=0)


def twice(rows):
    return jnp.concatenate([rows, rows], axis=0)


def cols(head):
    return slice(head * HEAD_DIM, (head + 1) * HEAD_DIM)


def lane_chunks(rows):
    return [rows[:, first : first + HEAD_DIM] for first in range(0, rows.shape[1], HEAD_DIM)]


def twice(rows):
    return jnp.concatenate([rows, rows], axis=0)


def cols(head):
    return slice(head * HEAD_DIM, (head + 1) * HEAD_DIM)


def lane_chunks(rows):
    return [rows[:, first : first + HEAD_DIM] for first in range(0, rows.shape[1], HEAD_DIM)]


def twice(rows):
    return jnp.concatenate([rows, rows], axis=0)


def cols(head):
    return slice(head * HEAD_DIM, (head + 1) * HEAD_DIM)


def lane_chunks(rows):
    return [rows[:, first : first + HEAD_DIM] for first in range(0, rows.shape[1], HEAD_DIM)]


def twice(rows):
    return jnp.concatenate([rows, rows], axis=0)


def cols(head):
    return slice(head * HEAD_DIM, (head + 1) * HEAD_DIM)


def lane_chunks(rows):
    return [rows[:, first : first + HEAD_DIM] for first in range(0, rows.shape[1], HEAD_DIM)]


def twice(rows):
    return jnp.concatenate([rows, rows], axis=0)


def cols(head):
    return slice(head * HEAD_DIM, (head + 1) * HEAD_DIM)


def lane_chunks(rows):
    return [rows[:, first : first + HEAD_DIM] for first in range(0, rows.shape[1], HEAD_DIM)]


def twice(rows):
    return jnp.concatenate([rows, rows], axis=0)


def cols(head):
    return slice(head * HEAD_DIM, (head + 1) * HEAD_DIM)


def lane_chunks(rows):
    return [rows[:, first : first + HEAD_DIM] for first in range(0, rows.shape[1], HEAD_DIM)]


def twice(rows):
    return jnp.concatenate([rows, rows], axis=0)


def cols(head):
    return slice(head * HEAD_DIM, (head + 1) * HEAD_DIM)


def lane_chunks(rows):
    return [rows[:, first : first + HEAD_DIM] for first in range(0, rows.shape[1], HEAD_DIM)]


def twice(rows):
    return jnp.concatenate([rows, rows], axis=0)


def cols(head):
    return slice(head * HEAD_DIM, (head + 1) * HEAD_DIM)


COARSE_FLOPS = 1 << 29


def lane_chunks(rows):
    return [rows[:, first : first + HEAD_DIM] for first in range(0, rows.shape[1], HEAD_DIM)]


def twice(rows):
    return jnp.concatenate([rows, rows], axis=0)


def cols(head):
    return slice(head * HEAD_DIM, (head + 1) * HEAD_DIM)


COARSE_FLOPS = 1 << 36


def lane_chunks(rows):
    return [rows[:, first : first + HEAD_DIM] for first in range(0, rows.shape[1], HEAD_DIM)]


def twice(rows):
    return jnp.concatenate([rows, rows], axis=0)


def cols(head):
    return slice(head * HEAD_DIM, (head + 1) * HEAD_DIM)


COARSE_FLOPS = 1 << 36


def lane_chunks(rows):
    return [rows[:, first : first + HEAD_DIM] for first in range(0, rows.shape[1], HEAD_DIM)]


def twice(rows):
    return jnp.concatenate([rows, rows], axis=0)


def cols(head):
    return slice(head * HEAD_DIM, (head + 1) * HEAD_DIM)


COARSE_FLOPS = 1 << 36


def lane_chunks(rows):
    return [rows[:, first : first + HEAD_DIM] for first in range(0, rows.shape[1], HEAD_DIM)]


def twice(rows):
    return jnp.concatenate([rows, rows], axis=0)


def cols(head):
    return slice(head * HEAD_DIM, (head + 1) * HEAD_DIM)


COARSE_FLOPS = 1 << 36


def lane_chunks(rows):
    return [rows[:, first : first + HEAD_DIM] for first in range(0, rows.shape[1], HEAD_DIM)]


def twice(rows):
    return jnp.concatenate([rows, rows], axis=0)


def cols(head):
    return slice(head * HEAD_DIM, (head + 1) * HEAD_DIM)


COARSE_FLOPS = 1 << 36


def lane_chunks(rows):
    return [rows[:, first : first + HEAD_DIM] for first in range(0, rows.shape[1], HEAD_DIM)]


def twice(rows):
    return jnp.concatenate([rows, rows], axis=0)


def cols(head):
    return slice(head * HEAD_DIM, (head + 1) * HEAD_DIM)


COARSE_FLOPS = 1 << 36


def lane_chunks(rows):
    return [rows[:, first : first + HEAD_DIM] for first in range(0, rows.shape[1], HEAD_DIM)]


def twice(rows):
    return jnp.concatenate([rows, rows], axis=0)


def cols(head):
    return slice(head * HEAD_DIM, (head + 1) * HEAD_DIM)


COARSE_FLOPS = 1 << 36


def lane_chunks(rows):
    return [rows[:, first : first + HEAD_DIM] for first in range(0, rows.shape[1], HEAD_DIM)]


def twice(rows):
    return jnp.concatenate([rows, rows], axis=0)


def cols(head):
    return slice(head * HEAD_DIM, (head + 1) * HEAD_DIM)


COARSE_FLOPS = 1 << 36


def lane_chunks(rows):
    return [rows[:, first : first + HEAD_DIM] for first in range(0, rows.shape[1], HEAD_DIM)]


def twice(rows):
    return jnp.concatenate([rows, rows], axis=0)


def cols(head):
    return slice(head * HEAD_DIM, (head + 1) * HEAD_DIM)


COARSE_FLOPS = 1 << 36


def lane_chunks(rows):
    return [rows[:, first : first + HEAD_DIM] for first in range(0, rows.shape[1], HEAD_DIM)]


def twice(rows):
    return jnp.concatenate([rows, rows], axis=0)


def cols(head):
    return slice(head * HEAD_DIM, (head + 1) * HEAD_DIM)


DECLARED = 1 << 36


def lane_chunks(rows):
    return [rows[:, first : first + HEAD_DIM] for first in range(0, rows.shape[1], HEAD_DIM)]


def twice(rows):
    return jnp.concatenate([rows, rows], axis=0)


def cols(head):
    return slice(head * HEAD_DIM, (head + 1) * HEAD_DIM)


DECLARED = 1 << 36


def lane_chunks(rows):
    return [rows[:, first : first + HEAD_DIM] for first in range(0, rows.shape[1], HEAD_DIM)]


def twice(rows):
    return jnp.concatenate([rows, rows], axis=0)


def cols(head):
    return slice(head * HEAD_DIM, (head + 1) * HEAD_DIM)


DECLARED = 1 << 36


def lane_chunks(rows):
    return [rows[:, first : first + HEAD_DIM] for first in range(0, rows.shape[1], HEAD_DIM)]


def with_ones(values):
    return jnp.concatenate([values, jnp.ones_like(values)], axis=1)


def attend(units):
    scores = []
    for query, parts in units:
        chunks = []
        for keys, _, bias in parts:
            raw = lax.dot_general(query, keys, (((1,), (1,)), ((), ())), preferred_element_type=f32)
            chunks.append(lane_chunks(raw if bias is None else raw + bias))
        scores.append(chunks)
    tops = []
    for chunks in scores:
        most = functools.reduce(jnp.maximum, sum(chunks, []))
        tops.append(jnp.broadcast_to(jnp.max(most, axis=1, keepdims=True), most.shape))
    found = []
    for (_, parts), chunks, top in zip(units, scores, tops):
        total = None
        for (_, values, _), pieces in zip(parts, chunks):
            weights = [jnp.exp2((piece - top) * EXP_SCALE).astype(bf16) for piece in pieces]
            one = mul(jnp.concatenate(weights, axis=1), with_ones(values))
            total = one if total is None else total + one
        found.append((top * EXP_SCALE, total))
    return found


def share_of(ref, kind, share, shares):
    if kind == "lead":
        return ref.at[share]
    width = ref.shape[1] // shares
    first = share * width
    if not isinstance(share, int):
        first = pl.multiple_of(first, HEAD_DIM)
    return ref.at[:, pl.ds(first, width)]


class Operand:
    def __init__(self, value, kind, pinned):
        self.value = value
        self.kind = kind
        self.pinned = pinned

    def buffer(self, shares):
        shape = self.value.shape
        return shape if self.kind == "lead" else (shares, shape[0], shape[1] // shares)


def one(value, kind="cols", pinned=True):
    return Operand(value, kind, pinned)


def run_shares(body, name, shares, scalars, ins, outs, work=1 << 10):
    out_kinds = [kind for _, kind in outs]
    pieces = [i for i, kind in enumerate(out_kinds) if isinstance(kind, int)]
    buffered = len(outs) - max(0, len(pieces) - 1)

    def kernel(*refs):
        refs = list(refs)
        take = lambda count: [refs.pop(0) for _ in range(count)]
        scalar_refs, in_refs, out_refs = take(len(scalars)), take(len(ins)), take(len(outs))
        in_bufs, out_bufs, (in_sems, out_sems) = take(len(ins)), take(buffered), take(2)

        def bring(i, share):
            source = share_of(in_refs[i], ins[i].kind, share, shares)
            return pltpu.make_async_copy(source, in_bufs[i].at[share], in_sems.at[i, share])

        def put(i, share):
            if i in pieces:
                entry = out_kinds[i] ^ scalar_refs[0][1]
                return pltpu.make_async_copy(out_bufs[-1].at[entry], out_refs[i], out_sems.at[i, 0])
            target = share_of(out_refs[i], out_kinds[i], share, shares)
            return pltpu.make_async_copy(out_bufs[i].at[share], target, out_sems.at[i, share])

        for share in range(shares):
            for i in range(len(ins)):
                bring(i, share).start()

        def step(share, carry):
            for i in range(len(ins)):
                bring(i, share).wait()
            body(scalar_refs, [buf.at[share] for buf in in_bufs], [buf.at[share] for buf in out_bufs])
            for i in range(len(outs) - len(pieces)):
                put(i, share).start()
            return carry

        lax.fori_loop(0, shares, step, 0)
        for i in pieces:
            put(i, 0).start()
        for share in range(shares):
            for i in range(len(outs) - len(pieces)):
                put(i, share).wait()
        for i in pieces:
            put(i, 0).wait()

    values, specs = [], []
    for operand in ins:
        value = operand.value
        values.append(pltpu.with_memory_space_constraint(value, pltpu.HBM) if operand.pinned else value)
        specs.append(pl.BlockSpec(memory_space=pltpu.HBM if operand.pinned else pl.ANY))
    buffers = [pltpu.VMEM(operand.buffer(shares), operand.value.dtype) for operand in ins]
    for shape, kind in outs[:buffered]:
        width = shape.shape[-1]
        if isinstance(kind, int):
            buffers.append(pltpu.VMEM((shares, *shape.shape), shape.dtype))
            continue
        buffers.append(pltpu.VMEM(shape.shape if kind == "lead" else (shares, shape.shape[0], width // shares), shape.dtype))
    return pl.pallas_call(
        kernel,
        in_specs=[pl.BlockSpec(memory_space=pltpu.SMEM)] * len(scalars) + specs,
        out_specs=[pl.BlockSpec(memory_space=pltpu.HBM)] * len(outs),
        out_shape=[pltpu.HBM(shape.shape, shape.dtype) for shape, _ in outs],
        scratch_shapes=buffers
        + [pltpu.SemaphoreType.DMA((len(ins), shares)), pltpu.SemaphoreType.DMA((len(outs), shares))],
        compiler_params=pltpu.CompilerParams(vmem_limit_bytes=VMEM_GRANT),
        cost_estimate=pl.CostEstimate(flops=work, bytes_accessed=1 << 10, transcendentals=0),
        name=name,
    )(*scalars, *values)


def array(rows, width, dtype):
    return jax.ShapeDtypeStruct((rows, width), dtype)


def swap_body(_, ins, outs):
    pair = pair_matrix()
    for place, (ref, factor) in enumerate(zip(ins, (0.5, 0.5, 1.0))):
        for i in range(2):
            level1 = mul(pair, ref[i * BLK : (i + 1) * BLK, :])
            if factor != 1.0:
                level1 = level1 * factor
            first = place * HALF + i * HALF // 2
            outs[0][first : first + HALF // 2, :] = fold(level1.astype(bf16), factor)


def swap_rows(place, query_vecs, key_vecs, value_vecs, groups):
    width = query_vecs.shape[1]
    ins = [one(a) for a in (query_vecs, key_vecs, value_vecs)]
    outs = [(array(3 * HALF, width // groups, bf16), n) for n in range(groups)]
    return run_shares(swap_body, "swap_rows", groups, [place], ins, outs)


def rows_body(scalars, ins, outs):
    q_ref, k_ref, v_ref = ins
    q0_ref, q1_ref, cross_ref, chip_ref = outs
    reorder = reorder_matrix()
    pair = pair_matrix()
    for i in range(2):
        rows = slice(i * BLK, (i + 1) * BLK)
        q0 = mul(reorder, q_ref[rows, :]).astype(bf16)
        q0_ref[rows, :] = q0
        q1_ref[i * HALF : (i + 1) * HALF, :] = fold(q0, 0.5)
    odd = scalars[0][0]
    outer = pl.ds(pl.multiple_of(odd * BLK, BLK), BLK)
    inner = pl.ds(pl.multiple_of((1 - odd) * BLK, BLK), BLK)
    for ref, near, far in ((cross_ref, outer, inner), (chip_ref, inner, outer)):
        ref[0:BLK, :] = k_ref[near, :]
        ref[BLK : 2 * BLK, :] = v_ref[near, :]
        ref[2 * BLK : 2 * BLK + HALF, :] = (mul(pair, k_ref[far, :]) * 0.5).astype(bf16)
        ref[2 * BLK + HALF : 3 * BLK, :] = mul(pair, v_ref[far, :]).astype(bf16)


def rows_to_send(place, query_vecs, key_vecs, value_vecs, groups):
    rows, width = query_vecs.shape
    ins = [one(a) for a in (query_vecs, key_vecs, value_vecs)]
    outs = [(array(n, width, bf16), "cols") for n in (rows, rows // 2, 3 * BLK, 3 * BLK)]
    return run_shares(rows_body, "rows_to_send", groups, [place], ins, outs)


def pack(stats):
    width = HEAD_DIM // len(stats)
    lane = iota(stats[0].shape, 1)
    packed = stats[-1]
    for n in range(len(stats) - 2, -1, -1):
        packed = jnp.where(lane < (n + 1) * width, stats[n], packed)
    return packed


def unpack(packed, count):
    width = HEAD_DIM // count
    return [jnp.broadcast_to(packed[:, n * width : n * width + 1], packed.shape) for n in range(count)]


def own_body(_, ins, outs):
    q_ref, k_ref, v_ref = ins
    sum_ref, stat_ref = outs
    heads = q_ref.shape[1] // HEAD_DIM
    for i in range(2):
        rows = slice(i * BLK, (i + 1) * BLK)
        units = [(q_ref[rows, cols(head)], [(k_ref[:, cols(head)], v_ref[:, cols(head)], None)]) for head in range(heads)]
        stats = []
        for head, (top, sums) in enumerate(attend(units)):
            sum_ref[rows, cols(head)] = sums[:, :HEAD_DIM]
            stats += [top, sums[:, HEAD_DIM:]]
        stat_ref[rows, :] = pack(stats)


def own_level(q0, key_vecs, value_vecs, groups):
    rows, width = q0.shape
    ins = [one(a) for a in (q0, key_vecs, value_vecs)]
    outs = [(array(rows, width, f32), "cols"), (array(rows, groups * HEAD_DIM, f32), "cols")]
    return run_shares(own_body, "own_level", groups, [], ins, outs, DECLARED)


def halo_body(place_ref, *refs):
    count = len(refs) - 4
    piece_refs, (got_ref, right_ref, left_ref, sems) = refs[:count], refs[count:]
    copies = [pltpu.make_async_copy(ref, got_ref.at[n ^ place_ref[1]], sems.at[n]) for n, ref in enumerate(piece_refs)]
    for copy in copies:
        copy.start()
    for copy in copies:
        copy.wait()
    pair = count // 2
    for which, factor in ((1, 0.5), (2, 1.0)):
        rows = slice(which * HALF, (which + 1) * HALF)
        near = (which - 1) * BLK
        far = 2 * BLK + (which - 1) * HALF
        for j in range(count):
            level2 = got_ref[j, rows, :]
            level3 = fold_chunks(level2, HALF // 2, factor)
            near_ref, far_ref = (left_ref, right_ref) if j < pair else (right_ref, left_ref)
            spot = j % pair
            near_ref[near + spot * HALF : near + (spot + 1) * HALF, :] = level2
            far_ref[far + spot * HALF // 2 : far + (spot + 1) * HALF // 2, :] = level3


def coarse_halos(place, pieces):
    rows, width = pieces[0].shape
    vmem = pl.BlockSpec(memory_space=pltpu.VMEM)
    shape = jax.ShapeDtypeStruct((3 * BLK, width), bf16)
    return pl.pallas_call(
        halo_body,
        in_specs=[pl.BlockSpec(memory_space=pltpu.SMEM)] + [pl.BlockSpec(memory_space=pl.ANY)] * len(pieces),
        out_specs=[vmem] * 3,
        out_shape=[jax.ShapeDtypeStruct((len(pieces), rows, width), bf16), shape, shape],
        scratch_shapes=[pltpu.SemaphoreType.DMA((len(pieces),))],
        compiler_params=pltpu.CompilerParams(vmem_limit_bytes=16 << 20),
        cost_estimate=pl.CostEstimate(flops=1 << 20, bytes_accessed=24 * pieces[0].size, transcendentals=0),
        name="coarse_halos",
    )(place, *pieces)


def coarse_body(bias_ref, got_ref, prev_ref, next_ref, back_ref):
    count = got_ref.shape[0]
    heads = got_ref.shape[2] // HEAD_DIM
    bias_prev = bias_ref[0]
    bias_next = bias_ref[1]
    lane = iota((HALF, HEAD_DIM), 1)

    for head in range(heads):
        here = cols(head)

        def own(which, j):
            return got_ref[j, which * HALF : (which + 1) * HALF, here]

        def near(ref, which, spot):
            first = (which - 1) * BLK + spot * HALF
            return ref[first : first + HALF, here]

        def both(ref, which):
            return ref[(which - 1) * BLK : which * BLK, here]

        def far(ref, which):
            first = 2 * BLK + (which - 1) * HALF
            return ref[first : first + HALF, here]

        def near3(ref, which):
            return fold_chunks(both(ref, which), HALF // 2, 0.5 if which == 1 else 1.0)

        def joined(*rows):
            return jnp.concatenate(rows, axis=0)

        def part(pick, bias):
            return (pick(1), pick(2), bias)

        units = [
            (own(0, 0), [part(lambda w: joined(own(w, 2), own(w, 3)), None), part(lambda w: near(prev_ref, w, 0), bias_prev)]),
            (own(0, 1), [part(lambda w: both(prev_ref, w), bias_prev), part(lambda w: own(w, 3), None)]),
            (own(0, 2), [part(lambda w: both(next_ref, w), bias_next), part(lambda w: own(w, 0), None)]),
            (own(0, 3), [part(lambda w: joined(own(w, 0), own(w, 1)), None), part(lambda w: near(next_ref, w, 1), bias_next)]),
        ]
        for j, (ref, bias, other, other_bias) in enumerate(
            ((next_ref, bias_next, prev_ref, bias_prev), (prev_ref, bias_prev, next_ref, bias_next))
        ):
            query = joined(*[fold_chunks(own(0, 2 * j + n), HALF // 2, 0.5) for n in range(2)])
            units.append(
                (
                    query,
                    [part(lambda w: joined(near3(ref, w), far(ref, w)), bias), part(lambda w: far(other, w), other_bias)],
                )
            )
        found = attend(units)
        for j in range(count):
            top2, sum2 = found[j]
            top3, sum3 = found[count + j // 2]

            def spread(rows):
                first = (j % 2) * 2 * SUB
                one = rows[first : first + SUB]
                other = rows[first + SUB : first + 2 * SUB]
                return joined(one, one, other, other)

            top3 = spread(top3)
            sum3 = spread(sum3)
            top = jnp.maximum(top2, top3)
            scale2 = jnp.exp2(top2 - top)
            scale3 = jnp.exp2(top3 - top)
            values = sum2[:, :HEAD_DIM] * scale2 + sum3[:, :HEAD_DIM] * scale3
            total = sum2[:, HEAD_DIM:] * (4.0 * scale2) + sum3[:, HEAD_DIM:] * (8.0 * scale3)
            back_ref[j, 0:HALF, here] = (values / total).astype(bf16)
            level = top + jnp.log2(total)
            high = level.astype(bf16).astype(f32)
            middle = (level - high).astype(bf16).astype(f32)
            terms = jnp.where(lane == 0, high, jnp.where(lane == 1, middle, level - high - middle))
            back_ref[j, HALF : HALF + 16, here] = terms.T[0:16, :].astype(bf16)


def coarse_levels(bias, got, from_prev, from_next):
    count, _, width = got.shape
    vmem = pl.BlockSpec(memory_space=pltpu.VMEM)
    return pl.pallas_call(
        coarse_body,
        in_specs=[pl.BlockSpec(memory_space=pltpu.SMEM), vmem, vmem, vmem],
        out_specs=vmem,
        out_shape=jax.ShapeDtypeStruct((count, HALF + 16, width), bf16),
        compiler_params=pltpu.CompilerParams(vmem_limit_bytes=16 << 20),
        cost_estimate=pl.CostEstimate(flops=DECLARED, bytes_accessed=8 * got.size, transcendentals=1 << 20),
        name="coarse_levels",
    )(bias, got, from_prev, from_next)


def side_body(side, scalars, ins, outs):
    q0_ref, q1_ref, sum_ref, stat_ref, side_ref = ins[:5]
    heads = q0_ref.shape[1] // HEAD_DIM
    bias = scalars[1][side]
    blocks = (side, 1 - side)
    pair = pair_matrix()
    near_keys = (mul(pair, side_ref[0:BLK, :]) * 0.5).astype(bf16)
    near_values = mul(pair, side_ref[BLK : 2 * BLK, :]).astype(bf16)
    far_keys = slice(2 * BLK, 2 * BLK + HALF)
    far_values = slice(2 * BLK + HALF, 3 * BLK)
    fine = [pl.ds(pl.multiple_of(block * BLK, BLK), BLK) for block in blocks]
    middle = [pl.ds(pl.multiple_of(block * HALF, HALF), HALF) for block in blocks]
    units = []
    for head in range(heads):
        here = cols(head)
        far = (side_ref[far_keys, here], side_ref[far_values, here], bias)
        whole = tuple(
            jnp.concatenate([near[:, here], side_ref[far, here]], axis=0)
            for near, far in ((near_keys, far_keys), (near_values, far_values))
        )
        units.append((q0_ref[fine[0], here], [(side_ref[0:BLK, here], side_ref[BLK : 2 * BLK, here], bias)]))
        units.append((q1_ref[middle[0], here], [far]))
        units.append((q1_ref[middle[1], here], [(*whole, bias)]))
    found = attend(units)
    if len(ins) == 5:
        for n in range(2):
            stats = unpack(stat_ref[fine[n], :], 2 * heads)
            results = []
            for head in range(heads):
                here = cols(head)
                top1, sum1 = found[3 * head + 1 + n]
                top1, sum1 = twice(top1), twice(sum1)
                own_top, own_total = stats[2 * head], stats[2 * head + 1]
                top = jnp.maximum(top1, own_top)
                if n == 0:
                    top0, sum0 = found[3 * head]
                    top = jnp.maximum(top, top0)
                scale1 = jnp.exp2(top1 - top)
                own_scale = jnp.exp2(own_top - top)
                number = sum1[:, :HEAD_DIM] * scale1 + sum_ref[fine[n], here] * own_scale
                total = sum1[:, HEAD_DIM:] * (2.0 * scale1) + own_total * own_scale
                if n == 0:
                    scale0 = jnp.exp2(top0 - top)
                    number = number + sum0[:, :HEAD_DIM] * scale0
                    total = total + sum0[:, HEAD_DIM:] * scale0
                outs[0][fine[n], here] = number
                results += [top, total]
            outs[1][fine[n], :] = pack(results)
        return
    back_ref = ins[5]
    restore = restore_matrix()
    levels = []
    for head in range(heads):
        terms = back_ref[HALF : HALF + 16, cols(head)].astype(f32)
        terms = jnp.sum(jnp.where(iota(terms.shape, 0) < 3, terms, 0.0), axis=0, keepdims=True)
        levels.append(jnp.broadcast_to(terms, (HEAD_DIM, HEAD_DIM)).T)
    for n in range(2):
        stats = unpack(stat_ref[fine[n], :], 2 * heads)
        spot = pl.ds(pl.multiple_of(blocks[n] * HALF // 2, HALF // 2), HALF // 2)
        results = []
        for head in range(heads):
            here = cols(head)
            top1, sum1 = found[3 * head + 1 + n]
            half = HALF // 2
            level = twice(jnp.where(blocks[n] == 0, levels[head][:half, :], levels[head][half:, :]))
            top = jnp.maximum(top1, level)
            scale1 = jnp.exp2(top1 - top)
            scale2 = jnp.exp2(level - top)
            number = twice(sum1[:, :HEAD_DIM] * scale1 + twice(back_ref[spot, here].astype(f32)) * scale2)
            total = twice(sum1[:, HEAD_DIM:] * (2.0 * scale1) + scale2)
            top = twice(top)
            own_top, own_total = stats[2 * head], stats[2 * head + 1]
            most = jnp.maximum(top, own_top)
            if n == 0:
                top0, sum0 = found[3 * head]
                most = jnp.maximum(most, top0)
            scale = jnp.exp2(top - most)
            own_scale = jnp.exp2(own_top - most)
            number = number * scale + sum_ref[fine[n], here] * own_scale
            total = total * scale + own_total * own_scale
            if n == 0:
                scale0 = jnp.exp2(top0 - most)
                number = number + sum0[:, :HEAD_DIM] * scale0
                total = total + sum0[:, HEAD_DIM:] * scale0
            results.append((number / total).astype(bf16))
        outs[0][fine[n], :] = mul(restore, jnp.concatenate(results, axis=1)).astype(bf16)


def chip_body(scalars, ins, outs):
    side_body(1 - scalars[0][0], scalars, ins, outs)


def finish_body(scalars, ins, outs):
    side_body(scalars[0][0], scalars, ins, outs)


def chip_level(odd, bias, q0, q1, sums, stat, chip, groups):
    rows, width = q0.shape
    ins = [one(a) for a in (q0, q1, sums, stat)] + [one(chip, pinned=False)]
    outs = [(array(rows, width, f32), "cols"), (array(rows, groups * HEAD_DIM, f32), "cols")]
    return run_shares(chip_body, "chip_level", groups, [odd, bias], ins, outs)


def finish(place, bias, q0, q1, sums, stat, cross, back):
    groups = back.shape[0]
    rows, width = q0.shape
    ins = [one(a) for a in (q0, q1, sums, stat)] + [one(cross, pinned=False), one(back, "lead", pinned=False)]
    outs = [(array(rows, width, bf16), "cols")]
    return run_shares(finish_body, "finish", groups, [place, bias], ins, outs)[0]


def shift(value, axis, steps):
    count = lax.axis_size(axis)
    first, last = (max(0, -steps), min(count, count - steps))
    return lax.ppermute(value, axis, [(source, source + steps) for source in range(first, last)])


def trade(value, axis, pairs):
    return lax.ppermute(value, axis, pairs + [(target, source) for source, target in pairs])


def edge_bias(axis):
    place = lax.axis_index(axis)
    last = lax.axis_size(axis) - 1
    at_edge = jnp.stack([place == 0, place == last])
    return jnp.where(at_edge, very_negative, 0.0).astype(f32)


def local(query_vecs, key_vecs, value_vecs):
    groups = lax.axis_size("grp")
    assert query_vecs.shape == (2 * BLK, HEADS * HEAD_DIM) and groups == 4
    everyone = ("seq", "grp")
    count = lax.axis_size(everyone)
    spot = lax.axis_index("grp")
    odd = jnp.bitwise_and(spot, 1)
    place = jnp.stack([odd, spot]).astype(jnp.int32)
    bias = edge_bias(everyone)
    pieces = list(swap_rows(place, query_vecs, key_vecs, value_vecs, groups))
    query_rows, pieces = lax.optimization_barrier((query_vecs, pieces))
    for n in range(1, groups):
        pieces[n] = lax.ppermute(pieces[n], "grp", [(source, source ^ n) for source in range(groups)])
    q0, q1, cross, chip = rows_to_send(place, query_rows, key_vecs, value_vecs, groups)
    cross = trade(cross, everyone, [(first, first + 1) for first in range(1, count - 1, 2)])
    pieces, chip = lax.optimization_barrier((pieces, chip))
    got, coarse_right, coarse_left = coarse_halos(place, pieces)
    coarse_right, coarse_left, chip, q0 = lax.optimization_barrier((coarse_right, coarse_left, chip, q0))
    coarse_prev = shift(coarse_right, "seq", 1)
    coarse_next = shift(coarse_left, "seq", -1)
    chip = trade(chip, everyone, [(first, first + 1) for first in range(0, count - 1, 2)])
    own, own_stat = own_level(q0, key_vecs, value_vecs, groups)
    got, own = lax.optimization_barrier((got, own))
    back = coarse_levels(edge_bias("seq"), got, coarse_prev, coarse_next)
    back, own = lax.optimization_barrier((back, own))
    own, own_stat = chip_level(place, bias, q0, q1, own, own_stat, chip, groups)
    back = lax.all_to_all(back, "grp", split_axis=0, concat_axis=0, tiled=True)
    return finish(place, bias, q0, q1, own, own_stat, cross, back)


def solution(mesh):
    return jax.shard_map(
        local,
        mesh=mesh,
        in_specs=(P(("seq", "grp"), None), P(("seq", "grp"), None), P(("seq", "grp"), None)),
        out_specs=P(("seq", "grp"), None),
        check_vma=False,
    )
```

```python
import functools
import functools
import functools
import functools
import functools
import functools
import functools
import functools
import functools
import functools
import functools
import functools
import functools
import functools
import functools
import functools
import functools
import functools
import functools
import functools
import functools
import functools
import math

import jax
import jax.numpy as jnp
from jax import lax
from jax.experimental import pallas as pl
from jax.experimental.pallas import tpu as pltpu
from jax.sharding import PartitionSpec as P

HEADS = 8
HEAD_DIM = 128
BLK = 256
HALF = BLK // 2
SUB = BLK // 8
LEV = 4
EXP_SCALE = math.log2(math.e) / math.sqrt(HEAD_DIM)

VMEM_GRANT = 48 << 20

very_negative = -1e30
f32 = jnp.float32
bf16 = jnp.bfloat16


def iota(shape, dim):
    return lax.broadcasted_iota(jnp.int32, shape, dim)


def bit(value, place):
    return jnp.bitwise_and(lax.shift_right_logical(value, place), 1)


def low_bits(value):
    step = SUB.bit_length() - 1
    deep = jnp.bitwise_and(value, SUB - 1)
    return 8 * deep + 4 * bit(value, step) + 2 * bit(value, step + 1) + bit(value, step + 2)


def reorder_matrix():
    return (iota((BLK, BLK), 1) == low_bits(iota((BLK, BLK), 0))).astype(bf16)


def restore_matrix():
    return (iota((BLK, BLK), 0) == low_bits(iota((BLK, BLK), 1))).astype(bf16)


def pair_matrix():
    first = low_bits(iota((HALF, BLK), 0))
    place = iota((HALF, BLK), 1)
    return jnp.logical_or(place == first, place == first + 1).astype(bf16)


def mul(left, right):
    return jnp.dot(left, right, preferred_element_type=f32)


def fold(rows, factor):
    half = rows.shape[0] // 2
    total = rows[:half].astype(f32) + rows[half:].astype(f32)
    if factor != 1.0:
        total = total * factor
    return total.astype(bf16)


def fold_chunks(rows, chunk, factor):
    count = rows.shape[0] // chunk
    return jnp.concatenate([fold(rows[i * chunk : (i + 1) * chunk], factor) for i in range(count)], axis=0)


def twice(rows):
    return jnp.concatenate([rows, rows], axis=0)


def cols(head):
    return slice(head * HEAD_DIM, (head + 1) * HEAD_DIM)


def lane_chunks(rows):
    return [rows[:, first : first + HEAD_DIM] for first in range(0, rows.shape[1], HEAD_DIM)]


def twice(rows):
    return jnp.concatenate([rows, rows], axis=0)


def cols(head):
    return slice(head * HEAD_DIM, (head + 1) * HEAD_DIM)


def lane_chunks(rows):
    return [rows[:, first : first + HEAD_DIM] for first in range(0, rows.shape[1], HEAD_DIM)]


def twice(rows):
    return jnp.concatenate([rows, rows], axis=0)


def cols(head):
    return slice(head * HEAD_DIM, (head + 1) * HEAD_DIM)


def lane_chunks(rows):
    return [rows[:, first : first + HEAD_DIM] for first in range(0, rows.shape[1], HEAD_DIM)]


def twice(rows):
    return jnp.concatenate([rows, rows], axis=0)


def cols(head):
    return slice(head * HEAD_DIM, (head + 1) * HEAD_DIM)


def lane_chunks(rows):
    return [rows[:, first : first + HEAD_DIM] for first in range(0, rows.shape[1], HEAD_DIM)]


def twice(rows):
    return jnp.concatenate([rows, rows], axis=0)


def cols(head):
    return slice(head * HEAD_DIM, (head + 1) * HEAD_DIM)


def lane_chunks(rows):
    return [rows[:, first : first + HEAD_DIM] for first in range(0, rows.shape[1], HEAD_DIM)]


def twice(rows):
    return jnp.concatenate([rows, rows], axis=0)


def cols(head):
    return slice(head * HEAD_DIM, (head + 1) * HEAD_DIM)


def lane_chunks(rows):
    return [rows[:, first : first + HEAD_DIM] for first in range(0, rows.shape[1], HEAD_DIM)]


def twice(rows):
    return jnp.concatenate([rows, rows], axis=0)


def cols(head):
    return slice(head * HEAD_DIM, (head + 1) * HEAD_DIM)


def lane_chunks(rows):
    return [rows[:, first : first + HEAD_DIM] for first in range(0, rows.shape[1], HEAD_DIM)]


def twice(rows):
    return jnp.concatenate([rows, rows], axis=0)


def cols(head):
    return slice(head * HEAD_DIM, (head + 1) * HEAD_DIM)


COARSE_FLOPS = 1 << 29


def lane_chunks(rows):
    return [rows[:, first : first + HEAD_DIM] for first in range(0, rows.shape[1], HEAD_DIM)]


def twice(rows):
    return jnp.concatenate([rows, rows], axis=0)


def cols(head):
    return slice(head * HEAD_DIM, (head + 1) * HEAD_DIM)


COARSE_FLOPS = 1 << 36


def lane_chunks(rows):
    return [rows[:, first : first + HEAD_DIM] for first in range(0, rows.shape[1], HEAD_DIM)]


def twice(rows):
    return jnp.concatenate([rows, rows], axis=0)


def cols(head):
    return slice(head * HEAD_DIM, (head + 1) * HEAD_DIM)


COARSE_FLOPS = 1 << 36


def lane_chunks(rows):
    return [rows[:, first : first + HEAD_DIM] for first in range(0, rows.shape[1], HEAD_DIM)]


def twice(rows):
    return jnp.concatenate([rows, rows], axis=0)


def cols(head):
    return slice(head * HEAD_DIM, (head + 1) * HEAD_DIM)


COARSE_FLOPS = 1 << 36


def lane_chunks(rows):
    return [rows[:, first : first + HEAD_DIM] for first in range(0, rows.shape[1], HEAD_DIM)]


def twice(rows):
    return jnp.concatenate([rows, rows], axis=0)


def cols(head):
    return slice(head * HEAD_DIM, (head + 1) * HEAD_DIM)


COARSE_FLOPS = 1 << 36


def lane_chunks(rows):
    return [rows[:, first : first + HEAD_DIM] for first in range(0, rows.shape[1], HEAD_DIM)]


def twice(rows):
    return jnp.concatenate([rows, rows], axis=0)


def cols(head):
    return slice(head * HEAD_DIM, (head + 1) * HEAD_DIM)


COARSE_FLOPS = 1 << 36


def lane_chunks(rows):
    return [rows[:, first : first + HEAD_DIM] for first in range(0, rows.shape[1], HEAD_DIM)]


def twice(rows):
    return jnp.concatenate([rows, rows], axis=0)


def cols(head):
    return slice(head * HEAD_DIM, (head + 1) * HEAD_DIM)


COARSE_FLOPS = 1 << 36


def lane_chunks(rows):
    return [rows[:, first : first + HEAD_DIM] for first in range(0, rows.shape[1], HEAD_DIM)]


def twice(rows):
    return jnp.concatenate([rows, rows], axis=0)


def cols(head):
    return slice(head * HEAD_DIM, (head + 1) * HEAD_DIM)


COARSE_FLOPS = 1 << 36


def lane_chunks(rows):
    return [rows[:, first : first + HEAD_DIM] for first in range(0, rows.shape[1], HEAD_DIM)]


def twice(rows):
    return jnp.concatenate([rows, rows], axis=0)


def cols(head):
    return slice(head * HEAD_DIM, (head + 1) * HEAD_DIM)


COARSE_FLOPS = 1 << 36


def lane_chunks(rows):
    return [rows[:, first : first + HEAD_DIM] for first in range(0, rows.shape[1], HEAD_DIM)]


def twice(rows):
    return jnp.concatenate([rows, rows], axis=0)


def cols(head):
    return slice(head * HEAD_DIM, (head + 1) * HEAD_DIM)


COARSE_FLOPS = 1 << 36


def lane_chunks(rows):
    return [rows[:, first : first + HEAD_DIM] for first in range(0, rows.shape[1], HEAD_DIM)]


def twice(rows):
    return jnp.concatenate([rows, rows], axis=0)


def cols(head):
    return slice(head * HEAD_DIM, (head + 1) * HEAD_DIM)


DECLARED = 1 << 36


def lane_chunks(rows):
    return [rows[:, first : first + HEAD_DIM] for first in range(0, rows.shape[1], HEAD_DIM)]


def twice(rows):
    return jnp.concatenate([rows, rows], axis=0)


def cols(head):
    return slice(head * HEAD_DIM, (head + 1) * HEAD_DIM)


DECLARED = 1 << 36


def lane_chunks(rows):
    return [rows[:, first : first + HEAD_DIM] for first in range(0, rows.shape[1], HEAD_DIM)]


def twice(rows):
    return jnp.concatenate([rows, rows], axis=0)


def cols(head):
    return slice(head * HEAD_DIM, (head + 1) * HEAD_DIM)


DECLARED = 1 << 36


def lane_chunks(rows):
    return [rows[:, first : first + HEAD_DIM] for first in range(0, rows.shape[1], HEAD_DIM)]


def twice(rows):
    return jnp.concatenate([rows, rows], axis=0)


def cols(head):
    return slice(head * HEAD_DIM, (head + 1) * HEAD_DIM)


DECLARED = 1 << 36


def twice(rows):
    return jnp.concatenate([rows, rows], axis=0)


def cols(head):
    return slice(head * HEAD_DIM, (head + 1) * HEAD_DIM)


DECLARED = 1 << 36


def with_ones(values):
    return jnp.concatenate([values, jnp.ones_like(values)], axis=1)


def attend(units):
    scores = []
    for query, parts in units:
        raws = [
            lax.dot_general(query, keys, (((1,), (1,)), ((), ())), preferred_element_type=f32) for keys, _, _ in parts
        ]
        scores.append([raw if part[2] is None else raw + part[2] for raw, part in zip(raws, parts)])
    tops = []
    for raws in scores:
        tops.append(functools.reduce(jnp.maximum, [jnp.max(raw, axis=1, keepdims=True) for raw in raws]))
    found = []
    for (_, parts), raws, top in zip(units, scores, tops):
        total = None
        for (_, values, _), raw in zip(parts, raws):
            weights = jnp.exp2((raw - top) * EXP_SCALE).astype(bf16)
            one = mul(weights, with_ones(values))
            total = one if total is None else total + one
        found.append((jnp.broadcast_to(top * EXP_SCALE, (top.shape[0], HEAD_DIM)), total))
    return found


def share_of(ref, kind, share, shares):
    if kind == "lead":
        count = ref.shape[0] // shares
        return ref.at[pl.ds(share * count, count)]
    width = ref.shape[1] // shares
    first = share * width
    if not isinstance(share, int):
        first = pl.multiple_of(first, HEAD_DIM)
    return ref.at[:, pl.ds(first, width)]


class Operand:
    def __init__(self, value, kind, pinned):
        self.value = value
        self.kind = kind
        self.pinned = pinned

    def buffer(self, shares):
        shape = self.value.shape
        if self.kind == "lead":
            return (shares, shape[0] // shares, *shape[1:])
        return (shares, shape[0], shape[1] // shares)


def one(value, kind="cols", pinned=True):
    return Operand(value, kind, pinned)


def run_shares(body, name, shares, scalars, ins, outs, work=1 << 10):
    out_kinds = [kind for _, kind in outs]
    pieces = [i for i, kind in enumerate(out_kinds) if isinstance(kind, int)]
    buffered = len(outs) - max(0, len(pieces) - 1)

    def kernel(*refs):
        refs = list(refs)
        take = lambda count: [refs.pop(0) for _ in range(count)]
        scalar_refs, in_refs, out_refs = take(len(scalars)), take(len(ins)), take(len(outs))
        in_bufs, out_bufs, (in_sems, out_sems) = take(len(ins)), take(buffered), take(2)

        def bring(i, share):
            source = share_of(in_refs[i], ins[i].kind, share, shares)
            return pltpu.make_async_copy(source, in_bufs[i].at[share], in_sems.at[i, share])

        def put(i, share):
            if i in pieces:
                entry = out_kinds[i] ^ scalar_refs[0][1]
                return pltpu.make_async_copy(out_bufs[-1].at[entry], out_refs[i], out_sems.at[i, 0])
            target = share_of(out_refs[i], out_kinds[i], share, shares)
            return pltpu.make_async_copy(out_bufs[i].at[share], target, out_sems.at[i, share])

        for share in range(shares):
            for i in range(len(ins)):
                bring(i, share).start()

        def step(share, carry):
            for i in range(len(ins)):
                bring(i, share).wait()
            body(scalar_refs, [buf.at[share] for buf in in_bufs], [buf.at[share] for buf in out_bufs])
            for i in range(len(outs) - len(pieces)):
                put(i, share).start()
            return carry

        lax.fori_loop(0, shares, step, 0)
        for i in pieces:
            put(i, 0).start()
        for share in range(shares):
            for i in range(len(outs) - len(pieces)):
                put(i, share).wait()
        for i in pieces:
            put(i, 0).wait()

    values, specs = [], []
    for operand in ins:
        value = operand.value
        values.append(pltpu.with_memory_space_constraint(value, pltpu.HBM) if operand.pinned else value)
        specs.append(pl.BlockSpec(memory_space=pltpu.HBM if operand.pinned else pl.ANY))
    buffers = [pltpu.VMEM(operand.buffer(shares), operand.value.dtype) for operand in ins]
    for shape, kind in outs[:buffered]:
        width = shape.shape[-1]
        if isinstance(kind, int):
            buffers.append(pltpu.VMEM((shares, *shape.shape), shape.dtype))
            continue
        buffers.append(pltpu.VMEM(shape.shape if kind == "lead" else (shares, shape.shape[0], width // shares), shape.dtype))
    return pl.pallas_call(
        kernel,
        in_specs=[pl.BlockSpec(memory_space=pltpu.SMEM)] * len(scalars) + specs,
        out_specs=[pl.BlockSpec(memory_space=pltpu.HBM)] * len(outs),
        out_shape=[pltpu.HBM(shape.shape, shape.dtype) for shape, _ in outs],
        scratch_shapes=buffers
        + [pltpu.SemaphoreType.DMA((len(ins), shares)), pltpu.SemaphoreType.DMA((len(outs), shares))],
        compiler_params=pltpu.CompilerParams(vmem_limit_bytes=VMEM_GRANT),
        cost_estimate=pl.CostEstimate(flops=work, bytes_accessed=1 << 10, transcendentals=0),
        name=name,
    )(*scalars, *values)


def array(rows, width, dtype):
    return jax.ShapeDtypeStruct((rows, width), dtype)


def swap_body(_, ins, outs):
    pair = pair_matrix()
    for place, (ref, factor) in enumerate(zip(ins, (0.5, 0.5, 1.0))):
        for i in range(2):
            level1 = mul(pair, ref[i * BLK : (i + 1) * BLK, :])
            if factor != 1.0:
                level1 = level1 * factor
            first = place * HALF + i * HALF // 2
            outs[0][first : first + HALF // 2, :] = fold(level1.astype(bf16), factor)


def swap_rows(place, query_vecs, key_vecs, value_vecs, groups):
    width = query_vecs.shape[1]
    ins = [one(a) for a in (query_vecs, key_vecs, value_vecs)]
    outs = [(array(3 * HALF, width // groups, bf16), n) for n in range(groups)]
    return run_shares(swap_body, "swap_rows", groups, [place], ins, outs)


def rows_body(scalars, ins, outs):
    q_ref, k_ref, v_ref = ins
    q0_ref, q1_ref, cross_ref, chip_ref = outs
    reorder = reorder_matrix()
    pair = pair_matrix()
    for i in range(2):
        rows = slice(i * BLK, (i + 1) * BLK)
        q0 = mul(reorder, q_ref[rows, :]).astype(bf16)
        q0_ref[rows, :] = q0
        q1_ref[i * HALF : (i + 1) * HALF, :] = fold(q0, 0.5)
    odd = scalars[0][0]
    outer = pl.ds(pl.multiple_of(odd * BLK, BLK), BLK)
    inner = pl.ds(pl.multiple_of((1 - odd) * BLK, BLK), BLK)
    for ref, near, far in ((cross_ref, outer, inner), (chip_ref, inner, outer)):
        ref[0:BLK, :] = k_ref[near, :]
        ref[BLK : 2 * BLK, :] = v_ref[near, :]
        ref[2 * BLK : 2 * BLK + HALF, :] = (mul(pair, k_ref[far, :]) * 0.5).astype(bf16)
        ref[2 * BLK + HALF : 3 * BLK, :] = mul(pair, v_ref[far, :]).astype(bf16)


def rows_to_send(place, query_vecs, key_vecs, value_vecs, groups):
    rows, width = query_vecs.shape
    ins = [one(a) for a in (query_vecs, key_vecs, value_vecs)]
    outs = [(array(n, width, bf16), "cols") for n in (rows, rows // 2, 3 * BLK, 3 * BLK)]
    return run_shares(rows_body, "rows_to_send", groups, [place], ins, outs)


def pack(stats):
    width = HEAD_DIM // len(stats)
    lane = iota(stats[0].shape, 1)
    packed = stats[-1]
    for n in range(len(stats) - 2, -1, -1):
        packed = jnp.where(lane < (n + 1) * width, stats[n], packed)
    return packed


def unpack(packed, head):
    lanes = [head * HEAD_DIM // 2 + n * HEAD_DIM // 4 for n in range(2)]
    return [jnp.broadcast_to(packed[:, lane : lane + 1], packed.shape) for lane in lanes]


def own_body(_, ins, outs):
    q_ref, k_ref, v_ref = ins
    sum_ref, stat_ref = outs
    heads = q_ref.shape[1] // HEAD_DIM
    for i in range(2):
        rows = slice(i * BLK, (i + 1) * BLK)
        units = [(q_ref[rows, cols(head)], [(k_ref[:, cols(head)], v_ref[:, cols(head)], None)]) for head in range(heads)]
        stats = []
        for head, (top, sums) in enumerate(attend(units)):
            sum_ref[rows, cols(head)] = sums[:, :HEAD_DIM]
            stats += [top, sums[:, HEAD_DIM:]]
        for n in range(0, heads, 2):
            stat_ref[rows, cols(n // 2)] = pack(stats[2 * n : 2 * n + 4])


def own_level(q0, key_vecs, value_vecs, groups):
    rows, width = q0.shape
    ins = [one(a) for a in (q0, key_vecs, value_vecs)]
    outs = [(array(rows, width, f32), "cols"), (array(rows, groups * HEAD_DIM, f32), "cols")]
    return run_shares(own_body, "own_level", groups // 2, [], ins, outs, DECLARED)


def halo_body(place_ref, *refs):
    count = len(refs) - 4
    piece_refs, (got_ref, right_ref, left_ref, sems) = refs[:count], refs[count:]
    copies = [pltpu.make_async_copy(ref, got_ref.at[n ^ place_ref[1]], sems.at[n]) for n, ref in enumerate(piece_refs)]
    for copy in copies:
        copy.start()
    for copy in copies:
        copy.wait()
    pair = count // 2
    for which, factor in ((1, 0.5), (2, 1.0)):
        rows = slice(which * HALF, (which + 1) * HALF)
        near = (which - 1) * BLK
        far = 2 * BLK + (which - 1) * HALF
        for j in range(count):
            level2 = got_ref[j, rows, :]
            level3 = fold_chunks(level2, HALF // 2, factor)
            near_ref, far_ref = (left_ref, right_ref) if j < pair else (right_ref, left_ref)
            spot = j % pair
            near_ref[near + spot * HALF : near + (spot + 1) * HALF, :] = level2
            far_ref[far + spot * HALF // 2 : far + (spot + 1) * HALF // 2, :] = level3


def coarse_halos(place, pieces):
    rows, width = pieces[0].shape
    vmem = pl.BlockSpec(memory_space=pltpu.VMEM)
    shape = jax.ShapeDtypeStruct((3 * BLK, width), bf16)
    return pl.pallas_call(
        halo_body,
        in_specs=[pl.BlockSpec(memory_space=pltpu.SMEM)] + [pl.BlockSpec(memory_space=pl.ANY)] * len(pieces),
        out_specs=[vmem] * 3,
        out_shape=[jax.ShapeDtypeStruct((len(pieces), rows, width), bf16), shape, shape],
        scratch_shapes=[pltpu.SemaphoreType.DMA((len(pieces),))],
        compiler_params=pltpu.CompilerParams(vmem_limit_bytes=16 << 20),
        cost_estimate=pl.CostEstimate(flops=1 << 20, bytes_accessed=24 * pieces[0].size, transcendentals=0),
        name="coarse_halos",
    )(place, *pieces)


def coarse_body(bias_ref, got_ref, prev_ref, next_ref, back_ref):
    count = got_ref.shape[0]
    heads = got_ref.shape[2] // HEAD_DIM
    bias_prev = bias_ref[0]
    bias_next = bias_ref[1]
    lane = iota((HALF, HEAD_DIM), 1)

    for head in range(heads):
        here = cols(head)

        def own(which, j):
            return got_ref[j, which * HALF : (which + 1) * HALF, here]

        def near(ref, which, spot):
            first = (which - 1) * BLK + spot * HALF
            return ref[first : first + HALF, here]

        def both(ref, which):
            return ref[(which - 1) * BLK : which * BLK, here]

        def far(ref, which):
            first = 2 * BLK + (which - 1) * HALF
            return ref[first : first + HALF, here]

        def near3(ref, which):
            return fold_chunks(both(ref, which), HALF // 2, 0.5 if which == 1 else 1.0)

        def joined(*rows):
            return jnp.concatenate(rows, axis=0)

        def part(pick, bias):
            return (pick(1), pick(2), bias)

        units = [
            (own(0, 0), [part(lambda w: joined(own(w, 2), own(w, 3)), None), part(lambda w: near(prev_ref, w, 0), bias_prev)]),
            (own(0, 1), [part(lambda w: both(prev_ref, w), bias_prev), part(lambda w: own(w, 3), None)]),
            (own(0, 2), [part(lambda w: both(next_ref, w), bias_next), part(lambda w: own(w, 0), None)]),
            (own(0, 3), [part(lambda w: joined(own(w, 0), own(w, 1)), None), part(lambda w: near(next_ref, w, 1), bias_next)]),
        ]
        for j, (ref, bias, other, other_bias) in enumerate(
            ((next_ref, bias_next, prev_ref, bias_prev), (prev_ref, bias_prev, next_ref, bias_next))
        ):
            query = joined(*[fold_chunks(own(0, 2 * j + n), HALF // 2, 0.5) for n in range(2)])
            units.append(
                (
                    query,
                    [part(lambda w: joined(near3(ref, w), far(ref, w)), bias), part(lambda w: far(other, w), other_bias)],
                )
            )
        found = attend(units)
        for j in range(count):
            top2, sum2 = found[j]
            top3, sum3 = found[count + j // 2]

            def spread(rows):
                first = (j % 2) * 2 * SUB
                one = rows[first : first + SUB]
                other = rows[first + SUB : first + 2 * SUB]
                return joined(one, one, other, other)

            top3 = spread(top3)
            sum3 = spread(sum3)
            top = jnp.maximum(top2, top3)
            scale2 = jnp.exp2(top2 - top)
            scale3 = jnp.exp2(top3 - top)
            values = sum2[:, :HEAD_DIM] * scale2 + sum3[:, :HEAD_DIM] * scale3
            total = sum2[:, HEAD_DIM:] * (4.0 * scale2) + sum3[:, HEAD_DIM:] * (8.0 * scale3)
            back_ref[j, 0:HALF, here] = (values / total).astype(bf16)
            level = top + jnp.log2(total)
            high = level.astype(bf16).astype(f32)
            middle = (level - high).astype(bf16).astype(f32)
            terms = jnp.where(lane == 0, high, jnp.where(lane == 1, middle, level - high - middle))
            back_ref[j, HALF : HALF + 16, here] = terms.T[0:16, :].astype(bf16)


def coarse_levels(bias, got, from_prev, from_next):
    count, _, width = got.shape
    vmem = pl.BlockSpec(memory_space=pltpu.VMEM)
    return pl.pallas_call(
        coarse_body,
        in_specs=[pl.BlockSpec(memory_space=pltpu.SMEM), vmem, vmem, vmem],
        out_specs=vmem,
        out_shape=jax.ShapeDtypeStruct((count, HALF + 16, width), bf16),
        compiler_params=pltpu.CompilerParams(vmem_limit_bytes=16 << 20),
        cost_estimate=pl.CostEstimate(flops=DECLARED, bytes_accessed=8 * got.size, transcendentals=1 << 20),
        name="coarse_levels",
    )(bias, got, from_prev, from_next)


def side_body(side, scalars, ins, outs):
    q0_ref, q1_ref, sum_ref, stat_ref, side_ref = ins[:5]
    heads = q0_ref.shape[1] // HEAD_DIM
    bias = scalars[1][side]
    blocks = (side, 1 - side)
    pair = pair_matrix()
    near_keys = (mul(pair, side_ref[0:BLK, :]) * 0.5).astype(bf16)
    near_values = mul(pair, side_ref[BLK : 2 * BLK, :]).astype(bf16)
    far_keys = slice(2 * BLK, 2 * BLK + HALF)
    far_values = slice(2 * BLK + HALF, 3 * BLK)
    fine = [pl.ds(pl.multiple_of(block * BLK, BLK), BLK) for block in blocks]
    middle = [pl.ds(pl.multiple_of(block * HALF, HALF), HALF) for block in blocks]
    units = []
    for head in range(heads):
        here = cols(head)
        far = (side_ref[far_keys, here], side_ref[far_values, here], None)
        whole = tuple(
            jnp.concatenate([near[:, here], side_ref[far, here]], axis=0)
            for near, far in ((near_keys, far_keys), (near_values, far_values))
        )
        units.append((q0_ref[fine[0], here], [(side_ref[0:BLK, here], side_ref[BLK : 2 * BLK, here], None)]))
        units.append((q1_ref[middle[0], here], [far]))
        units.append((q1_ref[middle[1], here], [(*whole, None)]))
    found = [(top + bias, sums) for top, sums in attend(units)]
    if len(ins) == 5:
        for n in range(2):
            results = []
            for head in range(heads):
                here = cols(head)
                top1, sum1 = found[3 * head + 1 + n]
                top1, sum1 = twice(top1), twice(sum1)
                own_top, own_total = unpack(stat_ref[fine[n], cols(head // 2)], head % 2)
                top = jnp.maximum(top1, own_top)
                if n == 0:
                    top0, sum0 = found[3 * head]
                    top = jnp.maximum(top, top0)
                scale1 = jnp.exp2(top1 - top)
                own_scale = jnp.exp2(own_top - top)
                number = sum1[:, :HEAD_DIM] * scale1 + sum_ref[fine[n], here] * own_scale
                total = sum1[:, HEAD_DIM:] * (2.0 * scale1) + own_total * own_scale
                if n == 0:
                    scale0 = jnp.exp2(top0 - top)
                    number = number + sum0[:, :HEAD_DIM] * scale0
                    total = total + sum0[:, HEAD_DIM:] * scale0
                outs[0][fine[n], here] = number
                results += [top, total]
            for m in range(0, heads, 2):
                outs[1][fine[n], cols(m // 2)] = pack(results[2 * m : 2 * m + 4])
        return
    back_ref = ins[5]
    restore = restore_matrix()
    levels = []
    for head in range(heads):
        terms = back_ref[head // 2, HALF : HALF + 16, cols(head % 2)].astype(f32)
        terms = jnp.sum(jnp.where(iota(terms.shape, 0) < 3, terms, 0.0), axis=0, keepdims=True)
        levels.append(jnp.broadcast_to(terms, (HEAD_DIM, HEAD_DIM)).T)
    for n in range(2):
        spot = pl.ds(pl.multiple_of(blocks[n] * HALF // 2, HALF // 2), HALF // 2)
        results = []
        for head in range(heads):
            here = cols(head)
            top1, sum1 = found[3 * head + 1 + n]
            half = HALF // 2
            level = twice(jnp.where(blocks[n] == 0, levels[head][:half, :], levels[head][half:, :]))
            top = jnp.maximum(top1, level)
            scale1 = jnp.exp2(top1 - top)
            scale2 = jnp.exp2(level - top)
            number = twice(sum1[:, :HEAD_DIM] * scale1 + twice(back_ref[head // 2, spot, cols(head % 2)].astype(f32)) * scale2)
            total = twice(sum1[:, HEAD_DIM:] * (2.0 * scale1) + scale2)
            top = twice(top)
            own_top, own_total = unpack(stat_ref[fine[n], cols(head // 2)], head % 2)
            most = jnp.maximum(top, own_top)
            if n == 0:
                top0, sum0 = found[3 * head]
                most = jnp.maximum(most, top0)
            scale = jnp.exp2(top - most)
            own_scale = jnp.exp2(own_top - most)
            number = number * scale + sum_ref[fine[n], here] * own_scale
            total = total * scale + own_total * own_scale
            if n == 0:
                scale0 = jnp.exp2(top0 - most)
                number = number + sum0[:, :HEAD_DIM] * scale0
                total = total + sum0[:, HEAD_DIM:] * scale0
            results.append((number / total).astype(bf16))
        outs[0][fine[n], :] = mul(restore, jnp.concatenate(results, axis=1)).astype(bf16)


def chip_body(scalars, ins, outs):
    side_body(1 - scalars[0][0], scalars, ins, outs)


def finish_body(scalars, ins, outs):
    side_body(scalars[0][0], scalars, ins, outs)


def chip_level(odd, bias, q0, q1, sums, stat, chip, groups):
    rows, width = q0.shape
    ins = [one(a) for a in (q0, q1, sums, stat)] + [one(chip, pinned=False)]
    outs = [(array(rows, width, f32), "cols"), (array(rows, groups * HEAD_DIM, f32), "cols")]
    return run_shares(chip_body, "chip_level", groups // 2, [odd, bias], ins, outs)


def finish(place, bias, q0, q1, sums, stat, cross, back):
    groups = back.shape[0]
    rows, width = q0.shape
    ins = [one(a) for a in (q0, q1, sums, stat)] + [one(cross, pinned=False), one(back, "lead", pinned=False)]
    outs = [(array(rows, width, bf16), "cols")]
    return run_shares(finish_body, "finish", groups // 2, [place, bias], ins, outs)[0]


def shift(value, axis, steps):
    count = lax.axis_size(axis)
    first, last = (max(0, -steps), min(count, count - steps))
    return lax.ppermute(value, axis, [(source, source + steps) for source in range(first, last)])


def trade(value, axis, pairs):
    return lax.ppermute(value, axis, pairs + [(target, source) for source, target in pairs])


def edge_bias(axis):
    place = lax.axis_index(axis)
    last = lax.axis_size(axis) - 1
    at_edge = jnp.stack([place == 0, place == last])
    return jnp.where(at_edge, very_negative, 0.0).astype(f32)


def local(query_vecs, key_vecs, value_vecs):
    groups = lax.axis_size("grp")
    assert query_vecs.shape == (2 * BLK, HEADS * HEAD_DIM) and groups == 4
    everyone = ("seq", "grp")
    count = lax.axis_size(everyone)
    spot = lax.axis_index("grp")
    odd = jnp.bitwise_and(spot, 1)
    place = jnp.stack([odd, spot]).astype(jnp.int32)
    bias = edge_bias(everyone)
    pieces = list(swap_rows(place, query_vecs, key_vecs, value_vecs, groups))
    query_rows, pieces = lax.optimization_barrier((query_vecs, pieces))
    for n in range(1, groups):
        pieces[n] = lax.ppermute(pieces[n], "grp", [(source, source ^ n) for source in range(groups)])
    q0, q1, cross, chip = rows_to_send(place, query_rows, key_vecs, value_vecs, groups)
    cross = trade(cross, everyone, [(first, first + 1) for first in range(1, count - 1, 2)])
    pieces, chip = lax.optimization_barrier((pieces, chip))
    got, coarse_right, coarse_left = coarse_halos(place, pieces)
    coarse_right, coarse_left, chip, q0 = lax.optimization_barrier((coarse_right, coarse_left, chip, q0))
    coarse_prev = shift(coarse_right, "seq", 1)
    coarse_next = shift(coarse_left, "seq", -1)
    chip = trade(chip, everyone, [(first, first + 1) for first in range(0, count - 1, 2)])
    own, own_stat = own_level(q0, key_vecs, value_vecs, groups)
    own, own_stat = chip_level(place, bias, q0, q1, own, own_stat, chip, groups)
    got, own = lax.optimization_barrier((got, own))
    back = coarse_levels(edge_bias("seq"), got, coarse_prev, coarse_next)
    back = lax.all_to_all(back, "grp", split_axis=0, concat_axis=0, tiled=True)
    return finish(place, bias, q0, q1, own, own_stat, cross, back)


def solution(mesh):
    return jax.shard_map(
        local,
        mesh=mesh,
        in_specs=(P(("seq", "grp"), None), P(("seq", "grp"), None), P(("seq", "grp"), None)),
        out_specs=P(("seq", "grp"), None),
        check_vma=False,
    )
```

```python
import functools
import functools
import functools
import functools
import functools
import functools
import functools
import functools
import functools
import functools
import functools
import functools
import functools
import functools
import functools
import functools
import functools
import functools
import functools
import functools
import functools
import functools
import functools
import math

import jax
import jax.numpy as jnp
from jax import lax
from jax.experimental import pallas as pl
from jax.experimental.pallas import tpu as pltpu
from jax.sharding import PartitionSpec as P

HEADS = 8
HEAD_DIM = 128
BLK = 256
HALF = BLK // 2
SUB = BLK // 8
LEV = 4
EXP_SCALE = math.log2(math.e) / math.sqrt(HEAD_DIM)

VMEM_GRANT = 48 << 20

very_negative = -1e30
f32 = jnp.float32
bf16 = jnp.bfloat16


def iota(shape, dim):
    return lax.broadcasted_iota(jnp.int32, shape, dim)


def bit(value, place):
    return jnp.bitwise_and(lax.shift_right_logical(value, place), 1)


def low_bits(value):
    step = SUB.bit_length() - 1
    deep = jnp.bitwise_and(value, SUB - 1)
    return 8 * deep + 4 * bit(value, step) + 2 * bit(value, step + 1) + bit(value, step + 2)


def reorder_matrix():
    return (iota((BLK, BLK), 1) == low_bits(iota((BLK, BLK), 0))).astype(bf16)


def restore_matrix():
    return (iota((BLK, BLK), 0) == low_bits(iota((BLK, BLK), 1))).astype(bf16)


def pair_matrix():
    first = low_bits(iota((HALF, BLK), 0))
    place = iota((HALF, BLK), 1)
    return jnp.logical_or(place == first, place == first + 1).astype(bf16)


def mul(left, right):
    return jnp.dot(left, right, preferred_element_type=f32)


def fold(rows, factor):
    half = rows.shape[0] // 2
    total = rows[:half].astype(f32) + rows[half:].astype(f32)
    if factor != 1.0:
        total = total * factor
    return total.astype(bf16)


def fold_chunks(rows, chunk, factor):
    count = rows.shape[0] // chunk
    return jnp.concatenate([fold(rows[i * chunk : (i + 1) * chunk], factor) for i in range(count)], axis=0)


def twice(rows):
    return jnp.concatenate([rows, rows], axis=0)


def cols(head):
    return slice(head * HEAD_DIM, (head + 1) * HEAD_DIM)


def lane_chunks(rows):
    return [rows[:, first : first + HEAD_DIM] for first in range(0, rows.shape[1], HEAD_DIM)]


def twice(rows):
    return jnp.concatenate([rows, rows], axis=0)


def cols(head):
    return slice(head * HEAD_DIM, (head + 1) * HEAD_DIM)


def lane_chunks(rows):
    return [rows[:, first : first + HEAD_DIM] for first in range(0, rows.shape[1], HEAD_DIM)]


def twice(rows):
    return jnp.concatenate([rows, rows], axis=0)


def cols(head):
    return slice(head * HEAD_DIM, (head + 1) * HEAD_DIM)


def lane_chunks(rows):
    return [rows[:, first : first + HEAD_DIM] for first in range(0, rows.shape[1], HEAD_DIM)]


def twice(rows):
    return jnp.concatenate([rows, rows], axis=0)


def cols(head):
    return slice(head * HEAD_DIM, (head + 1) * HEAD_DIM)


def lane_chunks(rows):
    return [rows[:, first : first + HEAD_DIM] for first in range(0, rows.shape[1], HEAD_DIM)]


def twice(rows):
    return jnp.concatenate([rows, rows], axis=0)


def cols(head):
    return slice(head * HEAD_DIM, (head + 1) * HEAD_DIM)


def lane_chunks(rows):
    return [rows[:, first : first + HEAD_DIM] for first in range(0, rows.shape[1], HEAD_DIM)]


def twice(rows):
    return jnp.concatenate([rows, rows], axis=0)


def cols(head):
    return slice(head * HEAD_DIM, (head + 1) * HEAD_DIM)


def lane_chunks(rows):
    return [rows[:, first : first + HEAD_DIM] for first in range(0, rows.shape[1], HEAD_DIM)]


def twice(rows):
    return jnp.concatenate([rows, rows], axis=0)


def cols(head):
    return slice(head * HEAD_DIM, (head + 1) * HEAD_DIM)


def lane_chunks(rows):
    return [rows[:, first : first + HEAD_DIM] for first in range(0, rows.shape[1], HEAD_DIM)]


def twice(rows):
    return jnp.concatenate([rows, rows], axis=0)


def cols(head):
    return slice(head * HEAD_DIM, (head + 1) * HEAD_DIM)


COARSE_FLOPS = 1 << 29


def lane_chunks(rows):
    return [rows[:, first : first + HEAD_DIM] for first in range(0, rows.shape[1], HEAD_DIM)]


def twice(rows):
    return jnp.concatenate([rows, rows], axis=0)


def cols(head):
    return slice(head * HEAD_DIM, (head + 1) * HEAD_DIM)


COARSE_FLOPS = 1 << 36


def lane_chunks(rows):
    return [rows[:, first : first + HEAD_DIM] for first in range(0, rows.shape[1], HEAD_DIM)]


def twice(rows):
    return jnp.concatenate([rows, rows], axis=0)


def cols(head):
    return slice(head * HEAD_DIM, (head + 1) * HEAD_DIM)


COARSE_FLOPS = 1 << 36


def lane_chunks(rows):
    return [rows[:, first : first + HEAD_DIM] for first in range(0, rows.shape[1], HEAD_DIM)]


def twice(rows):
    return jnp.concatenate([rows, rows], axis=0)


def cols(head):
    return slice(head * HEAD_DIM, (head + 1) * HEAD_DIM)


COARSE_FLOPS = 1 << 36


def lane_chunks(rows):
    return [rows[:, first : first + HEAD_DIM] for first in range(0, rows.shape[1], HEAD_DIM)]


def twice(rows):
    return jnp.concatenate([rows, rows], axis=0)


def cols(head):
    return slice(head * HEAD_DIM, (head + 1) * HEAD_DIM)


COARSE_FLOPS = 1 << 36


def lane_chunks(rows):
    return [rows[:, first : first + HEAD_DIM] for first in range(0, rows.shape[1], HEAD_DIM)]


def twice(rows):
    return jnp.concatenate([rows, rows], axis=0)


def cols(head):
    return slice(head * HEAD_DIM, (head + 1) * HEAD_DIM)


COARSE_FLOPS = 1 << 36


def lane_chunks(rows):
    return [rows[:, first : first + HEAD_DIM] for first in range(0, rows.shape[1], HEAD_DIM)]


def twice(rows):
    return jnp.concatenate([rows, rows], axis=0)


def cols(head):
    return slice(head * HEAD_DIM, (head + 1) * HEAD_DIM)


COARSE_FLOPS = 1 << 36


def lane_chunks(rows):
    return [rows[:, first : first + HEAD_DIM] for first in range(0, rows.shape[1], HEAD_DIM)]


def twice(rows):
    return jnp.concatenate([rows, rows], axis=0)


def cols(head):
    return slice(head * HEAD_DIM, (head + 1) * HEAD_DIM)


COARSE_FLOPS = 1 << 36


def lane_chunks(rows):
    return [rows[:, first : first + HEAD_DIM] for first in range(0, rows.shape[1], HEAD_DIM)]


def twice(rows):
    return jnp.concatenate([rows, rows], axis=0)


def cols(head):
    return slice(head * HEAD_DIM, (head + 1) * HEAD_DIM)


COARSE_FLOPS = 1 << 36


def lane_chunks(rows):
    return [rows[:, first : first + HEAD_DIM] for first in range(0, rows.shape[1], HEAD_DIM)]


def twice(rows):
    return jnp.concatenate([rows, rows], axis=0)


def cols(head):
    return slice(head * HEAD_DIM, (head + 1) * HEAD_DIM)


COARSE_FLOPS = 1 << 36


def lane_chunks(rows):
    return [rows[:, first : first + HEAD_DIM] for first in range(0, rows.shape[1], HEAD_DIM)]


def twice(rows):
    return jnp.concatenate([rows, rows], axis=0)


def cols(head):
    return slice(head * HEAD_DIM, (head + 1) * HEAD_DIM)


DECLARED = 1 << 36


def lane_chunks(rows):
    return [rows[:, first : first + HEAD_DIM] for first in range(0, rows.shape[1], HEAD_DIM)]


def twice(rows):
    return jnp.concatenate([rows, rows], axis=0)


def cols(head):
    return slice(head * HEAD_DIM, (head + 1) * HEAD_DIM)


DECLARED = 1 << 36


def lane_chunks(rows):
    return [rows[:, first : first + HEAD_DIM] for first in range(0, rows.shape[1], HEAD_DIM)]


def twice(rows):
    return jnp.concatenate([rows, rows], axis=0)


def cols(head):
    return slice(head * HEAD_DIM, (head + 1) * HEAD_DIM)


DECLARED = 1 << 36


def lane_chunks(rows):
    return [rows[:, first : first + HEAD_DIM] for first in range(0, rows.shape[1], HEAD_DIM)]


def twice(rows):
    return jnp.concatenate([rows, rows], axis=0)


def cols(head):
    return slice(head * HEAD_DIM, (head + 1) * HEAD_DIM)


DECLARED = 1 << 36


def twice(rows):
    return jnp.concatenate([rows, rows], axis=0)


def cols(head):
    return slice(head * HEAD_DIM, (head + 1) * HEAD_DIM)


DECLARED = 1 << 36


def twice(rows):
    return jnp.concatenate([rows, rows], axis=0)


def cols(head):
    return slice(head * HEAD_DIM, (head + 1) * HEAD_DIM)


DECLARED = 1 << 36


def with_ones(values):
    return jnp.concatenate([values, jnp.ones_like(values)], axis=1)


def attend(units):
    scores = []
    for query, parts in units:
        raws = [
            lax.dot_general(query, keys, (((1,), (1,)), ((), ())), preferred_element_type=f32) for keys, _, _ in parts
        ]
        scores.append([raw if part[2] is None else raw + part[2] for raw, part in zip(raws, parts)])
    tops = []
    for raws in scores:
        tops.append(functools.reduce(jnp.maximum, [jnp.max(raw, axis=1, keepdims=True) for raw in raws]))
    found = []
    for (_, parts), raws, top in zip(units, scores, tops):
        total = None
        for (_, values, _), raw in zip(parts, raws):
            weights = jnp.exp2((raw - top) * EXP_SCALE).astype(bf16)
            one = mul(weights, with_ones(values))
            total = one if total is None else total + one
        found.append((jnp.broadcast_to(top * EXP_SCALE, (top.shape[0], HEAD_DIM)), total))
    return found


def share_of(ref, share, shares):
    width = ref.shape[1] // shares
    first = share * width
    if not isinstance(share, int):
        first = pl.multiple_of(first, HEAD_DIM)
    return ref.at[:, pl.ds(first, width)]


class Operand:
    def __init__(self, values, pieces=False, pinned=False):
        self.values = values
        self.pieces = pieces
        self.pinned = pinned

    def buffer(self, shares):
        rows, width = self.values[0].shape
        if self.pieces:
            return (shares, len(self.values) // shares, rows, width)
        return (shares, rows, width // shares)


def one(value, pinned=True):
    return Operand([value], pinned=pinned)


def run_shares(body, name, shares, scalars, ins, outs, work=1 << 10):
    out_kinds = [kind for _, kind in outs]
    pieces = [i for i, kind in enumerate(out_kinds) if isinstance(kind, int)]
    buffered = len(outs) - max(0, len(pieces) - 1)

    first = [sum(len(operand.values) for operand in ins[:i]) for i in range(len(ins) + 1)]

    def kernel(*refs):
        refs = list(refs)
        take = lambda count: [refs.pop(0) for _ in range(count)]
        scalar_refs, in_refs, out_refs = take(len(scalars)), take(first[-1]), take(len(outs))
        in_bufs, out_bufs, (in_sems, out_sems) = take(len(ins)), take(buffered), take(2)

        def piece(i, n):
            entry = n ^ scalar_refs[0][1]
            count = len(ins[i].values) // shares
            target = in_bufs[i].at[lax.div(entry, count), lax.rem(entry, count)]
            return pltpu.make_async_copy(in_refs[first[i] + n], target, piece_sems.at[n])

        def bring(i, share, which=0):
            source = share_of(in_refs[first[i] + which], share, shares)
            return pltpu.make_async_copy(source, in_bufs[i].at[share], in_sems.at[i, share])

        def begin(i, share):
            if len(ins[i].values) == 1:
                bring(i, share).start()
            else:
                pl.when(scalar_refs[0][2] == 1)(lambda: bring(i, share, 0).start())
                pl.when(scalar_refs[0][2] != 1)(lambda: bring(i, share, 1).start())

        whole = [i for i, operand in enumerate(ins) if not operand.pieces]
        split = [(i, n) for i, operand in enumerate(ins) if operand.pieces for n in range(len(operand.values))]
        piece_sems = refs.pop(0)

        def put(i, share):
            if i in pieces:
                entry = out_kinds[i] ^ scalar_refs[0][1]
                return pltpu.make_async_copy(out_bufs[-1].at[entry], out_refs[i], out_sems.at[i, 0])
            target = share_of(out_refs[i], share, shares)
            return pltpu.make_async_copy(out_bufs[i].at[share], target, out_sems.at[i, share])

        for share in range(shares):
            for i in whole:
                begin(i, share)
            if share == 0:
                for i, n in split:
                    piece(i, n).start()
        for i, n in split:
            piece(i, n).wait()

        def step(share, carry):
            for i in whole:
                bring(i, share).wait()
            body(scalar_refs, [buf.at[share] for buf in in_bufs], [buf.at[share] for buf in out_bufs])
            for i in range(len(outs) - len(pieces)):
                put(i, share).start()
            return carry

        lax.fori_loop(0, shares, step, 0)
        for i in pieces:
            put(i, 0).start()
        for share in range(shares):
            for i in range(len(outs) - len(pieces)):
                put(i, share).wait()
        for i in pieces:
            put(i, 0).wait()

    values, specs = [], []
    for operand in ins:
        for value in operand.values:
            values.append(pltpu.with_memory_space_constraint(value, pltpu.HBM) if operand.pinned else value)
            specs.append(pl.BlockSpec(memory_space=pltpu.HBM if operand.pinned else pl.ANY))
    buffers = [pltpu.VMEM(operand.buffer(shares), operand.values[0].dtype) for operand in ins]
    for shape, kind in outs[:buffered]:
        width = shape.shape[-1]
        if isinstance(kind, int):
            buffers.append(pltpu.VMEM((shares, *shape.shape), shape.dtype))
            continue
        buffers.append(pltpu.VMEM((shares, shape.shape[0], width // shares), shape.dtype))
    return pl.pallas_call(
        kernel,
        in_specs=[pl.BlockSpec(memory_space=pltpu.SMEM)] * len(scalars) + specs,
        out_specs=[pl.BlockSpec(memory_space=pltpu.HBM)] * len(outs),
        out_shape=[pltpu.HBM(shape.shape, shape.dtype) for shape, _ in outs],
        scratch_shapes=buffers
        + [pltpu.SemaphoreType.DMA((len(ins), shares)), pltpu.SemaphoreType.DMA((len(outs), shares))]
        + [pltpu.SemaphoreType.DMA((max(len(operand.values) for operand in ins),))],
        compiler_params=pltpu.CompilerParams(vmem_limit_bytes=VMEM_GRANT),
        cost_estimate=pl.CostEstimate(flops=work, bytes_accessed=1 << 10, transcendentals=0),
        name=name,
    )(*scalars, *values)


def array(rows, width, dtype):
    return jax.ShapeDtypeStruct((rows, width), dtype)


def swap_body(_, ins, outs):
    pair = pair_matrix()
    for place, (ref, factor) in enumerate(zip(ins, (0.5, 0.5, 1.0))):
        for i in range(2):
            level1 = mul(pair, ref[i * BLK : (i + 1) * BLK, :])
            if factor != 1.0:
                level1 = level1 * factor
            first = place * HALF + i * HALF // 2
            outs[0][first : first + HALF // 2, :] = fold(level1.astype(bf16), factor)


def swap_rows(place, query_vecs, key_vecs, value_vecs, groups):
    width = query_vecs.shape[1]
    ins = [one(a) for a in (query_vecs, key_vecs, value_vecs)]
    outs = [(array(3 * HALF, width // groups, bf16), n) for n in range(groups)]
    return run_shares(swap_body, "swap_rows", groups, [place], ins, outs)


def rows_body(scalars, ins, outs):
    q_ref, k_ref, v_ref = ins
    q0_ref, q1_ref, cross_ref, chip_ref = outs
    reorder = reorder_matrix()
    pair = pair_matrix()
    for i in range(2):
        rows = slice(i * BLK, (i + 1) * BLK)
        q0 = mul(reorder, q_ref[rows, :]).astype(bf16)
        q0_ref[rows, :] = q0
        q1_ref[i * HALF : (i + 1) * HALF, :] = fold(q0, 0.5)
    odd = scalars[0][0]
    outer = pl.ds(pl.multiple_of(odd * BLK, BLK), BLK)
    inner = pl.ds(pl.multiple_of((1 - odd) * BLK, BLK), BLK)
    for ref, near, far in ((cross_ref, outer, inner), (chip_ref, inner, outer)):
        ref[0:BLK, :] = k_ref[near, :]
        ref[BLK : 2 * BLK, :] = v_ref[near, :]
        ref[2 * BLK : 2 * BLK + HALF, :] = (mul(pair, k_ref[far, :]) * 0.5).astype(bf16)
        ref[2 * BLK + HALF : 3 * BLK, :] = mul(pair, v_ref[far, :]).astype(bf16)


def rows_to_send(place, query_vecs, key_vecs, value_vecs, groups):
    rows, width = query_vecs.shape
    ins = [one(a) for a in (query_vecs, key_vecs, value_vecs)]
    outs = [(array(n, width, bf16), "cols") for n in (rows, rows // 2, 3 * BLK, 3 * BLK)]
    return run_shares(rows_body, "rows_to_send", groups, [place], ins, outs)


def pack(stats):
    width = HEAD_DIM // len(stats)
    lane = iota(stats[0].shape, 1)
    packed = stats[-1]
    for n in range(len(stats) - 2, -1, -1):
        packed = jnp.where(lane < (n + 1) * width, stats[n], packed)
    return packed


def unpack(packed, head):
    lanes = [head * HEAD_DIM // 2 + n * HEAD_DIM // 4 for n in range(2)]
    return [jnp.broadcast_to(packed[:, lane : lane + 1], packed.shape) for lane in lanes]


def own_body(_, ins, outs):
    q_ref, k_ref, v_ref = ins
    sum_ref, stat_ref = outs
    heads = q_ref.shape[1] // HEAD_DIM
    for i in range(2):
        rows = slice(i * BLK, (i + 1) * BLK)
        units = [(q_ref[rows, cols(head)], [(k_ref[:, cols(head)], v_ref[:, cols(head)], None)]) for head in range(heads)]
        stats = []
        for head, (top, sums) in enumerate(attend(units)):
            sum_ref[rows, cols(head)] = sums[:, :HEAD_DIM]
            stats += [top, sums[:, HEAD_DIM:]]
        for n in range(0, heads, 2):
            stat_ref[rows, cols(n // 2)] = pack(stats[2 * n : 2 * n + 4])


def own_level(q0, key_vecs, value_vecs, groups):
    rows, width = q0.shape
    ins = [one(a) for a in (q0, key_vecs, value_vecs)]
    outs = [(array(rows, width, f32), "cols"), (array(rows, groups * HEAD_DIM, f32), "cols")]
    return run_shares(own_body, "own_level", groups // 2, [], ins, outs, DECLARED)


def halo_body(place_ref, *refs):
    count = len(refs) - 4
    piece_refs, (got_ref, right_ref, left_ref, sems) = refs[:count], refs[count:]
    copies = [pltpu.make_async_copy(ref, got_ref.at[n ^ place_ref[1]], sems.at[n]) for n, ref in enumerate(piece_refs)]
    for copy in copies:
        copy.start()
    for copy in copies:
        copy.wait()
    pair = count // 2
    for which, factor in ((1, 0.5), (2, 1.0)):
        rows = slice(which * HALF, (which + 1) * HALF)
        near = (which - 1) * BLK
        far = 2 * BLK + (which - 1) * HALF
        for j in range(count):
            level2 = got_ref[j, rows, :]
            level3 = fold_chunks(level2, HALF // 2, factor)
            near_ref, far_ref = (left_ref, right_ref) if j < pair else (right_ref, left_ref)
            spot = j % pair
            near_ref[near + spot * HALF : near + (spot + 1) * HALF, :] = level2
            far_ref[far + spot * HALF // 2 : far + (spot + 1) * HALF // 2, :] = level3


def coarse_halos(place, pieces):
    rows, width = pieces[0].shape
    vmem = pl.BlockSpec(memory_space=pltpu.VMEM)
    shape = jax.ShapeDtypeStruct((3 * BLK, width), bf16)
    return pl.pallas_call(
        halo_body,
        in_specs=[pl.BlockSpec(memory_space=pltpu.SMEM)] + [pl.BlockSpec(memory_space=pl.ANY)] * len(pieces),
        out_specs=[vmem] * 3,
        out_shape=[jax.ShapeDtypeStruct((len(pieces), rows, width), bf16), shape, shape],
        scratch_shapes=[pltpu.SemaphoreType.DMA((len(pieces),))],
        compiler_params=pltpu.CompilerParams(vmem_limit_bytes=16 << 20),
        cost_estimate=pl.CostEstimate(flops=1 << 20, bytes_accessed=24 * pieces[0].size, transcendentals=0),
        name="coarse_halos",
    )(place, *pieces)


def coarse_body(place_ref, bias_ref, got_ref, prev_ref, next_ref, *refs):
    *out_refs, back_ref, sems = refs
    count = got_ref.shape[0]
    heads = got_ref.shape[2] // HEAD_DIM
    bias_prev = bias_ref[0]
    bias_next = bias_ref[1]
    lane = iota((HALF, HEAD_DIM), 1)

    for head in range(heads):
        here = cols(head)

        def own(which, j):
            return got_ref[j, which * HALF : (which + 1) * HALF, here]

        def near(ref, which, spot):
            first = (which - 1) * BLK + spot * HALF
            return ref[first : first + HALF, here]

        def both(ref, which):
            return ref[(which - 1) * BLK : which * BLK, here]

        def far(ref, which):
            first = 2 * BLK + (which - 1) * HALF
            return ref[first : first + HALF, here]

        def near3(ref, which):
            return fold_chunks(both(ref, which), HALF // 2, 0.5 if which == 1 else 1.0)

        def joined(*rows):
            return jnp.concatenate(rows, axis=0)

        def part(pick, bias):
            return (pick(1), pick(2), bias)

        units = [
            (own(0, 0), [part(lambda w: joined(own(w, 2), own(w, 3)), None), part(lambda w: near(prev_ref, w, 0), bias_prev)]),
            (own(0, 1), [part(lambda w: both(prev_ref, w), bias_prev), part(lambda w: own(w, 3), None)]),
            (own(0, 2), [part(lambda w: both(next_ref, w), bias_next), part(lambda w: own(w, 0), None)]),
            (own(0, 3), [part(lambda w: joined(own(w, 0), own(w, 1)), None), part(lambda w: near(next_ref, w, 1), bias_next)]),
        ]
        for j, (ref, bias, other, other_bias) in enumerate(
            ((next_ref, bias_next, prev_ref, bias_prev), (prev_ref, bias_prev, next_ref, bias_next))
        ):
            query = joined(*[fold_chunks(own(0, 2 * j + n), HALF // 2, 0.5) for n in range(2)])
            units.append(
                (
                    query,
                    [part(lambda w: joined(near3(ref, w), far(ref, w)), bias), part(lambda w: far(other, w), other_bias)],
                )
            )
        found = attend(units)
        for j in range(count):
            top2, sum2 = found[j]
            top3, sum3 = found[count + j // 2]

            def spread(rows):
                first = (j % 2) * 2 * SUB
                one = rows[first : first + SUB]
                other = rows[first + SUB : first + 2 * SUB]
                return joined(one, one, other, other)

            top3 = spread(top3)
            sum3 = spread(sum3)
            top = jnp.maximum(top2, top3)
            scale2 = jnp.exp2(top2 - top)
            scale3 = jnp.exp2(top3 - top)
            values = sum2[:, :HEAD_DIM] * scale2 + sum3[:, :HEAD_DIM] * scale3
            total = sum2[:, HEAD_DIM:] * (4.0 * scale2) + sum3[:, HEAD_DIM:] * (8.0 * scale3)
            back_ref[j, 0:HALF, here] = (values / total).astype(bf16)
            level = top + jnp.log2(total)
            high = level.astype(bf16).astype(f32)
            middle = (level - high).astype(bf16).astype(f32)
            terms = jnp.where(lane == 0, high, jnp.where(lane == 1, middle, level - high - middle))
            back_ref[j, HALF : HALF + 16, here] = terms.T[0:16, :].astype(bf16)
    copies = [
        pltpu.make_async_copy(back_ref.at[n ^ place_ref[1]], ref, sems.at[n]) for n, ref in enumerate(out_refs)
    ]
    for copy in copies:
        copy.start()
    for copy in copies:
        copy.wait()


def coarse_levels(place, bias, got, from_prev, from_next):
    count, _, width = got.shape
    vmem = pl.BlockSpec(memory_space=pltpu.VMEM)
    smem = pl.BlockSpec(memory_space=pltpu.SMEM)
    rows = HALF + 16
    return pl.pallas_call(
        coarse_body,
        in_specs=[smem, smem, vmem, vmem, vmem],
        out_specs=[pl.BlockSpec(memory_space=pl.ANY)] * count,
        out_shape=[array(rows, width, bf16)] * count,
        scratch_shapes=[pltpu.VMEM((count, rows, width), bf16), pltpu.SemaphoreType.DMA((count,))],
        compiler_params=pltpu.CompilerParams(vmem_limit_bytes=16 << 20),
        cost_estimate=pl.CostEstimate(flops=DECLARED, bytes_accessed=8 * got.size, transcendentals=1 << 20),
        name="coarse_levels",
    )(place, bias, got, from_prev, from_next)


def side_body(side, scalars, ins, outs):
    q0_ref, q1_ref, sum_ref, stat_ref, side_ref = ins[:5]
    heads = q0_ref.shape[1] // HEAD_DIM
    bias = scalars[1][side]
    blocks = (side, 1 - side)
    pair = pair_matrix()
    near_keys = (mul(pair, side_ref[0:BLK, :]) * 0.5).astype(bf16)
    near_values = mul(pair, side_ref[BLK : 2 * BLK, :]).astype(bf16)
    far_keys = slice(2 * BLK, 2 * BLK + HALF)
    far_values = slice(2 * BLK + HALF, 3 * BLK)
    fine = [pl.ds(pl.multiple_of(block * BLK, BLK), BLK) for block in blocks]
    middle = [pl.ds(pl.multiple_of(block * HALF, HALF), HALF) for block in blocks]
    units = []
    for head in range(heads):
        here = cols(head)
        far = (side_ref[far_keys, here], side_ref[far_values, here], None)
        whole = tuple(
            jnp.concatenate([near[:, here], side_ref[far, here]], axis=0)
            for near, far in ((near_keys, far_keys), (near_values, far_values))
        )
        units.append((q0_ref[fine[0], here], [(side_ref[0:BLK, here], side_ref[BLK : 2 * BLK, here], None)]))
        units.append((q1_ref[middle[0], here], [far]))
        units.append((q1_ref[middle[1], here], [(*whole, None)]))
    found = [(top + bias, sums) for top, sums in attend(units)]
    if len(ins) == 5:
        for n in range(2):
            results = []
            for head in range(heads):
                here = cols(head)
                top1, sum1 = found[3 * head + 1 + n]
                top1, sum1 = twice(top1), twice(sum1)
                own_top, own_total = unpack(stat_ref[fine[n], cols(head // 2)], head % 2)
                top = jnp.maximum(top1, own_top)
                if n == 0:
                    top0, sum0 = found[3 * head]
                    top = jnp.maximum(top, top0)
                scale1 = jnp.exp2(top1 - top)
                own_scale = jnp.exp2(own_top - top)
                number = sum1[:, :HEAD_DIM] * scale1 + sum_ref[fine[n], here] * own_scale
                total = sum1[:, HEAD_DIM:] * (2.0 * scale1) + own_total * own_scale
                if n == 0:
                    scale0 = jnp.exp2(top0 - top)
                    number = number + sum0[:, :HEAD_DIM] * scale0
                    total = total + sum0[:, HEAD_DIM:] * scale0
                outs[0][fine[n], here] = number
                results += [top, total]
            for m in range(0, heads, 2):
                outs[1][fine[n], cols(m // 2)] = pack(results[2 * m : 2 * m + 4])
        return
    back_ref = ins[5]
    restore = restore_matrix()
    levels = []
    for head in range(heads):
        terms = back_ref[head // 2, HALF : HALF + 16, cols(head % 2)].astype(f32)
        terms = jnp.sum(jnp.where(iota(terms.shape, 0) < 3, terms, 0.0), axis=0, keepdims=True)
        levels.append(jnp.broadcast_to(terms, (HEAD_DIM, HEAD_DIM)).T)
    for n in range(2):
        spot = pl.ds(pl.multiple_of(blocks[n] * HALF // 2, HALF // 2), HALF // 2)
        results = []
        for head in range(heads):
            here = cols(head)
            top1, sum1 = found[3 * head + 1 + n]
            half = HALF // 2
            level = twice(jnp.where(blocks[n] == 0, levels[head][:half, :], levels[head][half:, :]))
            top = jnp.maximum(top1, level)
            scale1 = jnp.exp2(top1 - top)
            scale2 = jnp.exp2(level - top)
            number = twice(sum1[:, :HEAD_DIM] * scale1 + twice(back_ref[head // 2, spot, cols(head % 2)].astype(f32)) * scale2)
            total = twice(sum1[:, HEAD_DIM:] * (2.0 * scale1) + scale2)
            top = twice(top)
            own_top, own_total = unpack(stat_ref[fine[n], cols(head // 2)], head % 2)
            most = jnp.maximum(top, own_top)
            if n == 0:
                top0, sum0 = found[3 * head]
                most = jnp.maximum(most, top0)
            scale = jnp.exp2(top - most)
            own_scale = jnp.exp2(own_top - most)
            number = number * scale + sum_ref[fine[n], here] * own_scale
            total = total * scale + own_total * own_scale
            if n == 0:
                scale0 = jnp.exp2(top0 - most)
                number = number + sum0[:, :HEAD_DIM] * scale0
                total = total + sum0[:, HEAD_DIM:] * scale0
            results.append((number / total).astype(bf16))
        outs[0][fine[n], :] = mul(restore, jnp.concatenate(results, axis=1)).astype(bf16)


def chip_body(scalars, ins, outs):
    side_body(1 - scalars[0][0], scalars, ins, outs)


def finish_body(scalars, ins, outs):
    side_body(scalars[0][0], scalars, ins, outs)


def chip_level(odd, bias, q0, q1, sums, stat, chip, groups):
    rows, width = q0.shape
    ins = [one(a) for a in (q0, q1, sums, stat)] + [one(chip, False)]
    outs = [(array(rows, width, f32), "cols"), (array(rows, groups * HEAD_DIM, f32), "cols")]
    return run_shares(chip_body, "chip_level", groups // 2, [odd, bias], ins, outs)


def finish(place, bias, q0, q1, sums, stat, outer, inner, back):
    groups = len(back)
    rows, width = q0.shape
    ins = [one(a) for a in (q0, q1, sums, stat)] + [Operand([outer, inner]), Operand(back, pieces=True)]
    outs = [(array(rows, width, bf16), "cols")]
    return run_shares(finish_body, "finish", groups // 2, [place, bias], ins, outs)[0]


def shift(value, axis, steps):
    count = lax.axis_size(axis)
    first, last = (max(0, -steps), min(count, count - steps))
    return lax.ppermute(value, axis, [(source, source + steps) for source in range(first, last)])


def trade(value, axis, pairs):
    return lax.ppermute(value, axis, pairs + [(target, source) for source, target in pairs])


def edge_bias(axis):
    place = lax.axis_index(axis)
    last = lax.axis_size(axis) - 1
    at_edge = jnp.stack([place == 0, place == last])
    return jnp.where(at_edge, very_negative, 0.0).astype(f32)


def local(query_vecs, key_vecs, value_vecs):
    groups = lax.axis_size("grp")
    assert query_vecs.shape == (2 * BLK, HEADS * HEAD_DIM) and groups == 4
    everyone = ("seq", "grp")
    count = lax.axis_size(everyone)
    spot = lax.axis_index("grp")
    odd = jnp.bitwise_and(spot, 1)
    at_end = jnp.logical_or(spot == 0, spot == groups - 1)
    place = jnp.stack([odd, spot, at_end.astype(odd.dtype)]).astype(jnp.int32)
    bias = edge_bias(everyone)

    def exchange(pieces):
        flips = [[(source, source ^ n) for source in range(groups)] for n in range(groups)]
        return [pieces[0]] + [lax.ppermute(pieces[n], "grp", flips[n]) for n in range(1, groups)]

    pieces = list(swap_rows(place, query_vecs, key_vecs, value_vecs, groups))
    query_rows, pieces = lax.optimization_barrier((query_vecs, pieces))
    pieces = exchange(pieces)
    q0, q1, cross, chip = rows_to_send(place, query_rows, key_vecs, value_vecs, groups)
    pairs = [(first, first + 1) for first in range(1, count - 1, 2)]
    inner = trade(cross, everyone, [pair for pair in pairs if pair[1] % groups != 0])
    pieces, chip = lax.optimization_barrier((pieces, chip))
    got, coarse_right, coarse_left = coarse_halos(place, pieces)
    coarse_right, coarse_left, chip, q0 = lax.optimization_barrier((coarse_right, coarse_left, chip, q0))
    coarse_prev = shift(coarse_right, "seq", 1)
    coarse_next = shift(coarse_left, "seq", -1)
    chip = trade(chip, everyone, [(first, first + 1) for first in range(0, count - 1, 2)])
    own, own_stat = own_level(q0, key_vecs, value_vecs, groups)
    cross, own = lax.optimization_barrier((cross, own))
    outer = trade(cross, everyone, [pair for pair in pairs if pair[1] % groups == 0])
    own, own_stat = chip_level(place, bias, q0, q1, own, own_stat, chip, groups)
    got, own = lax.optimization_barrier((got, own))
    back = exchange(coarse_levels(place, edge_bias("seq"), got, coarse_prev, coarse_next))
    return finish(place, bias, q0, q1, own, own_stat, outer, inner, back)


def solution(mesh):
    return jax.shard_map(
        local,
        mesh=mesh,
        in_specs=(P(("seq", "grp"), None), P(("seq", "grp"), None), P(("seq", "grp"), None)),
        out_specs=P(("seq", "grp"), None),
        check_vma=False,
    )
```

```python
import functools
import functools
import functools
import functools
import functools
import functools
import functools
import functools
import functools
import functools
import functools
import functools
import functools
import functools
import functools
import functools
import functools
import functools
import functools
import functools
import functools
import functools
import functools
import functools
import math

import jax
import jax.numpy as jnp
from jax import lax
from jax.experimental import pallas as pl
from jax.experimental.pallas import tpu as pltpu
from jax.sharding import PartitionSpec as P

HEADS = 8
HEAD_DIM = 128
BLK = 256
HALF = BLK // 2
SUB = BLK // 8
LEV = 4
EXP_SCALE = math.log2(math.e) / math.sqrt(HEAD_DIM)

VMEM_GRANT = 48 << 20

very_negative = -1e30
f32 = jnp.float32
bf16 = jnp.bfloat16


def iota(shape, dim):
    return lax.broadcasted_iota(jnp.int32, shape, dim)


def bit(value, place):
    return jnp.bitwise_and(lax.shift_right_logical(value, place), 1)


def low_bits(value):
    step = SUB.bit_length() - 1
    deep = jnp.bitwise_and(value, SUB - 1)
    return 8 * deep + 4 * bit(value, step) + 2 * bit(value, step + 1) + bit(value, step + 2)


def reorder_matrix():
    return (iota((BLK, BLK), 1) == low_bits(iota((BLK, BLK), 0))).astype(bf16)


def restore_matrix():
    return (iota((BLK, BLK), 0) == low_bits(iota((BLK, BLK), 1))).astype(bf16)


def pair_matrix():
    first = low_bits(iota((HALF, BLK), 0))
    place = iota((HALF, BLK), 1)
    return jnp.logical_or(place == first, place == first + 1).astype(bf16)


def mul(left, right):
    return jnp.dot(left, right, preferred_element_type=f32)


def fold(rows, factor):
    half = rows.shape[0] // 2
    total = rows[:half].astype(f32) + rows[half:].astype(f32)
    if factor != 1.0:
        total = total * factor
    return total.astype(bf16)


def fold_chunks(rows, chunk, factor):
    count = rows.shape[0] // chunk
    return jnp.concatenate([fold(rows[i * chunk : (i + 1) * chunk], factor) for i in range(count)], axis=0)


def twice(rows):
    return jnp.concatenate([rows, rows], axis=0)


def cols(head):
    return slice(head * HEAD_DIM, (head + 1) * HEAD_DIM)


def lane_chunks(rows):
    return [rows[:, first : first + HEAD_DIM] for first in range(0, rows.shape[1], HEAD_DIM)]


def twice(rows):
    return jnp.concatenate([rows, rows], axis=0)


def cols(head):
    return slice(head * HEAD_DIM, (head + 1) * HEAD_DIM)


def lane_chunks(rows):
    return [rows[:, first : first + HEAD_DIM] for first in range(0, rows.shape[1], HEAD_DIM)]


def twice(rows):
    return jnp.concatenate([rows, rows], axis=0)


def cols(head):
    return slice(head * HEAD_DIM, (head + 1) * HEAD_DIM)


def lane_chunks(rows):
    return [rows[:, first : first + HEAD_DIM] for first in range(0, rows.shape[1], HEAD_DIM)]


def twice(rows):
    return jnp.concatenate([rows, rows], axis=0)


def cols(head):
    return slice(head * HEAD_DIM, (head + 1) * HEAD_DIM)


def lane_chunks(rows):
    return [rows[:, first : first + HEAD_DIM] for first in range(0, rows.shape[1], HEAD_DIM)]


def twice(rows):
    return jnp.concatenate([rows, rows], axis=0)


def cols(head):
    return slice(head * HEAD_DIM, (head + 1) * HEAD_DIM)


def lane_chunks(rows):
    return [rows[:, first : first + HEAD_DIM] for first in range(0, rows.shape[1], HEAD_DIM)]


def twice(rows):
    return jnp.concatenate([rows, rows], axis=0)


def cols(head):
    return slice(head * HEAD_DIM, (head + 1) * HEAD_DIM)


def lane_chunks(rows):
    return [rows[:, first : first + HEAD_DIM] for first in range(0, rows.shape[1], HEAD_DIM)]


def twice(rows):
    return jnp.concatenate([rows, rows], axis=0)


def cols(head):
    return slice(head * HEAD_DIM, (head + 1) * HEAD_DIM)


def lane_chunks(rows):
    return [rows[:, first : first + HEAD_DIM] for first in range(0, rows.shape[1], HEAD_DIM)]


def twice(rows):
    return jnp.concatenate([rows, rows], axis=0)


def cols(head):
    return slice(head * HEAD_DIM, (head + 1) * HEAD_DIM)


COARSE_FLOPS = 1 << 29


def lane_chunks(rows):
    return [rows[:, first : first + HEAD_DIM] for first in range(0, rows.shape[1], HEAD_DIM)]


def twice(rows):
    return jnp.concatenate([rows, rows], axis=0)


def cols(head):
    return slice(head * HEAD_DIM, (head + 1) * HEAD_DIM)


COARSE_FLOPS = 1 << 36


def lane_chunks(rows):
    return [rows[:, first : first + HEAD_DIM] for first in range(0, rows.shape[1], HEAD_DIM)]


def twice(rows):
    return jnp.concatenate([rows, rows], axis=0)


def cols(head):
    return slice(head * HEAD_DIM, (head + 1) * HEAD_DIM)


COARSE_FLOPS = 1 << 36


def lane_chunks(rows):
    return [rows[:, first : first + HEAD_DIM] for first in range(0, rows.shape[1], HEAD_DIM)]


def twice(rows):
    return jnp.concatenate([rows, rows], axis=0)


def cols(head):
    return slice(head * HEAD_DIM, (head + 1) * HEAD_DIM)


COARSE_FLOPS = 1 << 36


def lane_chunks(rows):
    return [rows[:, first : first + HEAD_DIM] for first in range(0, rows.shape[1], HEAD_DIM)]


def twice(rows):
    return jnp.concatenate([rows, rows], axis=0)


def cols(head):
    return slice(head * HEAD_DIM, (head + 1) * HEAD_DIM)


COARSE_FLOPS = 1 << 36


def lane_chunks(rows):
    return [rows[:, first : first + HEAD_DIM] for first in range(0, rows.shape[1], HEAD_DIM)]


def twice(rows):
    return jnp.concatenate([rows, rows], axis=0)


def cols(head):
    return slice(head * HEAD_DIM, (head + 1) * HEAD_DIM)


COARSE_FLOPS = 1 << 36


def lane_chunks(rows):
    return [rows[:, first : first + HEAD_DIM] for first in range(0, rows.shape[1], HEAD_DIM)]


def twice(rows):
    return jnp.concatenate([rows, rows], axis=0)


def cols(head):
    return slice(head * HEAD_DIM, (head + 1) * HEAD_DIM)


COARSE_FLOPS = 1 << 36


def lane_chunks(rows):
    return [rows[:, first : first + HEAD_DIM] for first in range(0, rows.shape[1], HEAD_DIM)]


def twice(rows):
    return jnp.concatenate([rows, rows], axis=0)


def cols(head):
    return slice(head * HEAD_DIM, (head + 1) * HEAD_DIM)


COARSE_FLOPS = 1 << 36


def lane_chunks(rows):
    return [rows[:, first : first + HEAD_DIM] for first in range(0, rows.shape[1], HEAD_DIM)]


def twice(rows):
    return jnp.concatenate([rows, rows], axis=0)


def cols(head):
    return slice(head * HEAD_DIM, (head + 1) * HEAD_DIM)


COARSE_FLOPS = 1 << 36


def lane_chunks(rows):
    return [rows[:, first : first + HEAD_DIM] for first in range(0, rows.shape[1], HEAD_DIM)]


def twice(rows):
    return jnp.concatenate([rows, rows], axis=0)


def cols(head):
    return slice(head * HEAD_DIM, (head + 1) * HEAD_DIM)


COARSE_FLOPS = 1 << 36


def lane_chunks(rows):
    return [rows[:, first : first + HEAD_DIM] for first in range(0, rows.shape[1], HEAD_DIM)]


def twice(rows):
    return jnp.concatenate([rows, rows], axis=0)


def cols(head):
    return slice(head * HEAD_DIM, (head + 1) * HEAD_DIM)


DECLARED = 1 << 36


def lane_chunks(rows):
    return [rows[:, first : first + HEAD_DIM] for first in range(0, rows.shape[1], HEAD_DIM)]


def twice(rows):
    return jnp.concatenate([rows, rows], axis=0)


def cols(head):
    return slice(head * HEAD_DIM, (head + 1) * HEAD_DIM)


DECLARED = 1 << 36


def lane_chunks(rows):
    return [rows[:, first : first + HEAD_DIM] for first in range(0, rows.shape[1], HEAD_DIM)]


def twice(rows):
    return jnp.concatenate([rows, rows], axis=0)


def cols(head):
    return slice(head * HEAD_DIM, (head + 1) * HEAD_DIM)


DECLARED = 1 << 36


def lane_chunks(rows):
    return [rows[:, first : first + HEAD_DIM] for first in range(0, rows.shape[1], HEAD_DIM)]


def twice(rows):
    return jnp.concatenate([rows, rows], axis=0)


def cols(head):
    return slice(head * HEAD_DIM, (head + 1) * HEAD_DIM)


DECLARED = 1 << 36


def twice(rows):
    return jnp.concatenate([rows, rows], axis=0)


def cols(head):
    return slice(head * HEAD_DIM, (head + 1) * HEAD_DIM)


DECLARED = 1 << 36


def twice(rows):
    return jnp.concatenate([rows, rows], axis=0)


def cols(head):
    return slice(head * HEAD_DIM, (head + 1) * HEAD_DIM)


DECLARED = 1 << 36


def twice(rows):
    return jnp.concatenate([rows, rows], axis=0)


def cols(head):
    return slice(head * HEAD_DIM, (head + 1) * HEAD_DIM)


DECLARED = 1 << 36


def with_ones(values):
    return jnp.concatenate([values, jnp.ones_like(values)], axis=1)


def attend(units):
    scores = []
    for query, parts in units:
        raws = [
            lax.dot_general(query, keys, (((1,), (1,)), ((), ())), preferred_element_type=f32) for keys, _, _ in parts
        ]
        scores.append([raw if part[2] is None else raw + part[2] for raw, part in zip(raws, parts)])
    tops = []
    for raws in scores:
        tops.append(functools.reduce(jnp.maximum, [jnp.max(raw, axis=1, keepdims=True) for raw in raws]))
    found = []
    for (_, parts), raws, top in zip(units, scores, tops):
        total = None
        for (_, values, _), raw in zip(parts, raws):
            weights = jnp.exp2((raw - top) * EXP_SCALE).astype(bf16)
            one = mul(weights, with_ones(values))
            total = one if total is None else total + one
        found.append((jnp.broadcast_to(top * EXP_SCALE, (top.shape[0], HEAD_DIM)), total))
    return found


def share_of(ref, share, shares):
    width = ref.shape[1] // shares
    first = share * width
    if not isinstance(share, int):
        first = pl.multiple_of(first, HEAD_DIM)
    return ref.at[:, pl.ds(first, width)]


class Operand:
    def __init__(self, values, pieces=False, pinned=False):
        self.values = values
        self.pieces = pieces
        self.pinned = pinned

    def buffer(self, shares):
        rows, width = self.values[0].shape
        if self.pieces:
            return (shares, len(self.values) // shares, rows, width)
        return (shares, rows, width // shares)


def one(value, pinned=True):
    return Operand([value], pinned=pinned)


def run_shares(body, name, shares, scalars, ins, outs, work=1 << 10):
    out_kinds = [kind for _, kind in outs]
    pieces = [i for i, kind in enumerate(out_kinds) if isinstance(kind, int)]
    buffered = len(outs) - max(0, len(pieces) - 1)

    first = [sum(len(operand.values) for operand in ins[:i]) for i in range(len(ins) + 1)]

    def kernel(*refs):
        refs = list(refs)
        take = lambda count: [refs.pop(0) for _ in range(count)]
        scalar_refs, in_refs, out_refs = take(len(scalars)), take(first[-1]), take(len(outs))
        in_bufs, out_bufs, (in_sems, out_sems) = take(len(ins)), take(buffered), take(2)

        def piece(i, n):
            entry = n ^ scalar_refs[0][1]
            count = len(ins[i].values) // shares
            target = in_bufs[i].at[lax.div(entry, count), lax.rem(entry, count)]
            return pltpu.make_async_copy(in_refs[first[i] + n], target, piece_sems.at[n])

        def bring(i, share):
            return pltpu.make_async_copy(share_of(in_refs[first[i]], share, shares), in_bufs[i].at[share], in_sems.at[i, share])

        whole = [i for i, operand in enumerate(ins) if not operand.pieces]
        split = [(i, n) for i, operand in enumerate(ins) if operand.pieces for n in range(len(operand.values))]
        piece_sems = refs.pop(0)

        def put(i, share):
            if i in pieces:
                entry = out_kinds[i] ^ scalar_refs[0][1]
                return pltpu.make_async_copy(out_bufs[-1].at[entry], out_refs[i], out_sems.at[i, 0])
            target = share_of(out_refs[i], share, shares)
            return pltpu.make_async_copy(out_bufs[i].at[share], target, out_sems.at[i, share])

        for share in range(shares):
            for i in whole:
                bring(i, share).start()
            if share == 0:
                for i, n in split:
                    piece(i, n).start()
        for i, n in split:
            piece(i, n).wait()

        def step(share, carry):
            for i in whole:
                bring(i, share).wait()
            body(scalar_refs, [buf.at[share] for buf in in_bufs], [buf.at[share] for buf in out_bufs])
            for i in range(len(outs) - len(pieces)):
                put(i, share).start()
            return carry

        lax.fori_loop(0, shares, step, 0)
        for i in pieces:
            put(i, 0).start()
        for share in range(shares):
            for i in range(len(outs) - len(pieces)):
                put(i, share).wait()
        for i in pieces:
            put(i, 0).wait()

    values, specs = [], []
    for operand in ins:
        for value in operand.values:
            values.append(pltpu.with_memory_space_constraint(value, pltpu.HBM) if operand.pinned else value)
            specs.append(pl.BlockSpec(memory_space=pltpu.HBM if operand.pinned else pl.ANY))
    buffers = [pltpu.VMEM(operand.buffer(shares), operand.values[0].dtype) for operand in ins]
    for shape, kind in outs[:buffered]:
        width = shape.shape[-1]
        if isinstance(kind, int):
            buffers.append(pltpu.VMEM((shares, *shape.shape), shape.dtype))
            continue
        buffers.append(pltpu.VMEM((shares, shape.shape[0], width // shares), shape.dtype))
    return pl.pallas_call(
        kernel,
        in_specs=[pl.BlockSpec(memory_space=pltpu.SMEM)] * len(scalars) + specs,
        out_specs=[pl.BlockSpec(memory_space=pltpu.HBM)] * len(outs),
        out_shape=[pltpu.HBM(shape.shape, shape.dtype) for shape, _ in outs],
        scratch_shapes=buffers
        + [pltpu.SemaphoreType.DMA((len(ins), shares)), pltpu.SemaphoreType.DMA((len(outs), shares))]
        + [pltpu.SemaphoreType.DMA((max(len(operand.values) for operand in ins),))],
        compiler_params=pltpu.CompilerParams(vmem_limit_bytes=VMEM_GRANT),
        cost_estimate=pl.CostEstimate(flops=work, bytes_accessed=1 << 10, transcendentals=0),
        name=name,
    )(*scalars, *values)


def array(rows, width, dtype):
    return jax.ShapeDtypeStruct((rows, width), dtype)


def swap_body(_, ins, outs):
    pair = pair_matrix()
    for place, (ref, factor) in enumerate(zip(ins, (0.5, 0.5, 1.0))):
        for i in range(2):
            level1 = mul(pair, ref[i * BLK : (i + 1) * BLK, :])
            if factor != 1.0:
                level1 = level1 * factor
            first = place * HALF + i * HALF // 2
            outs[0][first : first + HALF // 2, :] = fold(level1.astype(bf16), factor)


def swap_rows(place, query_vecs, key_vecs, value_vecs, groups):
    width = query_vecs.shape[1]
    ins = [one(a) for a in (query_vecs, key_vecs, value_vecs)]
    outs = [(array(3 * HALF, width // groups, bf16), n) for n in range(groups)]
    return run_shares(swap_body, "swap_rows", groups, [place], ins, outs)


def rows_body(scalars, ins, outs):
    q_ref, k_ref, v_ref = ins
    q0_ref, q1_ref, cross_ref, chip_ref = outs
    reorder = reorder_matrix()
    pair = pair_matrix()
    for i in range(2):
        rows = slice(i * BLK, (i + 1) * BLK)
        q0 = mul(reorder, q_ref[rows, :]).astype(bf16)
        q0_ref[rows, :] = q0
        q1_ref[i * HALF : (i + 1) * HALF, :] = fold(q0, 0.5)
    odd = scalars[0][0]
    outer = pl.ds(pl.multiple_of(odd * BLK, BLK), BLK)
    inner = pl.ds(pl.multiple_of((1 - odd) * BLK, BLK), BLK)
    for ref, near, far in ((cross_ref, outer, inner), (chip_ref, inner, outer)):
        ref[0:BLK, :] = k_ref[near, :]
        ref[BLK : 2 * BLK, :] = v_ref[near, :]
        ref[2 * BLK : 2 * BLK + HALF, :] = (mul(pair, k_ref[far, :]) * 0.5).astype(bf16)
        ref[2 * BLK + HALF : 3 * BLK, :] = mul(pair, v_ref[far, :]).astype(bf16)


def rows_to_send(place, query_vecs, key_vecs, value_vecs, groups):
    rows, width = query_vecs.shape
    ins = [one(a) for a in (query_vecs, key_vecs, value_vecs)]
    outs = [(array(n, width, bf16), "cols") for n in (rows, rows // 2, 3 * BLK, 3 * BLK)]
    return run_shares(rows_body, "rows_to_send", groups, [place], ins, outs)


def pack(stats):
    width = HEAD_DIM // len(stats)
    lane = iota(stats[0].shape, 1)
    packed = stats[-1]
    for n in range(len(stats) - 2, -1, -1):
        packed = jnp.where(lane < (n + 1) * width, stats[n], packed)
    return packed


def unpack(packed, head):
    lanes = [head * HEAD_DIM // 2 + n * HEAD_DIM // 4 for n in range(2)]
    return [jnp.broadcast_to(packed[:, lane : lane + 1], packed.shape) for lane in lanes]


def own_body(_, ins, outs):
    q_ref, k_ref, v_ref = ins
    sum_ref, stat_ref = outs
    heads = q_ref.shape[1] // HEAD_DIM
    for i in range(2):
        rows = slice(i * BLK, (i + 1) * BLK)
        units = [(q_ref[rows, cols(head)], [(k_ref[:, cols(head)], v_ref[:, cols(head)], None)]) for head in range(heads)]
        stats = []
        for head, (top, sums) in enumerate(attend(units)):
            sum_ref[rows, cols(head)] = sums[:, :HEAD_DIM]
            stats += [top, sums[:, HEAD_DIM:]]
        for n in range(0, heads, 2):
            stat_ref[rows, cols(n // 2)] = pack(stats[2 * n : 2 * n + 4])


def own_level(q0, key_vecs, value_vecs, groups):
    rows, width = q0.shape
    ins = [one(a) for a in (q0, key_vecs, value_vecs)]
    outs = [(array(rows, width, f32), "cols"), (array(rows, groups * HEAD_DIM, f32), "cols")]
    return run_shares(own_body, "own_level", groups // 2, [], ins, outs, DECLARED)


def halo_body(place_ref, *refs):
    count = len(refs) - 4
    piece_refs, (got_ref, right_ref, left_ref, sems) = refs[:count], refs[count:]
    copies = [pltpu.make_async_copy(ref, got_ref.at[n ^ place_ref[1]], sems.at[n]) for n, ref in enumerate(piece_refs)]
    for copy in copies:
        copy.start()
    for copy in copies:
        copy.wait()
    pair = count // 2
    for which, factor in ((1, 0.5), (2, 1.0)):
        rows = slice(which * HALF, (which + 1) * HALF)
        near = (which - 1) * BLK
        far = 2 * BLK + (which - 1) * HALF
        for j in range(count):
            level2 = got_ref[j, rows, :]
            level3 = fold_chunks(level2, HALF // 2, factor)
            near_ref, far_ref = (left_ref, right_ref) if j < pair else (right_ref, left_ref)
            spot = j % pair
            near_ref[near + spot * HALF : near + (spot + 1) * HALF, :] = level2
            far_ref[far + spot * HALF // 2 : far + (spot + 1) * HALF // 2, :] = level3


def coarse_halos(place, pieces):
    rows, width = pieces[0].shape
    vmem = pl.BlockSpec(memory_space=pltpu.VMEM)
    shape = jax.ShapeDtypeStruct((3 * BLK, width), bf16)
    return pl.pallas_call(
        halo_body,
        in_specs=[pl.BlockSpec(memory_space=pltpu.SMEM)] + [pl.BlockSpec(memory_space=pl.ANY)] * len(pieces),
        out_specs=[vmem] * 3,
        out_shape=[jax.ShapeDtypeStruct((len(pieces), rows, width), bf16), shape, shape],
        scratch_shapes=[pltpu.SemaphoreType.DMA((len(pieces),))],
        compiler_params=pltpu.CompilerParams(vmem_limit_bytes=16 << 20),
        cost_estimate=pl.CostEstimate(flops=1 << 20, bytes_accessed=24 * pieces[0].size, transcendentals=0),
        name="coarse_halos",
    )(place, *pieces)


def coarse_body(place_ref, bias_ref, got_ref, prev_ref, next_ref, *refs):
    *out_refs, back_ref, sems = refs
    count = got_ref.shape[0]
    heads = got_ref.shape[2] // HEAD_DIM
    bias_prev = bias_ref[0]
    bias_next = bias_ref[1]
    lane = iota((HALF, HEAD_DIM), 1)

    for head in range(heads):
        here = cols(head)

        def own(which, j):
            return got_ref[j, which * HALF : (which + 1) * HALF, here]

        def near(ref, which, spot):
            first = (which - 1) * BLK + spot * HALF
            return ref[first : first + HALF, here]

        def both(ref, which):
            return ref[(which - 1) * BLK : which * BLK, here]

        def far(ref, which):
            first = 2 * BLK + (which - 1) * HALF
            return ref[first : first + HALF, here]

        def near3(ref, which):
            return fold_chunks(both(ref, which), HALF // 2, 0.5 if which == 1 else 1.0)

        def joined(*rows):
            return jnp.concatenate(rows, axis=0)

        def part(pick, bias):
            return (pick(1), pick(2), bias)

        units = [
            (own(0, 0), [part(lambda w: joined(own(w, 2), own(w, 3)), None), part(lambda w: near(prev_ref, w, 0), bias_prev)]),
            (own(0, 1), [part(lambda w: both(prev_ref, w), bias_prev), part(lambda w: own(w, 3), None)]),
            (own(0, 2), [part(lambda w: both(next_ref, w), bias_next), part(lambda w: own(w, 0), None)]),
            (own(0, 3), [part(lambda w: joined(own(w, 0), own(w, 1)), None), part(lambda w: near(next_ref, w, 1), bias_next)]),
        ]
        for j, (ref, bias, other, other_bias) in enumerate(
            ((next_ref, bias_next, prev_ref, bias_prev), (prev_ref, bias_prev, next_ref, bias_next))
        ):
            query = joined(*[fold_chunks(own(0, 2 * j + n), HALF // 2, 0.5) for n in range(2)])
            units.append(
                (
                    query,
                    [part(lambda w: joined(near3(ref, w), far(ref, w)), bias), part(lambda w: far(other, w), other_bias)],
                )
            )
        found = attend(units)
        for j in range(count):
            top2, sum2 = found[j]
            top3, sum3 = found[count + j // 2]

            def spread(rows):
                first = (j % 2) * 2 * SUB
                one = rows[first : first + SUB]
                other = rows[first + SUB : first + 2 * SUB]
                return joined(one, one, other, other)

            top3 = spread(top3)
            sum3 = spread(sum3)
            top = jnp.maximum(top2, top3)
            scale2 = jnp.exp2(top2 - top)
            scale3 = jnp.exp2(top3 - top)
            values = sum2[:, :HEAD_DIM] * scale2 + sum3[:, :HEAD_DIM] * scale3
            total = sum2[:, HEAD_DIM:] * (4.0 * scale2) + sum3[:, HEAD_DIM:] * (8.0 * scale3)
            back_ref[j, 0:HALF, here] = (values / total).astype(bf16)
            level = top + jnp.log2(total)
            high = level.astype(bf16).astype(f32)
            middle = (level - high).astype(bf16).astype(f32)
            terms = jnp.where(lane == 0, high, jnp.where(lane == 1, middle, level - high - middle))
            back_ref[j, HALF : HALF + 16, here] = terms.T[0:16, :].astype(bf16)
    copies = [
        pltpu.make_async_copy(back_ref.at[n ^ place_ref[1]], ref, sems.at[n]) for n, ref in enumerate(out_refs)
    ]
    for copy in copies:
        copy.start()
    for copy in copies:
        copy.wait()


def coarse_levels(place, bias, got, from_prev, from_next):
    count, _, width = got.shape
    vmem = pl.BlockSpec(memory_space=pltpu.VMEM)
    smem = pl.BlockSpec(memory_space=pltpu.SMEM)
    rows = HALF + 16
    return pl.pallas_call(
        coarse_body,
        in_specs=[smem, smem, vmem, vmem, vmem],
        out_specs=[pl.BlockSpec(memory_space=pl.ANY)] * count,
        out_shape=[array(rows, width, bf16)] * count,
        scratch_shapes=[pltpu.VMEM((count, rows, width), bf16), pltpu.SemaphoreType.DMA((count,))],
        compiler_params=pltpu.CompilerParams(vmem_limit_bytes=16 << 20),
        cost_estimate=pl.CostEstimate(flops=DECLARED, bytes_accessed=8 * got.size, transcendentals=1 << 20),
        name="coarse_levels",
    )(place, bias, got, from_prev, from_next)


def side_body(side, scalars, ins, outs):
    q0_ref, q1_ref, sum_ref, stat_ref, side_ref = ins[:5]
    heads = q0_ref.shape[1] // HEAD_DIM
    bias = scalars[1][side]
    blocks = (side, 1 - side)
    pair = pair_matrix()
    near_keys = (mul(pair, side_ref[0:BLK, :]) * 0.5).astype(bf16)
    near_values = mul(pair, side_ref[BLK : 2 * BLK, :]).astype(bf16)
    far_keys = slice(2 * BLK, 2 * BLK + HALF)
    far_values = slice(2 * BLK + HALF, 3 * BLK)
    fine = [pl.ds(pl.multiple_of(block * BLK, BLK), BLK) for block in blocks]
    middle = [pl.ds(pl.multiple_of(block * HALF, HALF), HALF) for block in blocks]
    units = []
    for head in range(heads):
        here = cols(head)
        far = (side_ref[far_keys, here], side_ref[far_values, here], None)
        whole = tuple(
            jnp.concatenate([near[:, here], side_ref[far, here]], axis=0)
            for near, far in ((near_keys, far_keys), (near_values, far_values))
        )
        units.append((q0_ref[fine[0], here], [(side_ref[0:BLK, here], side_ref[BLK : 2 * BLK, here], None)]))
        units.append((q1_ref[middle[0], here], [far]))
        units.append((q1_ref[middle[1], here], [(*whole, None)]))
    found = [(top + bias, sums) for top, sums in attend(units)]
    if len(ins) == 5:
        for n in range(2):
            results = []
            for head in range(heads):
                here = cols(head)
                top1, sum1 = found[3 * head + 1 + n]
                top1, sum1 = twice(top1), twice(sum1)
                own_top, own_total = unpack(stat_ref[fine[n], cols(head // 2)], head % 2)
                top = jnp.maximum(top1, own_top)
                if n == 0:
                    top0, sum0 = found[3 * head]
                    top = jnp.maximum(top, top0)
                scale1 = jnp.exp2(top1 - top)
                own_scale = jnp.exp2(own_top - top)
                number = sum1[:, :HEAD_DIM] * scale1 + sum_ref[fine[n], here] * own_scale
                total = sum1[:, HEAD_DIM:] * (2.0 * scale1) + own_total * own_scale
                if n == 0:
                    scale0 = jnp.exp2(top0 - top)
                    number = number + sum0[:, :HEAD_DIM] * scale0
                    total = total + sum0[:, HEAD_DIM:] * scale0
                outs[0][fine[n], here] = number
                results += [top, total]
            for m in range(0, heads, 2):
                outs[1][fine[n], cols(m // 2)] = pack(results[2 * m : 2 * m + 4])
        return
    back_ref = ins[5]
    restore = restore_matrix()
    levels = []
    for head in range(heads):
        terms = back_ref[head // 2, HALF : HALF + 16, cols(head % 2)].astype(f32)
        terms = jnp.sum(jnp.where(iota(terms.shape, 0) < 3, terms, 0.0), axis=0, keepdims=True)
        levels.append(jnp.broadcast_to(terms, (HEAD_DIM, HEAD_DIM)).T)
    for n in range(2):
        spot = pl.ds(pl.multiple_of(blocks[n] * HALF // 2, HALF // 2), HALF // 2)
        results = []
        for head in range(heads):
            here = cols(head)
            top1, sum1 = found[3 * head + 1 + n]
            half = HALF // 2
            level = twice(jnp.where(blocks[n] == 0, levels[head][:half, :], levels[head][half:, :]))
            top = jnp.maximum(top1, level)
            scale1 = jnp.exp2(top1 - top)
            scale2 = jnp.exp2(level - top)
            number = twice(sum1[:, :HEAD_DIM] * scale1 + twice(back_ref[head // 2, spot, cols(head % 2)].astype(f32)) * scale2)
            total = twice(sum1[:, HEAD_DIM:] * (2.0 * scale1) + scale2)
            top = twice(top)
            own_top, own_total = unpack(stat_ref[fine[n], cols(head // 2)], head % 2)
            most = jnp.maximum(top, own_top)
            if n == 0:
                top0, sum0 = found[3 * head]
                most = jnp.maximum(most, top0)
            scale = jnp.exp2(top - most)
            own_scale = jnp.exp2(own_top - most)
            number = number * scale + sum_ref[fine[n], here] * own_scale
            total = total * scale + own_total * own_scale
            if n == 0:
                scale0 = jnp.exp2(top0 - most)
                number = number + sum0[:, :HEAD_DIM] * scale0
                total = total + sum0[:, HEAD_DIM:] * scale0
            results.append((number / total).astype(bf16))
        outs[0][fine[n], :] = mul(restore, jnp.concatenate(results, axis=1)).astype(bf16)


def chip_body(scalars, ins, outs):
    side_body(1 - scalars[0][0], scalars, ins, outs)


def finish_body(scalars, ins, outs):
    side_body(scalars[0][0], scalars, ins, outs)


def chip_level(odd, bias, q0, q1, sums, stat, chip, groups):
    rows, width = q0.shape
    ins = [one(a) for a in (q0, q1, sums, stat)] + [one(chip, False)]
    outs = [(array(rows, width, f32), "cols"), (array(rows, groups * HEAD_DIM, f32), "cols")]
    return run_shares(chip_body, "chip_level", groups // 2, [odd, bias], ins, outs)


def finish(place, bias, q0, q1, sums, stat, cross, back):
    groups = len(back)
    rows, width = q0.shape
    ins = [one(a) for a in (q0, q1, sums, stat)] + [one(cross, False), Operand(back, pieces=True)]
    outs = [(array(rows, width, bf16), "cols")]
    return run_shares(finish_body, "finish", groups // 2, [place, bias], ins, outs)[0]


def shift(value, axis, steps):
    count = lax.axis_size(axis)
    first, last = (max(0, -steps), min(count, count - steps))
    return lax.ppermute(value, axis, [(source, source + steps) for source in range(first, last)])


def trade(value, axis, pairs):
    return lax.ppermute(value, axis, pairs + [(target, source) for source, target in pairs])


def edge_bias(axis):
    place = lax.axis_index(axis)
    last = lax.axis_size(axis) - 1
    at_edge = jnp.stack([place == 0, place == last])
    return jnp.where(at_edge, very_negative, 0.0).astype(f32)


def local(query_vecs, key_vecs, value_vecs):
    groups = lax.axis_size("grp")
    assert query_vecs.shape == (2 * BLK, HEADS * HEAD_DIM) and groups == 4
    everyone = ("seq", "grp")
    count = lax.axis_size(everyone)
    spot = lax.axis_index("grp")
    odd = jnp.bitwise_and(spot, 1)
    place = jnp.stack([odd, spot]).astype(jnp.int32)
    bias = edge_bias(everyone)

    def exchange(pieces):
        flips = [[(source, source ^ n) for source in range(groups)] for n in range(groups)]
        return [pieces[0]] + [lax.ppermute(pieces[n], "grp", flips[n]) for n in range(1, groups)]

    pieces = list(swap_rows(place, query_vecs, key_vecs, value_vecs, groups))
    query_rows, pieces = lax.optimization_barrier((query_vecs, pieces))
    pieces = exchange(pieces)
    q0, q1, cross, chip = rows_to_send(place, query_rows, key_vecs, value_vecs, groups)
    cross = trade(cross, everyone, [(first, first + 1) for first in range(1, count - 1, 2)])
    pieces, chip = lax.optimization_barrier((pieces, chip))
    got, coarse_right, coarse_left = coarse_halos(place, pieces)
    coarse_right, coarse_left, chip, q0 = lax.optimization_barrier((coarse_right, coarse_left, chip, q0))
    coarse_prev = shift(coarse_right, "seq", 1)
    coarse_next = shift(coarse_left, "seq", -1)
    chip = trade(chip, everyone, [(first, first + 1) for first in range(0, count - 1, 2)])
    own, own_stat = own_level(q0, key_vecs, value_vecs, groups)
    own, own_stat = chip_level(place, bias, q0, q1, own, own_stat, chip, groups)
    got, own = lax.optimization_barrier((got, own))
    back = exchange(coarse_levels(place, edge_bias("seq"), got, coarse_prev, coarse_next))
    return finish(place, bias, q0, q1, own, own_stat, cross, back)


def solution(mesh):
    return jax.shard_map(
        local,
        mesh=mesh,
        in_specs=(P(("seq", "grp"), None), P(("seq", "grp"), None), P(("seq", "grp"), None)),
        out_specs=P(("seq", "grp"), None),
        check_vma=False,
    )
```

```python
import functools
import math

import jax
import jax.numpy as jnp
from jax import lax
from jax.experimental import pallas as pl
from jax.experimental.pallas import tpu as pltpu
from jax.sharding import PartitionSpec as P

HEADS = 8
HEAD_DIM = 128
BLK = 256
HALF = BLK // 2
SUB = BLK // 8
LEV = 4
EXP_SCALE = math.log2(math.e) / math.sqrt(HEAD_DIM)

VMEM_GRANT = 48 << 20

very_negative = -1e30
f32 = jnp.float32
bf16 = jnp.bfloat16


def iota(shape, dim):
    return lax.broadcasted_iota(jnp.int32, shape, dim)


def bit(value, place):
    return jnp.bitwise_and(lax.shift_right_logical(value, place), 1)


def low_bits(value):
    step = SUB.bit_length() - 1
    deep = jnp.bitwise_and(value, SUB - 1)
    return 8 * deep + 4 * bit(value, step) + 2 * bit(value, step + 1) + bit(value, step + 2)


def reorder_matrix():
    return (iota((BLK, BLK), 1) == low_bits(iota((BLK, BLK), 0))).astype(bf16)


def restore_matrix():
    return (iota((BLK, BLK), 0) == low_bits(iota((BLK, BLK), 1))).astype(bf16)


def pair_matrix():
    first = low_bits(iota((HALF, BLK), 0))
    place = iota((HALF, BLK), 1)
    return jnp.logical_or(place == first, place == first + 1).astype(bf16)


def mul(left, right):
    return jnp.dot(left, right, preferred_element_type=f32)


def fold(rows, factor):
    half = rows.shape[0] // 2
    total = rows[:half].astype(f32) + rows[half:].astype(f32)
    if factor != 1.0:
        total = total * factor
    return total.astype(bf16)


def fold_chunks(rows, chunk, factor):
    count = rows.shape[0] // chunk
    return jnp.concatenate([fold(rows[i * chunk : (i + 1) * chunk], factor) for i in range(count)], axis=0)


def twice(rows):
    return jnp.concatenate([rows, rows], axis=0)


def cols(head):
    return slice(head * HEAD_DIM, (head + 1) * HEAD_DIM)


DECLARED = 1 << 36


def with_ones(values):
    return jnp.concatenate([values, jnp.ones_like(values)], axis=1)


def attend(units):
    scores = []
    for query, parts in units:
        raws = [
            lax.dot_general(query, keys, (((1,), (1,)), ((), ())), preferred_element_type=f32) for keys, _, _ in parts
        ]
        scores.append([raw if part[2] is None else raw + part[2] for raw, part in zip(raws, parts)])
    tops = []
    for raws in scores:
        tops.append(functools.reduce(jnp.maximum, [jnp.max(raw, axis=1, keepdims=True) for raw in raws]))
    found = []
    for (_, parts), raws, top in zip(units, scores, tops):
        total = None
        for (_, values, _), raw in zip(parts, raws):
            weights = jnp.exp2((raw - top) * EXP_SCALE).astype(bf16)
            one = mul(weights, with_ones(values))
            total = one if total is None else total + one
        found.append((jnp.broadcast_to(top * EXP_SCALE, (top.shape[0], HEAD_DIM)), total))
    return found


def share_of(ref, share, shares):
    width = ref.shape[1] // shares
    first = share * width
    if not isinstance(share, int):
        first = pl.multiple_of(first, HEAD_DIM)
    return ref.at[:, pl.ds(first, width)]


class Operand:
    def __init__(self, values, pieces=False, pinned=False):
        self.values = values
        self.pieces = pieces
        self.pinned = pinned

    def buffer(self, shares):
        rows, width = self.values[0].shape
        if self.pieces:
            return (shares, len(self.values) // shares, rows, width)
        return (shares, rows, width // shares)


def one(value, pinned=True):
    return Operand([value], pinned=pinned)


def run_shares(body, name, shares, scalars, ins, outs, work=1 << 10):
    out_kinds = [kind for _, kind in outs]
    pieces = [i for i, kind in enumerate(out_kinds) if isinstance(kind, int)]
    buffered = len(outs) - max(0, len(pieces) - 1)

    first = [sum(len(operand.values) for operand in ins[:i]) for i in range(len(ins) + 1)]

    def kernel(*refs):
        refs = list(refs)
        take = lambda count: [refs.pop(0) for _ in range(count)]
        scalar_refs, in_refs, out_refs = take(len(scalars)), take(first[-1]), take(len(outs))
        in_bufs, out_bufs, (in_sems, out_sems) = take(len(ins)), take(buffered), take(2)

        def piece(i, n):
            entry = n ^ scalar_refs[0][1]
            count = len(ins[i].values) // shares
            target = in_bufs[i].at[lax.div(entry, count), lax.rem(entry, count)]
            return pltpu.make_async_copy(in_refs[first[i] + n], target, piece_sems.at[n])

        def bring(i, share, which=0):
            source = share_of(in_refs[first[i] + which], share, shares)
            return pltpu.make_async_copy(source, in_bufs[i].at[share], in_sems.at[i, share])

        def begin(i, share):
            if len(ins[i].values) == 1:
                bring(i, share).start()
            else:
                pl.when(scalar_refs[0][2] == 1)(lambda: bring(i, share, 0).start())
                pl.when(scalar_refs[0][2] != 1)(lambda: bring(i, share, 1).start())

        whole = [i for i, operand in enumerate(ins) if not operand.pieces]
        split = [(i, n) for i, operand in enumerate(ins) if operand.pieces for n in range(len(operand.values))]
        piece_sems = refs.pop(0)

        def put(i, share):
            if i in pieces:
                entry = out_kinds[i] ^ scalar_refs[0][1]
                return pltpu.make_async_copy(out_bufs[-1].at[entry], out_refs[i], out_sems.at[i, 0])
            target = share_of(out_refs[i], share, shares)
            return pltpu.make_async_copy(out_bufs[i].at[share], target, out_sems.at[i, share])

        for share in range(shares):
            for i in whole:
                begin(i, share)
            if share == 0:
                for i, n in split:
                    piece(i, n).start()
        for i, n in split:
            piece(i, n).wait()

        def step(share, carry):
            for i in whole:
                bring(i, share).wait()
            body(scalar_refs, [buf.at[share] for buf in in_bufs], [buf.at[share] for buf in out_bufs])
            for i in range(len(outs) - len(pieces)):
                put(i, share).start()
            return carry

        lax.fori_loop(0, shares, step, 0)
        for i in pieces:
            put(i, 0).start()
        for share in range(shares):
            for i in range(len(outs) - len(pieces)):
                put(i, share).wait()
        for i in pieces:
            put(i, 0).wait()

    values, specs = [], []
    for operand in ins:
        for value in operand.values:
            values.append(pltpu.with_memory_space_constraint(value, pltpu.HBM) if operand.pinned else value)
            specs.append(pl.BlockSpec(memory_space=pltpu.HBM if operand.pinned else pl.ANY))
    buffers = [pltpu.VMEM(operand.buffer(shares), operand.values[0].dtype) for operand in ins]
    for shape, kind in outs[:buffered]:
        width = shape.shape[-1]
        if isinstance(kind, int):
            buffers.append(pltpu.VMEM((shares, *shape.shape), shape.dtype))
            continue
        buffers.append(pltpu.VMEM((shares, shape.shape[0], width // shares), shape.dtype))
    return pl.pallas_call(
        kernel,
        in_specs=[pl.BlockSpec(memory_space=pltpu.SMEM)] * len(scalars) + specs,
        out_specs=[pl.BlockSpec(memory_space=pltpu.HBM)] * len(outs),
        out_shape=[pltpu.HBM(shape.shape, shape.dtype) for shape, _ in outs],
        scratch_shapes=buffers
        + [pltpu.SemaphoreType.DMA((len(ins), shares)), pltpu.SemaphoreType.DMA((len(outs), shares))]
        + [pltpu.SemaphoreType.DMA((max(len(operand.values) for operand in ins),))],
        compiler_params=pltpu.CompilerParams(vmem_limit_bytes=VMEM_GRANT),
        cost_estimate=pl.CostEstimate(flops=work, bytes_accessed=1 << 10, transcendentals=0),
        name=name,
    )(*scalars, *values)


def array(rows, width, dtype):
    return jax.ShapeDtypeStruct((rows, width), dtype)


def swap_body(_, ins, outs):
    pair = pair_matrix()
    for place, (ref, factor) in enumerate(zip(ins, (0.5, 0.5, 1.0))):
        for i in range(2):
            level1 = mul(pair, ref[i * BLK : (i + 1) * BLK, :])
            if factor != 1.0:
                level1 = level1 * factor
            first = place * HALF + i * HALF // 2
            outs[0][first : first + HALF // 2, :] = fold(level1.astype(bf16), factor)


def swap_rows(place, query_vecs, key_vecs, value_vecs, groups):
    width = query_vecs.shape[1]
    ins = [one(a) for a in (query_vecs, key_vecs, value_vecs)]
    outs = [(array(3 * HALF, width // groups, bf16), n) for n in range(groups)]
    return run_shares(swap_body, "swap_rows", groups, [place], ins, outs)


def rows_body(scalars, ins, outs):
    q_ref, k_ref, v_ref = ins
    q0_ref, q1_ref, cross_ref, chip_ref = outs
    reorder = reorder_matrix()
    pair = pair_matrix()
    for i in range(2):
        rows = slice(i * BLK, (i + 1) * BLK)
        q0 = mul(reorder, q_ref[rows, :]).astype(bf16)
        q0_ref[rows, :] = q0
        q1_ref[i * HALF : (i + 1) * HALF, :] = fold(q0, 0.5)
    odd = scalars[0][0]
    outer = pl.ds(pl.multiple_of(odd * BLK, BLK), BLK)
    inner = pl.ds(pl.multiple_of((1 - odd) * BLK, BLK), BLK)
    for ref, near, far in ((cross_ref, outer, inner), (chip_ref, inner, outer)):
        ref[0:BLK, :] = k_ref[near, :]
        ref[BLK : 2 * BLK, :] = v_ref[near, :]
        ref[2 * BLK : 2 * BLK + HALF, :] = (mul(pair, k_ref[far, :]) * 0.5).astype(bf16)
        ref[2 * BLK + HALF : 3 * BLK, :] = mul(pair, v_ref[far, :]).astype(bf16)


def rows_to_send(place, query_vecs, key_vecs, value_vecs, groups):
    rows, width = query_vecs.shape
    ins = [one(a) for a in (query_vecs, key_vecs, value_vecs)]
    outs = [(array(n, width, bf16), "cols") for n in (rows, rows // 2, 3 * BLK, 3 * BLK)]
    return run_shares(rows_body, "rows_to_send", groups, [place], ins, outs)


def pack(stats):
    width = HEAD_DIM // len(stats)
    lane = iota(stats[0].shape, 1)
    packed = stats[-1]
    for n in range(len(stats) - 2, -1, -1):
        packed = jnp.where(lane < (n + 1) * width, stats[n], packed)
    return packed


def unpack(packed, head):
    lanes = [head * HEAD_DIM // 2 + n * HEAD_DIM // 4 for n in range(2)]
    return [jnp.broadcast_to(packed[:, lane : lane + 1], packed.shape) for lane in lanes]


def own_body(_, ins, outs):
    q_ref, k_ref, v_ref = ins
    sum_ref, stat_ref = outs
    heads = q_ref.shape[1] // HEAD_DIM
    for i in range(2):
        rows = slice(i * BLK, (i + 1) * BLK)
        units = [(q_ref[rows, cols(head)], [(k_ref[:, cols(head)], v_ref[:, cols(head)], None)]) for head in range(heads)]
        stats = []
        for head, (top, sums) in enumerate(attend(units)):
            sum_ref[rows, cols(head)] = sums[:, :HEAD_DIM]
            stats += [top, sums[:, HEAD_DIM:]]
        for n in range(0, heads, 2):
            stat_ref[rows, cols(n // 2)] = pack(stats[2 * n : 2 * n + 4])


def own_level(q0, key_vecs, value_vecs, groups):
    rows, width = q0.shape
    ins = [one(a) for a in (q0, key_vecs, value_vecs)]
    outs = [(array(rows, width, f32), "cols"), (array(rows, groups * HEAD_DIM, f32), "cols")]
    return run_shares(own_body, "own_level", groups // 2, [], ins, outs, DECLARED)


def halo_body(place_ref, *refs):
    count = len(refs) - 4
    piece_refs, (got_ref, right_ref, left_ref, sems) = refs[:count], refs[count:]
    copies = [pltpu.make_async_copy(ref, got_ref.at[n ^ place_ref[1]], sems.at[n]) for n, ref in enumerate(piece_refs)]
    for copy in copies:
        copy.start()
    for copy in copies:
        copy.wait()
    pair = count // 2
    for which, factor in ((1, 0.5), (2, 1.0)):
        rows = slice(which * HALF, (which + 1) * HALF)
        near = (which - 1) * BLK
        far = 2 * BLK + (which - 1) * HALF
        for j in range(count):
            level2 = got_ref[j, rows, :]
            level3 = fold_chunks(level2, HALF // 2, factor)
            near_ref, far_ref = (left_ref, right_ref) if j < pair else (right_ref, left_ref)
            spot = j % pair
            near_ref[near + spot * HALF : near + (spot + 1) * HALF, :] = level2
            far_ref[far + spot * HALF // 2 : far + (spot + 1) * HALF // 2, :] = level3


def coarse_halos(place, pieces):
    rows, width = pieces[0].shape
    vmem = pl.BlockSpec(memory_space=pltpu.VMEM)
    shape = jax.ShapeDtypeStruct((3 * BLK, width), bf16)
    return pl.pallas_call(
        halo_body,
        in_specs=[pl.BlockSpec(memory_space=pltpu.SMEM)] + [pl.BlockSpec(memory_space=pl.ANY)] * len(pieces),
        out_specs=[vmem] * 3,
        out_shape=[jax.ShapeDtypeStruct((len(pieces), rows, width), bf16), shape, shape],
        scratch_shapes=[pltpu.SemaphoreType.DMA((len(pieces),))],
        compiler_params=pltpu.CompilerParams(vmem_limit_bytes=16 << 20),
        cost_estimate=pl.CostEstimate(flops=1 << 20, bytes_accessed=24 * pieces[0].size, transcendentals=0),
        name="coarse_halos",
    )(place, *pieces)


def coarse_body(place_ref, bias_ref, got_ref, prev_ref, next_ref, *refs):
    *out_refs, back_ref, sems = refs
    count = got_ref.shape[0]
    heads = got_ref.shape[2] // HEAD_DIM
    bias_prev = bias_ref[0]
    bias_next = bias_ref[1]
    lane = iota((HALF, HEAD_DIM), 1)

    for head in range(heads):
        here = cols(head)

        def own(which, j):
            return got_ref[j, which * HALF : (which + 1) * HALF, here]

        def near(ref, which, spot):
            first = (which - 1) * BLK + spot * HALF
            return ref[first : first + HALF, here]

        def both(ref, which):
            return ref[(which - 1) * BLK : which * BLK, here]

        def far(ref, which):
            first = 2 * BLK + (which - 1) * HALF
            return ref[first : first + HALF, here]

        def near3(ref, which):
            return fold_chunks(both(ref, which), HALF // 2, 0.5 if which == 1 else 1.0)

        def joined(*rows):
            return jnp.concatenate(rows, axis=0)

        def part(pick, bias):
            return (pick(1), pick(2), bias)

        units = [
            (own(0, 0), [part(lambda w: joined(own(w, 2), own(w, 3)), None), part(lambda w: near(prev_ref, w, 0), bias_prev)]),
            (own(0, 1), [part(lambda w: both(prev_ref, w), bias_prev), part(lambda w: own(w, 3), None)]),
            (own(0, 2), [part(lambda w: both(next_ref, w), bias_next), part(lambda w: own(w, 0), None)]),
            (own(0, 3), [part(lambda w: joined(own(w, 0), own(w, 1)), None), part(lambda w: near(next_ref, w, 1), bias_next)]),
        ]
        for j, (ref, bias, other, other_bias) in enumerate(
            ((next_ref, bias_next, prev_ref, bias_prev), (prev_ref, bias_prev, next_ref, bias_next))
        ):
            query = joined(*[fold_chunks(own(0, 2 * j + n), HALF // 2, 0.5) for n in range(2)])
            units.append(
                (
                    query,
                    [part(lambda w: joined(near3(ref, w), far(ref, w)), bias), part(lambda w: far(other, w), other_bias)],
                )
            )
        found = attend(units)
        for j in range(count):
            top2, sum2 = found[j]
            top3, sum3 = found[count + j // 2]

            def spread(rows):
                first = (j % 2) * 2 * SUB
                one = rows[first : first + SUB]
                other = rows[first + SUB : first + 2 * SUB]
                return joined(one, one, other, other)

            top3 = spread(top3)
            sum3 = spread(sum3)
            top = jnp.maximum(top2, top3)
            scale2 = jnp.exp2(top2 - top)
            scale3 = jnp.exp2(top3 - top)
            values = sum2[:, :HEAD_DIM] * scale2 + sum3[:, :HEAD_DIM] * scale3
            total = sum2[:, HEAD_DIM:] * (4.0 * scale2) + sum3[:, HEAD_DIM:] * (8.0 * scale3)
            back_ref[j, 0:HALF, here] = (values / total).astype(bf16)
            level = top + jnp.log2(total)
            high = level.astype(bf16).astype(f32)
            middle = (level - high).astype(bf16).astype(f32)
            terms = jnp.where(lane == 0, high, jnp.where(lane == 1, middle, level - high - middle))
            back_ref[j, HALF : HALF + 16, here] = terms.T[0:16, :].astype(bf16)
    copies = [
        pltpu.make_async_copy(back_ref.at[n ^ place_ref[1]], ref, sems.at[n]) for n, ref in enumerate(out_refs)
    ]
    for copy in copies:
        copy.start()
    for copy in copies:
        copy.wait()


def coarse_levels(place, bias, got, from_prev, from_next):
    count, _, width = got.shape
    vmem = pl.BlockSpec(memory_space=pltpu.VMEM)
    smem = pl.BlockSpec(memory_space=pltpu.SMEM)
    rows = HALF + 16
    return pl.pallas_call(
        coarse_body,
        in_specs=[smem, smem, vmem, vmem, vmem],
        out_specs=[pl.BlockSpec(memory_space=pl.ANY)] * count,
        out_shape=[array(rows, width, bf16)] * count,
        scratch_shapes=[pltpu.VMEM((count, rows, width), bf16), pltpu.SemaphoreType.DMA((count,))],
        compiler_params=pltpu.CompilerParams(vmem_limit_bytes=16 << 20),
        cost_estimate=pl.CostEstimate(flops=DECLARED, bytes_accessed=8 * got.size, transcendentals=1 << 20),
        name="coarse_levels",
    )(place, bias, got, from_prev, from_next)


def side_body(side, scalars, ins, outs):
    q0_ref, q1_ref, sum_ref, stat_ref, side_ref = ins[:5]
    heads = q0_ref.shape[1] // HEAD_DIM
    bias = scalars[1][side]
    blocks = (side, 1 - side)
    pair = pair_matrix()
    near_keys = (mul(pair, side_ref[0:BLK, :]) * 0.5).astype(bf16)
    near_values = mul(pair, side_ref[BLK : 2 * BLK, :]).astype(bf16)
    far_keys = slice(2 * BLK, 2 * BLK + HALF)
    far_values = slice(2 * BLK + HALF, 3 * BLK)
    fine = [pl.ds(pl.multiple_of(block * BLK, BLK), BLK) for block in blocks]
    middle = [pl.ds(pl.multiple_of(block * HALF, HALF), HALF) for block in blocks]
    units = []
    for head in range(heads):
        here = cols(head)
        far = (side_ref[far_keys, here], side_ref[far_values, here], None)
        whole = tuple(
            jnp.concatenate([near[:, here], side_ref[far, here]], axis=0)
            for near, far in ((near_keys, far_keys), (near_values, far_values))
        )
        units.append((q0_ref[fine[0], here], [(side_ref[0:BLK, here], side_ref[BLK : 2 * BLK, here], None)]))
        units.append((q1_ref[middle[0], here], [far]))
        units.append((q1_ref[middle[1], here], [(*whole, None)]))
    found = [(top + bias, sums) for top, sums in attend(units)]
    if len(ins) == 5:
        for n in range(2):
            results = []
            for head in range(heads):
                here = cols(head)
                top1, sum1 = found[3 * head + 1 + n]
                top1, sum1 = twice(top1), twice(sum1)
                own_top, own_total = unpack(stat_ref[fine[n], cols(head // 2)], head % 2)
                top = jnp.maximum(top1, own_top)
                if n == 0:
                    top0, sum0 = found[3 * head]
                    top = jnp.maximum(top, top0)
                scale1 = jnp.exp2(top1 - top)
                own_scale = jnp.exp2(own_top - top)
                number = sum1[:, :HEAD_DIM] * scale1 + sum_ref[fine[n], here] * own_scale
                total = sum1[:, HEAD_DIM:] * (2.0 * scale1) + own_total * own_scale
                if n == 0:
                    scale0 = jnp.exp2(top0 - top)
                    number = number + sum0[:, :HEAD_DIM] * scale0
                    total = total + sum0[:, HEAD_DIM:] * scale0
                outs[0][fine[n], here] = number
                results += [top, total]
            for m in range(0, heads, 2):
                outs[1][fine[n], cols(m // 2)] = pack(results[2 * m : 2 * m + 4])
        return
    back_ref = ins[5]
    restore = restore_matrix()
    levels = []
    for head in range(heads):
        terms = back_ref[head // 2, HALF : HALF + 16, cols(head % 2)].astype(f32)
        terms = jnp.sum(jnp.where(iota(terms.shape, 0) < 3, terms, 0.0), axis=0, keepdims=True)
        levels.append(jnp.broadcast_to(terms, (HEAD_DIM, HEAD_DIM)).T)
    for n in range(2):
        spot = pl.ds(pl.multiple_of(blocks[n] * HALF // 2, HALF // 2), HALF // 2)
        results = []
        for head in range(heads):
            here = cols(head)
            top1, sum1 = found[3 * head + 1 + n]
            half = HALF // 2
            level = twice(jnp.where(blocks[n] == 0, levels[head][:half, :], levels[head][half:, :]))
            top = jnp.maximum(top1, level)
            scale1 = jnp.exp2(top1 - top)
            scale2 = jnp.exp2(level - top)
            number = twice(sum1[:, :HEAD_DIM] * scale1 + twice(back_ref[head // 2, spot, cols(head % 2)].astype(f32)) * scale2)
            total = twice(sum1[:, HEAD_DIM:] * (2.0 * scale1) + scale2)
            top = twice(top)
            own_top, own_total = unpack(stat_ref[fine[n], cols(head // 2)], head % 2)
            most = jnp.maximum(top, own_top)
            if n == 0:
                top0, sum0 = found[3 * head]
                most = jnp.maximum(most, top0)
            scale = jnp.exp2(top - most)
            own_scale = jnp.exp2(own_top - most)
            number = number * scale + sum_ref[fine[n], here] * own_scale
            total = total * scale + own_total * own_scale
            if n == 0:
                scale0 = jnp.exp2(top0 - most)
                number = number + sum0[:, :HEAD_DIM] * scale0
                total = total + sum0[:, HEAD_DIM:] * scale0
            results.append((number / total).astype(bf16))
        outs[0][fine[n], :] = mul(restore, jnp.concatenate(results, axis=1)).astype(bf16)


def chip_body(scalars, ins, outs):
    side_body(1 - scalars[0][0], scalars, ins, outs)


def finish_body(scalars, ins, outs):
    side_body(scalars[0][0], scalars, ins, outs)


def chip_level(odd, bias, q0, q1, sums, stat, chip, groups):
    rows, width = q0.shape
    ins = [one(a) for a in (q0, q1, sums, stat)] + [one(chip, False)]
    outs = [(array(rows, width, f32), "cols"), (array(rows, groups * HEAD_DIM, f32), "cols")]
    return run_shares(chip_body, "chip_level", groups // 2, [odd, bias], ins, outs)


def finish(place, bias, q0, q1, sums, stat, relayed, cross, back):
    groups = len(back)
    rows, width = q0.shape
    ins = [one(a) for a in (q0, q1, sums, stat)] + [Operand([relayed, cross]), Operand(back, pieces=True)]
    outs = [(array(rows, width, bf16), "cols")]
    return run_shares(finish_body, "finish", groups // 2, [place, bias], ins, outs)[0]


def shift(value, axis, steps):
    count = lax.axis_size(axis)
    first, last = (max(0, -steps), min(count, count - steps))
    return lax.ppermute(value, axis, [(source, source + steps) for source in range(first, last)])


def trade(value, axis, pairs):
    return lax.ppermute(value, axis, pairs + [(target, source) for source, target in pairs])


def ways_across(count, groups):
    def beside(device):
        other = (device // groups ^ 1) * groups + device % groups
        return other if other < count else device

    pairs = [(before, before + 1) for before in range(1, count - 1, 2)]
    direct = [(behind, before) for before, behind in pairs]
    direct += [(before, behind) for before, behind in pairs if behind % groups != 0]
    relay = [(device, beside(device)) for device in range(groups - 1, count, groups)]
    onward = [(beside(before), behind) for before, behind in pairs if behind % groups == 0]
    return direct, relay, onward


def edge_bias(axis):
    place = lax.axis_index(axis)
    last = lax.axis_size(axis) - 1
    at_edge = jnp.stack([place == 0, place == last])
    return jnp.where(at_edge, very_negative, 0.0).astype(f32)


def local(query_vecs, key_vecs, value_vecs):
    groups = lax.axis_size("grp")
    assert query_vecs.shape == (2 * BLK, HEADS * HEAD_DIM) and groups == 4
    everyone = ("seq", "grp")
    count = lax.axis_size(everyone)
    spot = lax.axis_index("grp")
    odd = jnp.bitwise_and(spot, 1)
    at_start = (spot == 0).astype(odd.dtype)
    place = jnp.stack([odd, spot, at_start]).astype(jnp.int32)
    bias = edge_bias(everyone)

    def exchange(pieces):
        flips = [[(source, source ^ n) for source in range(groups)] for n in range(groups)]
        return [pieces[0]] + [lax.ppermute(pieces[n], "grp", flips[n]) for n in range(1, groups)]

    pieces = list(swap_rows(place, query_vecs, key_vecs, value_vecs, groups))
    query_rows, pieces = lax.optimization_barrier((query_vecs, pieces))
    pieces = exchange(pieces)
    query_rows, pieces[1] = lax.optimization_barrier((query_rows, pieces[1]))
    q0, q1, cross, chip = rows_to_send(place, query_rows, key_vecs, value_vecs, groups)
    direct, relay, onward = ways_across(count, groups)
    relayed = lax.ppermute(cross, everyone, relay)
    cross = lax.ppermute(cross, everyone, direct)
    pieces, chip = lax.optimization_barrier((pieces, chip))
    got, coarse_right, coarse_left = coarse_halos(place, pieces)
    coarse_right, coarse_left, chip, q0 = lax.optimization_barrier((coarse_right, coarse_left, chip, q0))
    coarse_prev = shift(coarse_right, "seq", 1)
    coarse_next = shift(coarse_left, "seq", -1)
    chip = trade(chip, everyone, [(first, first + 1) for first in range(0, count - 1, 2)])
    own, own_stat = own_level(q0, key_vecs, value_vecs, groups)
    relayed, own = lax.optimization_barrier((relayed, own))
    relayed = lax.ppermute(relayed, everyone, onward)
    own, own_stat = chip_level(place, bias, q0, q1, own, own_stat, chip, groups)
    got, own = lax.optimization_barrier((got, own))
    back = exchange(coarse_levels(place, edge_bias("seq"), got, coarse_prev, coarse_next))
    return finish(place, bias, q0, q1, own, own_stat, relayed, cross, back)


def solution(mesh):
    return jax.shard_map(
        local,
        mesh=mesh,
        in_specs=(P(("seq", "grp"), None), P(("seq", "grp"), None), P(("seq", "grp"), None)),
        out_specs=P(("seq", "grp"), None),
        check_vma=False,
    )
```

```python
import functools
import math

import jax
import jax.numpy as jnp
from jax import lax
from jax.experimental import pallas as pl
from jax.experimental.pallas import tpu as pltpu
from jax.sharding import PartitionSpec as P

HEADS = 8
HEAD_DIM = 128
BLK = 256
HALF = BLK // 2
SUB = BLK // 8
LEV = 4
EXP_SCALE = math.log2(math.e) / math.sqrt(HEAD_DIM)

VMEM_GRANT = 48 << 20

very_negative = -1e30
f32 = jnp.float32
bf16 = jnp.bfloat16


def iota(shape, dim):
    return lax.broadcasted_iota(jnp.int32, shape, dim)


def bit(value, place):
    return jnp.bitwise_and(lax.shift_right_logical(value, place), 1)


def low_bits(value):
    step = SUB.bit_length() - 1
    deep = jnp.bitwise_and(value, SUB - 1)
    return 8 * deep + 4 * bit(value, step) + 2 * bit(value, step + 1) + bit(value, step + 2)


def reorder_matrix():
    return (iota((BLK, BLK), 1) == low_bits(iota((BLK, BLK), 0))).astype(bf16)


def restore_matrix():
    return (iota((BLK, BLK), 0) == low_bits(iota((BLK, BLK), 1))).astype(bf16)


def pair_matrix():
    first = low_bits(iota((HALF, BLK), 0))
    place = iota((HALF, BLK), 1)
    return jnp.logical_or(place == first, place == first + 1).astype(bf16)


def mul(left, right):
    return jnp.dot(left, right, preferred_element_type=f32)


def fold(rows, factor):
    half = rows.shape[0] // 2
    total = rows[:half].astype(f32) + rows[half:].astype(f32)
    if factor != 1.0:
        total = total * factor
    return total.astype(bf16)


def fold_chunks(rows, chunk, factor):
    count = rows.shape[0] // chunk
    return jnp.concatenate([fold(rows[i * chunk : (i + 1) * chunk], factor) for i in range(count)], axis=0)


def twice(rows):
    return jnp.concatenate([rows, rows], axis=0)


def cols(head):
    return slice(head * HEAD_DIM, (head + 1) * HEAD_DIM)


DECLARED = 1 << 36


def with_ones(values):
    return jnp.concatenate([values, jnp.ones_like(values)], axis=1)


def attend(units):
    scores = []
    for query, parts in units:
        raws = [
            lax.dot_general(query, keys, (((1,), (1,)), ((), ())), preferred_element_type=f32) for keys, _, _ in parts
        ]
        scores.append([raw if part[2] is None else raw + part[2] for raw, part in zip(raws, parts)])
    tops = []
    for raws in scores:
        tops.append(functools.reduce(jnp.maximum, [jnp.max(raw, axis=1, keepdims=True) for raw in raws]))
    found = []
    for (_, parts), raws, top in zip(units, scores, tops):
        total = None
        for (_, values, _), raw in zip(parts, raws):
            weights = jnp.exp2((raw - top) * EXP_SCALE).astype(bf16)
            one = mul(weights, with_ones(values))
            total = one if total is None else total + one
        found.append((jnp.broadcast_to(top * EXP_SCALE, (top.shape[0], HEAD_DIM)), total))
    return found


def share_of(ref, share, shares):
    width = ref.shape[1] // shares
    first = share * width
    if not isinstance(share, int):
        first = pl.multiple_of(first, HEAD_DIM)
    return ref.at[:, pl.ds(first, width)]


class Operand:
    def __init__(self, values, pieces=False, pinned=False):
        self.values = values
        self.pieces = pieces
        self.pinned = pinned

    def buffer(self, shares):
        rows, width = self.values[0].shape
        if self.pieces:
            return (shares, len(self.values) // shares, rows, width)
        return (shares, rows, width // shares)


def one(value, pinned=True):
    return Operand([value], pinned=pinned)


def run_shares(body, name, shares, scalars, ins, outs, work=1 << 10):
    out_kinds = [kind for _, kind in outs]
    pieces = [i for i, kind in enumerate(out_kinds) if isinstance(kind, int)]
    buffered = len(outs) - max(0, len(pieces) - 1)

    first = [sum(len(operand.values) for operand in ins[:i]) for i in range(len(ins) + 1)]

    def kernel(*refs):
        refs = list(refs)
        take = lambda count: [refs.pop(0) for _ in range(count)]
        scalar_refs, in_refs, out_refs = take(len(scalars)), take(first[-1]), take(len(outs))
        in_bufs, out_bufs, (in_sems, out_sems) = take(len(ins)), take(buffered), take(2)

        def piece(i, n):
            entry = n ^ scalar_refs[0][1]
            count = len(ins[i].values) // shares
            target = in_bufs[i].at[lax.div(entry, count), lax.rem(entry, count)]
            return pltpu.make_async_copy(in_refs[first[i] + n], target, piece_sems.at[n])

        def bring(i, share):
            return pltpu.make_async_copy(share_of(in_refs[first[i]], share, shares), in_bufs[i].at[share], in_sems.at[i, share])

        whole = [i for i, operand in enumerate(ins) if not operand.pieces]
        split = [(i, n) for i, operand in enumerate(ins) if operand.pieces for n in range(len(operand.values))]
        piece_sems = refs.pop(0)

        def put(i, share):
            if i in pieces:
                entry = out_kinds[i] ^ scalar_refs[0][1]
                return pltpu.make_async_copy(out_bufs[-1].at[entry], out_refs[i], out_sems.at[i, 0])
            target = share_of(out_refs[i], share, shares)
            return pltpu.make_async_copy(out_bufs[i].at[share], target, out_sems.at[i, share])

        for share in range(shares):
            for i in whole:
                bring(i, share).start()
            if share == 0:
                for i, n in split:
                    piece(i, n).start()
        for i, n in split:
            piece(i, n).wait()

        def step(share, carry):
            for i in whole:
                bring(i, share).wait()
            body(scalar_refs, [buf.at[share] for buf in in_bufs], [buf.at[share] for buf in out_bufs])
            for i in range(len(outs) - len(pieces)):
                put(i, share).start()
            return carry

        lax.fori_loop(0, shares, step, 0)
        for i in pieces:
            put(i, 0).start()
        for share in range(shares):
            for i in range(len(outs) - len(pieces)):
                put(i, share).wait()
        for i in pieces:
            put(i, 0).wait()

    values, specs = [], []
    for operand in ins:
        for value in operand.values:
            values.append(pltpu.with_memory_space_constraint(value, pltpu.HBM) if operand.pinned else value)
            specs.append(pl.BlockSpec(memory_space=pltpu.HBM if operand.pinned else pl.ANY))
    buffers = [pltpu.VMEM(operand.buffer(shares), operand.values[0].dtype) for operand in ins]
    for shape, kind in outs[:buffered]:
        width = shape.shape[-1]
        if isinstance(kind, int):
            buffers.append(pltpu.VMEM((shares, *shape.shape), shape.dtype))
            continue
        buffers.append(pltpu.VMEM((shares, shape.shape[0], width // shares), shape.dtype))
    return pl.pallas_call(
        kernel,
        in_specs=[pl.BlockSpec(memory_space=pltpu.SMEM)] * len(scalars) + specs,
        out_specs=[pl.BlockSpec(memory_space=pltpu.HBM)] * len(outs),
        out_shape=[pltpu.HBM(shape.shape, shape.dtype) for shape, _ in outs],
        scratch_shapes=buffers
        + [pltpu.SemaphoreType.DMA((len(ins), shares)), pltpu.SemaphoreType.DMA((len(outs), shares))]
        + [pltpu.SemaphoreType.DMA((max(len(operand.values) for operand in ins),))],
        compiler_params=pltpu.CompilerParams(vmem_limit_bytes=VMEM_GRANT),
        cost_estimate=pl.CostEstimate(flops=work, bytes_accessed=1 << 10, transcendentals=0),
        name=name,
    )(*scalars, *values)


def array(rows, width, dtype):
    return jax.ShapeDtypeStruct((rows, width), dtype)


def swap_body(_, ins, outs):
    pair = pair_matrix()
    for place, (ref, factor) in enumerate(zip(ins, (0.5, 0.5, 1.0))):
        for i in range(2):
            level1 = mul(pair, ref[i * BLK : (i + 1) * BLK, :])
            if factor != 1.0:
                level1 = level1 * factor
            first = place * HALF + i * HALF // 2
            outs[0][first : first + HALF // 2, :] = fold(level1.astype(bf16), factor)


def swap_rows(place, query_vecs, key_vecs, value_vecs, groups):
    width = query_vecs.shape[1]
    ins = [one(a) for a in (query_vecs, key_vecs, value_vecs)]
    outs = [(array(3 * HALF, width // groups, bf16), n) for n in range(groups)]
    return run_shares(swap_body, "swap_rows", groups, [place], ins, outs)


def rows_body(scalars, ins, outs):
    q_ref, k_ref, v_ref = ins
    q0_ref, q1_ref, near_ref, far_ref, chip_ref = outs
    reorder = reorder_matrix()
    pair = pair_matrix()
    for i in range(2):
        rows = slice(i * BLK, (i + 1) * BLK)
        q0 = mul(reorder, q_ref[rows, :]).astype(bf16)
        q0_ref[rows, :] = q0
        q1_ref[i * HALF : (i + 1) * HALF, :] = fold(q0, 0.5)
    odd = scalars[0][0]
    outer = pl.ds(pl.multiple_of(odd * BLK, BLK), BLK)
    inner = pl.ds(pl.multiple_of((1 - odd) * BLK, BLK), BLK)
    for ref, far_rows, first, near, far in ((near_ref, far_ref, 0, outer, inner), (chip_ref, chip_ref, 2 * BLK, inner, outer)):
        ref[0:BLK, :] = k_ref[near, :]
        ref[BLK : 2 * BLK, :] = v_ref[near, :]
        far_rows[first : first + HALF, :] = (mul(pair, k_ref[far, :]) * 0.5).astype(bf16)
        far_rows[first + HALF : first + BLK, :] = mul(pair, v_ref[far, :]).astype(bf16)


def rows_to_send(place, query_vecs, key_vecs, value_vecs, groups):
    rows, width = query_vecs.shape
    ins = [one(a) for a in (query_vecs, key_vecs, value_vecs)]
    outs = [(array(n, width, bf16), "cols") for n in (rows, rows // 2, 2 * BLK, BLK, 3 * BLK)]
    return run_shares(rows_body, "rows_to_send", groups, [place], ins, outs)


def pack(stats):
    width = HEAD_DIM // len(stats)
    lane = iota(stats[0].shape, 1)
    packed = stats[-1]
    for n in range(len(stats) - 2, -1, -1):
        packed = jnp.where(lane < (n + 1) * width, stats[n], packed)
    return packed


def unpack(packed, head):
    lanes = [head * HEAD_DIM // 2 + n * HEAD_DIM // 4 for n in range(2)]
    return [jnp.broadcast_to(packed[:, lane : lane + 1], packed.shape) for lane in lanes]


def own_body(_, ins, outs):
    q_ref, k_ref, v_ref = ins
    sum_ref, stat_ref = outs
    heads = q_ref.shape[1] // HEAD_DIM
    for i in range(2):
        rows = slice(i * BLK, (i + 1) * BLK)
        units = [(q_ref[rows, cols(head)], [(k_ref[:, cols(head)], v_ref[:, cols(head)], None)]) for head in range(heads)]
        stats = []
        for head, (top, sums) in enumerate(attend(units)):
            sum_ref[rows, cols(head)] = sums[:, :HEAD_DIM]
            stats += [top, sums[:, HEAD_DIM:]]
        for n in range(0, heads, 2):
            stat_ref[rows, cols(n // 2)] = pack(stats[2 * n : 2 * n + 4])


def own_level(q0, key_vecs, value_vecs, groups):
    rows, width = q0.shape
    ins = [one(a) for a in (q0, key_vecs, value_vecs)]
    outs = [(array(rows, width, f32), "cols"), (array(rows, groups * HEAD_DIM, f32), "cols")]
    return run_shares(own_body, "own_level", groups // 2, [], ins, outs, DECLARED)


def halo_body(place_ref, *refs):
    count = len(refs) - 4
    piece_refs, (got_ref, right_ref, left_ref, sems) = refs[:count], refs[count:]
    copies = [pltpu.make_async_copy(ref, got_ref.at[n ^ place_ref[1]], sems.at[n]) for n, ref in enumerate(piece_refs)]
    for copy in copies:
        copy.start()
    for copy in copies:
        copy.wait()
    pair = count // 2
    for which, factor in ((1, 0.5), (2, 1.0)):
        rows = slice(which * HALF, (which + 1) * HALF)
        near = (which - 1) * BLK
        far = 2 * BLK + (which - 1) * HALF
        for j in range(count):
            level2 = got_ref[j, rows, :]
            level3 = fold_chunks(level2, HALF // 2, factor)
            near_ref, far_ref = (left_ref, right_ref) if j < pair else (right_ref, left_ref)
            spot = j % pair
            near_ref[near + spot * HALF : near + (spot + 1) * HALF, :] = level2
            far_ref[far + spot * HALF // 2 : far + (spot + 1) * HALF // 2, :] = level3


def coarse_halos(place, pieces):
    rows, width = pieces[0].shape
    vmem = pl.BlockSpec(memory_space=pltpu.VMEM)
    shape = jax.ShapeDtypeStruct((3 * BLK, width), bf16)
    return pl.pallas_call(
        halo_body,
        in_specs=[pl.BlockSpec(memory_space=pltpu.SMEM)] + [pl.BlockSpec(memory_space=pl.ANY)] * len(pieces),
        out_specs=[vmem] * 3,
        out_shape=[jax.ShapeDtypeStruct((len(pieces), rows, width), bf16), shape, shape],
        scratch_shapes=[pltpu.SemaphoreType.DMA((len(pieces),))],
        compiler_params=pltpu.CompilerParams(vmem_limit_bytes=16 << 20),
        cost_estimate=pl.CostEstimate(flops=1 << 20, bytes_accessed=24 * pieces[0].size, transcendentals=0),
        name="coarse_halos",
    )(place, *pieces)


def coarse_body(place_ref, bias_ref, got_ref, prev_ref, next_ref, *refs):
    *out_refs, back_ref, sems = refs
    count = got_ref.shape[0]
    heads = got_ref.shape[2] // HEAD_DIM
    bias_prev = bias_ref[0]
    bias_next = bias_ref[1]
    lane = iota((HALF, HEAD_DIM), 1)

    for head in range(heads):
        here = cols(head)

        def own(which, j):
            return got_ref[j, which * HALF : (which + 1) * HALF, here]

        def near(ref, which, spot):
            first = (which - 1) * BLK + spot * HALF
            return ref[first : first + HALF, here]

        def both(ref, which):
            return ref[(which - 1) * BLK : which * BLK, here]

        def far(ref, which):
            first = 2 * BLK + (which - 1) * HALF
            return ref[first : first + HALF, here]

        def near3(ref, which):
            return fold_chunks(both(ref, which), HALF // 2, 0.5 if which == 1 else 1.0)

        def joined(*rows):
            return jnp.concatenate(rows, axis=0)

        def part(pick, bias):
            return (pick(1), pick(2), bias)

        units = [
            (own(0, 0), [part(lambda w: joined(own(w, 2), own(w, 3)), None), part(lambda w: near(prev_ref, w, 0), bias_prev)]),
            (own(0, 1), [part(lambda w: both(prev_ref, w), bias_prev), part(lambda w: own(w, 3), None)]),
            (own(0, 2), [part(lambda w: both(next_ref, w), bias_next), part(lambda w: own(w, 0), None)]),
            (own(0, 3), [part(lambda w: joined(own(w, 0), own(w, 1)), None), part(lambda w: near(next_ref, w, 1), bias_next)]),
        ]
        for j, (ref, bias, other, other_bias) in enumerate(
            ((next_ref, bias_next, prev_ref, bias_prev), (prev_ref, bias_prev, next_ref, bias_next))
        ):
            query = joined(*[fold_chunks(own(0, 2 * j + n), HALF // 2, 0.5) for n in range(2)])
            units.append(
                (
                    query,
                    [part(lambda w: joined(near3(ref, w), far(ref, w)), bias), part(lambda w: far(other, w), other_bias)],
                )
            )
        found = attend(units)
        for j in range(count):
            top2, sum2 = found[j]
            top3, sum3 = found[count + j // 2]

            def spread(rows):
                first = (j % 2) * 2 * SUB
                one = rows[first : first + SUB]
                other = rows[first + SUB : first + 2 * SUB]
                return joined(one, one, other, other)

            top3 = spread(top3)
            sum3 = spread(sum3)
            top = jnp.maximum(top2, top3)
            scale2 = jnp.exp2(top2 - top)
            scale3 = jnp.exp2(top3 - top)
            values = sum2[:, :HEAD_DIM] * scale2 + sum3[:, :HEAD_DIM] * scale3
            total = sum2[:, HEAD_DIM:] * (4.0 * scale2) + sum3[:, HEAD_DIM:] * (8.0 * scale3)
            back_ref[j, 0:HALF, here] = (values / total).astype(bf16)
            level = top + jnp.log2(total)
            high = level.astype(bf16).astype(f32)
            middle = (level - high).astype(bf16).astype(f32)
            terms = jnp.where(lane == 0, high, jnp.where(lane == 1, middle, level - high - middle))
            back_ref[j, HALF : HALF + 16, here] = terms.T[0:16, :].astype(bf16)
    copies = [
        pltpu.make_async_copy(back_ref.at[n ^ place_ref[1]], ref, sems.at[n]) for n, ref in enumerate(out_refs)
    ]
    for copy in copies:
        copy.start()
    for copy in copies:
        copy.wait()


def coarse_levels(place, bias, got, from_prev, from_next):
    count, _, width = got.shape
    vmem = pl.BlockSpec(memory_space=pltpu.VMEM)
    smem = pl.BlockSpec(memory_space=pltpu.SMEM)
    rows = HALF + 16
    return pl.pallas_call(
        coarse_body,
        in_specs=[smem, smem, vmem, vmem, vmem],
        out_specs=[pl.BlockSpec(memory_space=pl.ANY)] * count,
        out_shape=[array(rows, width, bf16)] * count,
        scratch_shapes=[pltpu.VMEM((count, rows, width), bf16), pltpu.SemaphoreType.DMA((count,))],
        compiler_params=pltpu.CompilerParams(vmem_limit_bytes=16 << 20),
        cost_estimate=pl.CostEstimate(flops=DECLARED, bytes_accessed=8 * got.size, transcendentals=1 << 20),
        name="coarse_levels",
    )(place, bias, got, from_prev, from_next)


def unpack_level(back_ref, head):
    terms = back_ref[head // 2, HALF : HALF + 16, cols(head % 2)].astype(f32)
    terms = jnp.sum(jnp.where(iota(terms.shape, 0) < 3, terms, 0.0), axis=0, keepdims=True)
    return jnp.broadcast_to(terms, (HEAD_DIM, HEAD_DIM)).T


def side_body(side, with_near, with_far, scalars, ins, outs):
    q0_ref, q1_ref, sum_ref, stat_ref, side_ref = ins[:5]
    back_ref = ins[5] if len(ins) > 5 else None
    heads = q0_ref.shape[1] // HEAD_DIM
    bias = scalars[1][side]
    blocks = (side, 1 - side)
    fine = [pl.ds(pl.multiple_of(block * BLK, BLK), BLK) for block in blocks]
    middle = [pl.ds(pl.multiple_of(block * HALF, HALF), HALF) for block in blocks]
    if with_near:
        pair = pair_matrix()
        near_keys = (mul(pair, side_ref[0:BLK, :]) * 0.5).astype(bf16)
        near_values = mul(pair, side_ref[BLK : 2 * BLK, :]).astype(bf16)
    start = 2 * BLK if with_near else 0
    far_keys, far_values = (slice(start + n * HALF, start + (n + 1) * HALF) for n in range(2))
    units, names = [], []
    for head in range(heads):
        here = cols(head)
        far = (side_ref[far_keys, here], side_ref[far_values, here]) if with_far else None
        near = (near_keys[:, here], near_values[:, here]) if with_near else None
        whole = [part for part in (near, far) if part is not None]
        whole = [jnp.concatenate([part[n] for part in whole], axis=0) if len(whole) > 1 else whole[0][n] for n in range(2)]
        if with_near:
            units.append((q0_ref[fine[0], here], [(side_ref[0:BLK, here], side_ref[BLK : 2 * BLK, here], None)]))
            names.append((head, 0, 0))
        if with_far:
            units.append((q1_ref[middle[0], here], [(*far, None)]))
            names.append((head, 0, 1))
        units.append((q1_ref[middle[1], here], [(*whole, None)]))
        names.append((head, 1, 1))
    found = {name: (top + bias, sums) for name, (top, sums) in zip(names, attend(units))}
    restore = None if back_ref is None else restore_matrix()
    levels = None if back_ref is None else [unpack_level(back_ref, head) for head in range(heads)]
    for n in range(2):
        spot = pl.ds(pl.multiple_of(blocks[n] * HALF // 2, HALF // 2), HALF // 2)
        results, stats = [], []
        for head in range(heads):
            here = cols(head)
            own_top, own_total = unpack(stat_ref[fine[n], cols(head // 2)], head % 2)
            parts = [(own_top, sum_ref[fine[n], here], own_total)]
            if (head, n, 0) in found:
                top, sums = found[head, n, 0]
                parts.append((top, sums[:, :HEAD_DIM], sums[:, HEAD_DIM:]))
            if (head, n, 1) in found:
                top, sums = found[head, n, 1]
                number, total = sums[:, :HEAD_DIM], 2.0 * sums[:, HEAD_DIM:]
                if back_ref is not None:
                    half = HALF // 2
                    level = twice(jnp.where(blocks[n] == 0, levels[head][:half, :], levels[head][half:, :]))
                    most = jnp.maximum(top, level)
                    scale = jnp.exp2(top - most)
                    coarse = jnp.exp2(level - most)
                    number = number * scale + twice(back_ref[head // 2, spot, cols(head % 2)].astype(f32)) * coarse
                    total = total * scale + coarse
                    top = most
                parts.append((twice(top), twice(number), twice(total)))
            most = functools.reduce(jnp.maximum, [part[0] for part in parts])
            scales = [jnp.exp2(part[0] - most) for part in parts]
            number = sum(part[1] * scale for part, scale in zip(parts, scales))
            total = sum(part[2] * scale for part, scale in zip(parts, scales))
            if back_ref is None:
                outs[0][fine[n], here] = number
                stats += [most, total]
            else:
                results.append((number / total).astype(bf16))
        if back_ref is None:
            for m in range(0, heads, 2):
                outs[1][fine[n], cols(m // 2)] = pack(stats[2 * m : 2 * m + 4])
        else:
            outs[0][fine[n], :] = mul(restore, jnp.concatenate(results, axis=1)).astype(bf16)


def chip_body(scalars, ins, outs):
    side_body(1 - scalars[0][0], True, True, scalars, ins, outs)


def near_body(scalars, ins, outs):
    side_body(scalars[0][0], True, False, scalars, ins, outs)


def finish_body(scalars, ins, outs):
    side_body(scalars[0][0], False, True, scalars, ins, outs)


def side_level(body, name, place, bias, q0, q1, sums, stat, rows, groups):
    count, width = q0.shape
    ins = [one(a) for a in (q0, q1, sums, stat)] + [one(rows, False)]
    outs = [(array(count, width, f32), "cols"), (array(count, groups * HEAD_DIM, f32), "cols")]
    return run_shares(body, name, groups // 2, [place, bias], ins, outs)


def finish(place, bias, q0, q1, sums, stat, far, back):
    groups = len(back)
    rows, width = q0.shape
    ins = [one(a) for a in (q0, q1, sums, stat)] + [one(far, False), Operand(back, pieces=True)]
    outs = [(array(rows, width, bf16), "cols")]
    return run_shares(finish_body, "finish", groups // 2, [place, bias], ins, outs)[0]


def shift(value, axis, steps):
    count = lax.axis_size(axis)
    first, last = (max(0, -steps), min(count, count - steps))
    return lax.ppermute(value, axis, [(source, source + steps) for source in range(first, last)])


def trade(value, axis, pairs):
    return lax.ppermute(value, axis, pairs + [(target, source) for source, target in pairs])


def edge_bias(axis):
    place = lax.axis_index(axis)
    last = lax.axis_size(axis) - 1
    at_edge = jnp.stack([place == 0, place == last])
    return jnp.where(at_edge, very_negative, 0.0).astype(f32)


def local(query_vecs, key_vecs, value_vecs):
    groups = lax.axis_size("grp")
    assert query_vecs.shape == (2 * BLK, HEADS * HEAD_DIM) and groups == 4
    everyone = ("seq", "grp")
    count = lax.axis_size(everyone)
    spot = lax.axis_index("grp")
    odd = jnp.bitwise_and(spot, 1)
    place = jnp.stack([odd, spot]).astype(jnp.int32)
    bias = edge_bias(everyone)

    def exchange(pieces):
        flips = [[(source, source ^ n) for source in range(groups)] for n in range(groups)]
        return [pieces[0]] + [lax.ppermute(pieces[n], "grp", flips[n]) for n in range(1, groups)]

    pieces = list(swap_rows(place, query_vecs, key_vecs, value_vecs, groups))
    query_rows, pieces = lax.optimization_barrier((query_vecs, pieces))
    pieces = exchange(pieces)
    q0, q1, near, far, chip = rows_to_send(place, query_rows, key_vecs, value_vecs, groups)
    off_chip = [(device, device + 1) for device in range(1, count - 1, 2)]
    near = trade(near, everyone, off_chip)
    far, pieces[1] = lax.optimization_barrier((far, pieces[1]))
    far = trade(far, everyone, off_chip)
    pieces, chip = lax.optimization_barrier((pieces, chip))
    got, coarse_right, coarse_left = coarse_halos(place, pieces)
    coarse_right, coarse_left, chip, q0 = lax.optimization_barrier((coarse_right, coarse_left, chip, q0))
    coarse_prev = shift(coarse_right, "seq", 1)
    coarse_next = shift(coarse_left, "seq", -1)
    chip = trade(chip, everyone, [(device, device + 1) for device in range(0, count - 1, 2)])
    own, own_stat = own_level(q0, key_vecs, value_vecs, groups)
    own, own_stat = side_level(chip_body, "chip_level", place, bias, q0, q1, own, own_stat, chip, groups)
    own, own_stat = side_level(near_body, "near_level", place, bias, q0, q1, own, own_stat, near, groups)
    got, own = lax.optimization_barrier((got, own))
    back = exchange(coarse_levels(place, edge_bias("seq"), got, coarse_prev, coarse_next))
    return finish(place, bias, q0, q1, own, own_stat, far, back)


def solution(mesh):
    return jax.shard_map(
        local,
        mesh=mesh,
        in_specs=(P(("seq", "grp"), None), P(("seq", "grp"), None), P(("seq", "grp"), None)),
        out_specs=P(("seq", "grp"), None),
        check_vma=False,
    )
```

```python
import functools
import math

import jax
import jax.numpy as jnp
from jax import lax
from jax.experimental import pallas as pl
from jax.experimental.pallas import tpu as pltpu
from jax.sharding import PartitionSpec as P

HEADS = 8
HEAD_DIM = 128
BLK = 256
HALF = BLK // 2
SUB = BLK // 8
LEV = 4
EXP_SCALE = math.log2(math.e) / math.sqrt(HEAD_DIM)

VMEM_GRANT = 24 << 20

very_negative = -1e30
f32 = jnp.float32
bf16 = jnp.bfloat16


def iota(shape, dim):
    return lax.broadcasted_iota(jnp.int32, shape, dim)


def bit(value, place):
    return jnp.bitwise_and(lax.shift_right_logical(value, place), 1)


def low_bits(value):
    step = SUB.bit_length() - 1
    deep = jnp.bitwise_and(value, SUB - 1)
    return 8 * deep + 4 * bit(value, step) + 2 * bit(value, step + 1) + bit(value, step + 2)


def reorder_matrix():
    return (iota((BLK, BLK), 1) == low_bits(iota((BLK, BLK), 0))).astype(bf16)


def restore_matrix():
    return (iota((BLK, BLK), 0) == low_bits(iota((BLK, BLK), 1))).astype(bf16)


def pair_matrix():
    first = low_bits(iota((HALF, BLK), 0))
    place = iota((HALF, BLK), 1)
    return jnp.logical_or(place == first, place == first + 1).astype(bf16)


def mul(left, right):
    return jnp.dot(left, right, preferred_element_type=f32)


def fold(rows, factor):
    half = rows.shape[0] // 2
    total = rows[:half].astype(f32) + rows[half:].astype(f32)
    if factor != 1.0:
        total = total * factor
    return total.astype(bf16)


def fold_chunks(rows, chunk, factor):
    count = rows.shape[0] // chunk
    return jnp.concatenate([fold(rows[i * chunk : (i + 1) * chunk], factor) for i in range(count)], axis=0)


def twice(rows):
    return jnp.concatenate([rows, rows], axis=0)


def cols(head):
    return slice(head * HEAD_DIM, (head + 1) * HEAD_DIM)


DECLARED = 1 << 36


def with_ones(values):
    return jnp.concatenate([values, jnp.ones_like(values)], axis=1)


def attend(units):
    scores = []
    for query, parts in units:
        raws = [
            lax.dot_general(query, keys, (((1,), (1,)), ((), ())), preferred_element_type=f32) for keys, _, _ in parts
        ]
        scores.append([raw if part[2] is None else raw + part[2] for raw, part in zip(raws, parts)])
    tops = []
    for raws in scores:
        tops.append(functools.reduce(jnp.maximum, [jnp.max(raw, axis=1, keepdims=True) for raw in raws]))
    found = []
    for (_, parts), raws, top in zip(units, scores, tops):
        total = None
        for (_, values, _), raw in zip(parts, raws):
            weights = jnp.exp2((raw - top) * EXP_SCALE).astype(bf16)
            one = mul(weights, with_ones(values))
            total = one if total is None else total + one
        found.append((jnp.broadcast_to(top * EXP_SCALE, (top.shape[0], HEAD_DIM)), total))
    return found


def share_of(ref, share, shares):
    width = ref.shape[1] // shares
    first = share * width
    if not isinstance(share, int):
        first = pl.multiple_of(first, HEAD_DIM)
    return ref.at[:, pl.ds(first, width)]


def run_shares(body, name, shares, scalars, ins, outs, work=1 << 10):
    moved_in = [i for i, (kind, _) in enumerate(ins) if kind in ("cols", "got")]
    moved_out = [i for i, (kind, _) in enumerate(outs) if kind == "cols"]
    as_list = lambda pair: list(pair[1]) if pair[0] == "pieces" else [pair[1]]
    buffer_shape = {
        "cols": lambda value: (shares, value.shape[0], value.shape[1] // shares),
        "got": lambda value: (shares, value.shape[0], value.shape[1] // shares),
        "kept": lambda value: None,
        "pieces": lambda values: (shares, len(values) // shares, *values[0].shape),
    }

    def kernel(*refs):
        refs = list(refs)
        take = lambda count: [refs.pop(0) for _ in range(count)]
        scalar_refs = take(len(scalars))
        in_refs = [take(len(as_list(pair))) for pair in ins]
        out_refs = [take(len(as_list(pair))) for pair in outs]
        in_bufs = [in_refs[i][0] if ins[i][0] == "kept" else refs.pop(0) for i in range(len(ins))]
        out_bufs = [out_refs[i][0] if outs[i][0] == "kept" else refs.pop(0) for i in range(len(outs))]
        in_sems, out_sems, piece_sems = take(3)

        def bring(i, share):
            return pltpu.make_async_copy(share_of(in_refs[i][0], share, shares), in_bufs[i].at[share], in_sems.at[i, share])

        def put(i, share):
            return pltpu.make_async_copy(out_bufs[i].at[share], share_of(out_refs[i][0], share, shares), out_sems.at[i, share])

        def spot_of(buffer, n):
            entry = n ^ scalar_refs[0][1]
            return buffer.at[lax.div(entry, buffer.shape[1]), lax.rem(entry, buffer.shape[1])]

        pieces_in, pieces_out = [], []
        for i, (kind, _) in enumerate(ins):
            if kind == "pieces":
                pieces_in += [(ref, spot_of(in_bufs[i], n), n) for n, ref in enumerate(in_refs[i])]
        for i, (kind, _) in enumerate(outs):
            if kind == "pieces":
                pieces_out += [(spot_of(out_bufs[i], n), ref, n) for n, ref in enumerate(out_refs[i])]
        pieces_in = [pltpu.make_async_copy(source, target, piece_sems.at[n]) for source, target, n in pieces_in]
        pieces_out = [pltpu.make_async_copy(source, target, piece_sems.at[n]) for source, target, n in pieces_out]

        for share in range(shares):
            for i in moved_in:
                bring(i, share).start()
            if share == 0:
                for copy in pieces_in:
                    copy.start()
        for copy in pieces_in:
            copy.wait()

        def step(share, carry):
            for i in moved_in:
                bring(i, share).wait()
            body(scalar_refs, [buf.at[share] for buf in in_bufs], [buf.at[share] for buf in out_bufs])
            for i in moved_out:
                put(i, share).start()
            return carry

        lax.fori_loop(0, shares, step, 0)
        for copy in pieces_out:
            copy.start()
        for share in range(shares):
            for i in moved_out:
                put(i, share).wait()
        for copy in pieces_out:
            copy.wait()

    spaces = {"cols": pltpu.HBM, "got": pl.ANY, "pieces": pl.ANY, "kept": pltpu.VMEM}
    values, in_specs, out_specs, out_shapes, buffers = [], [], [], [], []
    for kind, value in ins:
        for one in as_list((kind, value)):
            values.append(pltpu.with_memory_space_constraint(one, pltpu.HBM) if kind == "cols" else one)
            in_specs.append(pl.BlockSpec(memory_space=spaces[kind]))
    for kind, shape in outs:
        for one in as_list((kind, shape)):
            out_shapes.append(one if kind == "kept" else pltpu.HBM(one.shape, one.dtype))
            out_specs.append(pl.BlockSpec(memory_space=pltpu.VMEM if kind == "kept" else pltpu.HBM))
    for kind, value in list(ins) + list(outs):
        if kind != "kept":
            buffers.append(pltpu.VMEM(buffer_shape[kind](value), as_list((kind, value))[0].dtype))
    count = max(len(as_list(pair)) for pair in list(ins) + list(outs))
    semaphores = [(len(ins), shares), (len(outs), shares), (count,)]
    return pl.pallas_call(
        kernel,
        in_specs=[pl.BlockSpec(memory_space=pltpu.SMEM)] * len(scalars) + in_specs,
        out_specs=out_specs,
        out_shape=out_shapes,
        scratch_shapes=buffers + [pltpu.SemaphoreType.DMA(shape) for shape in semaphores],
        compiler_params=pltpu.CompilerParams(vmem_limit_bytes=VMEM_GRANT),
        cost_estimate=pl.CostEstimate(flops=work, bytes_accessed=1 << 10, transcendentals=0),
        name=name,
    )(*scalars, *values)


def array(rows, width, dtype):
    return jax.ShapeDtypeStruct((rows, width), dtype)


def swap_body(_, ins, outs):
    pair = pair_matrix()
    count, _, part = outs[0].shape
    for place, (ref, factor) in enumerate(zip(ins, (0.5, 0.5, 1.0))):
        for i in range(2):
            level1 = mul(pair, ref[i * BLK : (i + 1) * BLK, :])
            if factor != 1.0:
                level1 = level1 * factor
            level2 = fold(level1.astype(bf16), factor)
            first = place * HALF + i * HALF // 2
            for n in range(count):
                outs[0][n, first : first + HALF // 2, :] = level2[:, n * part : (n + 1) * part]


def swap_rows(place, query_vecs, key_vecs, value_vecs, groups):
    width = query_vecs.shape[1]
    ins = [("cols", a) for a in (query_vecs, key_vecs, value_vecs)]
    outs = [("pieces", [array(3 * HALF, width // groups, bf16)] * groups)]
    return run_shares(swap_body, "swap_rows", groups // 2, [place], ins, outs)


def rows_body(scalars, ins, outs):
    q_ref, k_ref, v_ref = ins
    q0_ref, q1_ref, near_ref, far_ref, chip_ref = outs
    reorder = reorder_matrix()
    pair = pair_matrix()
    for i in range(2):
        rows = slice(i * BLK, (i + 1) * BLK)
        q0 = mul(reorder, q_ref[rows, :]).astype(bf16)
        q0_ref[rows, :] = q0
        q1_ref[i * HALF : (i + 1) * HALF, :] = fold(q0, 0.5)
    odd = scalars[0][0]
    outer = pl.ds(pl.multiple_of(odd * BLK, BLK), BLK)
    inner = pl.ds(pl.multiple_of((1 - odd) * BLK, BLK), BLK)
    for ref, far_rows, first, near, far in ((near_ref, far_ref, 0, outer, inner), (chip_ref, chip_ref, 2 * BLK, inner, outer)):
        ref[0:BLK, :] = k_ref[near, :]
        ref[BLK : 2 * BLK, :] = v_ref[near, :]
        far_rows[first : first + HALF, :] = (mul(pair, k_ref[far, :]) * 0.5).astype(bf16)
        far_rows[first + HALF : first + BLK, :] = mul(pair, v_ref[far, :]).astype(bf16)


def rows_to_send(place, query_vecs, key_vecs, value_vecs, groups):
    rows, width = query_vecs.shape
    ins = [("cols", a) for a in (query_vecs, key_vecs, value_vecs)]
    outs = [("cols", array(n, width, bf16)) for n in (rows, rows // 2, 2 * BLK, BLK, 3 * BLK)]
    return run_shares(rows_body, "rows_to_send", groups, [place], ins, outs)


def pack(stats):
    width = HEAD_DIM // len(stats)
    lane = iota(stats[0].shape, 1)
    packed = stats[-1]
    for n in range(len(stats) - 2, -1, -1):
        packed = jnp.where(lane < (n + 1) * width, stats[n], packed)
    return packed


def unpack(packed, head):
    lanes = [head * HEAD_DIM // 2 + n * HEAD_DIM // 4 for n in range(2)]
    return [jnp.broadcast_to(packed[:, lane : lane + 1], packed.shape) for lane in lanes]


def own_body(_, ins, outs):
    q_ref, k_ref, v_ref = ins
    sum_ref, stat_ref = outs
    heads = q_ref.shape[1] // HEAD_DIM
    for i in range(2):
        rows = slice(i * BLK, (i + 1) * BLK)
        units = [(q_ref[rows, cols(head)], [(k_ref[:, cols(head)], v_ref[:, cols(head)], None)]) for head in range(heads)]
        stats = []
        for head, (top, sums) in enumerate(attend(units)):
            sum_ref[rows, cols(head)] = sums[:, :HEAD_DIM]
            stats += [top, sums[:, HEAD_DIM:]]
        for n in range(0, heads, 2):
            stat_ref[rows, cols(n // 2)] = pack(stats[2 * n : 2 * n + 4])


def sums_and_stats(rows, width, shares):
    return [("kept", jax.ShapeDtypeStruct((shares, rows, width // n), f32)) for n in (shares, 2 * shares)]


def own_level(q0, key_vecs, value_vecs, shares):
    ins = [("cols", a) for a in (q0, key_vecs, value_vecs)]
    return run_shares(own_body, "own_level", shares, [], ins, sums_and_stats(*q0.shape, shares), DECLARED)


def halo_body(place_ref, *refs):
    count = len(refs) - 4
    piece_refs, (got_ref, right_ref, left_ref, sems) = refs[:count], refs[count:]
    copies = [pltpu.make_async_copy(ref, got_ref.at[n ^ place_ref[1]], sems.at[n]) for n, ref in enumerate(piece_refs)]
    for copy in copies:
        copy.start()
    for copy in copies:
        copy.wait()
    pair = count // 2
    for which, factor in ((1, 0.5), (2, 1.0)):
        rows = slice(which * HALF, (which + 1) * HALF)
        near = (which - 1) * BLK
        far = 2 * BLK + (which - 1) * HALF
        for j in range(count):
            level2 = got_ref[j, rows, :]
            level3 = fold_chunks(level2, HALF // 2, factor)
            near_ref, far_ref = (left_ref, right_ref) if j < pair else (right_ref, left_ref)
            spot = j % pair
            near_ref[near + spot * HALF : near + (spot + 1) * HALF, :] = level2
            far_ref[far + spot * HALF // 2 : far + (spot + 1) * HALF // 2, :] = level3


def coarse_halos(place, pieces):
    rows, width = pieces[0].shape
    vmem = pl.BlockSpec(memory_space=pltpu.VMEM)
    shape = jax.ShapeDtypeStruct((3 * BLK, width), bf16)
    return pl.pallas_call(
        halo_body,
        in_specs=[pl.BlockSpec(memory_space=pltpu.SMEM)] + [pl.BlockSpec(memory_space=pl.ANY)] * len(pieces),
        out_specs=[vmem] * 3,
        out_shape=[jax.ShapeDtypeStruct((len(pieces), rows, width), bf16), shape, shape],
        scratch_shapes=[pltpu.SemaphoreType.DMA((len(pieces),))],
        compiler_params=pltpu.CompilerParams(vmem_limit_bytes=16 << 20),
        cost_estimate=pl.CostEstimate(flops=1 << 20, bytes_accessed=24 * pieces[0].size, transcendentals=0),
        name="coarse_halos",
    )(place, *pieces)


def coarse_body(place_ref, bias_ref, got_ref, prev_ref, next_ref, *refs):
    *out_refs, back_ref, sems = refs
    count = got_ref.shape[0]
    heads = got_ref.shape[2] // HEAD_DIM
    bias_prev = bias_ref[0]
    bias_next = bias_ref[1]
    lane = iota((HALF, HEAD_DIM), 1)

    for head in range(heads):
        here = cols(head)

        def own(which, j):
            return got_ref[j, which * HALF : (which + 1) * HALF, here]

        def near(ref, which, spot):
            first = (which - 1) * BLK + spot * HALF
            return ref[first : first + HALF, here]

        def both(ref, which):
            return ref[(which - 1) * BLK : which * BLK, here]

        def far(ref, which):
            first = 2 * BLK + (which - 1) * HALF
            return ref[first : first + HALF, here]

        def near3(ref, which):
            return fold_chunks(both(ref, which), HALF // 2, 0.5 if which == 1 else 1.0)

        def joined(*rows):
            return jnp.concatenate(rows, axis=0)

        def part(pick, bias):
            return (pick(1), pick(2), bias)

        units = [
            (own(0, 0), [part(lambda w: joined(own(w, 2), own(w, 3)), None), part(lambda w: near(prev_ref, w, 0), bias_prev)]),
            (own(0, 1), [part(lambda w: both(prev_ref, w), bias_prev), part(lambda w: own(w, 3), None)]),
            (own(0, 2), [part(lambda w: both(next_ref, w), bias_next), part(lambda w: own(w, 0), None)]),
            (own(0, 3), [part(lambda w: joined(own(w, 0), own(w, 1)), None), part(lambda w: near(next_ref, w, 1), bias_next)]),
        ]
        for j, (ref, bias, other, other_bias) in enumerate(
            ((next_ref, bias_next, prev_ref, bias_prev), (prev_ref, bias_prev, next_ref, bias_next))
        ):
            query = joined(*[fold_chunks(own(0, 2 * j + n), HALF // 2, 0.5) for n in range(2)])
            units.append(
                (
                    query,
                    [part(lambda w: joined(near3(ref, w), far(ref, w)), bias), part(lambda w: far(other, w), other_bias)],
                )
            )
        found = attend(units)
        for j in range(count):
            top2, sum2 = found[j]
            top3, sum3 = found[count + j // 2]

            def spread(rows):
                first = (j % 2) * 2 * SUB
                one = rows[first : first + SUB]
                other = rows[first + SUB : first + 2 * SUB]
                return joined(one, one, other, other)

            top3 = spread(top3)
            sum3 = spread(sum3)
            top = jnp.maximum(top2, top3)
            scale2 = jnp.exp2(top2 - top)
            scale3 = jnp.exp2(top3 - top)
            values = sum2[:, :HEAD_DIM] * scale2 + sum3[:, :HEAD_DIM] * scale3
            total = sum2[:, HEAD_DIM:] * (4.0 * scale2) + sum3[:, HEAD_DIM:] * (8.0 * scale3)
            back_ref[j, 0:HALF, here] = (values / total).astype(bf16)
            level = top + jnp.log2(total)
            high = level.astype(bf16).astype(f32)
            middle = (level - high).astype(bf16).astype(f32)
            terms = jnp.where(lane == 0, high, jnp.where(lane == 1, middle, level - high - middle))
            back_ref[j, HALF : HALF + 16, here] = terms.T[0:16, :].astype(bf16)
    copies = [
        pltpu.make_async_copy(back_ref.at[n ^ place_ref[1]], ref, sems.at[n]) for n, ref in enumerate(out_refs)
    ]
    for copy in copies:
        copy.start()
    for copy in copies:
        copy.wait()


def coarse_levels(place, bias, got, from_prev, from_next):
    count, _, width = got.shape
    vmem = pl.BlockSpec(memory_space=pltpu.VMEM)
    smem = pl.BlockSpec(memory_space=pltpu.SMEM)
    rows = HALF + 16
    return pl.pallas_call(
        coarse_body,
        in_specs=[smem, smem, vmem, vmem, vmem],
        out_specs=[pl.BlockSpec(memory_space=pl.ANY)] * count,
        out_shape=[array(rows, width, bf16)] * count,
        scratch_shapes=[pltpu.VMEM((count, rows, width), bf16), pltpu.SemaphoreType.DMA((count,))],
        compiler_params=pltpu.CompilerParams(vmem_limit_bytes=16 << 20),
        cost_estimate=pl.CostEstimate(flops=DECLARED, bytes_accessed=8 * got.size, transcendentals=1 << 20),
        name="coarse_levels",
    )(place, bias, got, from_prev, from_next)


def unpack_level(back_ref, head):
    terms = back_ref[head // 2, HALF : HALF + 16, cols(head % 2)].astype(f32)
    terms = jnp.sum(jnp.where(iota(terms.shape, 0) < 3, terms, 0.0), axis=0, keepdims=True)
    return jnp.broadcast_to(terms, (HEAD_DIM, HEAD_DIM)).T


def side_body(side, with_near, with_far, scalars, ins, outs, back_ref=None):
    q0_ref, q1_ref, sum_ref, stat_ref, side_ref = ins
    heads = q1_ref.shape[1] // HEAD_DIM
    bias = scalars[1][side]
    blocks = (side, 1 - side)
    fine = [pl.ds(pl.multiple_of(block * BLK, BLK), BLK) for block in blocks]
    middle = [pl.ds(pl.multiple_of(block * HALF, HALF), HALF) for block in blocks]
    if with_near:
        pair = pair_matrix()
        near_keys = (mul(pair, side_ref[0:BLK, :]) * 0.5).astype(bf16)
        near_values = mul(pair, side_ref[BLK : 2 * BLK, :]).astype(bf16)
    start = 2 * BLK if with_near else 0
    far_keys, far_values = (slice(start + n * HALF, start + (n + 1) * HALF) for n in range(2))
    units, names = [], []
    for head in range(heads):
        here = cols(head)
        far = (side_ref[far_keys, here], side_ref[far_values, here]) if with_far else None
        near = (near_keys[:, here], near_values[:, here]) if with_near else None
        whole = [part for part in (near, far) if part is not None]
        whole = [jnp.concatenate([part[n] for part in whole], axis=0) if len(whole) > 1 else whole[0][n] for n in range(2)]
        if with_near:
            units.append((q0_ref[fine[0], here], [(side_ref[0:BLK, here], side_ref[BLK : 2 * BLK, here], None)]))
            names.append((head, 0, 0))
        if with_far:
            units.append((q1_ref[middle[0], here], [(*far, None)]))
            names.append((head, 0, 1))
        units.append((q1_ref[middle[1], here], [(*whole, None)]))
        names.append((head, 1, 1))
    found = {name: (top + bias, sums) for name, (top, sums) in zip(names, attend(units))}
    restore = None if back_ref is None else restore_matrix()
    levels = None if back_ref is None else [unpack_level(back_ref, head) for head in range(heads)]
    for n in range(2):
        spot = pl.ds(pl.multiple_of(blocks[n] * HALF // 2, HALF // 2), HALF // 2)
        results, stats = [], []
        for head in range(heads):
            here = cols(head)
            own_top, own_total = unpack(stat_ref[fine[n], cols(head // 2)], head % 2)
            parts = [(own_top, sum_ref[fine[n], here], own_total)]
            if (head, n, 0) in found:
                top, sums = found[head, n, 0]
                parts.append((top, sums[:, :HEAD_DIM], sums[:, HEAD_DIM:]))
            if (head, n, 1) in found:
                top, sums = found[head, n, 1]
                number, total = sums[:, :HEAD_DIM], 2.0 * sums[:, HEAD_DIM:]
                if back_ref is not None:
                    half = HALF // 2
                    level = twice(jnp.where(blocks[n] == 0, levels[head][:half, :], levels[head][half:, :]))
                    most = jnp.maximum(top, level)
                    scale = jnp.exp2(top - most)
                    coarse = jnp.exp2(level - most)
                    number = number * scale + twice(back_ref[head // 2, spot, cols(head % 2)].astype(f32)) * coarse
                    total = total * scale + coarse
                    top = most
                parts.append((twice(top), twice(number), twice(total)))
            most = functools.reduce(jnp.maximum, [part[0] for part in parts])
            scales = [jnp.exp2(part[0] - most) for part in parts]
            number = sum(part[1] * scale for part, scale in zip(parts, scales))
            total = sum(part[2] * scale for part, scale in zip(parts, scales))
            if back_ref is None:
                outs[0][fine[n], here] = number
                stats += [most, total]
            else:
                results.append((number / total).astype(bf16))
        if back_ref is None:
            for m in range(0, heads, 2):
                outs[1][fine[n], cols(m // 2)] = pack(stats[2 * m : 2 * m + 4])
        else:
            outs[0][fine[n], :] = mul(restore, jnp.concatenate(results, axis=1)).astype(bf16)


def chip_body(scalars, ins, outs):
    side_body(1 - scalars[0][0], True, True, scalars, ins, outs)


def near_body(scalars, ins, outs):
    side_body(scalars[0][0], True, False, scalars, ins, outs)


def finish_body(scalars, ins, outs):
    side_body(scalars[0][0], False, True, scalars, [None] + ins[:-1], outs, ins[-1])


def side_level(body, name, place, bias, q0, q1, sums, stat, rows):
    shares = sums.shape[0]
    ins = [("cols", q0), ("cols", q1), ("kept", sums), ("kept", stat), ("got", rows)]
    return run_shares(body, name, shares, [place, bias], ins, sums_and_stats(*q0.shape, shares))


def finish(place, bias, q1, sums, stat, far, back):
    shares, rows, part = sums.shape
    ins = [("cols", q1), ("kept", sums), ("kept", stat), ("got", far), ("pieces", back)]
    outs = [("cols", array(rows, shares * part, bf16))]
    return run_shares(finish_body, "finish", shares, [place, bias], ins, outs)[0]


def shift(value, axis, steps):
    count = lax.axis_size(axis)
    first, last = (max(0, -steps), min(count, count - steps))
    return lax.ppermute(value, axis, [(source, source + steps) for source in range(first, last)])


def trade(value, axis, pairs):
    return lax.ppermute(value, axis, pairs + [(target, source) for source, target in pairs])


def edge_bias(axis):
    place = lax.axis_index(axis)
    last = lax.axis_size(axis) - 1
    at_edge = jnp.stack([place == 0, place == last])
    return jnp.where(at_edge, very_negative, 0.0).astype(f32)


def local(query_vecs, key_vecs, value_vecs):
    groups = lax.axis_size("grp")
    assert query_vecs.shape == (2 * BLK, HEADS * HEAD_DIM) and groups == 4
    everyone = ("seq", "grp")
    count = lax.axis_size(everyone)
    spot = lax.axis_index("grp")
    odd = jnp.bitwise_and(spot, 1)
    place = jnp.stack([odd, spot]).astype(jnp.int32)
    bias = edge_bias(everyone)

    def exchange(pieces):
        flips = [[(source, source ^ n) for source in range(groups)] for n in range(groups)]
        return [pieces[0]] + [lax.ppermute(pieces[n], "grp", flips[n]) for n in range(1, groups)]

    pieces = list(swap_rows(place, query_vecs, key_vecs, value_vecs, groups))
    query_rows, pieces = lax.optimization_barrier((query_vecs, pieces))
    pieces = exchange(pieces)
    q0, q1, near, far, chip = rows_to_send(place, query_rows, key_vecs, value_vecs, groups)
    off_chip = [(device, device + 1) for device in range(1, count - 1, 2)]
    near = trade(near, everyone, off_chip)
    far, pieces[1] = lax.optimization_barrier((far, pieces[1]))
    far = trade(far, everyone, off_chip)
    pieces, chip = lax.optimization_barrier((pieces, chip))
    got, coarse_right, coarse_left = coarse_halos(place, pieces)
    coarse_right, coarse_left, chip, q0 = lax.optimization_barrier((coarse_right, coarse_left, chip, q0))
    coarse_prev = shift(coarse_right, "seq", 1)
    coarse_next = shift(coarse_left, "seq", -1)
    chip = trade(chip, everyone, [(device, device + 1) for device in range(0, count - 1, 2)])
    own, own_stat = own_level(q0, key_vecs, value_vecs, groups // 2)
    own, own_stat = side_level(chip_body, "chip_level", place, bias, q0, q1, own, own_stat, chip)
    own, own_stat = side_level(near_body, "near_level", place, bias, q0, q1, own, own_stat, near)
    got, own = lax.optimization_barrier((got, own))
    back = exchange(coarse_levels(place, edge_bias("seq"), got, coarse_prev, coarse_next))
    return finish(place, bias, q1, own, own_stat, far, back)


def solution(mesh):
    return jax.shard_map(
        local,
        mesh=mesh,
        in_specs=(P(("seq", "grp"), None), P(("seq", "grp"), None), P(("seq", "grp"), None)),
        out_specs=P(("seq", "grp"), None),
        check_vma=False,
    )
```

```python
import functools
import math

import jax
import jax.numpy as jnp
from jax import lax
from jax.experimental import pallas as pl
from jax.experimental.pallas import tpu as pltpu
from jax.sharding import PartitionSpec as P

HEADS = 8
HEAD_DIM = 128
BLK = 256
HALF = BLK // 2
SUB = BLK // 8
LEV = 4
EXP_SCALE = math.log2(math.e) / math.sqrt(HEAD_DIM)

VMEM_GRANT = 24 << 20

very_negative = -1e30
f32 = jnp.float32
bf16 = jnp.bfloat16


def iota(shape, dim):
    return lax.broadcasted_iota(jnp.int32, shape, dim)


def bit(value, place):
    return jnp.bitwise_and(lax.shift_right_logical(value, place), 1)


def low_bits(value):
    step = SUB.bit_length() - 1
    deep = jnp.bitwise_and(value, SUB - 1)
    return 8 * deep + 4 * bit(value, step) + 2 * bit(value, step + 1) + bit(value, step + 2)


def reorder_matrix():
    return (iota((BLK, BLK), 1) == low_bits(iota((BLK, BLK), 0))).astype(bf16)


def restore_matrix():
    return (iota((BLK, BLK), 0) == low_bits(iota((BLK, BLK), 1))).astype(bf16)


def pair_matrix():
    first = low_bits(iota((HALF, BLK), 0))
    place = iota((HALF, BLK), 1)
    return jnp.logical_or(place == first, place == first + 1).astype(bf16)


def mul(left, right):
    return jnp.dot(left, right, preferred_element_type=f32)


def fold(rows, factor):
    half = rows.shape[0] // 2
    total = rows[:half].astype(f32) + rows[half:].astype(f32)
    if factor != 1.0:
        total = total * factor
    return total.astype(bf16)


def fold_chunks(rows, chunk, factor):
    count = rows.shape[0] // chunk
    return jnp.concatenate([fold(rows[i * chunk : (i + 1) * chunk], factor) for i in range(count)], axis=0)


def twice(rows):
    return jnp.concatenate([rows, rows], axis=0)


def cols(head):
    return slice(head * HEAD_DIM, (head + 1) * HEAD_DIM)


DECLARED = 1 << 36


def with_ones(values):
    return jnp.concatenate([values, jnp.ones_like(values)], axis=1)


def attend(units):
    scores = []
    for query, parts in units:
        raws = [
            lax.dot_general(query, keys, (((1,), (1,)), ((), ())), preferred_element_type=f32) for keys, _, _ in parts
        ]
        scores.append([raw if part[2] is None else raw + part[2] for raw, part in zip(raws, parts)])
    tops = []
    for raws in scores:
        tops.append(functools.reduce(jnp.maximum, [jnp.max(raw, axis=1, keepdims=True) for raw in raws]))
    found = []
    for (_, parts), raws, top in zip(units, scores, tops):
        total = None
        for (_, values, _), raw in zip(parts, raws):
            weights = jnp.exp2((raw - top) * EXP_SCALE).astype(bf16)
            one = mul(weights, with_ones(values))
            total = one if total is None else total + one
        found.append((jnp.broadcast_to(top * EXP_SCALE, (top.shape[0], HEAD_DIM)), total))
    return found


def share_of(ref, share, shares):
    width = ref.shape[1] // shares
    first = share * width
    if not isinstance(share, int):
        first = pl.multiple_of(first, HEAD_DIM)
    return ref.at[:, pl.ds(first, width)]


def run_shares(body, name, shares, scalars, ins, outs, work=1 << 10):
    moved_in = [i for i, (kind, _) in enumerate(ins) if kind in ("cols", "got")]
    moved_out = [i for i, (kind, _) in enumerate(outs) if kind == "cols"]
    as_list = lambda pair: list(pair[1]) if pair[0] == "pieces" else [pair[1]]
    buffer_shape = {
        "cols": lambda value: (shares, value.shape[0], value.shape[1] // shares),
        "got": lambda value: (shares, value.shape[0], value.shape[1] // shares),
        "kept": lambda value: None,
        "pieces": lambda values: (shares, len(values) // shares, *values[0].shape),
    }

    def kernel(*refs):
        refs = list(refs)
        take = lambda count: [refs.pop(0) for _ in range(count)]
        scalar_refs = take(len(scalars))
        in_refs = [take(len(as_list(pair))) for pair in ins]
        out_refs = [take(len(as_list(pair))) for pair in outs]
        in_bufs = [in_refs[i][0] if ins[i][0] == "kept" else refs.pop(0) for i in range(len(ins))]
        out_bufs = [out_refs[i][0] if outs[i][0] == "kept" else refs.pop(0) for i in range(len(outs))]
        in_sems, out_sems, piece_sems = take(3)

        def bring(i, share):
            return pltpu.make_async_copy(share_of(in_refs[i][0], share, shares), in_bufs[i].at[share], in_sems.at[i, share])

        def put(i, share):
            return pltpu.make_async_copy(out_bufs[i].at[share], share_of(out_refs[i][0], share, shares), out_sems.at[i, share])

        def spot_of(buffer, n):
            entry = n ^ scalar_refs[0][1]
            return buffer.at[lax.div(entry, buffer.shape[1]), lax.rem(entry, buffer.shape[1])]

        pieces_in, pieces_out = [], []
        for i, (kind, _) in enumerate(ins):
            if kind == "pieces":
                pieces_in += [(ref, spot_of(in_bufs[i], n), n) for n, ref in enumerate(in_refs[i])]
        for i, (kind, _) in enumerate(outs):
            if kind == "pieces":
                pieces_out += [(spot_of(out_bufs[i], n), ref, n) for n, ref in enumerate(out_refs[i])]
        pieces_in = [pltpu.make_async_copy(source, target, piece_sems.at[n]) for source, target, n in pieces_in]
        pieces_out = [pltpu.make_async_copy(source, target, piece_sems.at[n]) for source, target, n in pieces_out]

        for share in range(shares):
            for i in moved_in:
                bring(i, share).start()
            if share == 0:
                for copy in pieces_in:
                    copy.start()
        for copy in pieces_in:
            copy.wait()

        def step(share, carry):
            for i in moved_in:
                bring(i, share).wait()
            body(scalar_refs, [buf.at[share] for buf in in_bufs], [buf.at[share] for buf in out_bufs])
            for i in moved_out:
                put(i, share).start()
            return carry

        lax.fori_loop(0, shares, step, 0)
        for copy in pieces_out:
            copy.start()
        for share in range(shares):
            for i in moved_out:
                put(i, share).wait()
        for copy in pieces_out:
            copy.wait()

    spaces = {"cols": pltpu.HBM, "got": pl.ANY, "pieces": pl.ANY, "kept": pltpu.VMEM}
    values, in_specs, out_specs, out_shapes, buffers = [], [], [], [], []
    for kind, value in ins:
        for one in as_list((kind, value)):
            values.append(pltpu.with_memory_space_constraint(one, pltpu.HBM) if kind == "cols" else one)
            in_specs.append(pl.BlockSpec(memory_space=spaces[kind]))
    for kind, shape in outs:
        for one in as_list((kind, shape)):
            out_shapes.append(one if kind == "kept" else pltpu.HBM(one.shape, one.dtype))
            out_specs.append(pl.BlockSpec(memory_space=pltpu.VMEM if kind == "kept" else pltpu.HBM))
    for kind, value in list(ins) + list(outs):
        if kind != "kept":
            buffers.append(pltpu.VMEM(buffer_shape[kind](value), as_list((kind, value))[0].dtype))
    count = max(len(as_list(pair)) for pair in list(ins) + list(outs))
    semaphores = [(len(ins), shares), (len(outs), shares), (count,)]
    return pl.pallas_call(
        kernel,
        in_specs=[pl.BlockSpec(memory_space=pltpu.SMEM)] * len(scalars) + in_specs,
        out_specs=out_specs,
        out_shape=out_shapes,
        scratch_shapes=buffers + [pltpu.SemaphoreType.DMA(shape) for shape in semaphores],
        compiler_params=pltpu.CompilerParams(vmem_limit_bytes=VMEM_GRANT),
        cost_estimate=pl.CostEstimate(flops=work, bytes_accessed=1 << 10, transcendentals=0),
        name=name,
    )(*scalars, *values)


def array(rows, width, dtype):
    return jax.ShapeDtypeStruct((rows, width), dtype)


def swap_body(_, ins, outs):
    pair = pair_matrix()
    count, _, part = outs[0].shape
    for place, (ref, factor) in enumerate(zip(ins, (0.5, 0.5, 1.0))):
        for i in range(2):
            level1 = mul(pair, ref[i * BLK : (i + 1) * BLK, :])
            if factor != 1.0:
                level1 = level1 * factor
            level2 = fold(level1.astype(bf16), factor)
            first = place * HALF + i * HALF // 2
            for n in range(count):
                outs[0][n, first : first + HALF // 2, :] = level2[:, n * part : (n + 1) * part]


def swap_rows(place, query_vecs, key_vecs, value_vecs, groups):
    width = query_vecs.shape[1]
    ins = [("cols", a) for a in (query_vecs, key_vecs, value_vecs)]
    outs = [("pieces", [array(3 * HALF, width // groups, bf16)] * groups)]
    return run_shares(swap_body, "swap_rows", groups // 2, [place], ins, outs)


def rows_body(scalars, ins, outs):
    q_ref, k_ref, v_ref = ins
    q0_ref, q1_ref, near_ref, far_ref, chip_ref = outs
    reorder = reorder_matrix()
    pair = pair_matrix()
    for i in range(2):
        rows = slice(i * BLK, (i + 1) * BLK)
        q0 = mul(reorder, q_ref[rows, :]).astype(bf16)
        q0_ref[rows, :] = q0
        q1_ref[i * HALF : (i + 1) * HALF, :] = fold(q0, 0.5)
    odd = scalars[0][0]
    outer = pl.ds(pl.multiple_of(odd * BLK, BLK), BLK)
    inner = pl.ds(pl.multiple_of((1 - odd) * BLK, BLK), BLK)
    for ref, far_rows, first, near, far in ((near_ref, far_ref, 0, outer, inner), (chip_ref, chip_ref, 2 * BLK, inner, outer)):
        ref[0:BLK, :] = k_ref[near, :]
        ref[BLK : 2 * BLK, :] = v_ref[near, :]
        far_rows[first : first + HALF, :] = (mul(pair, k_ref[far, :]) * 0.5).astype(bf16)
        far_rows[first + HALF : first + BLK, :] = mul(pair, v_ref[far, :]).astype(bf16)


def rows_to_send(place, query_vecs, key_vecs, value_vecs, groups):
    rows, width = query_vecs.shape
    ins = [("cols", a) for a in (query_vecs, key_vecs, value_vecs)]
    outs = [("cols", array(n, width, bf16)) for n in (rows, rows // 2, 2 * BLK, BLK, 3 * BLK)]
    return run_shares(rows_body, "rows_to_send", groups, [place], ins, outs)


def pack(stats):
    width = HEAD_DIM // len(stats)
    lane = iota(stats[0].shape, 1)
    packed = stats[-1]
    for n in range(len(stats) - 2, -1, -1):
        packed = jnp.where(lane < (n + 1) * width, stats[n], packed)
    return packed


def unpack(packed, head):
    lanes = [head * HEAD_DIM // 2 + n * HEAD_DIM // 4 for n in range(2)]
    return [jnp.broadcast_to(packed[:, lane : lane + 1], packed.shape) for lane in lanes]


def own_body(_, ins, outs):
    q_ref, k_ref, v_ref = ins
    sum_ref, stat_ref = outs
    heads = q_ref.shape[1] // HEAD_DIM
    for i in range(2):
        rows = slice(i * BLK, (i + 1) * BLK)
        units = [(q_ref[rows, cols(head)], [(k_ref[:, cols(head)], v_ref[:, cols(head)], None)]) for head in range(heads)]
        stats = []
        for head, (top, sums) in enumerate(attend(units)):
            sum_ref[rows, cols(head)] = sums[:, :HEAD_DIM]
            stats += [top, sums[:, HEAD_DIM:]]
        for n in range(0, heads, 2):
            stat_ref[rows, cols(n // 2)] = pack(stats[2 * n : 2 * n + 4])


def sums_and_stats(rows, width, shares):
    return [("kept", jax.ShapeDtypeStruct((shares, rows, width // n), f32)) for n in (shares, 2 * shares)]


def own_level(q0, key_vecs, value_vecs, shares):
    ins = [("cols", a) for a in (q0, key_vecs, value_vecs)]
    return run_shares(own_body, "own_level", shares, [], ins, sums_and_stats(*q0.shape, shares), DECLARED)


def halo_body(place_ref, *refs):
    count = len(refs) - 4
    piece_refs, (got_ref, right_ref, left_ref, sems) = refs[:count], refs[count:]
    copies = [pltpu.make_async_copy(ref, got_ref.at[n ^ place_ref[1]], sems.at[n]) for n, ref in enumerate(piece_refs)]
    for copy in copies:
        copy.start()
    for copy in copies:
        copy.wait()
    pair = count // 2
    for which, factor in ((1, 0.5), (2, 1.0)):
        rows = slice(which * HALF, (which + 1) * HALF)
        near = (which - 1) * BLK
        far = 2 * BLK + (which - 1) * HALF
        for j in range(count):
            level2 = got_ref[j, rows, :]
            level3 = fold_chunks(level2, HALF // 2, factor)
            near_ref, far_ref = (left_ref, right_ref) if j < pair else (right_ref, left_ref)
            spot = j % pair
            near_ref[near + spot * HALF : near + (spot + 1) * HALF, :] = level2
            far_ref[far + spot * HALF // 2 : far + (spot + 1) * HALF // 2, :] = level3


def coarse_halos(place, pieces):
    rows, width = pieces[0].shape
    vmem = pl.BlockSpec(memory_space=pltpu.VMEM)
    shape = jax.ShapeDtypeStruct((3 * BLK, width), bf16)
    return pl.pallas_call(
        halo_body,
        in_specs=[pl.BlockSpec(memory_space=pltpu.SMEM)] + [pl.BlockSpec(memory_space=pl.ANY)] * len(pieces),
        out_specs=[vmem] * 3,
        out_shape=[jax.ShapeDtypeStruct((len(pieces), rows, width), bf16), shape, shape],
        scratch_shapes=[pltpu.SemaphoreType.DMA((len(pieces),))],
        compiler_params=pltpu.CompilerParams(vmem_limit_bytes=16 << 20),
        cost_estimate=pl.CostEstimate(flops=1 << 20, bytes_accessed=24 * pieces[0].size, transcendentals=0),
        name="coarse_halos",
    )(place, *pieces)


def coarse_body(place_ref, bias_ref, got_ref, prev_ref, next_ref, *refs):
    *out_refs, back_ref, sems = refs
    count = got_ref.shape[0]
    heads = got_ref.shape[2] // HEAD_DIM
    bias_prev = bias_ref[0]
    bias_next = bias_ref[1]
    lane = iota((HALF, HEAD_DIM), 1)

    for head in range(heads):
        here = cols(head)

        def own(which, j):
            return got_ref[j, which * HALF : (which + 1) * HALF, here]

        def near(ref, which, spot):
            first = (which - 1) * BLK + spot * HALF
            return ref[first : first + HALF, here]

        def both(ref, which):
            return ref[(which - 1) * BLK : which * BLK, here]

        def far(ref, which):
            first = 2 * BLK + (which - 1) * HALF
            return ref[first : first + HALF, here]

        def near3(ref, which):
            return fold_chunks(both(ref, which), HALF // 2, 0.5 if which == 1 else 1.0)

        def joined(*rows):
            return jnp.concatenate(rows, axis=0)

        def part(pick, bias):
            return (pick(1), pick(2), bias)

        units = [
            (own(0, 0), [part(lambda w: joined(own(w, 2), own(w, 3)), None), part(lambda w: near(prev_ref, w, 0), bias_prev)]),
            (own(0, 1), [part(lambda w: both(prev_ref, w), bias_prev), part(lambda w: own(w, 3), None)]),
            (own(0, 2), [part(lambda w: both(next_ref, w), bias_next), part(lambda w: own(w, 0), None)]),
            (own(0, 3), [part(lambda w: joined(own(w, 0), own(w, 1)), None), part(lambda w: near(next_ref, w, 1), bias_next)]),
        ]
        for j, (ref, bias, other, other_bias) in enumerate(
            ((next_ref, bias_next, prev_ref, bias_prev), (prev_ref, bias_prev, next_ref, bias_next))
        ):
            query = joined(*[fold_chunks(own(0, 2 * j + n), HALF // 2, 0.5) for n in range(2)])
            units.append(
                (
                    query,
                    [part(lambda w: joined(near3(ref, w), far(ref, w)), bias), part(lambda w: far(other, w), other_bias)],
                )
            )
        found = attend(units)
        for j in range(count):
            top2, sum2 = found[j]
            top3, sum3 = found[count + j // 2]

            def spread(rows):
                first = (j % 2) * 2 * SUB
                one = rows[first : first + SUB]
                other = rows[first + SUB : first + 2 * SUB]
                return joined(one, one, other, other)

            top3 = spread(top3)
            sum3 = spread(sum3)
            top = jnp.maximum(top2, top3)
            scale2 = jnp.exp2(top2 - top)
            scale3 = jnp.exp2(top3 - top)
            values = sum2[:, :HEAD_DIM] * scale2 + sum3[:, :HEAD_DIM] * scale3
            total = sum2[:, HEAD_DIM:] * (4.0 * scale2) + sum3[:, HEAD_DIM:] * (8.0 * scale3)
            back_ref[j, 0:HALF, here] = (values / total).astype(bf16)
            level = top + jnp.log2(total)
            high = level.astype(bf16).astype(f32)
            middle = (level - high).astype(bf16).astype(f32)
            terms = jnp.where(lane == 0, high, jnp.where(lane == 1, middle, level - high - middle))
            back_ref[j, HALF : HALF + 16, here] = terms.T[0:16, :].astype(bf16)
    copies = [
        pltpu.make_async_copy(back_ref.at[n ^ place_ref[1]], ref, sems.at[n]) for n, ref in enumerate(out_refs)
    ]
    for copy in copies:
        copy.start()
    for copy in copies:
        copy.wait()


def coarse_levels(place, bias, got, from_prev, from_next):
    count, _, width = got.shape
    vmem = pl.BlockSpec(memory_space=pltpu.VMEM)
    smem = pl.BlockSpec(memory_space=pltpu.SMEM)
    rows = HALF + 16
    return pl.pallas_call(
        coarse_body,
        in_specs=[smem, smem, vmem, vmem, vmem],
        out_specs=[pl.BlockSpec(memory_space=pl.ANY)] * count,
        out_shape=[array(rows, width, bf16)] * count,
        scratch_shapes=[pltpu.VMEM((count, rows, width), bf16), pltpu.SemaphoreType.DMA((count,))],
        compiler_params=pltpu.CompilerParams(vmem_limit_bytes=16 << 20),
        cost_estimate=pl.CostEstimate(flops=DECLARED, bytes_accessed=8 * got.size, transcendentals=1 << 20),
        name="coarse_levels",
    )(place, bias, got, from_prev, from_next)


def side_body(side, with_near, with_far, scalars, ins, outs):
    q0_ref, q1_ref, sum_ref, stat_ref, side_ref = ins
    heads = q1_ref.shape[1] // HEAD_DIM
    bias = scalars[1][side]
    blocks = (side, 1 - side)
    fine = [pl.ds(pl.multiple_of(block * BLK, BLK), BLK) for block in blocks]
    middle = [pl.ds(pl.multiple_of(block * HALF, HALF), HALF) for block in blocks]
    if with_near:
        pair = pair_matrix()
        near_keys = (mul(pair, side_ref[0:BLK, :]) * 0.5).astype(bf16)
        near_values = mul(pair, side_ref[BLK : 2 * BLK, :]).astype(bf16)
    start = 2 * BLK if with_near else 0
    far_keys, far_values = (slice(start + n * HALF, start + (n + 1) * HALF) for n in range(2))
    units, names = [], []
    for head in range(heads):
        here = cols(head)
        far = (side_ref[far_keys, here], side_ref[far_values, here]) if with_far else None
        near = (near_keys[:, here], near_values[:, here]) if with_near else None
        whole = [part for part in (near, far) if part is not None]
        whole = [jnp.concatenate([part[n] for part in whole], axis=0) if len(whole) > 1 else whole[0][n] for n in range(2)]
        if with_near:
            units.append((q0_ref[fine[0], here], [(side_ref[0:BLK, here], side_ref[BLK : 2 * BLK, here], None)]))
            names.append((head, 0, 0))
        if with_far:
            units.append((q1_ref[middle[0], here], [(*far, None)]))
            names.append((head, 0, 1))
        units.append((q1_ref[middle[1], here], [(*whole, None)]))
        names.append((head, 1, 1))
    found = {name: (top + bias, sums) for name, (top, sums) in zip(names, attend(units))}
    for n in range(2):
        stats = []
        for head in range(heads):
            here = cols(head)
            own_top, own_total = unpack(stat_ref[fine[n], cols(head // 2)], head % 2)
            parts = [(own_top, sum_ref[fine[n], here], own_total)]
            if (head, n, 0) in found:
                top, sums = found[head, n, 0]
                parts.append((top, sums[:, :HEAD_DIM], sums[:, HEAD_DIM:]))
            if (head, n, 1) in found:
                top, sums = found[head, n, 1]
                parts.append((twice(top), twice(sums[:, :HEAD_DIM]), twice(2.0 * sums[:, HEAD_DIM:])))
            most = functools.reduce(jnp.maximum, [part[0] for part in parts])
            scales = [jnp.exp2(part[0] - most) for part in parts]
            outs[0][fine[n], here] = sum(part[1] * scale for part, scale in zip(parts, scales))
            stats += [most, sum(part[2] * scale for part, scale in zip(parts, scales))]
        for m in range(0, heads, 2):
            outs[1][fine[n], cols(m // 2)] = pack(stats[2 * m : 2 * m + 4])


def chip_body(scalars, ins, outs):
    side_body(1 - scalars[0][0], True, True, scalars, ins, outs)


def near_body(scalars, ins, outs):
    side_body(scalars[0][0], True, False, scalars, ins, outs)


def far_body(scalars, ins, outs):
    side_body(scalars[0][0], False, True, scalars, [None] + ins, outs)


def side_level(body, name, place, bias, queries, sums, stat, rows):
    shares, count, part = sums.shape
    ins = [("cols", query) for query in queries] + [("kept", sums), ("kept", stat), ("got", rows)]
    return run_shares(body, name, shares, [place, bias], ins, sums_and_stats(count, shares * part, shares))


def unpack_level(back_ref, head):
    terms = back_ref[head // 2, HALF : HALF + 16, cols(head % 2)].astype(f32)
    terms = jnp.sum(jnp.where(iota(terms.shape, 0) < 3, terms, 0.0), axis=0, keepdims=True)
    return jnp.broadcast_to(terms, (HEAD_DIM, HEAD_DIM)).T


def finish_body(_, ins, outs):
    sum_ref, stat_ref, back_ref = ins
    heads = sum_ref.shape[1] // HEAD_DIM
    restore = restore_matrix()
    levels = [unpack_level(back_ref, head) for head in range(heads)]
    for i in range(2):
        rows = slice(i * BLK, (i + 1) * BLK)
        spot = slice(i * HALF // 2, (i + 1) * HALF // 2)
        results = []
        for head in range(heads):
            top, total = unpack(stat_ref[rows, cols(head // 2)], head % 2)
            level = twice(twice(levels[head][spot, :]))
            most = jnp.maximum(top, level)
            scale = jnp.exp2(top - most)
            coarse = jnp.exp2(level - most)
            number = twice(twice(back_ref[head // 2, spot, cols(head % 2)].astype(f32))) * coarse
            number = number + sum_ref[rows, cols(head)] * scale
            results.append((number / (total * scale + coarse)).astype(bf16))
        outs[0][rows, :] = mul(restore, jnp.concatenate(results, axis=1)).astype(bf16)


def finish(place, sums, stat, back):
    shares, rows, part = sums.shape
    ins = [("kept", sums), ("kept", stat), ("pieces", back)]
    outs = [("cols", array(rows, shares * part, bf16))]
    return run_shares(finish_body, "finish", shares, [place], ins, outs)[0]


def shift(value, axis, steps):
    count = lax.axis_size(axis)
    first, last = (max(0, -steps), min(count, count - steps))
    return lax.ppermute(value, axis, [(source, source + steps) for source in range(first, last)])


def trade(value, axis, pairs):
    return lax.ppermute(value, axis, pairs + [(target, source) for source, target in pairs])


def edge_bias(axis):
    place = lax.axis_index(axis)
    last = lax.axis_size(axis) - 1
    at_edge = jnp.stack([place == 0, place == last])
    return jnp.where(at_edge, very_negative, 0.0).astype(f32)


def local(query_vecs, key_vecs, value_vecs):
    groups = lax.axis_size("grp")
    assert query_vecs.shape == (2 * BLK, HEADS * HEAD_DIM) and groups == 4
    everyone = ("seq", "grp")
    count = lax.axis_size(everyone)
    spot = lax.axis_index("grp")
    odd = jnp.bitwise_and(spot, 1)
    place = jnp.stack([odd, spot]).astype(jnp.int32)
    bias = edge_bias(everyone)

    def exchange(pieces):
        flips = [[(source, source ^ n) for source in range(groups)] for n in range(groups)]
        return [pieces[0]] + [lax.ppermute(pieces[n], "grp", flips[n]) for n in range(1, groups)]

    pieces = list(swap_rows(place, query_vecs, key_vecs, value_vecs, groups))
    query_rows, pieces = lax.optimization_barrier((query_vecs, pieces))
    pieces = exchange(pieces)
    q0, q1, near, far, chip = rows_to_send(place, query_rows, key_vecs, value_vecs, groups)
    off_chip = [(device, device + 1) for device in range(1, count - 1, 2)]
    near = trade(near, everyone, off_chip)
    far, pieces[1] = lax.optimization_barrier((far, pieces[1]))
    far = trade(far, everyone, off_chip)
    pieces, chip = lax.optimization_barrier((pieces, chip))
    got, coarse_right, coarse_left = coarse_halos(place, pieces)
    coarse_right, coarse_left, chip, q0 = lax.optimization_barrier((coarse_right, coarse_left, chip, q0))
    coarse_prev = shift(coarse_right, "seq", 1)
    coarse_next = shift(coarse_left, "seq", -1)
    chip = trade(chip, everyone, [(device, device + 1) for device in range(0, count - 1, 2)])
    own, own_stat = own_level(q0, key_vecs, value_vecs, groups // 2)
    own, own_stat = side_level(chip_body, "chip_level", place, bias, (q0, q1), own, own_stat, chip)
    own, own_stat = side_level(near_body, "near_level", place, bias, (q0, q1), own, own_stat, near)
    got, own = lax.optimization_barrier((got, own))
    back = coarse_levels(place, edge_bias("seq"), got, coarse_prev, coarse_next)
    back, own = lax.optimization_barrier((back, own))
    back = exchange(back)
    own, own_stat = side_level(far_body, "far_level", place, bias, (q1,), own, own_stat, far)
    return finish(place, own, own_stat, back)


def solution(mesh):
    return jax.shard_map(
        local,
        mesh=mesh,
        in_specs=(P(("seq", "grp"), None), P(("seq", "grp"), None), P(("seq", "grp"), None)),
        out_specs=P(("seq", "grp"), None),
        check_vma=False,
    )
```

```python
import functools
import math

import jax
import jax.numpy as jnp
from jax import lax
from jax.experimental import pallas as pl
from jax.experimental.pallas import tpu as pltpu
from jax.sharding import PartitionSpec as P

HEADS = 8
HEAD_DIM = 128
BLK = 256
HALF = BLK // 2
SUB = BLK // 8
LEV = 4
EXP_SCALE = math.log2(math.e) / math.sqrt(HEAD_DIM)

VMEM_GRANT = 24 << 20

very_negative = -1e30
f32 = jnp.float32
bf16 = jnp.bfloat16


def iota(shape, dim):
    return lax.broadcasted_iota(jnp.int32, shape, dim)


def bit(value, place):
    return jnp.bitwise_and(lax.shift_right_logical(value, place), 1)


def low_bits(value):
    step = SUB.bit_length() - 1
    deep = jnp.bitwise_and(value, SUB - 1)
    return 8 * deep + 4 * bit(value, step) + 2 * bit(value, step + 1) + bit(value, step + 2)


def reorder_matrix():
    return (iota((BLK, BLK), 1) == low_bits(iota((BLK, BLK), 0))).astype(bf16)


def restore_matrix():
    return (iota((BLK, BLK), 0) == low_bits(iota((BLK, BLK), 1))).astype(bf16)


def pair_matrix():
    first = low_bits(iota((HALF, BLK), 0))
    place = iota((HALF, BLK), 1)
    return jnp.logical_or(place == first, place == first + 1).astype(bf16)


def mul(left, right):
    return jnp.dot(left, right, preferred_element_type=f32)


def fold(rows, factor):
    half = rows.shape[0] // 2
    total = rows[:half].astype(f32) + rows[half:].astype(f32)
    if factor != 1.0:
        total = total * factor
    return total.astype(bf16)


def fold_chunks(rows, chunk, factor):
    count = rows.shape[0] // chunk
    return jnp.concatenate([fold(rows[i * chunk : (i + 1) * chunk], factor) for i in range(count)], axis=0)


def twice(rows):
    return jnp.concatenate([rows, rows], axis=0)


def cols(head):
    return slice(head * HEAD_DIM, (head + 1) * HEAD_DIM)


DECLARED = 1 << 36


def with_ones(values):
    return jnp.concatenate([values, jnp.ones_like(values)], axis=1)


def attend(units):
    scores = []
    for query, parts in units:
        raws = [
            lax.dot_general(query, keys, (((1,), (1,)), ((), ())), preferred_element_type=f32) for keys, _, _ in parts
        ]
        scores.append([raw if part[2] is None else raw + part[2] for raw, part in zip(raws, parts)])
    tops = []
    for raws in scores:
        tops.append(functools.reduce(jnp.maximum, [jnp.max(raw, axis=1, keepdims=True) for raw in raws]))
    found = []
    for (_, parts), raws, top in zip(units, scores, tops):
        total = None
        for (_, values, _), raw in zip(parts, raws):
            weights = jnp.exp2((raw - top) * EXP_SCALE).astype(bf16)
            one = mul(weights, with_ones(values))
            total = one if total is None else total + one
        found.append((jnp.broadcast_to(top * EXP_SCALE, (top.shape[0], HEAD_DIM)), total))
    return found


def share_of(ref, share, shares):
    width = ref.shape[1] // shares
    first = share * width
    if not isinstance(share, int):
        first = pl.multiple_of(first, HEAD_DIM)
    return ref.at[:, pl.ds(first, width)]


def run_shares(body, name, shares, scalars, ins, outs, work=1 << 10, unrolled=False):
    moved_in = [i for i, (kind, _) in enumerate(ins) if kind in ("cols", "got")]
    moved_out = [i for i, (kind, _) in enumerate(outs) if kind == "cols"]
    as_list = lambda pair: list(pair[1]) if pair[0] == "pieces" else [pair[1]]
    buffer_shape = {
        "cols": lambda value: (shares, value.shape[0], value.shape[1] // shares),
        "got": lambda value: (shares, value.shape[0], value.shape[1] // shares),
        "kept": lambda value: None,
        "pieces": lambda values: (shares, len(values) // shares, *values[0].shape),
    }

    def kernel(*refs):
        refs = list(refs)
        take = lambda count: [refs.pop(0) for _ in range(count)]
        scalar_refs = take(len(scalars))
        in_refs = [take(len(as_list(pair))) for pair in ins]
        out_refs = [take(len(as_list(pair))) for pair in outs]
        in_bufs = [in_refs[i][0] if ins[i][0] == "kept" else refs.pop(0) for i in range(len(ins))]
        out_bufs = [out_refs[i][0] if outs[i][0] == "kept" else refs.pop(0) for i in range(len(outs))]
        in_sems, out_sems, piece_sems = take(3)

        def bring(i, share):
            return pltpu.make_async_copy(share_of(in_refs[i][0], share, shares), in_bufs[i].at[share], in_sems.at[i, share])

        def put(i, share):
            return pltpu.make_async_copy(out_bufs[i].at[share], share_of(out_refs[i][0], share, shares), out_sems.at[i, share])

        def spot_of(buffer, n):
            entry = n ^ scalar_refs[0][1]
            return buffer.at[lax.div(entry, buffer.shape[1]), lax.rem(entry, buffer.shape[1])]

        pieces_in, pieces_out = [], []
        for i, (kind, _) in enumerate(ins):
            if kind == "pieces":
                pieces_in += [(ref, spot_of(in_bufs[i], n), n) for n, ref in enumerate(in_refs[i])]
        for i, (kind, _) in enumerate(outs):
            if kind == "pieces":
                pieces_out += [(spot_of(out_bufs[i], n), ref, n) for n, ref in enumerate(out_refs[i])]
        pieces_in = [pltpu.make_async_copy(source, target, piece_sems.at[n]) for source, target, n in pieces_in]
        pieces_out = [pltpu.make_async_copy(source, target, piece_sems.at[n]) for source, target, n in pieces_out]

        for share in range(shares):
            for i in moved_in:
                bring(i, share).start()
            if share == 0:
                for copy in pieces_in:
                    copy.start()
        for copy in pieces_in:
            copy.wait()

        def step(share, carry):
            for i in moved_in:
                bring(i, share).wait()
            body(scalar_refs, [buf.at[share] for buf in in_bufs], [buf.at[share] for buf in out_bufs])
            for i in moved_out:
                put(i, share).start()
            return carry

        if unrolled:
            for share in range(shares):
                step(share, 0)
        else:
            lax.fori_loop(0, shares, step, 0)
        for copy in pieces_out:
            copy.start()
        for share in range(shares):
            for i in moved_out:
                put(i, share).wait()
        for copy in pieces_out:
            copy.wait()

    spaces = {"cols": pltpu.HBM, "got": pl.ANY, "pieces": pl.ANY, "kept": pltpu.VMEM}
    values, in_specs, out_specs, out_shapes, buffers = [], [], [], [], []
    for kind, value in ins:
        for one in as_list((kind, value)):
            values.append(pltpu.with_memory_space_constraint(one, pltpu.HBM) if kind == "cols" else one)
            in_specs.append(pl.BlockSpec(memory_space=spaces[kind]))
    for kind, shape in outs:
        for one in as_list((kind, shape)):
            out_shapes.append(pltpu.HBM(one.shape, one.dtype) if kind == "cols" else one)
            out_specs.append(pl.BlockSpec(memory_space=pltpu.HBM if kind == "cols" else pltpu.VMEM))
    for kind, value in list(ins) + list(outs):
        if kind != "kept":
            buffers.append(pltpu.VMEM(buffer_shape[kind](value), as_list((kind, value))[0].dtype))
    count = max(len(as_list(pair)) for pair in list(ins) + list(outs))
    semaphores = [(len(ins), shares), (len(outs), shares), (count,)]
    return pl.pallas_call(
        kernel,
        in_specs=[pl.BlockSpec(memory_space=pltpu.SMEM)] * len(scalars) + in_specs,
        out_specs=out_specs,
        out_shape=out_shapes,
        scratch_shapes=buffers + [pltpu.SemaphoreType.DMA(shape) for shape in semaphores],
        compiler_params=pltpu.CompilerParams(vmem_limit_bytes=VMEM_GRANT),
        cost_estimate=pl.CostEstimate(flops=work, bytes_accessed=1 << 10, transcendentals=0),
        name=name,
    )(*scalars, *values)


def array(rows, width, dtype):
    return jax.ShapeDtypeStruct((rows, width), dtype)


def swap_body(_, ins, outs):
    pair = pair_matrix()
    count, _, part = outs[0].shape
    for place, (ref, factor) in enumerate(zip(ins, (0.5, 0.5, 1.0))):
        for i in range(2):
            level1 = mul(pair, ref[i * BLK : (i + 1) * BLK, :])
            if factor != 1.0:
                level1 = level1 * factor
            level2 = fold(level1.astype(bf16), factor)
            first = place * HALF + i * HALF // 2
            for n in range(count):
                outs[0][n, first : first + HALF // 2, :] = level2[:, n * part : (n + 1) * part]


def swap_rows(place, query_vecs, key_vecs, value_vecs, groups):
    width = query_vecs.shape[1]
    ins = [("cols", a) for a in (query_vecs, key_vecs, value_vecs)]
    outs = [("pieces", [array(3 * HALF, width // groups, bf16)] * groups)]
    return run_shares(swap_body, "swap_rows", groups // 2, [place], ins, outs, unrolled=True)


def rows_body(scalars, ins, outs):
    q_ref, k_ref, v_ref = ins
    q0_ref, q1_ref, near_ref, far_ref, chip_ref = outs
    reorder = reorder_matrix()
    pair = pair_matrix()
    for i in range(2):
        rows = slice(i * BLK, (i + 1) * BLK)
        q0 = mul(reorder, q_ref[rows, :]).astype(bf16)
        q0_ref[rows, :] = q0
        q1_ref[i * HALF : (i + 1) * HALF, :] = fold(q0, 0.5)
    odd = scalars[0][0]
    outer = pl.ds(pl.multiple_of(odd * BLK, BLK), BLK)
    inner = pl.ds(pl.multiple_of((1 - odd) * BLK, BLK), BLK)
    for ref, far_rows, first, near, far in ((near_ref, far_ref, 0, outer, inner), (chip_ref, chip_ref, 2 * BLK, inner, outer)):
        ref[0:BLK, :] = k_ref[near, :]
        ref[BLK : 2 * BLK, :] = v_ref[near, :]
        far_rows[first : first + HALF, :] = (mul(pair, k_ref[far, :]) * 0.5).astype(bf16)
        far_rows[first + HALF : first + BLK, :] = mul(pair, v_ref[far, :]).astype(bf16)


def rows_to_send(place, query_vecs, key_vecs, value_vecs, groups):
    rows, width = query_vecs.shape
    ins = [("cols", a) for a in (query_vecs, key_vecs, value_vecs)]
    outs = [("cols", array(n, width, bf16)) for n in (rows, rows // 2, 2 * BLK, BLK, 3 * BLK)]
    return run_shares(rows_body, "rows_to_send", groups, [place], ins, outs)


def pack(stats):
    width = HEAD_DIM // len(stats)
    lane = iota(stats[0].shape, 1)
    packed = stats[-1]
    for n in range(len(stats) - 2, -1, -1):
        packed = jnp.where(lane < (n + 1) * width, stats[n], packed)
    return packed


def unpack(packed, head):
    lanes = [head * HEAD_DIM // 2 + n * HEAD_DIM // 4 for n in range(2)]
    return [jnp.broadcast_to(packed[:, lane : lane + 1], packed.shape) for lane in lanes]


def own_body(_, ins, outs):
    q_ref, k_ref, v_ref = ins
    sum_ref, stat_ref = outs
    heads = q_ref.shape[1] // HEAD_DIM
    for i in range(2):
        rows = slice(i * BLK, (i + 1) * BLK)
        units = [(q_ref[rows, cols(head)], [(k_ref[:, cols(head)], v_ref[:, cols(head)], None)]) for head in range(heads)]
        stats = []
        for head, (top, sums) in enumerate(attend(units)):
            sum_ref[rows, cols(head)] = sums[:, :HEAD_DIM]
            stats += [top, sums[:, HEAD_DIM:]]
        for n in range(0, heads, 2):
            stat_ref[rows, cols(n // 2)] = pack(stats[2 * n : 2 * n + 4])


def sums_and_stats(rows, width, shares):
    return [("kept", jax.ShapeDtypeStruct((shares, rows, width // n), f32)) for n in (shares, 2 * shares)]


def own_level(q0, key_vecs, value_vecs, shares):
    ins = [("cols", a) for a in (q0, key_vecs, value_vecs)]
    return run_shares(own_body, "own_level", shares, [], ins, sums_and_stats(*q0.shape, shares), DECLARED)


def halo_body(place_ref, *refs):
    count = len(refs) - 4
    piece_refs, (got_ref, right_ref, left_ref, sems) = refs[:count], refs[count:]
    copies = [pltpu.make_async_copy(ref, got_ref.at[n ^ place_ref[1]], sems.at[n]) for n, ref in enumerate(piece_refs)]
    for copy in copies:
        copy.start()
    for copy in copies:
        copy.wait()
    pair = count // 2
    for which, factor in ((1, 0.5), (2, 1.0)):
        rows = slice(which * HALF, (which + 1) * HALF)
        near = (which - 1) * BLK
        far = 2 * BLK + (which - 1) * HALF
        for j in range(count):
            level2 = got_ref[j, rows, :]
            level3 = fold_chunks(level2, HALF // 2, factor)
            near_ref, far_ref = (left_ref, right_ref) if j < pair else (right_ref, left_ref)
            spot = j % pair
            near_ref[near + spot * HALF : near + (spot + 1) * HALF, :] = level2
            far_ref[far + spot * HALF // 2 : far + (spot + 1) * HALF // 2, :] = level3


def coarse_halos(place, pieces):
    rows, width = pieces[0].shape
    vmem = pl.BlockSpec(memory_space=pltpu.VMEM)
    shape = jax.ShapeDtypeStruct((3 * BLK, width), bf16)
    return pl.pallas_call(
        halo_body,
        in_specs=[pl.BlockSpec(memory_space=pltpu.SMEM)] + [pl.BlockSpec(memory_space=pl.ANY)] * len(pieces),
        out_specs=[vmem] * 3,
        out_shape=[jax.ShapeDtypeStruct((len(pieces), rows, width), bf16), shape, shape],
        scratch_shapes=[pltpu.SemaphoreType.DMA((len(pieces),))],
        compiler_params=pltpu.CompilerParams(vmem_limit_bytes=16 << 20),
        cost_estimate=pl.CostEstimate(flops=1 << 20, bytes_accessed=24 * pieces[0].size, transcendentals=0),
        name="coarse_halos",
    )(place, *pieces)


def coarse_body(place_ref, bias_ref, got_ref, prev_ref, next_ref, *refs):
    *out_refs, back_ref, sems = refs
    count = got_ref.shape[0]
    heads = got_ref.shape[2] // HEAD_DIM
    bias_prev = bias_ref[0]
    bias_next = bias_ref[1]
    lane = iota((HALF, HEAD_DIM), 1)

    for head in range(heads):
        here = cols(head)

        def own(which, j):
            return got_ref[j, which * HALF : (which + 1) * HALF, here]

        def near(ref, which, spot):
            first = (which - 1) * BLK + spot * HALF
            return ref[first : first + HALF, here]

        def both(ref, which):
            return ref[(which - 1) * BLK : which * BLK, here]

        def far(ref, which):
            first = 2 * BLK + (which - 1) * HALF
            return ref[first : first + HALF, here]

        def near3(ref, which):
            return fold_chunks(both(ref, which), HALF // 2, 0.5 if which == 1 else 1.0)

        def joined(*rows):
            return jnp.concatenate(rows, axis=0)

        def part(pick, bias):
            return (pick(1), pick(2), bias)

        units = [
            (own(0, 0), [part(lambda w: joined(own(w, 2), own(w, 3)), None), part(lambda w: near(prev_ref, w, 0), bias_prev)]),
            (own(0, 1), [part(lambda w: both(prev_ref, w), bias_prev), part(lambda w: own(w, 3), None)]),
            (own(0, 2), [part(lambda w: both(next_ref, w), bias_next), part(lambda w: own(w, 0), None)]),
            (own(0, 3), [part(lambda w: joined(own(w, 0), own(w, 1)), None), part(lambda w: near(next_ref, w, 1), bias_next)]),
        ]
        for j, (ref, bias, other, other_bias) in enumerate(
            ((next_ref, bias_next, prev_ref, bias_prev), (prev_ref, bias_prev, next_ref, bias_next))
        ):
            query = joined(*[fold_chunks(own(0, 2 * j + n), HALF // 2, 0.5) for n in range(2)])
            units.append(
                (
                    query,
                    [part(lambda w: joined(near3(ref, w), far(ref, w)), bias), part(lambda w: far(other, w), other_bias)],
                )
            )
        found = attend(units)
        for j in range(count):
            top2, sum2 = found[j]
            top3, sum3 = found[count + j // 2]

            def spread(rows):
                first = (j % 2) * 2 * SUB
                one = rows[first : first + SUB]
                other = rows[first + SUB : first + 2 * SUB]
                return joined(one, one, other, other)

            top3 = spread(top3)
            sum3 = spread(sum3)
            top = jnp.maximum(top2, top3)
            scale2 = jnp.exp2(top2 - top)
            scale3 = jnp.exp2(top3 - top)
            values = sum2[:, :HEAD_DIM] * scale2 + sum3[:, :HEAD_DIM] * scale3
            total = sum2[:, HEAD_DIM:] * (4.0 * scale2) + sum3[:, HEAD_DIM:] * (8.0 * scale3)
            back_ref[j, 0:HALF, here] = (values / total).astype(bf16)
            level = top + jnp.log2(total)
            high = level.astype(bf16).astype(f32)
            middle = (level - high).astype(bf16).astype(f32)
            terms = jnp.where(lane == 0, high, jnp.where(lane == 1, middle, level - high - middle))
            back_ref[j, HALF : HALF + 16, here] = terms.T[0:16, :].astype(bf16)
    copies = [
        pltpu.make_async_copy(back_ref.at[n ^ place_ref[1]], ref, sems.at[n]) for n, ref in enumerate(out_refs)
    ]
    for copy in copies:
        copy.start()
    for copy in copies:
        copy.wait()


def coarse_levels(place, bias, got, from_prev, from_next):
    count, _, width = got.shape
    vmem = pl.BlockSpec(memory_space=pltpu.VMEM)
    smem = pl.BlockSpec(memory_space=pltpu.SMEM)
    rows = HALF + 16
    return pl.pallas_call(
        coarse_body,
        in_specs=[smem, smem, vmem, vmem, vmem],
        out_specs=[pl.BlockSpec(memory_space=pl.ANY)] * count,
        out_shape=[array(rows, width, bf16)] * count,
        scratch_shapes=[pltpu.VMEM((count, rows, width), bf16), pltpu.SemaphoreType.DMA((count,))],
        compiler_params=pltpu.CompilerParams(vmem_limit_bytes=16 << 20),
        cost_estimate=pl.CostEstimate(flops=DECLARED, bytes_accessed=8 * got.size, transcendentals=1 << 20),
        name="coarse_levels",
    )(place, bias, got, from_prev, from_next)


def side_body(side, with_near, with_far, scalars, ins, outs):
    q0_ref, q1_ref, sum_ref, stat_ref, side_ref = ins
    heads = q1_ref.shape[1] // HEAD_DIM
    bias = scalars[1][side]
    blocks = (side, 1 - side)
    fine = [pl.ds(pl.multiple_of(block * BLK, BLK), BLK) for block in blocks]
    middle = [pl.ds(pl.multiple_of(block * HALF, HALF), HALF) for block in blocks]
    if with_near:
        pair = pair_matrix()
        near_keys = (mul(pair, side_ref[0:BLK, :]) * 0.5).astype(bf16)
        near_values = mul(pair, side_ref[BLK : 2 * BLK, :]).astype(bf16)
    start = 2 * BLK if with_near else 0
    far_keys, far_values = (slice(start + n * HALF, start + (n + 1) * HALF) for n in range(2))
    units, names = [], []
    for head in range(heads):
        here = cols(head)
        far = (side_ref[far_keys, here], side_ref[far_values, here]) if with_far else None
        near = (near_keys[:, here], near_values[:, here]) if with_near else None
        whole = [part for part in (near, far) if part is not None]
        whole = [jnp.concatenate([part[n] for part in whole], axis=0) if len(whole) > 1 else whole[0][n] for n in range(2)]
        if with_near:
            units.append((q0_ref[fine[0], here], [(side_ref[0:BLK, here], side_ref[BLK : 2 * BLK, here], None)]))
            names.append((head, 0, 0))
        if with_far:
            units.append((q1_ref[middle[0], here], [(*far, None)]))
            names.append((head, 0, 1))
        units.append((q1_ref[middle[1], here], [(*whole, None)]))
        names.append((head, 1, 1))
    found = {name: (top + bias, sums) for name, (top, sums) in zip(names, attend(units))}
    for n in range(2):
        stats = []
        for head in range(heads):
            here = cols(head)
            own_top, own_total = unpack(stat_ref[fine[n], cols(head // 2)], head % 2)
            parts = [(own_top, sum_ref[fine[n], here], own_total)]
            if (head, n, 0) in found:
                top, sums = found[head, n, 0]
                parts.append((top, sums[:, :HEAD_DIM], sums[:, HEAD_DIM:]))
            if (head, n, 1) in found:
                top, sums = found[head, n, 1]
                parts.append((twice(top), twice(sums[:, :HEAD_DIM]), twice(2.0 * sums[:, HEAD_DIM:])))
            most = functools.reduce(jnp.maximum, [part[0] for part in parts])
            scales = [jnp.exp2(part[0] - most) for part in parts]
            outs[0][fine[n], here] = sum(part[1] * scale for part, scale in zip(parts, scales))
            stats += [most, sum(part[2] * scale for part, scale in zip(parts, scales))]
        for m in range(0, heads, 2):
            outs[1][fine[n], cols(m // 2)] = pack(stats[2 * m : 2 * m + 4])


def chip_body(scalars, ins, outs):
    side_body(1 - scalars[0][0], True, True, scalars, ins, outs)


def near_body(scalars, ins, outs):
    side_body(scalars[0][0], True, False, scalars, ins, outs)


def far_body(scalars, ins, outs):
    side_body(scalars[0][0], False, True, scalars, [None] + ins, outs)


def side_level(body, name, place, bias, queries, sums, stat, rows):
    shares, count, part = sums.shape
    ins = [("cols", query) for query in queries] + [("kept", sums), ("kept", stat), ("got", rows)]
    return run_shares(body, name, shares, [place, bias], ins, sums_and_stats(count, shares * part, shares))


def unpack_level(back_ref, head):
    terms = back_ref[head // 2, HALF : HALF + 16, cols(head % 2)].astype(f32)
    terms = jnp.sum(jnp.where(iota(terms.shape, 0) < 3, terms, 0.0), axis=0, keepdims=True)
    return jnp.broadcast_to(terms, (HEAD_DIM, HEAD_DIM)).T


def finish_body(_, ins, outs):
    sum_ref, stat_ref, back_ref = ins
    heads = sum_ref.shape[1] // HEAD_DIM
    restore = restore_matrix()
    levels = [unpack_level(back_ref, head) for head in range(heads)]
    for i in range(2):
        rows = slice(i * BLK, (i + 1) * BLK)
        spot = slice(i * HALF // 2, (i + 1) * HALF // 2)
        results = []
        for head in range(heads):
            top, total = unpack(stat_ref[rows, cols(head // 2)], head % 2)
            level = twice(twice(levels[head][spot, :]))
            lead = top - level
            smaller = jnp.exp2(-jnp.abs(lead))
            scale = jnp.where(lead >= 0.0, 1.0, smaller)
            coarse = jnp.where(lead >= 0.0, smaller, 1.0)
            number = twice(twice(back_ref[head // 2, spot, cols(head % 2)].astype(f32))) * coarse
            number = number + sum_ref[rows, cols(head)] * scale
            total = total * scale + coarse
            guess = pl.reciprocal(total, approx=True)
            results.append((number * (guess * (2.0 - total * guess))).astype(bf16))
        outs[0][rows, :] = mul(restore, jnp.concatenate(results, axis=1)).astype(bf16)


def finish(place, sums, stat, back):
    shares, rows, part = sums.shape
    ins = [("kept", sums), ("kept", stat), ("pieces", back)]
    outs = [("cols", array(rows, shares * part, bf16))]
    return run_shares(finish_body, "finish", shares, [place], ins, outs, unrolled=True)[0]


def shift(value, axis, steps):
    count = lax.axis_size(axis)
    first, last = (max(0, -steps), min(count, count - steps))
    return lax.ppermute(value, axis, [(source, source + steps) for source in range(first, last)])


def trade(value, axis, pairs):
    return lax.ppermute(value, axis, pairs + [(target, source) for source, target in pairs])


def edge_bias(axis):
    place = lax.axis_index(axis)
    last = lax.axis_size(axis) - 1
    at_edge = jnp.stack([place == 0, place == last])
    return jnp.where(at_edge, very_negative, 0.0).astype(f32)


def local(query_vecs, key_vecs, value_vecs):
    groups = lax.axis_size("grp")
    assert query_vecs.shape == (2 * BLK, HEADS * HEAD_DIM) and groups == 4
    everyone = ("seq", "grp")
    count = lax.axis_size(everyone)
    spot = lax.axis_index("grp")
    odd = jnp.bitwise_and(spot, 1)
    place = jnp.stack([odd, spot]).astype(jnp.int32)
    bias = edge_bias(everyone)

    def exchange(pieces):
        flips = [[(source, source ^ n) for source in range(groups)] for n in range(groups)]
        return [pieces[0]] + [lax.ppermute(pieces[n], "grp", flips[n]) for n in range(1, groups)]

    pieces = list(swap_rows(place, query_vecs, key_vecs, value_vecs, groups))
    query_rows, pieces = lax.optimization_barrier((query_vecs, pieces))
    pieces = exchange(pieces)
    q0, q1, near, far, chip = rows_to_send(place, query_rows, key_vecs, value_vecs, groups)
    off_chip = [(device, device + 1) for device in range(1, count - 1, 2)]
    near = trade(near, everyone, off_chip)
    far, pieces[1] = lax.optimization_barrier((far, pieces[1]))
    far = trade(far, everyone, off_chip)
    pieces, chip = lax.optimization_barrier((pieces, chip))
    got, coarse_right, coarse_left = coarse_halos(place, pieces)
    coarse_right, coarse_left, chip, q0 = lax.optimization_barrier((coarse_right, coarse_left, chip, q0))
    coarse_prev = shift(coarse_right, "seq", 1)
    coarse_next = shift(coarse_left, "seq", -1)
    chip = trade(chip, everyone, [(device, device + 1) for device in range(0, count - 1, 2)])
    own, own_stat = own_level(q0, key_vecs, value_vecs, groups // 2)
    own, own_stat = side_level(chip_body, "chip_level", place, bias, (q0, q1), own, own_stat, chip)
    own, own_stat = side_level(near_body, "near_level", place, bias, (q0, q1), own, own_stat, near)
    got, own = lax.optimization_barrier((got, own))
    back = coarse_levels(place, edge_bias("seq"), got, coarse_prev, coarse_next)
    back, own = lax.optimization_barrier((back, own))
    back = exchange(back)
    own, own_stat = side_level(far_body, "far_level", place, bias, (q1,), own, own_stat, far)
    return finish(place, own, own_stat, back)


def solution(mesh):
    return jax.shard_map(
        local,
        mesh=mesh,
        in_specs=(P(("seq", "grp"), None), P(("seq", "grp"), None), P(("seq", "grp"), None)),
        out_specs=P(("seq", "grp"), None),
        check_vma=False,
    )
```

```python
import functools
import math

import jax
import jax.numpy as jnp
from jax import lax
from jax.experimental import pallas as pl
from jax.experimental.pallas import tpu as pltpu
from jax.sharding import PartitionSpec as P

HEADS = 8
HEAD_DIM = 128
BLK = 256
HALF = BLK // 2
SUB = BLK // 8
LEV = 4
EXP_SCALE = math.log2(math.e) / math.sqrt(HEAD_DIM)

VMEM_GRANT = 24 << 20

very_negative = -1e30
f32 = jnp.float32
bf16 = jnp.bfloat16


def iota(shape, dim):
    return lax.broadcasted_iota(jnp.int32, shape, dim)


def bit(value, place):
    return jnp.bitwise_and(lax.shift_right_logical(value, place), 1)


def low_bits(value):
    step = SUB.bit_length() - 1
    deep = jnp.bitwise_and(value, SUB - 1)
    return 8 * deep + 4 * bit(value, step) + 2 * bit(value, step + 1) + bit(value, step + 2)


def reorder_matrix():
    return (iota((BLK, BLK), 1) == low_bits(iota((BLK, BLK), 0))).astype(bf16)


def restore_matrix():
    return (iota((BLK, BLK), 0) == low_bits(iota((BLK, BLK), 1))).astype(bf16)


def pair_matrix():
    first = low_bits(iota((HALF, BLK), 0))
    place = iota((HALF, BLK), 1)
    return jnp.logical_or(place == first, place == first + 1).astype(bf16)


def mul(left, right):
    return jnp.dot(left, right, preferred_element_type=f32)


def fold(rows, factor):
    half = rows.shape[0] // 2
    total = rows[:half].astype(f32) + rows[half:].astype(f32)
    if factor != 1.0:
        total = total * factor
    return total.astype(bf16)


def fold_chunks(rows, chunk, factor):
    count = rows.shape[0] // chunk
    return jnp.concatenate([fold(rows[i * chunk : (i + 1) * chunk], factor) for i in range(count)], axis=0)


def twice(rows):
    return jnp.concatenate([rows, rows], axis=0)


def cols(head):
    return slice(head * HEAD_DIM, (head + 1) * HEAD_DIM)


DECLARED = 1 << 36


def with_ones(values):
    return jnp.concatenate([values, jnp.ones_like(values)], axis=1)


def attend(units):
    scores = []
    for query, parts in units:
        raws = [
            lax.dot_general(query, keys, (((1,), (1,)), ((), ())), preferred_element_type=f32) for keys, _, _ in parts
        ]
        scores.append([raw if part[2] is None else raw + part[2] for raw, part in zip(raws, parts)])
    tops = []
    for raws in scores:
        tops.append(functools.reduce(jnp.maximum, [jnp.max(raw, axis=1, keepdims=True) for raw in raws]))
    found = []
    for (_, parts), raws, top in zip(units, scores, tops):
        total = None
        for (_, values, _), raw in zip(parts, raws):
            weights = jnp.exp2((raw - top) * EXP_SCALE).astype(bf16)
            one = mul(weights, with_ones(values))
            total = one if total is None else total + one
        found.append((jnp.broadcast_to(top * EXP_SCALE, (top.shape[0], HEAD_DIM)), total))
    return found


def share_of(ref, share, shares):
    width = ref.shape[1] // shares
    first = share * width
    if not isinstance(share, int):
        first = pl.multiple_of(first, HEAD_DIM)
    return ref.at[:, pl.ds(first, width)]


def run_shares(body, name, shares, scalars, ins, outs, work=1 << 10, unrolled=False):
    moved_in = [i for i, (kind, _) in enumerate(ins) if kind in ("cols", "got")]
    moved_out = [i for i, (kind, _) in enumerate(outs) if kind == "cols"]
    as_list = lambda pair: list(pair[1]) if pair[0] == "pieces" else [pair[1]]
    buffer_shape = {
        "cols": lambda value: (shares, value.shape[0], value.shape[1] // shares),
        "got": lambda value: (shares, value.shape[0], value.shape[1] // shares),
        "kept": lambda value: None,
        "pieces": lambda values: (shares, len(values) // shares, *values[0].shape),
    }

    def kernel(*refs):
        refs = list(refs)
        take = lambda count: [refs.pop(0) for _ in range(count)]
        scalar_refs = take(len(scalars))
        in_refs = [take(len(as_list(pair))) for pair in ins]
        out_refs = [take(len(as_list(pair))) for pair in outs]
        in_bufs = [in_refs[i][0] if ins[i][0] == "kept" else refs.pop(0) for i in range(len(ins))]
        out_bufs = [out_refs[i][0] if outs[i][0] == "kept" else refs.pop(0) for i in range(len(outs))]
        in_sems, out_sems, piece_sems = take(3)

        def bring(i, share):
            return pltpu.make_async_copy(share_of(in_refs[i][0], share, shares), in_bufs[i].at[share], in_sems.at[i, share])

        def put(i, share):
            return pltpu.make_async_copy(out_bufs[i].at[share], share_of(out_refs[i][0], share, shares), out_sems.at[i, share])

        def spot_of(buffer, n):
            entry = n ^ scalar_refs[0][1]
            return buffer.at[lax.div(entry, buffer.shape[1]), lax.rem(entry, buffer.shape[1])]

        pieces_in, pieces_out = [], []
        for i, (kind, _) in enumerate(ins):
            if kind == "pieces":
                pieces_in += [(ref, spot_of(in_bufs[i], n), n) for n, ref in enumerate(in_refs[i])]
        for i, (kind, _) in enumerate(outs):
            if kind == "pieces":
                pieces_out += [(spot_of(out_bufs[i], n), ref, n) for n, ref in enumerate(out_refs[i])]
        pieces_in = [pltpu.make_async_copy(source, target, piece_sems.at[n]) for source, target, n in pieces_in]
        pieces_out = [pltpu.make_async_copy(source, target, piece_sems.at[n]) for source, target, n in pieces_out]

        for share in range(shares):
            for i in moved_in:
                bring(i, share).start()
            if share == 0:
                for copy in pieces_in:
                    copy.start()
        for copy in pieces_in:
            copy.wait()

        def views(operands, buffers, share):
            result = []
            for (kind, value), buffer in zip(operands, buffers):
                count = value.shape[0] // shares if kind == "kept" else None
                result.append(buffer.at[share] if count is None else buffer.at[pl.ds(share * count, count)])
            return result

        def step(share, carry):
            for i in moved_in:
                bring(i, share).wait()
            body(scalar_refs, views(ins, in_bufs, share), views(outs, out_bufs, share))
            for i in moved_out:
                put(i, share).start()
            return carry

        if unrolled:
            for share in range(shares):
                step(share, 0)
        else:
            lax.fori_loop(0, shares, step, 0)
        for copy in pieces_out:
            copy.start()
        for share in range(shares):
            for i in moved_out:
                put(i, share).wait()
        for copy in pieces_out:
            copy.wait()

    spaces = {"cols": pltpu.HBM, "got": pl.ANY, "pieces": pl.ANY, "kept": pltpu.VMEM}
    values, in_specs, out_specs, out_shapes, buffers = [], [], [], [], []
    for kind, value in ins:
        for one in as_list((kind, value)):
            values.append(pltpu.with_memory_space_constraint(one, pltpu.HBM) if kind == "cols" else one)
            in_specs.append(pl.BlockSpec(memory_space=spaces[kind]))
    for kind, shape in outs:
        for one in as_list((kind, shape)):
            out_shapes.append(pltpu.HBM(one.shape, one.dtype) if kind == "cols" else one)
            out_specs.append(pl.BlockSpec(memory_space=pltpu.HBM if kind == "cols" else pltpu.VMEM))
    for kind, value in list(ins) + list(outs):
        if kind != "kept":
            buffers.append(pltpu.VMEM(buffer_shape[kind](value), as_list((kind, value))[0].dtype))
    count = max(len(as_list(pair)) for pair in list(ins) + list(outs))
    semaphores = [(len(ins), shares), (len(outs), shares), (count,)]
    return pl.pallas_call(
        kernel,
        in_specs=[pl.BlockSpec(memory_space=pltpu.SMEM)] * len(scalars) + in_specs,
        out_specs=out_specs,
        out_shape=out_shapes,
        scratch_shapes=buffers + [pltpu.SemaphoreType.DMA(shape) for shape in semaphores],
        compiler_params=pltpu.CompilerParams(vmem_limit_bytes=VMEM_GRANT),
        cost_estimate=pl.CostEstimate(flops=work, bytes_accessed=1 << 10, transcendentals=0),
        name=name,
    )(*scalars, *values)


def array(rows, width, dtype):
    return jax.ShapeDtypeStruct((rows, width), dtype)


def swap_body(_, ins, outs):
    pair = pair_matrix()
    count, _, part = outs[0].shape
    for place, (ref, factor) in enumerate(zip(ins, (0.5, 0.5, 1.0))):
        for i in range(2):
            level1 = mul(pair, ref[i * BLK : (i + 1) * BLK, :])
            if factor != 1.0:
                level1 = level1 * factor
            level2 = fold(level1.astype(bf16), factor)
            first = place * HALF + i * HALF // 2
            for n in range(count):
                outs[0][n, first : first + HALF // 2, :] = level2[:, n * part : (n + 1) * part]


def swap_rows(place, query_vecs, key_vecs, value_vecs, groups):
    width = query_vecs.shape[1]
    ins = [("cols", a) for a in (query_vecs, key_vecs, value_vecs)]
    outs = [("pieces", [array(3 * HALF, width // groups, bf16)] * groups)]
    return run_shares(swap_body, "swap_rows", groups // 2, [place], ins, outs, unrolled=True)


def rows_body(scalars, ins, outs):
    q_ref, k_ref, v_ref = ins
    q0_ref, q1_ref, near_ref, far_ref, chip_ref = outs
    reorder = reorder_matrix()
    pair = pair_matrix()
    for i in range(2):
        rows = slice(i * BLK, (i + 1) * BLK)
        q0 = mul(reorder, q_ref[rows, :]).astype(bf16)
        q0_ref[rows, :] = q0
        q1_ref[i * HALF : (i + 1) * HALF, :] = fold(q0, 0.5)
    odd = scalars[0][0]
    outer = pl.ds(pl.multiple_of(odd * BLK, BLK), BLK)
    inner = pl.ds(pl.multiple_of((1 - odd) * BLK, BLK), BLK)
    for ref, far_rows, first, near, far in ((near_ref, far_ref, 0, outer, inner), (chip_ref, chip_ref, 2 * BLK, inner, outer)):
        ref[0:BLK, :] = k_ref[near, :]
        ref[BLK : 2 * BLK, :] = v_ref[near, :]
        far_rows[first : first + HALF, :] = (mul(pair, k_ref[far, :]) * 0.5).astype(bf16)
        far_rows[first + HALF : first + BLK, :] = mul(pair, v_ref[far, :]).astype(bf16)


def rows_to_send(place, query_vecs, key_vecs, value_vecs, groups):
    rows, width = query_vecs.shape
    ins = [("cols", a) for a in (query_vecs, key_vecs, value_vecs)]
    outs = [("cols", array(n, width, bf16)) for n in (rows, rows // 2, 2 * BLK, BLK, 3 * BLK)]
    return run_shares(rows_body, "rows_to_send", groups, [place], ins, outs)


def pack(stats):
    width = HEAD_DIM // len(stats)
    lane = iota(stats[0].shape, 1)
    packed = stats[-1]
    for n in range(len(stats) - 2, -1, -1):
        packed = jnp.where(lane < (n + 1) * width, stats[n], packed)
    return packed


def unpack(packed, head):
    lanes = [head * HEAD_DIM // 2 + n * HEAD_DIM // 4 for n in range(2)]
    return [jnp.broadcast_to(packed[:, lane : lane + 1], packed.shape) for lane in lanes]


def own_body(_, ins, outs):
    q_ref, k_ref, v_ref = ins
    sum_ref, stat_ref = outs
    heads = q_ref.shape[1] // HEAD_DIM
    for i in range(2):
        rows = slice(i * BLK, (i + 1) * BLK)
        units = [(q_ref[rows, cols(head)], [(k_ref[:, cols(head)], v_ref[:, cols(head)], None)]) for head in range(heads)]
        stats = []
        for head, (top, sums) in enumerate(attend(units)):
            sum_ref[head // 2, rows, cols(head % 2)] = sums[:, :HEAD_DIM]
            stats += [top, sums[:, HEAD_DIM:]]
        for n in range(0, heads, 2):
            stat_ref[n // 2, rows, :] = pack(stats[2 * n : 2 * n + 4])


def sums_and_stats(rows, width, groups):
    return [("kept", jax.ShapeDtypeStruct((groups, rows, lanes), f32)) for lanes in (width // groups, HEAD_DIM)]


def own_level(q0, key_vecs, value_vecs, groups):
    ins = [("cols", a) for a in (q0, key_vecs, value_vecs)]
    return run_shares(own_body, "own_level", groups // 2, [], ins, sums_and_stats(*q0.shape, groups), DECLARED)


def halo_body(place_ref, *refs):
    count = len(refs) - 4
    piece_refs, (got_ref, right_ref, left_ref, sems) = refs[:count], refs[count:]
    copies = [pltpu.make_async_copy(ref, got_ref.at[n ^ place_ref[1]], sems.at[n]) for n, ref in enumerate(piece_refs)]
    for copy in copies:
        copy.start()
    for copy in copies:
        copy.wait()
    pair = count // 2
    for which, factor in ((1, 0.5), (2, 1.0)):
        rows = slice(which * HALF, (which + 1) * HALF)
        near = (which - 1) * BLK
        far = 2 * BLK + (which - 1) * HALF
        for j in range(count):
            level2 = got_ref[j, rows, :]
            level3 = fold_chunks(level2, HALF // 2, factor)
            near_ref, far_ref = (left_ref, right_ref) if j < pair else (right_ref, left_ref)
            spot = j % pair
            near_ref[near + spot * HALF : near + (spot + 1) * HALF, :] = level2
            far_ref[far + spot * HALF // 2 : far + (spot + 1) * HALF // 2, :] = level3


def coarse_halos(place, pieces):
    rows, width = pieces[0].shape
    vmem = pl.BlockSpec(memory_space=pltpu.VMEM)
    shape = jax.ShapeDtypeStruct((3 * BLK, width), bf16)
    return pl.pallas_call(
        halo_body,
        in_specs=[pl.BlockSpec(memory_space=pltpu.SMEM)] + [pl.BlockSpec(memory_space=pl.ANY)] * len(pieces),
        out_specs=[vmem] * 3,
        out_shape=[jax.ShapeDtypeStruct((len(pieces), rows, width), bf16), shape, shape],
        scratch_shapes=[pltpu.SemaphoreType.DMA((len(pieces),))],
        compiler_params=pltpu.CompilerParams(vmem_limit_bytes=16 << 20),
        cost_estimate=pl.CostEstimate(flops=1 << 20, bytes_accessed=24 * pieces[0].size, transcendentals=0),
        name="coarse_halos",
    )(place, *pieces)


def coarse_body(place_ref, bias_ref, got_ref, prev_ref, next_ref, *refs):
    *out_refs, back_ref, sems = refs
    count = got_ref.shape[0]
    heads = got_ref.shape[2] // HEAD_DIM
    bias_prev = bias_ref[0]
    bias_next = bias_ref[1]
    lane = iota((HALF, HEAD_DIM), 1)

    units = []
    for head in range(heads):
        here = cols(head)

        def own(which, j):
            return got_ref[j, which * HALF : (which + 1) * HALF, here]

        def near(ref, which, spot):
            first = (which - 1) * BLK + spot * HALF
            return ref[first : first + HALF, here]

        def both(ref, which):
            return ref[(which - 1) * BLK : which * BLK, here]

        def far(ref, which):
            first = 2 * BLK + (which - 1) * HALF
            return ref[first : first + HALF, here]

        def near3(ref, which):
            return fold_chunks(both(ref, which), HALF // 2, 0.5 if which == 1 else 1.0)

        def joined(*rows):
            return jnp.concatenate(rows, axis=0)

        def part(pick, bias):
            return (pick(1), pick(2), bias)

        units += [
            (own(0, 0), [part(lambda w: joined(own(w, 2), own(w, 3)), None), part(lambda w: near(prev_ref, w, 0), bias_prev)]),
            (own(0, 1), [part(lambda w: both(prev_ref, w), bias_prev), part(lambda w: own(w, 3), None)]),
            (own(0, 2), [part(lambda w: both(next_ref, w), bias_next), part(lambda w: own(w, 0), None)]),
            (own(0, 3), [part(lambda w: joined(own(w, 0), own(w, 1)), None), part(lambda w: near(next_ref, w, 1), bias_next)]),
        ]
        for j, (ref, bias, other, other_bias) in enumerate(
            ((next_ref, bias_next, prev_ref, bias_prev), (prev_ref, bias_prev, next_ref, bias_next))
        ):
            query = joined(*[fold_chunks(own(0, 2 * j + n), HALF // 2, 0.5) for n in range(2)])
            units.append(
                (
                    query,
                    [part(lambda w: joined(near3(ref, w), far(ref, w)), bias), part(lambda w: far(other, w), other_bias)],
                )
            )
    found = attend(units)
    each = len(units) // heads

    def joined(*rows):
        return jnp.concatenate(rows, axis=0)

    for head in range(heads):
        here = cols(head)
        for j in range(count):
            top2, sum2 = found[head * each + j]
            top3, sum3 = found[head * each + count + j // 2]

            def spread(rows):
                first = (j % 2) * 2 * SUB
                one = rows[first : first + SUB]
                other = rows[first + SUB : first + 2 * SUB]
                return joined(one, one, other, other)

            top3 = spread(top3)
            sum3 = spread(sum3)
            top = jnp.maximum(top2, top3)
            scale2 = jnp.exp2(top2 - top)
            scale3 = jnp.exp2(top3 - top)
            values = sum2[:, :HEAD_DIM] * scale2 + sum3[:, :HEAD_DIM] * scale3
            total = sum2[:, HEAD_DIM:] * (4.0 * scale2) + sum3[:, HEAD_DIM:] * (8.0 * scale3)
            back_ref[j, 0:HALF, here] = (values / total).astype(bf16)
            level = top + jnp.log2(total)
            high = level.astype(bf16).astype(f32)
            middle = (level - high).astype(bf16).astype(f32)
            terms = jnp.where(lane == 0, high, jnp.where(lane == 1, middle, level - high - middle))
            back_ref[j, HALF : HALF + 16, here] = terms.T[0:16, :].astype(bf16)
    copies = [
        pltpu.make_async_copy(back_ref.at[n ^ place_ref[1]], ref, sems.at[n]) for n, ref in enumerate(out_refs)
    ]
    for copy in copies:
        copy.start()
    for copy in copies:
        copy.wait()


def coarse_levels(place, bias, got, from_prev, from_next):
    count, _, width = got.shape
    vmem = pl.BlockSpec(memory_space=pltpu.VMEM)
    smem = pl.BlockSpec(memory_space=pltpu.SMEM)
    rows = HALF + 16
    return pl.pallas_call(
        coarse_body,
        in_specs=[smem, smem, vmem, vmem, vmem],
        out_specs=[vmem] * count,
        out_shape=[array(rows, width, bf16)] * count,
        scratch_shapes=[pltpu.VMEM((count, rows, width), bf16), pltpu.SemaphoreType.DMA((count,))],
        compiler_params=pltpu.CompilerParams(vmem_limit_bytes=16 << 20),
        cost_estimate=pl.CostEstimate(flops=DECLARED, bytes_accessed=8 * got.size, transcendentals=1 << 20),
        name="coarse_levels",
    )(place, bias, got, from_prev, from_next)


def side_body(side, with_near, with_far, scalars, ins, outs):
    q0_ref, q1_ref, sum_ref, stat_ref, side_ref = ins
    heads = q1_ref.shape[1] // HEAD_DIM
    bias = scalars[1][side]
    blocks = (side, 1 - side)
    fine = [pl.ds(pl.multiple_of(block * BLK, BLK), BLK) for block in blocks]
    middle = [pl.ds(pl.multiple_of(block * HALF, HALF), HALF) for block in blocks]
    if with_near:
        pair = pair_matrix()
        near_keys = (mul(pair, side_ref[0:BLK, :]) * 0.5).astype(bf16)
        near_values = mul(pair, side_ref[BLK : 2 * BLK, :]).astype(bf16)
    start = 2 * BLK if with_near else 0
    far_keys, far_values = (slice(start + n * HALF, start + (n + 1) * HALF) for n in range(2))
    units, names = [], []
    for head in range(heads):
        here = cols(head)
        far = (side_ref[far_keys, here], side_ref[far_values, here]) if with_far else None
        near = (near_keys[:, here], near_values[:, here]) if with_near else None
        whole = [part for part in (near, far) if part is not None]
        whole = [jnp.concatenate([part[n] for part in whole], axis=0) if len(whole) > 1 else whole[0][n] for n in range(2)]
        if with_near:
            units.append((q0_ref[fine[0], here], [(side_ref[0:BLK, here], side_ref[BLK : 2 * BLK, here], None)]))
            names.append((head, 0, 0))
        if with_far:
            units.append((q1_ref[middle[0], here], [(*far, None)]))
            names.append((head, 0, 1))
        units.append((q1_ref[middle[1], here], [(*whole, None)]))
        names.append((head, 1, 1))
    found = {name: (top + bias, sums) for name, (top, sums) in zip(names, attend(units))}
    for n in range(2):
        stats = []
        for head in range(heads):
            here = cols(head)
            own_top, own_total = unpack(stat_ref[head // 2, fine[n], :], head % 2)
            parts = [(own_top, sum_ref[head // 2, fine[n], cols(head % 2)], own_total)]
            if (head, n, 0) in found:
                top, sums = found[head, n, 0]
                parts.append((top, sums[:, :HEAD_DIM], sums[:, HEAD_DIM:]))
            if (head, n, 1) in found:
                top, sums = found[head, n, 1]
                parts.append((twice(top), twice(sums[:, :HEAD_DIM]), twice(2.0 * sums[:, HEAD_DIM:])))
            most = functools.reduce(jnp.maximum, [part[0] for part in parts])
            scales = [jnp.exp2(part[0] - most) for part in parts]
            outs[0][head // 2, fine[n], cols(head % 2)] = sum(part[1] * scale for part, scale in zip(parts, scales))
            stats += [most, sum(part[2] * scale for part, scale in zip(parts, scales))]
        for m in range(0, heads, 2):
            outs[1][m // 2, fine[n], :] = pack(stats[2 * m : 2 * m + 4])


def chip_body(scalars, ins, outs):
    side_body(1 - scalars[0][0], True, True, scalars, ins, outs)


def near_body(scalars, ins, outs):
    side_body(scalars[0][0], True, False, scalars, ins, outs)


def far_body(scalars, ins, outs):
    side_body(scalars[0][0], False, True, scalars, [None] + ins, outs)


def side_level(body, name, place, bias, queries, sums, stat, rows):
    groups, count, part = sums.shape
    ins = [("cols", query) for query in queries] + [("kept", sums), ("kept", stat), ("got", rows)]
    return run_shares(body, name, groups // 2, [place, bias], ins, sums_and_stats(count, groups * part, groups))


def finish_body(place_ref, sum_ref, stat_ref, *refs):
    groups = sum_ref.shape[0]
    back_refs, (out_ref, done_ref, sems) = refs[:groups], refs[groups:]
    part = sum_ref.shape[2]
    restore = restore_matrix()
    copies = []
    for n, back_ref in enumerate(back_refs):
        entry = n ^ place_ref[1]
        levels = []
        for head in range(part // HEAD_DIM):
            terms = back_ref[HALF : HALF + 16, cols(head)].astype(f32)
            terms = jnp.sum(jnp.where(iota(terms.shape, 0) < 3, terms, 0.0), axis=0, keepdims=True)
            levels.append(jnp.broadcast_to(terms, (HEAD_DIM, HEAD_DIM)).T)
        for i in range(2):
            rows = slice(i * BLK, (i + 1) * BLK)
            spot = slice(i * HALF // 2, (i + 1) * HALF // 2)
            results = []
            for head, level in enumerate(levels):
                top, total = unpack(stat_ref[entry, rows, :], head)
                level = twice(twice(level[spot, :]))
                lead = top - level
                smaller = jnp.exp2(-jnp.abs(lead))
                scale = jnp.where(lead >= 0.0, 1.0, smaller)
                coarse = jnp.where(lead >= 0.0, smaller, 1.0)
                number = twice(twice(back_ref[spot, cols(head)].astype(f32))) * coarse
                number = number + sum_ref[entry, rows, cols(head)] * scale
                total = total * scale + coarse
                guess = pl.reciprocal(total, approx=True)
                results.append((number * (guess * (2.0 - total * guess))).astype(bf16))
            done_ref[n, rows, :] = mul(restore, jnp.concatenate(results, axis=1)).astype(bf16)
        columns = pl.ds(pl.multiple_of(entry * part, HEAD_DIM), part)
        copies.append(pltpu.make_async_copy(done_ref.at[n], out_ref.at[:, columns], sems.at[n]))
        copies[-1].start()
    for copy in copies:
        copy.wait()


def finish(place, sums, stat, back):
    groups, rows, part = sums.shape
    vmem = pl.BlockSpec(memory_space=pltpu.VMEM)
    return pl.pallas_call(
        finish_body,
        in_specs=[pl.BlockSpec(memory_space=pltpu.SMEM)] + [vmem] * (2 + groups),
        out_specs=pl.BlockSpec(memory_space=pltpu.HBM),
        out_shape=pltpu.HBM((rows, groups * part), bf16),
        scratch_shapes=[pltpu.VMEM((groups, rows, part), bf16), pltpu.SemaphoreType.DMA((groups,))],
        compiler_params=pltpu.CompilerParams(vmem_limit_bytes=VMEM_GRANT),
        cost_estimate=pl.CostEstimate(flops=1 << 10, bytes_accessed=1 << 10, transcendentals=0),
        name="finish",
    )(place, sums, stat, *back)


def shift(value, axis, steps):
    count = lax.axis_size(axis)
    first, last = (max(0, -steps), min(count, count - steps))
    return lax.ppermute(value, axis, [(source, source + steps) for source in range(first, last)])


def trade(value, axis, pairs):
    return lax.ppermute(value, axis, pairs + [(target, source) for source, target in pairs])


def edge_bias(axis):
    place = lax.axis_index(axis)
    last = lax.axis_size(axis) - 1
    at_edge = jnp.stack([place == 0, place == last])
    return jnp.where(at_edge, very_negative, 0.0).astype(f32)


def local(query_vecs, key_vecs, value_vecs):
    groups = lax.axis_size("grp")
    assert query_vecs.shape == (2 * BLK, HEADS * HEAD_DIM) and groups == 4
    everyone = ("seq", "grp")
    count = lax.axis_size(everyone)
    spot = lax.axis_index("grp")
    odd = jnp.bitwise_and(spot, 1)
    place = jnp.stack([odd, spot]).astype(jnp.int32)
    bias = edge_bias(everyone)

    def exchange(pieces):
        flips = [[(source, source ^ n) for source in range(groups)] for n in range(groups)]
        for n in range(groups - 1, 0, -1):
            pieces[n] = lax.ppermute(pieces[n], "grp", flips[n])
        return pieces

    pieces = list(swap_rows(place, query_vecs, key_vecs, value_vecs, groups))
    query_rows, pieces = lax.optimization_barrier((query_vecs, pieces))
    pieces = exchange(pieces)
    q0, q1, near, far, chip = rows_to_send(place, query_rows, key_vecs, value_vecs, groups)
    off_chip = [(device, device + 1) for device in range(1, count - 1, 2)]
    near = trade(near, everyone, off_chip)
    far, pieces[1] = lax.optimization_barrier((far, pieces[1]))
    far = trade(far, everyone, off_chip)
    pieces, chip = lax.optimization_barrier((pieces, chip))
    got, coarse_right, coarse_left = coarse_halos(place, pieces)
    coarse_right, coarse_left, chip, q0 = lax.optimization_barrier((coarse_right, coarse_left, chip, q0))
    coarse_prev = shift(coarse_right, "seq", 1)
    coarse_next = shift(coarse_left, "seq", -1)
    chip = trade(chip, everyone, [(device, device + 1) for device in range(0, count - 1, 2)])
    own, own_stat = own_level(q0, key_vecs, value_vecs, groups)
    own, own_stat = side_level(chip_body, "chip_level", place, bias, (q0, q1), own, own_stat, chip)
    own, own_stat = side_level(near_body, "near_level", place, bias, (q0, q1), own, own_stat, near)
    got, own = lax.optimization_barrier((got, own))
    back = coarse_levels(place, edge_bias("seq"), got, coarse_prev, coarse_next)
    back, own = lax.optimization_barrier((back, own))
    back = exchange(list(back))
    own, own_stat = side_level(far_body, "far_level", place, bias, (q1,), own, own_stat, far)
    return finish(place, own, own_stat, back)


def solution(mesh):
    return jax.shard_map(
        local,
        mesh=mesh,
        in_specs=(P(("seq", "grp"), None), P(("seq", "grp"), None), P(("seq", "grp"), None)),
        out_specs=P(("seq", "grp"), None),
        check_vma=False,
    )
```

```python
import functools
import math

import jax
import jax.numpy as jnp
from jax import lax
from jax.experimental import pallas as pl
from jax.experimental.pallas import tpu as pltpu
from jax.sharding import PartitionSpec as P

HEADS = 8
HEAD_DIM = 128
BLK = 256
HALF = BLK // 2
SUB = BLK // 8
LEV = 4
EXP_SCALE = math.log2(math.e) / math.sqrt(HEAD_DIM)

VMEM_GRANT = 24 << 20

very_negative = -1e30
f32 = jnp.float32
bf16 = jnp.bfloat16


def iota(shape, dim):
    return lax.broadcasted_iota(jnp.int32, shape, dim)


def bit(value, place):
    return jnp.bitwise_and(lax.shift_right_logical(value, place), 1)


def low_bits(value):
    step = SUB.bit_length() - 1
    deep = jnp.bitwise_and(value, SUB - 1)
    return 8 * deep + 4 * bit(value, step) + 2 * bit(value, step + 1) + bit(value, step + 2)


def reorder_matrix():
    return (iota((BLK, BLK), 1) == low_bits(iota((BLK, BLK), 0))).astype(bf16)


def restore_matrix():
    return (iota((BLK, BLK), 0) == low_bits(iota((BLK, BLK), 1))).astype(bf16)


def pair_matrix():
    first = low_bits(iota((HALF, BLK), 0))
    place = iota((HALF, BLK), 1)
    return jnp.logical_or(place == first, place == first + 1).astype(bf16)


def mul(left, right):
    return jnp.dot(left, right, preferred_element_type=f32)


def fold(rows, factor):
    half = rows.shape[0] // 2
    total = rows[:half].astype(f32) + rows[half:].astype(f32)
    if factor != 1.0:
        total = total * factor
    return total.astype(bf16)


def fold_chunks(rows, chunk, factor):
    count = rows.shape[0] // chunk
    return jnp.concatenate([fold(rows[i * chunk : (i + 1) * chunk], factor) for i in range(count)], axis=0)


def twice(rows):
    return jnp.concatenate([rows, rows], axis=0)


def cols(head):
    return slice(head * HEAD_DIM, (head + 1) * HEAD_DIM)


DECLARED = 1 << 36


def with_ones(values):
    return jnp.concatenate([values, jnp.ones_like(values)], axis=1)


def attend(units):
    scores = []
    for query, parts in units:
        raws = [
            lax.dot_general(query, keys, (((1,), (1,)), ((), ())), preferred_element_type=f32) for keys, _, _ in parts
        ]
        scores.append([raw if part[2] is None else raw + part[2] for raw, part in zip(raws, parts)])
    tops = []
    for raws in scores:
        tops.append(functools.reduce(jnp.maximum, [jnp.max(raw, axis=1, keepdims=True) for raw in raws]))
    found = []
    for (_, parts), raws, top in zip(units, scores, tops):
        total = None
        for (_, values, _), raw in zip(parts, raws):
            weights = jnp.exp2((raw - top) * EXP_SCALE).astype(bf16)
            one = mul(weights, with_ones(values))
            total = one if total is None else total + one
        found.append((jnp.broadcast_to(top * EXP_SCALE, (top.shape[0], HEAD_DIM)), total))
    return found


def share_of(ref, share, shares):
    width = ref.shape[1] // shares
    first = share * width
    if not isinstance(share, int):
        first = pl.multiple_of(first, HEAD_DIM)
    return ref.at[:, pl.ds(first, width)]


def run_shares(body, name, shares, scalars, ins, outs, work=1 << 10, unrolled=False):
    moved_in = [i for i, (kind, _) in enumerate(ins) if kind in ("cols", "got")]
    moved_out = [i for i, (kind, _) in enumerate(outs) if kind == "cols"]
    as_list = lambda pair: list(pair[1]) if pair[0] == "pieces" else [pair[1]]
    buffer_shape = {
        "cols": lambda value: (shares, value.shape[0], value.shape[1] // shares),
        "got": lambda value: (shares, value.shape[0], value.shape[1] // shares),
        "kept": lambda value: None,
        "pieces": lambda values: (shares, len(values) // shares, *values[0].shape),
    }

    def kernel(*refs):
        refs = list(refs)
        take = lambda count: [refs.pop(0) for _ in range(count)]
        scalar_refs = take(len(scalars))
        in_refs = [take(len(as_list(pair))) for pair in ins]
        out_refs = [take(len(as_list(pair))) for pair in outs]
        in_bufs = [in_refs[i][0] if ins[i][0] == "kept" else refs.pop(0) for i in range(len(ins))]
        out_bufs = [out_refs[i][0] if outs[i][0] == "kept" else refs.pop(0) for i in range(len(outs))]
        in_sems, out_sems, piece_sems = take(3)

        def bring(i, share):
            return pltpu.make_async_copy(share_of(in_refs[i][0], share, shares), in_bufs[i].at[share], in_sems.at[i, share])

        def put(i, share):
            return pltpu.make_async_copy(out_bufs[i].at[share], share_of(out_refs[i][0], share, shares), out_sems.at[i, share])

        def spot_of(buffer, n):
            entry = n ^ scalar_refs[0][1]
            return buffer.at[lax.div(entry, buffer.shape[1]), lax.rem(entry, buffer.shape[1])]

        pieces_in, pieces_out = [], []
        for i, (kind, _) in enumerate(ins):
            if kind == "pieces":
                pieces_in += [(ref, spot_of(in_bufs[i], n), n) for n, ref in enumerate(in_refs[i])]
        for i, (kind, _) in enumerate(outs):
            if kind == "pieces":
                pieces_out += [(spot_of(out_bufs[i], n), ref, n) for n, ref in enumerate(out_refs[i])]
        pieces_in = [pltpu.make_async_copy(source, target, piece_sems.at[n]) for source, target, n in pieces_in]
        pieces_out = [pltpu.make_async_copy(source, target, piece_sems.at[n]) for source, target, n in pieces_out]

        for share in range(shares):
            for i in moved_in:
                bring(i, share).start()
            if share == 0:
                for copy in pieces_in:
                    copy.start()
        for copy in pieces_in:
            copy.wait()

        def views(operands, buffers, share):
            result = []
            for (kind, value), buffer in zip(operands, buffers):
                count = value.shape[0] // shares if kind == "kept" else None
                result.append(buffer.at[share] if count is None else buffer.at[pl.ds(share * count, count)])
            return result

        def step(share, carry):
            for i in moved_in:
                bring(i, share).wait()
            body(scalar_refs, views(ins, in_bufs, share), views(outs, out_bufs, share))
            for i in moved_out:
                put(i, share).start()
            return carry

        if unrolled:
            for share in range(shares):
                step(share, 0)
        else:
            lax.fori_loop(0, shares, step, 0)
        for copy in pieces_out:
            copy.start()
        for share in range(shares):
            for i in moved_out:
                put(i, share).wait()
        for copy in pieces_out:
            copy.wait()

    spaces = {"cols": pltpu.HBM, "got": pl.ANY, "pieces": pl.ANY, "kept": pltpu.VMEM}
    values, in_specs, out_specs, out_shapes, buffers = [], [], [], [], []
    for kind, value in ins:
        for one in as_list((kind, value)):
            values.append(pltpu.with_memory_space_constraint(one, pltpu.HBM) if kind == "cols" else one)
            in_specs.append(pl.BlockSpec(memory_space=spaces[kind]))
    for kind, shape in outs:
        for one in as_list((kind, shape)):
            out_shapes.append(pltpu.HBM(one.shape, one.dtype) if kind == "cols" else one)
            out_specs.append(pl.BlockSpec(memory_space=pltpu.HBM if kind == "cols" else pltpu.VMEM))
    for kind, value in list(ins) + list(outs):
        if kind != "kept":
            buffers.append(pltpu.VMEM(buffer_shape[kind](value), as_list((kind, value))[0].dtype))
    count = max(len(as_list(pair)) for pair in list(ins) + list(outs))
    semaphores = [(len(ins), shares), (len(outs), shares), (count,)]
    return pl.pallas_call(
        kernel,
        in_specs=[pl.BlockSpec(memory_space=pltpu.SMEM)] * len(scalars) + in_specs,
        out_specs=out_specs,
        out_shape=out_shapes,
        scratch_shapes=buffers + [pltpu.SemaphoreType.DMA(shape) for shape in semaphores],
        compiler_params=pltpu.CompilerParams(vmem_limit_bytes=VMEM_GRANT),
        cost_estimate=pl.CostEstimate(flops=work, bytes_accessed=1 << 10, transcendentals=0),
        name=name,
    )(*scalars, *values)


def array(rows, width, dtype):
    return jax.ShapeDtypeStruct((rows, width), dtype)


def swap_body(place_ref, q_ref, k_ref, v_ref, *refs):
    groups = len(refs) - 4
    out_refs, (held, made, in_sems, out_sems) = refs[:groups], refs[groups:]
    part = made.shape[2]
    blocks = [pl.ds(i * BLK, BLK) for i in range(2)]
    arrive = [
        [pltpu.make_async_copy(ref.at[rows, :], held.at[n, rows, :], in_sems.at[n, i]) for i, rows in enumerate(blocks)]
        for n, ref in enumerate((q_ref, k_ref, v_ref))
    ]
    for copies in arrive:
        for copy in copies:
            copy.start()
    pair = pair_matrix()
    for n, factor in enumerate((0.5, 0.5, 1.0)):
        for i in range(2):
            arrive[n][i].wait()
            level1 = mul(pair, held[n, blocks[i], :])
            if factor != 1.0:
                level1 = level1 * factor
            level2 = fold(level1.astype(bf16), factor)
            first = n * HALF + i * HALF // 2
            for entry in range(groups):
                made[entry, first : first + HALF // 2, :] = level2[:, entry * part : (entry + 1) * part]
    leave = [pltpu.make_async_copy(made.at[n ^ place_ref[1]], ref, out_sems.at[n]) for n, ref in enumerate(out_refs)]
    for copy in leave:
        copy.start()
    for copy in leave:
        copy.wait()


def swap_rows(place, query_vecs, key_vecs, value_vecs, groups):
    rows, width = query_vecs.shape
    piece = array(3 * HALF, width // groups, bf16)
    vectors = (query_vecs, key_vecs, value_vecs)
    return pl.pallas_call(
        swap_body,
        in_specs=[pl.BlockSpec(memory_space=pltpu.SMEM)] + [pl.BlockSpec(memory_space=pltpu.HBM)] * 3,
        out_specs=[pl.BlockSpec(memory_space=pltpu.VMEM)] * groups,
        out_shape=[piece] * groups,
        scratch_shapes=[
            pltpu.VMEM((3, rows, width), bf16),
            pltpu.VMEM((groups, *piece.shape), bf16),
            pltpu.SemaphoreType.DMA((3, 2)),
            pltpu.SemaphoreType.DMA((groups,)),
        ],
        compiler_params=pltpu.CompilerParams(vmem_limit_bytes=VMEM_GRANT),
        cost_estimate=pl.CostEstimate(flops=1 << 10, bytes_accessed=1 << 10, transcendentals=0),
        name="swap_rows",
    )(place, *[pltpu.with_memory_space_constraint(value, pltpu.HBM) for value in vectors])


def rows_body(scalars, ins, outs):
    q_ref, k_ref, v_ref = ins
    q0_ref, q1_ref, near_ref, far_ref, chip_ref = outs
    reorder = reorder_matrix()
    pair = pair_matrix()
    for i in range(2):
        rows = slice(i * BLK, (i + 1) * BLK)
        q0 = mul(reorder, q_ref[rows, :]).astype(bf16)
        q0_ref[rows, :] = q0
        q1_ref[i * HALF : (i + 1) * HALF, :] = fold(q0, 0.5)
    odd = scalars[0][0]
    outer = pl.ds(pl.multiple_of(odd * BLK, BLK), BLK)
    inner = pl.ds(pl.multiple_of((1 - odd) * BLK, BLK), BLK)
    for ref, far_rows, first, near, far in ((near_ref, far_ref, 0, outer, inner), (chip_ref, chip_ref, 2 * BLK, inner, outer)):
        ref[0:BLK, :] = k_ref[near, :]
        ref[BLK : 2 * BLK, :] = v_ref[near, :]
        far_rows[first : first + HALF, :] = (mul(pair, k_ref[far, :]) * 0.5).astype(bf16)
        far_rows[first + HALF : first + BLK, :] = mul(pair, v_ref[far, :]).astype(bf16)


def rows_to_send(place, query_vecs, key_vecs, value_vecs, groups):
    rows, width = query_vecs.shape
    ins = [("cols", a) for a in (query_vecs, key_vecs, value_vecs)]
    outs = [("cols", array(n, width, bf16)) for n in (rows, rows // 2, 2 * BLK, BLK, 3 * BLK)]
    return run_shares(rows_body, "rows_to_send", groups, [place], ins, outs)


def pack(stats):
    lane = iota(stats[0].shape, 1)
    packed = stats[-1]
    for n in range(len(stats) - 2, -1, -1):
        packed = jnp.where(lane < (n + 1) * HEAD_DIM // 4, stats[n], packed)
    return packed


def unpack(packed, n):
    lane = n * HEAD_DIM // 4
    return jnp.broadcast_to(packed[:, lane : lane + 1], packed.shape)


def own_body(_, ins, outs):
    q_ref, k_ref, v_ref = ins
    sum_ref, stat_ref = outs
    heads = q_ref.shape[1] // HEAD_DIM
    for i in range(2):
        rows = slice(i * BLK, (i + 1) * BLK)
        units = [(q_ref[rows, cols(head)], [(k_ref[:, cols(head)], v_ref[:, cols(head)], None)]) for head in range(heads)]
        stats = []
        for head, (top, sums) in enumerate(attend(units)):
            sum_ref[head // 2, rows, cols(head % 2)] = sums[:, :HEAD_DIM]
            stats += [top, sums[:, HEAD_DIM:]]
        for n in range(0, heads, 2):
            stat_ref[n // 2, rows, :] = pack(stats[2 * n : 2 * n + 4 : 2] + stats[2 * n + 1 : 2 * n + 4 : 2])


def sums_and_stats(rows, width, groups):
    return [("kept", jax.ShapeDtypeStruct((groups, rows, lanes), f32)) for lanes in (width // groups, HEAD_DIM)]


def own_level(q0, key_vecs, value_vecs, groups):
    ins = [("cols", a) for a in (q0, key_vecs, value_vecs)]
    return run_shares(own_body, "own_level", groups // 2, [], ins, sums_and_stats(*q0.shape, groups), DECLARED)


def halo_body(place_ref, *refs):
    count = len(refs) - 4
    piece_refs, (got_ref, right_ref, left_ref, sems) = refs[:count], refs[count:]
    copies = [pltpu.make_async_copy(ref, got_ref.at[n ^ place_ref[1]], sems.at[n]) for n, ref in enumerate(piece_refs)]
    for copy in copies:
        copy.start()
    for copy in copies:
        copy.wait()
    pair = count // 2
    for which, factor in ((1, 0.5), (2, 1.0)):
        rows = slice(which * HALF, (which + 1) * HALF)
        near = (which - 1) * BLK
        far = 2 * BLK + (which - 1) * HALF
        for j in range(count):
            level2 = got_ref[j, rows, :]
            level3 = fold_chunks(level2, HALF // 2, factor)
            near_ref, far_ref = (left_ref, right_ref) if j < pair else (right_ref, left_ref)
            spot = j % pair
            near_ref[near + spot * HALF : near + (spot + 1) * HALF, :] = level2
            far_ref[far + spot * HALF // 2 : far + (spot + 1) * HALF // 2, :] = level3


def coarse_halos(place, pieces):
    rows, width = pieces[0].shape
    vmem = pl.BlockSpec(memory_space=pltpu.VMEM)
    shape = jax.ShapeDtypeStruct((3 * BLK, width), bf16)
    return pl.pallas_call(
        halo_body,
        in_specs=[pl.BlockSpec(memory_space=pltpu.SMEM)] + [pl.BlockSpec(memory_space=pl.ANY)] * len(pieces),
        out_specs=[vmem] * 3,
        out_shape=[jax.ShapeDtypeStruct((len(pieces), rows, width), bf16), shape, shape],
        scratch_shapes=[pltpu.SemaphoreType.DMA((len(pieces),))],
        compiler_params=pltpu.CompilerParams(vmem_limit_bytes=16 << 20),
        cost_estimate=pl.CostEstimate(flops=1 << 20, bytes_accessed=24 * pieces[0].size, transcendentals=0),
        name="coarse_halos",
    )(place, *pieces)


def coarse_body(place_ref, bias_ref, got_ref, prev_ref, next_ref, *refs):
    *out_refs, back_ref, sems = refs
    count = got_ref.shape[0]
    heads = got_ref.shape[2] // HEAD_DIM
    bias_prev = bias_ref[0]
    bias_next = bias_ref[1]
    lane = iota((HALF, HEAD_DIM), 1)

    units = []
    for head in range(heads):
        here = cols(head)

        def own(which, j):
            return got_ref[j, which * HALF : (which + 1) * HALF, here]

        def near(ref, which, spot):
            first = (which - 1) * BLK + spot * HALF
            return ref[first : first + HALF, here]

        def both(ref, which):
            return ref[(which - 1) * BLK : which * BLK, here]

        def far(ref, which):
            first = 2 * BLK + (which - 1) * HALF
            return ref[first : first + HALF, here]

        def near3(ref, which):
            return fold_chunks(both(ref, which), HALF // 2, 0.5 if which == 1 else 1.0)

        def joined(*rows):
            return jnp.concatenate(rows, axis=0)

        def part(pick, bias):
            return (pick(1), pick(2), bias)

        units += [
            (own(0, 0), [part(lambda w: joined(own(w, 2), own(w, 3)), None), part(lambda w: near(prev_ref, w, 0), bias_prev)]),
            (own(0, 1), [part(lambda w: both(prev_ref, w), bias_prev), part(lambda w: own(w, 3), None)]),
            (own(0, 2), [part(lambda w: both(next_ref, w), bias_next), part(lambda w: own(w, 0), None)]),
            (own(0, 3), [part(lambda w: joined(own(w, 0), own(w, 1)), None), part(lambda w: near(next_ref, w, 1), bias_next)]),
        ]
        for j, (ref, bias, other, other_bias) in enumerate(
            ((next_ref, bias_next, prev_ref, bias_prev), (prev_ref, bias_prev, next_ref, bias_next))
        ):
            query = joined(*[fold_chunks(own(0, 2 * j + n), HALF // 2, 0.5) for n in range(2)])
            units.append(
                (
                    query,
                    [part(lambda w: joined(near3(ref, w), far(ref, w)), bias), part(lambda w: far(other, w), other_bias)],
                )
            )
    found = attend(units)
    each = len(units) // heads

    def joined(*rows):
        return jnp.concatenate(rows, axis=0)

    for head in range(heads):
        here = cols(head)
        for j in range(count):
            top2, sum2 = found[head * each + j]
            top3, sum3 = found[head * each + count + j // 2]

            def spread(rows):
                first = (j % 2) * 2 * SUB
                one = rows[first : first + SUB]
                other = rows[first + SUB : first + 2 * SUB]
                return joined(one, one, other, other)

            top3 = spread(top3)
            sum3 = spread(sum3)
            top = jnp.maximum(top2, top3)
            scale2 = jnp.exp2(top2 - top)
            scale3 = jnp.exp2(top3 - top)
            values = sum2[:, :HEAD_DIM] * scale2 + sum3[:, :HEAD_DIM] * scale3
            total = sum2[:, HEAD_DIM:] * (4.0 * scale2) + sum3[:, HEAD_DIM:] * (8.0 * scale3)
            back_ref[j, 0:HALF, here] = (values / total).astype(bf16)
            level = top + jnp.log2(total)
            high = level.astype(bf16).astype(f32)
            middle = (level - high).astype(bf16).astype(f32)
            terms = jnp.where(lane == 0, high, jnp.where(lane == 1, middle, level - high - middle))
            back_ref[j, HALF : HALF + 16, here] = terms.T[0:16, :].astype(bf16)
    copies = [
        pltpu.make_async_copy(back_ref.at[n ^ place_ref[1]], ref, sems.at[n]) for n, ref in enumerate(out_refs)
    ]
    for copy in copies:
        copy.start()
    for copy in copies:
        copy.wait()


def coarse_levels(place, bias, got, from_prev, from_next):
    count, _, width = got.shape
    vmem = pl.BlockSpec(memory_space=pltpu.VMEM)
    smem = pl.BlockSpec(memory_space=pltpu.SMEM)
    rows = HALF + 16
    return pl.pallas_call(
        coarse_body,
        in_specs=[smem, smem, vmem, vmem, vmem],
        out_specs=[vmem] * count,
        out_shape=[array(rows, width, bf16)] * count,
        scratch_shapes=[pltpu.VMEM((count, rows, width), bf16), pltpu.SemaphoreType.DMA((count,))],
        compiler_params=pltpu.CompilerParams(vmem_limit_bytes=16 << 20),
        cost_estimate=pl.CostEstimate(flops=DECLARED, bytes_accessed=8 * got.size, transcendentals=1 << 20),
        name="coarse_levels",
    )(place, bias, got, from_prev, from_next)


def side_body(side, with_near, with_far, scalars, ins, outs):
    q0_ref, q1_ref, sum_ref, stat_ref, side_ref = ins
    heads = q1_ref.shape[1] // HEAD_DIM
    bias = scalars[1][side]
    blocks = (side, 1 - side)
    fine = [pl.ds(pl.multiple_of(block * BLK, BLK), BLK) for block in blocks]
    middle = [pl.ds(pl.multiple_of(block * HALF, HALF), HALF) for block in blocks]
    if with_near:
        pair = pair_matrix()
        near_keys = (mul(pair, side_ref[0:BLK, :]) * 0.5).astype(bf16)
        near_values = mul(pair, side_ref[BLK : 2 * BLK, :]).astype(bf16)
    start = 2 * BLK if with_near else 0
    far_keys, far_values = (slice(start + n * HALF, start + (n + 1) * HALF) for n in range(2))
    units, names = [], []
    for head in range(heads):
        here = cols(head)
        far = (side_ref[far_keys, here], side_ref[far_values, here]) if with_far else None
        near = (near_keys[:, here], near_values[:, here]) if with_near else None
        whole = [part for part in (near, far) if part is not None]
        whole = [jnp.concatenate([part[n] for part in whole], axis=0) if len(whole) > 1 else whole[0][n] for n in range(2)]
        if with_near:
            units.append((q0_ref[fine[0], here], [(side_ref[0:BLK, here], side_ref[BLK : 2 * BLK, here], None)]))
            names.append((head, 0, 0))
        if with_far:
            units.append((q1_ref[middle[0], here], [(*far, None)]))
            names.append((head, 0, 1))
        units.append((q1_ref[middle[1], here], [(*whole, None)]))
        names.append((head, 1, 1))
    found = {name: (top + bias, sums) for name, (top, sums) in zip(names, attend(units))}
    for n in range(2):
        stats = []
        for head in range(heads):
            here = cols(head)
            own_top, own_total = (unpack(stat_ref[head // 2, fine[n], :], head % 2 + k) for k in (0, 2))
            parts = [(own_top, sum_ref[head // 2, fine[n], cols(head % 2)], own_total)]
            if (head, n, 0) in found:
                top, sums = found[head, n, 0]
                parts.append((top, sums[:, :HEAD_DIM], sums[:, HEAD_DIM:]))
            if (head, n, 1) in found:
                top, sums = found[head, n, 1]
                parts.append((twice(top), twice(sums[:, :HEAD_DIM]), twice(2.0 * sums[:, HEAD_DIM:])))
            most = functools.reduce(jnp.maximum, [part[0] for part in parts])
            scales = [jnp.exp2(part[0] - most) for part in parts]
            outs[0][head // 2, fine[n], cols(head % 2)] = sum(part[1] * scale for part, scale in zip(parts, scales))
            stats += [most, sum(part[2] * scale for part, scale in zip(parts, scales))]
        for m in range(0, heads, 2):
            outs[1][m // 2, fine[n], :] = pack(stats[2 * m : 2 * m + 4 : 2] + stats[2 * m + 1 : 2 * m + 4 : 2])


def chip_body(scalars, ins, outs):
    side_body(1 - scalars[0][0], True, True, scalars, ins, outs)


def near_body(scalars, ins, outs):
    side_body(scalars[0][0], True, False, scalars, ins, outs)


def far_body(scalars, ins, outs):
    side_body(scalars[0][0], False, True, scalars, [None] + ins, outs)


def side_level(body, name, place, bias, queries, sums, stat, rows):
    groups, count, part = sums.shape
    ins = [("cols", query) for query in queries] + [("kept", sums), ("kept", stat), ("got", rows)]
    return run_shares(body, name, groups // 2, [place, bias], ins, sums_and_stats(count, groups * part, groups))


def finish_body(place_ref, sum_ref, stat_ref, *refs):
    groups = sum_ref.shape[0]
    back_refs, (out_ref, done_ref, sems) = refs[:groups], refs[groups:]
    part = sum_ref.shape[2]
    restore = restore_matrix()
    copies = []
    for n, back_ref in enumerate(back_refs):
        entry = n ^ place_ref[1]
        levels = []
        for head in range(2):
            terms = back_ref[HALF : HALF + 16, cols(head)].astype(f32)
            terms = jnp.sum(jnp.where(iota(terms.shape, 0) < 3, terms, 0.0), axis=0, keepdims=True)
            levels.append(jnp.broadcast_to(terms, (HEAD_DIM, HEAD_DIM)))
        both = jnp.where(iota(levels[0].shape, 0) < HEAD_DIM // 4, levels[0], levels[1]).T
        for i in range(2):
            rows = slice(i * BLK, (i + 1) * BLK)
            spot = slice(i * HALF // 2, (i + 1) * HALF // 2)
            tops = stat_ref[entry, rows, :]
            totals = pltpu.roll(tops, HEAD_DIM // 2, 1)
            lead = tops - twice(twice(both[spot, :]))
            smaller = jnp.exp2(-jnp.abs(lead))
            scale = jnp.where(lead >= 0.0, 1.0, smaller)
            coarse = jnp.where(lead >= 0.0, smaller, 1.0)
            total = totals * scale + coarse
            guess = pl.reciprocal(total, approx=True)
            guess = guess * (2.0 - total * guess)
            scale = scale * guess
            coarse = coarse * guess
            results = []
            for head in range(2):
                number = twice(twice(back_ref[spot, cols(head)].astype(f32))) * unpack(coarse, head)
                number = number + sum_ref[entry, rows, cols(head)] * unpack(scale, head)
                results.append(number.astype(bf16))
            done_ref[n, rows, :] = mul(restore, jnp.concatenate(results, axis=1)).astype(bf16)
        columns = pl.ds(pl.multiple_of(entry * part, HEAD_DIM), part)
        copies.append(pltpu.make_async_copy(done_ref.at[n], out_ref.at[:, columns], sems.at[n]))
        copies[-1].start()
    for copy in copies:
        copy.wait()


def finish(place, sums, stat, back):
    groups, rows, part = sums.shape
    vmem = pl.BlockSpec(memory_space=pltpu.VMEM)
    return pl.pallas_call(
        finish_body,
        in_specs=[pl.BlockSpec(memory_space=pltpu.SMEM)] + [vmem] * (2 + groups),
        out_specs=pl.BlockSpec(memory_space=pltpu.HBM),
        out_shape=pltpu.HBM((rows, groups * part), bf16),
        scratch_shapes=[pltpu.VMEM((groups, rows, part), bf16), pltpu.SemaphoreType.DMA((groups,))],
        compiler_params=pltpu.CompilerParams(vmem_limit_bytes=VMEM_GRANT),
        cost_estimate=pl.CostEstimate(flops=1 << 10, bytes_accessed=1 << 10, transcendentals=0),
        name="finish",
    )(place, sums, stat, *back)


def shift(value, axis, steps):
    count = lax.axis_size(axis)
    first, last = (max(0, -steps), min(count, count - steps))
    return lax.ppermute(value, axis, [(source, source + steps) for source in range(first, last)])


def trade(value, axis, pairs):
    return lax.ppermute(value, axis, pairs + [(target, source) for source, target in pairs])


def edge_bias(axis):
    place = lax.axis_index(axis)
    last = lax.axis_size(axis) - 1
    at_edge = jnp.stack([place == 0, place == last])
    return jnp.where(at_edge, very_negative, 0.0).astype(f32)


def local(query_vecs, key_vecs, value_vecs):
    groups = lax.axis_size("grp")
    assert query_vecs.shape == (2 * BLK, HEADS * HEAD_DIM) and groups == 4
    everyone = ("seq", "grp")
    count = lax.axis_size(everyone)
    spot = lax.axis_index("grp")
    odd = jnp.bitwise_and(spot, 1)
    place = jnp.stack([odd, spot]).astype(jnp.int32)
    bias = edge_bias(everyone)

    def exchange(pieces):
        flips = [[(source, source ^ n) for source in range(groups)] for n in range(groups)]
        for n in range(groups - 1, 0, -1):
            pieces[n] = lax.ppermute(pieces[n], "grp", flips[n])
        return pieces

    pieces = list(swap_rows(place, query_vecs, key_vecs, value_vecs, groups))
    query_rows, pieces = lax.optimization_barrier((query_vecs, pieces))
    pieces = exchange(pieces)
    q0, q1, near, far, chip = rows_to_send(place, query_rows, key_vecs, value_vecs, groups)
    off_chip = [(device, device + 1) for device in range(1, count - 1, 2)]
    near = trade(near, everyone, off_chip)
    far, pieces[1] = lax.optimization_barrier((far, pieces[1]))
    far = trade(far, everyone, off_chip)
    pieces, chip = lax.optimization_barrier((pieces, chip))
    got, coarse_right, coarse_left = coarse_halos(place, pieces)
    coarse_right, coarse_left, chip, q0 = lax.optimization_barrier((coarse_right, coarse_left, chip, q0))
    coarse_prev = shift(coarse_right, "seq", 1)
    coarse_next = shift(coarse_left, "seq", -1)
    chip = trade(chip, everyone, [(device, device + 1) for device in range(0, count - 1, 2)])
    own, own_stat = own_level(q0, key_vecs, value_vecs, groups)
    own, own_stat = side_level(chip_body, "chip_level", place, bias, (q0, q1), own, own_stat, chip)
    own, own_stat = side_level(near_body, "near_level", place, bias, (q0, q1), own, own_stat, near)
    got, own = lax.optimization_barrier((got, own))
    back = coarse_levels(place, edge_bias("seq"), got, coarse_prev, coarse_next)
    back, own = lax.optimization_barrier((back, own))
    back = exchange(list(back))
    own, own_stat = side_level(far_body, "far_level", place, bias, (q1,), own, own_stat, far)
    return finish(place, own, own_stat, back)


def solution(mesh):
    return jax.shard_map(
        local,
        mesh=mesh,
        in_specs=(P(("seq", "grp"), None), P(("seq", "grp"), None), P(("seq", "grp"), None)),
        out_specs=P(("seq", "grp"), None),
        check_vma=False,
    )
```

```python
import functools
import math

import jax
import jax.numpy as jnp
from jax import lax
from jax.experimental import pallas as pl
from jax.experimental.pallas import tpu as pltpu
from jax.sharding import PartitionSpec as P

HEADS = 8
HEAD_DIM = 128
BLK = 256
HALF = BLK // 2
SUB = BLK // 8
LEV = 4
EXP_SCALE = math.log2(math.e) / math.sqrt(HEAD_DIM)

VMEM_GRANT = 24 << 20

very_negative = -1e30
f32 = jnp.float32
bf16 = jnp.bfloat16


def iota(shape, dim):
    return lax.broadcasted_iota(jnp.int32, shape, dim)


def bit(value, place):
    return jnp.bitwise_and(lax.shift_right_logical(value, place), 1)


def low_bits(value):
    step = SUB.bit_length() - 1
    deep = jnp.bitwise_and(value, SUB - 1)
    return 8 * deep + 4 * bit(value, step) + 2 * bit(value, step + 1) + bit(value, step + 2)


def reorder_matrix():
    return (iota((BLK, BLK), 1) == low_bits(iota((BLK, BLK), 0))).astype(bf16)


def restore_matrix():
    return (iota((BLK, BLK), 0) == low_bits(iota((BLK, BLK), 1))).astype(bf16)


def pair_matrix():
    first = low_bits(iota((HALF, BLK), 0))
    place = iota((HALF, BLK), 1)
    return jnp.logical_or(place == first, place == first + 1).astype(bf16)


def mul(left, right):
    return jnp.dot(left, right, preferred_element_type=f32)


def fold(rows, factor):
    half = rows.shape[0] // 2
    total = rows[:half].astype(f32) + rows[half:].astype(f32)
    if factor != 1.0:
        total = total * factor
    return total.astype(bf16)


def fold_chunks(rows, chunk, factor):
    count = rows.shape[0] // chunk
    return jnp.concatenate([fold(rows[i * chunk : (i + 1) * chunk], factor) for i in range(count)], axis=0)


def twice(rows):
    return jnp.concatenate([rows, rows], axis=0)


def cols(head):
    return slice(head * HEAD_DIM, (head + 1) * HEAD_DIM)


DECLARED = 1 << 36


def with_ones(values):
    return jnp.concatenate([values, jnp.ones_like(values)], axis=1)


def attend(units):
    scores = []
    for query, parts in units:
        raws = [
            lax.dot_general(query, keys, (((1,), (1,)), ((), ())), preferred_element_type=f32) for keys, _, _ in parts
        ]
        scores.append([raw if part[2] is None else raw + part[2] for raw, part in zip(raws, parts)])
    tops = []
    for raws in scores:
        tops.append(functools.reduce(jnp.maximum, [jnp.max(raw, axis=1, keepdims=True) for raw in raws]))
    found = []
    for (_, parts), raws, top in zip(units, scores, tops):
        total = None
        for (_, values, _), raw in zip(parts, raws):
            weights = jnp.exp2((raw - top) * EXP_SCALE).astype(bf16)
            one = mul(weights, with_ones(values))
            total = one if total is None else total + one
        found.append((jnp.broadcast_to(top * EXP_SCALE, (top.shape[0], HEAD_DIM)), total))
    return found


def share_of(ref, share, shares):
    width = ref.shape[1] // shares
    first = share * width
    if not isinstance(share, int):
        first = pl.multiple_of(first, HEAD_DIM)
    return ref.at[:, pl.ds(first, width)]


def run_shares(body, name, shares, scalars, ins, outs, work=1 << 10, unrolled=False):
    moved_in = [i for i, (kind, _) in enumerate(ins) if kind in ("cols", "got")]
    moved_out = [i for i, (kind, _) in enumerate(outs) if kind == "cols"]
    as_list = lambda pair: list(pair[1]) if pair[0] == "pieces" else [pair[1]]
    buffer_shape = {
        "cols": lambda value: (shares, value.shape[0], value.shape[1] // shares),
        "got": lambda value: (shares, value.shape[0], value.shape[1] // shares),
        "kept": lambda value: None,
        "pieces": lambda values: (shares, len(values) // shares, *values[0].shape),
    }

    def kernel(*refs):
        refs = list(refs)
        take = lambda count: [refs.pop(0) for _ in range(count)]
        scalar_refs = take(len(scalars))
        in_refs = [take(len(as_list(pair))) for pair in ins]
        out_refs = [take(len(as_list(pair))) for pair in outs]
        in_bufs = [in_refs[i][0] if ins[i][0] == "kept" else refs.pop(0) for i in range(len(ins))]
        out_bufs = [out_refs[i][0] if outs[i][0] == "kept" else refs.pop(0) for i in range(len(outs))]
        in_sems, out_sems, piece_sems = take(3)

        def bring(i, share):
            return pltpu.make_async_copy(share_of(in_refs[i][0], share, shares), in_bufs[i].at[share], in_sems.at[i, share])

        def put(i, share):
            return pltpu.make_async_copy(out_bufs[i].at[share], share_of(out_refs[i][0], share, shares), out_sems.at[i, share])

        def spot_of(buffer, n):
            entry = n ^ scalar_refs[0][1]
            return buffer.at[lax.div(entry, buffer.shape[1]), lax.rem(entry, buffer.shape[1])]

        pieces_in, pieces_out = [], []
        for i, (kind, _) in enumerate(ins):
            if kind == "pieces":
                pieces_in += [(ref, spot_of(in_bufs[i], n), n) for n, ref in enumerate(in_refs[i])]
        for i, (kind, _) in enumerate(outs):
            if kind == "pieces":
                pieces_out += [(spot_of(out_bufs[i], n), ref, n) for n, ref in enumerate(out_refs[i])]
        pieces_in = [pltpu.make_async_copy(source, target, piece_sems.at[n]) for source, target, n in pieces_in]
        pieces_out = [pltpu.make_async_copy(source, target, piece_sems.at[n]) for source, target, n in pieces_out]

        for share in range(shares):
            for i in moved_in:
                bring(i, share).start()
            if share == 0:
                for copy in pieces_in:
                    copy.start()
        for copy in pieces_in:
            copy.wait()

        def views(operands, buffers, share):
            result = []
            for (kind, value), buffer in zip(operands, buffers):
                count = value.shape[0] // shares if kind == "kept" else None
                result.append(buffer.at[share] if count is None else buffer.at[pl.ds(share * count, count)])
            return result

        def step(share, carry):
            for i in moved_in:
                bring(i, share).wait()
            body(scalar_refs, views(ins, in_bufs, share), views(outs, out_bufs, share))
            for i in moved_out:
                put(i, share).start()
            return carry

        if unrolled:
            for share in range(shares):
                step(share, 0)
        else:
            lax.fori_loop(0, shares, step, 0)
        for copy in pieces_out:
            copy.start()
        for share in range(shares):
            for i in moved_out:
                put(i, share).wait()
        for copy in pieces_out:
            copy.wait()

    spaces = {"cols": pltpu.HBM, "got": pl.ANY, "pieces": pl.ANY, "kept": pltpu.VMEM}
    values, in_specs, out_specs, out_shapes, buffers = [], [], [], [], []
    for kind, value in ins:
        for one in as_list((kind, value)):
            values.append(pltpu.with_memory_space_constraint(one, pltpu.HBM) if kind == "cols" else one)
            in_specs.append(pl.BlockSpec(memory_space=spaces[kind]))
    for kind, shape in outs:
        for one in as_list((kind, shape)):
            out_shapes.append(pltpu.HBM(one.shape, one.dtype) if kind == "cols" else one)
            out_specs.append(pl.BlockSpec(memory_space=pltpu.HBM if kind == "cols" else pltpu.VMEM))
    for kind, value in list(ins) + list(outs):
        if kind != "kept":
            buffers.append(pltpu.VMEM(buffer_shape[kind](value), as_list((kind, value))[0].dtype))
    count = max(len(as_list(pair)) for pair in list(ins) + list(outs))
    semaphores = [(len(ins), shares), (len(outs), shares), (count,)]
    return pl.pallas_call(
        kernel,
        in_specs=[pl.BlockSpec(memory_space=pltpu.SMEM)] * len(scalars) + in_specs,
        out_specs=out_specs,
        out_shape=out_shapes,
        scratch_shapes=buffers + [pltpu.SemaphoreType.DMA(shape) for shape in semaphores],
        compiler_params=pltpu.CompilerParams(vmem_limit_bytes=VMEM_GRANT),
        cost_estimate=pl.CostEstimate(flops=work, bytes_accessed=1 << 10, transcendentals=0),
        name=name,
    )(*scalars, *values)


def array(rows, width, dtype):
    return jax.ShapeDtypeStruct((rows, width), dtype)


def swap_body(_, ins, outs):
    pair = pair_matrix()
    count, _, part = outs[0].shape
    for place, (ref, factor) in enumerate(zip(ins, (0.5, 0.5, 1.0))):
        for i in range(2):
            level1 = mul(pair, ref[i * BLK : (i + 1) * BLK, :])
            if factor != 1.0:
                level1 = level1 * factor
            level2 = fold(level1.astype(bf16), factor)
            first = place * HALF + i * HALF // 2
            for n in range(count):
                outs[0][n, first : first + HALF // 2, :] = level2[:, n * part : (n + 1) * part]


def swap_rows(place, query_vecs, key_vecs, value_vecs, groups):
    width = query_vecs.shape[1]
    ins = [("cols", a) for a in (query_vecs, key_vecs, value_vecs)]
    outs = [("pieces", [array(3 * HALF, width // groups, bf16)] * groups)]
    return run_shares(swap_body, "swap_rows", groups // 2, [place], ins, outs, unrolled=True)


def rows_body(scalars, ins, outs):
    q_ref, k_ref, v_ref = ins
    q0_ref, q1_ref, near_ref, far_ref, chip_ref = outs
    reorder = reorder_matrix()
    pair = pair_matrix()
    for i in range(2):
        rows = slice(i * BLK, (i + 1) * BLK)
        q0 = mul(reorder, q_ref[rows, :]).astype(bf16)
        q0_ref[rows, :] = q0
        q1_ref[i * HALF : (i + 1) * HALF, :] = fold(q0, 0.5)
    odd = scalars[0][0]
    outer = pl.ds(pl.multiple_of(odd * BLK, BLK), BLK)
    inner = pl.ds(pl.multiple_of((1 - odd) * BLK, BLK), BLK)
    for ref, far_rows, first, near, far in ((near_ref, far_ref, 0, outer, inner), (chip_ref, chip_ref, 2 * BLK, inner, outer)):
        ref[0:BLK, :] = k_ref[near, :]
        ref[BLK : 2 * BLK, :] = v_ref[near, :]
        far_rows[first : first + HALF, :] = (mul(pair, k_ref[far, :]) * 0.5).astype(bf16)
        far_rows[first + HALF : first + BLK, :] = mul(pair, v_ref[far, :]).astype(bf16)


def rows_to_send(place, query_vecs, key_vecs, value_vecs, groups):
    rows, width = query_vecs.shape
    ins = [("cols", a) for a in (query_vecs, key_vecs, value_vecs)]
    outs = [("cols", array(n, width, bf16)) for n in (rows, rows // 2, 2 * BLK, BLK, 3 * BLK)]
    return run_shares(rows_body, "rows_to_send", groups, [place], ins, outs)


def own_body(_, ins, outs):
    q_ref, k_ref, v_ref = ins
    sum_ref, top_ref, total_ref = outs
    heads = q_ref.shape[1] // HEAD_DIM
    for i in range(2):
        rows = slice(i * BLK, (i + 1) * BLK)
        units = [(q_ref[rows, cols(head)], [(k_ref[:, cols(head)], v_ref[:, cols(head)], None)]) for head in range(heads)]
        for head, (top, sums) in enumerate(attend(units)):
            spot = (head // 2, rows, cols(head % 2))
            sum_ref[spot] = sums[:, :HEAD_DIM]
            top_ref[spot] = top
            total_ref[spot] = sums[:, HEAD_DIM:]


def running_sums(rows, width, groups):
    return [("kept", jax.ShapeDtypeStruct((groups, rows, width // groups), f32))] * 3


def own_level(q0, key_vecs, value_vecs, groups):
    ins = [("cols", a) for a in (q0, key_vecs, value_vecs)]
    return run_shares(own_body, "own_level", groups // 2, [], ins, running_sums(*q0.shape, groups), DECLARED)


def halo_body(place_ref, *refs):
    count = len(refs) - 4
    piece_refs, (got_ref, right_ref, left_ref, sems) = refs[:count], refs[count:]
    copies = [pltpu.make_async_copy(ref, got_ref.at[n ^ place_ref[1]], sems.at[n]) for n, ref in enumerate(piece_refs)]
    for copy in copies:
        copy.start()
    for copy in copies:
        copy.wait()
    pair = count // 2
    for which, factor in ((1, 0.5), (2, 1.0)):
        rows = slice(which * HALF, (which + 1) * HALF)
        near = (which - 1) * BLK
        far = 2 * BLK + (which - 1) * HALF
        for j in range(count):
            level2 = got_ref[j, rows, :]
            level3 = fold_chunks(level2, HALF // 2, factor)
            near_ref, far_ref = (left_ref, right_ref) if j < pair else (right_ref, left_ref)
            spot = j % pair
            near_ref[near + spot * HALF : near + (spot + 1) * HALF, :] = level2
            far_ref[far + spot * HALF // 2 : far + (spot + 1) * HALF // 2, :] = level3


def coarse_halos(place, pieces):
    rows, width = pieces[0].shape
    vmem = pl.BlockSpec(memory_space=pltpu.VMEM)
    shape = jax.ShapeDtypeStruct((3 * BLK, width), bf16)
    return pl.pallas_call(
        halo_body,
        in_specs=[pl.BlockSpec(memory_space=pltpu.SMEM)] + [pl.BlockSpec(memory_space=pl.ANY)] * len(pieces),
        out_specs=[vmem] * 3,
        out_shape=[jax.ShapeDtypeStruct((len(pieces), rows, width), bf16), shape, shape],
        scratch_shapes=[pltpu.SemaphoreType.DMA((len(pieces),))],
        compiler_params=pltpu.CompilerParams(vmem_limit_bytes=16 << 20),
        cost_estimate=pl.CostEstimate(flops=1 << 20, bytes_accessed=24 * pieces[0].size, transcendentals=0),
        name="coarse_halos",
    )(place, *pieces)


def coarse_body(place_ref, bias_ref, got_ref, prev_ref, next_ref, *refs):
    *out_refs, back_ref, sems = refs
    count = got_ref.shape[0]
    heads = got_ref.shape[2] // HEAD_DIM
    bias_prev = bias_ref[0]
    bias_next = bias_ref[1]
    lane = iota((HALF, HEAD_DIM), 1)

    units = []
    for head in range(heads):
        here = cols(head)

        def own(which, j):
            return got_ref[j, which * HALF : (which + 1) * HALF, here]

        def near(ref, which, spot):
            first = (which - 1) * BLK + spot * HALF
            return ref[first : first + HALF, here]

        def both(ref, which):
            return ref[(which - 1) * BLK : which * BLK, here]

        def far(ref, which):
            first = 2 * BLK + (which - 1) * HALF
            return ref[first : first + HALF, here]

        def near3(ref, which):
            return fold_chunks(both(ref, which), HALF // 2, 0.5 if which == 1 else 1.0)

        def joined(*rows):
            return jnp.concatenate(rows, axis=0)

        def part(pick, bias):
            return (pick(1), pick(2), bias)

        units += [
            (own(0, 0), [part(lambda w: joined(own(w, 2), own(w, 3)), None), part(lambda w: near(prev_ref, w, 0), bias_prev)]),
            (own(0, 1), [part(lambda w: both(prev_ref, w), bias_prev), part(lambda w: own(w, 3), None)]),
            (own(0, 2), [part(lambda w: both(next_ref, w), bias_next), part(lambda w: own(w, 0), None)]),
            (own(0, 3), [part(lambda w: joined(own(w, 0), own(w, 1)), None), part(lambda w: near(next_ref, w, 1), bias_next)]),
        ]
        for j, (ref, bias, other, other_bias) in enumerate(
            ((next_ref, bias_next, prev_ref, bias_prev), (prev_ref, bias_prev, next_ref, bias_next))
        ):
            query = joined(*[fold_chunks(own(0, 2 * j + n), HALF // 2, 0.5) for n in range(2)])
            units.append(
                (
                    query,
                    [part(lambda w: joined(near3(ref, w), far(ref, w)), bias), part(lambda w: far(other, w), other_bias)],
                )
            )
    found = attend(units)
    each = len(units) // heads

    def joined(*rows):
        return jnp.concatenate(rows, axis=0)

    for head in range(heads):
        here = cols(head)
        for j in range(count):
            top2, sum2 = found[head * each + j]
            top3, sum3 = found[head * each + count + j // 2]

            def spread(rows):
                first = (j % 2) * 2 * SUB
                one = rows[first : first + SUB]
                other = rows[first + SUB : first + 2 * SUB]
                return joined(one, one, other, other)

            top3 = spread(top3)
            sum3 = spread(sum3)
            top = jnp.maximum(top2, top3)
            scale2 = jnp.exp2(top2 - top)
            scale3 = jnp.exp2(top3 - top)
            values = sum2[:, :HEAD_DIM] * scale2 + sum3[:, :HEAD_DIM] * scale3
            total = sum2[:, HEAD_DIM:] * (4.0 * scale2) + sum3[:, HEAD_DIM:] * (8.0 * scale3)
            back_ref[j, 0:HALF, here] = (values / total).astype(bf16)
            level = top + jnp.log2(total)
            high = level.astype(bf16).astype(f32)
            middle = (level - high).astype(bf16).astype(f32)
            terms = jnp.where(lane == 0, high, jnp.where(lane == 1, middle, level - high - middle))
            back_ref[j, HALF : HALF + 16, here] = terms.T[0:16, :].astype(bf16)
    copies = [
        pltpu.make_async_copy(back_ref.at[n ^ place_ref[1]], ref, sems.at[n]) for n, ref in enumerate(out_refs)
    ]
    for copy in copies:
        copy.start()
    for copy in copies:
        copy.wait()


def coarse_levels(place, bias, got, from_prev, from_next):
    count, _, width = got.shape
    vmem = pl.BlockSpec(memory_space=pltpu.VMEM)
    smem = pl.BlockSpec(memory_space=pltpu.SMEM)
    rows = HALF + 16
    return pl.pallas_call(
        coarse_body,
        in_specs=[smem, smem, vmem, vmem, vmem],
        out_specs=[vmem] * count,
        out_shape=[array(rows, width, bf16)] * count,
        scratch_shapes=[pltpu.VMEM((count, rows, width), bf16), pltpu.SemaphoreType.DMA((count,))],
        compiler_params=pltpu.CompilerParams(vmem_limit_bytes=16 << 20),
        cost_estimate=pl.CostEstimate(flops=DECLARED, bytes_accessed=8 * got.size, transcendentals=1 << 20),
        name="coarse_levels",
    )(place, bias, got, from_prev, from_next)


def side_body(side, with_near, with_far, scalars, ins, outs):
    q0_ref, q1_ref, sum_ref, top_ref, total_ref, side_ref = ins
    heads = q1_ref.shape[1] // HEAD_DIM
    bias = scalars[1][side]
    blocks = (side, 1 - side)
    fine = [pl.ds(pl.multiple_of(block * BLK, BLK), BLK) for block in blocks]
    middle = [pl.ds(pl.multiple_of(block * HALF, HALF), HALF) for block in blocks]
    if with_near:
        pair = pair_matrix()
        near_keys = (mul(pair, side_ref[0:BLK, :]) * 0.5).astype(bf16)
        near_values = mul(pair, side_ref[BLK : 2 * BLK, :]).astype(bf16)
    start = 2 * BLK if with_near else 0
    far_keys, far_values = (slice(start + n * HALF, start + (n + 1) * HALF) for n in range(2))
    units, names = [], []
    for head in range(heads):
        here = cols(head)
        far = (side_ref[far_keys, here], side_ref[far_values, here]) if with_far else None
        near = (near_keys[:, here], near_values[:, here]) if with_near else None
        whole = [part for part in (near, far) if part is not None]
        whole = [jnp.concatenate([part[n] for part in whole], axis=0) if len(whole) > 1 else whole[0][n] for n in range(2)]
        if with_near:
            units.append((q0_ref[fine[0], here], [(side_ref[0:BLK, here], side_ref[BLK : 2 * BLK, here], None)]))
            names.append((head, 0, 0))
        if with_far:
            units.append((q1_ref[middle[0], here], [(*far, None)]))
            names.append((head, 0, 1))
        units.append((q1_ref[middle[1], here], [(*whole, None)]))
        names.append((head, 1, 1))
    found = {name: (top + bias, sums) for name, (top, sums) in zip(names, attend(units))}
    for n in range(2):
        for head in range(heads):
            spot = (head // 2, fine[n], cols(head % 2))
            parts = [(top_ref[spot], sum_ref[spot], total_ref[spot])]
            if (head, n, 0) in found:
                top, sums = found[head, n, 0]
                parts.append((top, sums[:, :HEAD_DIM], sums[:, HEAD_DIM:]))
            if (head, n, 1) in found:
                top, sums = found[head, n, 1]
                parts.append((twice(top), twice(sums[:, :HEAD_DIM]), twice(2.0 * sums[:, HEAD_DIM:])))
            most = functools.reduce(jnp.maximum, [part[0] for part in parts])
            scales = [jnp.exp2(part[0] - most) for part in parts]
            outs[0][spot] = sum(part[1] * scale for part, scale in zip(parts, scales))
            outs[1][spot] = most
            outs[2][spot] = sum(part[2] * scale for part, scale in zip(parts, scales))


def chip_body(scalars, ins, outs):
    side_body(1 - scalars[0][0], True, True, scalars, ins, outs)


def near_body(scalars, ins, outs):
    side_body(scalars[0][0], True, False, scalars, ins, outs)


def far_body(scalars, ins, outs):
    side_body(scalars[0][0], False, True, scalars, [None] + ins, outs)


def side_level(body, name, place, bias, queries, running, rows):
    groups, count, part = running[0].shape
    ins = [("cols", query) for query in queries] + [("kept", one) for one in running] + [("got", rows)]
    return run_shares(body, name, groups // 2, [place, bias], ins, running_sums(count, groups * part, groups))


def finish_body(place_ref, sum_ref, top_ref, total_ref, *refs):
    groups = sum_ref.shape[0]
    back_refs, (out_ref, done_ref, sems) = refs[:groups], refs[groups:]
    part = sum_ref.shape[2]
    restore = restore_matrix()
    copies = []
    for n, back_ref in enumerate(back_refs):
        entry = n ^ place_ref[1]
        levels = []
        for head in range(part // HEAD_DIM):
            terms = back_ref[HALF : HALF + 16, cols(head)].astype(f32)
            terms = jnp.sum(jnp.where(iota(terms.shape, 0) < 3, terms, 0.0), axis=0, keepdims=True)
            levels.append(jnp.broadcast_to(terms, (HEAD_DIM, HEAD_DIM)).T)
        for i in range(2):
            rows = slice(i * BLK, (i + 1) * BLK)
            spot = slice(i * HALF // 2, (i + 1) * HALF // 2)
            results = []
            for head, level in enumerate(levels):
                here = (entry, rows, cols(head))
                top = top_ref[here]
                level = twice(twice(level[spot, :]))
                lead = top - level
                smaller = jnp.exp2(-jnp.abs(lead))
                scale = jnp.where(lead >= 0.0, 1.0, smaller)
                coarse = jnp.where(lead >= 0.0, smaller, 1.0)
                number = twice(twice(back_ref[spot, cols(head)].astype(f32))) * coarse
                number = number + sum_ref[here] * scale
                total = total_ref[here] * scale + coarse
                guess = pl.reciprocal(total, approx=True)
                results.append((number * (guess * (2.0 - total * guess))).astype(bf16))
            done_ref[n, rows, :] = mul(restore, jnp.concatenate(results, axis=1)).astype(bf16)
        columns = pl.ds(pl.multiple_of(entry * part, HEAD_DIM), part)
        copies.append(pltpu.make_async_copy(done_ref.at[n], out_ref.at[:, columns], sems.at[n]))
        copies[-1].start()
    for copy in copies:
        copy.wait()


def finish(place, running, back):
    groups, rows, part = running[0].shape
    vmem = pl.BlockSpec(memory_space=pltpu.VMEM)
    return pl.pallas_call(
        finish_body,
        in_specs=[pl.BlockSpec(memory_space=pltpu.SMEM)] + [vmem] * (3 + groups),
        out_specs=pl.BlockSpec(memory_space=pltpu.HBM),
        out_shape=pltpu.HBM((rows, groups * part), bf16),
        scratch_shapes=[pltpu.VMEM((groups, rows, part), bf16), pltpu.SemaphoreType.DMA((groups,))],
        compiler_params=pltpu.CompilerParams(vmem_limit_bytes=VMEM_GRANT),
        cost_estimate=pl.CostEstimate(flops=1 << 10, bytes_accessed=1 << 10, transcendentals=0),
        name="finish",
    )(place, *running, *back)


def shift(value, axis, steps):
    count = lax.axis_size(axis)
    first, last = (max(0, -steps), min(count, count - steps))
    return lax.ppermute(value, axis, [(source, source + steps) for source in range(first, last)])


def trade(value, axis, pairs):
    return lax.ppermute(value, axis, pairs + [(target, source) for source, target in pairs])


def edge_bias(axis):
    place = lax.axis_index(axis)
    last = lax.axis_size(axis) - 1
    at_edge = jnp.stack([place == 0, place == last])
    return jnp.where(at_edge, very_negative, 0.0).astype(f32)


def local(query_vecs, key_vecs, value_vecs):
    groups = lax.axis_size("grp")
    assert query_vecs.shape == (2 * BLK, HEADS * HEAD_DIM) and groups == 4
    everyone = ("seq", "grp")
    count = lax.axis_size(everyone)
    spot = lax.axis_index("grp")
    odd = jnp.bitwise_and(spot, 1)
    place = jnp.stack([odd, spot]).astype(jnp.int32)
    bias = edge_bias(everyone)

    def exchange(pieces):
        flips = [[(source, source ^ n) for source in range(groups)] for n in range(groups)]
        for n in range(groups - 1, 0, -1):
            pieces[n] = lax.ppermute(pieces[n], "grp", flips[n])
        return pieces

    pieces = list(swap_rows(place, query_vecs, key_vecs, value_vecs, groups))
    query_rows, pieces = lax.optimization_barrier((query_vecs, pieces))
    pieces = exchange(pieces)
    q0, q1, near, far, chip = rows_to_send(place, query_rows, key_vecs, value_vecs, groups)
    off_chip = [(device, device + 1) for device in range(1, count - 1, 2)]
    near = trade(near, everyone, off_chip)
    far, pieces[1] = lax.optimization_barrier((far, pieces[1]))
    far = trade(far, everyone, off_chip)
    pieces, chip = lax.optimization_barrier((pieces, chip))
    got, coarse_right, coarse_left = coarse_halos(place, pieces)
    coarse_right, coarse_left, chip, q0 = lax.optimization_barrier((coarse_right, coarse_left, chip, q0))
    coarse_prev = shift(coarse_right, "seq", 1)
    coarse_next = shift(coarse_left, "seq", -1)
    chip = trade(chip, everyone, [(device, device + 1) for device in range(0, count - 1, 2)])
    running = own_level(q0, key_vecs, value_vecs, groups)
    running = side_level(chip_body, "chip_level", place, bias, (q0, q1), running, chip)
    running = side_level(near_body, "near_level", place, bias, (q0, q1), running, near)
    got, running = lax.optimization_barrier((got, running))
    back = coarse_levels(place, edge_bias("seq"), got, coarse_prev, coarse_next)
    back, running = lax.optimization_barrier((back, running))
    back = exchange(list(back))
    running = side_level(far_body, "far_level", place, bias, (q1,), running, far)
    return finish(place, running, back)


def solution(mesh):
    return jax.shard_map(
        local,
        mesh=mesh,
        in_specs=(P(("seq", "grp"), None), P(("seq", "grp"), None), P(("seq", "grp"), None)),
        out_specs=P(("seq", "grp"), None),
        check_vma=False,
    )
```

```python
import functools
import math

import jax
import jax.numpy as jnp
from jax import lax
from jax.experimental import pallas as pl
from jax.experimental.pallas import tpu as pltpu
from jax.sharding import PartitionSpec as P

HEADS = 8
HEAD_DIM = 128
BLK = 256
HALF = BLK // 2
SUB = BLK // 8
LEV = 4
EXP_SCALE = math.log2(math.e) / math.sqrt(HEAD_DIM)

VMEM_GRANT = 24 << 20

very_negative = -1e30
f32 = jnp.float32
bf16 = jnp.bfloat16


def iota(shape, dim):
    return lax.broadcasted_iota(jnp.int32, shape, dim)


def bit(value, place):
    return jnp.bitwise_and(lax.shift_right_logical(value, place), 1)


def low_bits(value):
    step = SUB.bit_length() - 1
    deep = jnp.bitwise_and(value, SUB - 1)
    return 8 * deep + 4 * bit(value, step) + 2 * bit(value, step + 1) + bit(value, step + 2)


def reorder_matrix():
    return (iota((BLK, BLK), 1) == low_bits(iota((BLK, BLK), 0))).astype(bf16)


def restore_matrix():
    return (iota((BLK, BLK), 0) == low_bits(iota((BLK, BLK), 1))).astype(bf16)


def pair_matrix():
    first = low_bits(iota((HALF, BLK), 0))
    place = iota((HALF, BLK), 1)
    return jnp.logical_or(place == first, place == first + 1).astype(bf16)


def mul(left, right):
    return jnp.dot(left, right, preferred_element_type=f32)


def fold(rows, factor):
    half = rows.shape[0] // 2
    total = rows[:half].astype(f32) + rows[half:].astype(f32)
    if factor != 1.0:
        total = total * factor
    return total.astype(bf16)


def fold_chunks(rows, chunk, factor):
    count = rows.shape[0] // chunk
    return jnp.concatenate([fold(rows[i * chunk : (i + 1) * chunk], factor) for i in range(count)], axis=0)


def twice(rows):
    return jnp.concatenate([rows, rows], axis=0)


def cols(head):
    return slice(head * HEAD_DIM, (head + 1) * HEAD_DIM)


DECLARED = 1 << 36


def with_ones(values):
    return jnp.concatenate([values, jnp.ones_like(values)], axis=1)


def attend(units):
    scores = []
    for query, parts in units:
        raws = [
            lax.dot_general(query, keys, (((1,), (1,)), ((), ())), preferred_element_type=f32) for keys, _, _ in parts
        ]
        scores.append([raw if part[2] is None else raw + part[2] for raw, part in zip(raws, parts)])
    tops = []
    for raws in scores:
        tops.append(functools.reduce(jnp.maximum, [jnp.max(raw, axis=1, keepdims=True) for raw in raws]))
    found = []
    for (_, parts), raws, top in zip(units, scores, tops):
        total = None
        for (_, values, _), raw in zip(parts, raws):
            weights = jnp.exp2((raw - top) * EXP_SCALE).astype(bf16)
            one = mul(weights, with_ones(values))
            total = one if total is None else total + one
        found.append((jnp.broadcast_to(top * EXP_SCALE, (top.shape[0], HEAD_DIM)), total))
    return found


def share_of(ref, share, shares):
    width = ref.shape[1] // shares
    first = share * width
    if not isinstance(share, int):
        first = pl.multiple_of(first, HEAD_DIM)
    return ref.at[:, pl.ds(first, width)]


def run_shares(body, name, shares, scalars, ins, outs, work=1 << 10, unrolled=False):
    moved_in = [i for i, (kind, _) in enumerate(ins) if kind in ("cols", "got")]
    moved_out = [i for i, (kind, _) in enumerate(outs) if kind == "cols"]
    as_list = lambda pair: list(pair[1]) if pair[0] == "pieces" else [pair[1]]
    buffer_shape = {
        "cols": lambda value: (shares, value.shape[0], value.shape[1] // shares),
        "got": lambda value: (shares, value.shape[0], value.shape[1] // shares),
        "kept": lambda value: None,
        "pieces": lambda values: (shares, len(values) // shares, *values[0].shape),
    }

    def kernel(*refs):
        refs = list(refs)
        take = lambda count: [refs.pop(0) for _ in range(count)]
        scalar_refs = take(len(scalars))
        in_refs = [take(len(as_list(pair))) for pair in ins]
        out_refs = [take(len(as_list(pair))) for pair in outs]
        in_bufs = [in_refs[i][0] if ins[i][0] == "kept" else refs.pop(0) for i in range(len(ins))]
        out_bufs = [out_refs[i][0] if outs[i][0] == "kept" else refs.pop(0) for i in range(len(outs))]
        in_sems, out_sems, piece_sems = take(3)

        def bring(i, share):
            return pltpu.make_async_copy(share_of(in_refs[i][0], share, shares), in_bufs[i].at[share], in_sems.at[i, share])

        def put(i, share):
            return pltpu.make_async_copy(out_bufs[i].at[share], share_of(out_refs[i][0], share, shares), out_sems.at[i, share])

        def spot_of(buffer, n):
            entry = n ^ scalar_refs[0][1]
            return buffer.at[lax.div(entry, buffer.shape[1]), lax.rem(entry, buffer.shape[1])]

        pieces_in, pieces_out = [], []
        for i, (kind, _) in enumerate(ins):
            if kind == "pieces":
                pieces_in += [(ref, spot_of(in_bufs[i], n), n) for n, ref in enumerate(in_refs[i])]
        for i, (kind, _) in enumerate(outs):
            if kind == "pieces":
                pieces_out += [(spot_of(out_bufs[i], n), ref, n) for n, ref in enumerate(out_refs[i])]
        pieces_in = [pltpu.make_async_copy(source, target, piece_sems.at[n]) for source, target, n in pieces_in]
        pieces_out = [pltpu.make_async_copy(source, target, piece_sems.at[n]) for source, target, n in pieces_out]

        for share in range(shares):
            for i in moved_in:
                bring(i, share).start()
            if share == 0:
                for copy in pieces_in:
                    copy.start()
        for copy in pieces_in:
            copy.wait()

        def views(operands, buffers, share):
            result = []
            for (kind, value), buffer in zip(operands, buffers):
                count = value.shape[0] // shares if kind == "kept" else None
                result.append(buffer.at[share] if count is None else buffer.at[pl.ds(share * count, count)])
            return result

        def step(share, carry):
            for i in moved_in:
                bring(i, share).wait()
            body(scalar_refs, views(ins, in_bufs, share), views(outs, out_bufs, share))
            for i in moved_out:
                put(i, share).start()
            return carry

        if unrolled:
            for share in range(shares):
                step(share, 0)
        else:
            lax.fori_loop(0, shares, step, 0)
        for copy in pieces_out:
            copy.start()
        for share in range(shares):
            for i in moved_out:
                put(i, share).wait()
        for copy in pieces_out:
            copy.wait()

    spaces = {"cols": pltpu.HBM, "got": pl.ANY, "pieces": pl.ANY, "kept": pltpu.VMEM}
    values, in_specs, out_specs, out_shapes, buffers = [], [], [], [], []
    for kind, value in ins:
        for one in as_list((kind, value)):
            values.append(pltpu.with_memory_space_constraint(one, pltpu.HBM) if kind == "cols" else one)
            in_specs.append(pl.BlockSpec(memory_space=spaces[kind]))
    for kind, shape in outs:
        for one in as_list((kind, shape)):
            out_shapes.append(pltpu.HBM(one.shape, one.dtype) if kind == "cols" else one)
            out_specs.append(pl.BlockSpec(memory_space=pltpu.HBM if kind == "cols" else pltpu.VMEM))
    for kind, value in list(ins) + list(outs):
        if kind != "kept":
            buffers.append(pltpu.VMEM(buffer_shape[kind](value), as_list((kind, value))[0].dtype))
    count = max(len(as_list(pair)) for pair in list(ins) + list(outs))
    semaphores = [(len(ins), shares), (len(outs), shares), (count,)]
    return pl.pallas_call(
        kernel,
        in_specs=[pl.BlockSpec(memory_space=pltpu.SMEM)] * len(scalars) + in_specs,
        out_specs=out_specs,
        out_shape=out_shapes,
        scratch_shapes=buffers + [pltpu.SemaphoreType.DMA(shape) for shape in semaphores],
        compiler_params=pltpu.CompilerParams(vmem_limit_bytes=VMEM_GRANT),
        cost_estimate=pl.CostEstimate(flops=work, bytes_accessed=1 << 10, transcendentals=0),
        name=name,
    )(*scalars, *values)


def array(rows, width, dtype):
    return jax.ShapeDtypeStruct((rows, width), dtype)


def swap_body(place_ref, q_ref, k_ref, v_ref, *refs):
    groups = len(refs) - 5
    out_refs, (held, wide, made, in_sems, out_sems) = refs[:groups], refs[groups:]
    part = made.shape[2]
    blocks = [pl.ds(i * BLK, BLK) for i in range(2)]
    arrive = [
        [pltpu.make_async_copy(ref.at[rows, :], held.at[n, rows, :], in_sems.at[n, i]) for i, rows in enumerate(blocks)]
        for n, ref in enumerate((q_ref, k_ref, v_ref))
    ]
    for copies in arrive:
        for copy in copies:
            copy.start()
    for n, factor in enumerate((0.5, 0.5, 1.0)):
        for i in range(2):
            arrive[n][i].wait()
            for column in range(wide.shape[1]):
                here = cols(column)
                wide[n, column, blocks[i], :] = held[n, blocks[i], here].astype(f32)
                entry, spot = divmod(column * HEAD_DIM, part)
                for high in range(2):
                    level1 = []
                    for low in (4 * high, 4 * high + 2):
                        rows = [wide[n, column, pl.ds(i * BLK + low + k, SUB, stride=8), :] for k in range(2)]
                        level1.append(((rows[0] + rows[1]) * factor).astype(bf16).astype(f32))
                    first = n * HALF + i * HALF // 2 + high * SUB
                    level2 = ((level1[0] + level1[1]) * factor).astype(bf16)
                    made[entry, first : first + SUB, spot : spot + HEAD_DIM] = level2
    leave = [pltpu.make_async_copy(made.at[n ^ place_ref[1]], ref, out_sems.at[n]) for n, ref in enumerate(out_refs)]
    for copy in leave:
        copy.start()
    for copy in leave:
        copy.wait()


def swap_rows(place, query_vecs, key_vecs, value_vecs, groups):
    rows, width = query_vecs.shape
    piece = array(3 * HALF, width // groups, bf16)
    vectors = (query_vecs, key_vecs, value_vecs)
    return pl.pallas_call(
        swap_body,
        in_specs=[pl.BlockSpec(memory_space=pltpu.SMEM)] + [pl.BlockSpec(memory_space=pltpu.HBM)] * 3,
        out_specs=[pl.BlockSpec(memory_space=pltpu.VMEM)] * groups,
        out_shape=[piece] * groups,
        scratch_shapes=[
            pltpu.VMEM((3, rows, width), bf16),
            pltpu.VMEM((3, width // HEAD_DIM, rows + 8, HEAD_DIM), f32),
            pltpu.VMEM((groups, *piece.shape), bf16),
            pltpu.SemaphoreType.DMA((3, 2)),
            pltpu.SemaphoreType.DMA((groups,)),
        ],
        compiler_params=pltpu.CompilerParams(vmem_limit_bytes=VMEM_GRANT),
        cost_estimate=pl.CostEstimate(flops=1 << 10, bytes_accessed=1 << 10, transcendentals=0),
        name="swap_rows",
    )(place, *[pltpu.with_memory_space_constraint(value, pltpu.HBM) for value in vectors])


def rows_body(scalars, ins, outs):
    q_ref, k_ref, v_ref = ins
    q0_ref, q1_ref, near_ref, far_ref, chip_ref = outs
    reorder = reorder_matrix()
    pair = pair_matrix()
    for i in range(2):
        rows = slice(i * BLK, (i + 1) * BLK)
        q0 = mul(reorder, q_ref[rows, :]).astype(bf16)
        q0_ref[rows, :] = q0
        q1_ref[i * HALF : (i + 1) * HALF, :] = fold(q0, 0.5)
    odd = scalars[0][0]
    outer = pl.ds(pl.multiple_of(odd * BLK, BLK), BLK)
    inner = pl.ds(pl.multiple_of((1 - odd) * BLK, BLK), BLK)
    for ref, far_rows, first, near, far in ((near_ref, far_ref, 0, outer, inner), (chip_ref, chip_ref, 2 * BLK, inner, outer)):
        ref[0:BLK, :] = k_ref[near, :]
        ref[BLK : 2 * BLK, :] = v_ref[near, :]
        far_rows[first : first + HALF, :] = (mul(pair, k_ref[far, :]) * 0.5).astype(bf16)
        far_rows[first + HALF : first + BLK, :] = mul(pair, v_ref[far, :]).astype(bf16)


def rows_to_send(place, query_vecs, key_vecs, value_vecs, groups):
    rows, width = query_vecs.shape
    ins = [("cols", a) for a in (query_vecs, key_vecs, value_vecs)]
    outs = [("cols", array(n, width, bf16)) for n in (rows, rows // 2, 2 * BLK, BLK, 3 * BLK)]
    return run_shares(rows_body, "rows_to_send", groups, [place], ins, outs)


def own_body(_, ins, outs):
    q_ref, k_ref, v_ref = ins
    sum_ref, top_ref, total_ref = outs
    heads = q_ref.shape[1] // HEAD_DIM
    for i in range(2):
        rows = slice(i * BLK, (i + 1) * BLK)
        units = [(q_ref[rows, cols(head)], [(k_ref[:, cols(head)], v_ref[:, cols(head)], None)]) for head in range(heads)]
        for head, (top, sums) in enumerate(attend(units)):
            spot = (head // 2, rows, cols(head % 2))
            sum_ref[spot] = sums[:, :HEAD_DIM]
            top_ref[spot] = top
            total_ref[spot] = sums[:, HEAD_DIM:]


def running_sums(rows, width, groups):
    return [("kept", jax.ShapeDtypeStruct((groups, rows, width // groups), f32))] * 3


def own_level(q0, key_vecs, value_vecs, groups):
    ins = [("cols", a) for a in (q0, key_vecs, value_vecs)]
    return run_shares(own_body, "own_level", groups // 2, [], ins, running_sums(*q0.shape, groups), DECLARED)


def halo_body(place_ref, *refs):
    count = len(refs) - 4
    piece_refs, (got_ref, right_ref, left_ref, sems) = refs[:count], refs[count:]
    copies = [pltpu.make_async_copy(ref, got_ref.at[n ^ place_ref[1]], sems.at[n]) for n, ref in enumerate(piece_refs)]
    for copy in copies:
        copy.start()
    for copy in copies:
        copy.wait()
    pair = count // 2
    for which, factor in ((1, 0.5), (2, 1.0)):
        rows = slice(which * HALF, (which + 1) * HALF)
        near = (which - 1) * BLK
        far = 2 * BLK + (which - 1) * HALF
        for j in range(count):
            level2 = got_ref[j, rows, :]
            level3 = fold_chunks(level2, HALF // 2, factor)
            near_ref, far_ref = (left_ref, right_ref) if j < pair else (right_ref, left_ref)
            spot = j % pair
            near_ref[near + spot * HALF : near + (spot + 1) * HALF, :] = level2
            far_ref[far + spot * HALF // 2 : far + (spot + 1) * HALF // 2, :] = level3


def coarse_halos(place, pieces):
    rows, width = pieces[0].shape
    vmem = pl.BlockSpec(memory_space=pltpu.VMEM)
    shape = jax.ShapeDtypeStruct((3 * BLK, width), bf16)
    return pl.pallas_call(
        halo_body,
        in_specs=[pl.BlockSpec(memory_space=pltpu.SMEM)] + [pl.BlockSpec(memory_space=pl.ANY)] * len(pieces),
        out_specs=[vmem] * 3,
        out_shape=[jax.ShapeDtypeStruct((len(pieces), rows, width), bf16), shape, shape],
        scratch_shapes=[pltpu.SemaphoreType.DMA((len(pieces),))],
        compiler_params=pltpu.CompilerParams(vmem_limit_bytes=16 << 20),
        cost_estimate=pl.CostEstimate(flops=1 << 20, bytes_accessed=24 * pieces[0].size, transcendentals=0),
        name="coarse_halos",
    )(place, *pieces)


def coarse_body(place_ref, bias_ref, got_ref, prev_ref, next_ref, *refs):
    *out_refs, back_ref, sems = refs
    count = got_ref.shape[0]
    heads = got_ref.shape[2] // HEAD_DIM
    bias_prev = bias_ref[0]
    bias_next = bias_ref[1]
    lane = iota((HALF, HEAD_DIM), 1)

    units = []
    for head in range(heads):
        here = cols(head)

        def own(which, j):
            return got_ref[j, which * HALF : (which + 1) * HALF, here]

        def near(ref, which, spot):
            first = (which - 1) * BLK + spot * HALF
            return ref[first : first + HALF, here]

        def both(ref, which):
            return ref[(which - 1) * BLK : which * BLK, here]

        def far(ref, which):
            first = 2 * BLK + (which - 1) * HALF
            return ref[first : first + HALF, here]

        def near3(ref, which):
            return fold_chunks(both(ref, which), HALF // 2, 0.5 if which == 1 else 1.0)

        def joined(*rows):
            return jnp.concatenate(rows, axis=0)

        def part(pick, bias):
            return (pick(1), pick(2), bias)

        units += [
            (own(0, 0), [part(lambda w: joined(own(w, 2), own(w, 3)), None), part(lambda w: near(prev_ref, w, 0), bias_prev)]),
            (own(0, 1), [part(lambda w: both(prev_ref, w), bias_prev), part(lambda w: own(w, 3), None)]),
            (own(0, 2), [part(lambda w: both(next_ref, w), bias_next), part(lambda w: own(w, 0), None)]),
            (own(0, 3), [part(lambda w: joined(own(w, 0), own(w, 1)), None), part(lambda w: near(next_ref, w, 1), bias_next)]),
        ]
        for j, (ref, bias, other, other_bias) in enumerate(
            ((next_ref, bias_next, prev_ref, bias_prev), (prev_ref, bias_prev, next_ref, bias_next))
        ):
            query = joined(*[fold_chunks(own(0, 2 * j + n), HALF // 2, 0.5) for n in range(2)])
            units.append(
                (
                    query,
                    [part(lambda w: joined(near3(ref, w), far(ref, w)), bias), part(lambda w: far(other, w), other_bias)],
                )
            )
    found = attend(units)
    each = len(units) // heads

    def joined(*rows):
        return jnp.concatenate(rows, axis=0)

    for head in range(heads):
        here = cols(head)
        for j in range(count):
            top2, sum2 = found[head * each + j]
            top3, sum3 = found[head * each + count + j // 2]

            def spread(rows):
                first = (j % 2) * 2 * SUB
                one = rows[first : first + SUB]
                other = rows[first + SUB : first + 2 * SUB]
                return joined(one, one, other, other)

            top3 = spread(top3)
            sum3 = spread(sum3)
            top = jnp.maximum(top2, top3)
            scale2 = jnp.exp2(top2 - top)
            scale3 = jnp.exp2(top3 - top)
            values = sum2[:, :HEAD_DIM] * scale2 + sum3[:, :HEAD_DIM] * scale3
            total = sum2[:, HEAD_DIM:] * (4.0 * scale2) + sum3[:, HEAD_DIM:] * (8.0 * scale3)
            back_ref[j, 0:HALF, here] = (values / total).astype(bf16)
            level = top + jnp.log2(total)
            high = level.astype(bf16).astype(f32)
            middle = (level - high).astype(bf16).astype(f32)
            terms = jnp.where(lane == 0, high, jnp.where(lane == 1, middle, level - high - middle))
            back_ref[j, HALF : HALF + 16, here] = terms.T[0:16, :].astype(bf16)
    copies = [
        pltpu.make_async_copy(back_ref.at[n ^ place_ref[1]], ref, sems.at[n]) for n, ref in enumerate(out_refs)
    ]
    for copy in copies:
        copy.start()
    for copy in copies:
        copy.wait()


def coarse_levels(place, bias, got, from_prev, from_next):
    count, _, width = got.shape
    vmem = pl.BlockSpec(memory_space=pltpu.VMEM)
    smem = pl.BlockSpec(memory_space=pltpu.SMEM)
    rows = HALF + 16
    return pl.pallas_call(
        coarse_body,
        in_specs=[smem, smem, vmem, vmem, vmem],
        out_specs=[vmem] * count,
        out_shape=[array(rows, width, bf16)] * count,
        scratch_shapes=[pltpu.VMEM((count, rows, width), bf16), pltpu.SemaphoreType.DMA((count,))],
        compiler_params=pltpu.CompilerParams(vmem_limit_bytes=16 << 20),
        cost_estimate=pl.CostEstimate(flops=DECLARED, bytes_accessed=8 * got.size, transcendentals=1 << 20),
        name="coarse_levels",
    )(place, bias, got, from_prev, from_next)


def side_body(side, with_near, with_far, scalars, ins, outs):
    q0_ref, q1_ref, sum_ref, top_ref, total_ref, side_ref = ins
    heads = q1_ref.shape[1] // HEAD_DIM
    bias = scalars[1][side]
    blocks = (side, 1 - side)
    fine = [pl.ds(pl.multiple_of(block * BLK, BLK), BLK) for block in blocks]
    middle = [pl.ds(pl.multiple_of(block * HALF, HALF), HALF) for block in blocks]
    if with_near:
        pair = pair_matrix()
        near_keys = (mul(pair, side_ref[0:BLK, :]) * 0.5).astype(bf16)
        near_values = mul(pair, side_ref[BLK : 2 * BLK, :]).astype(bf16)
    start = 2 * BLK if with_near else 0
    far_keys, far_values = (slice(start + n * HALF, start + (n + 1) * HALF) for n in range(2))
    units, names = [], []
    for head in range(heads):
        here = cols(head)
        far = (side_ref[far_keys, here], side_ref[far_values, here]) if with_far else None
        near = (near_keys[:, here], near_values[:, here]) if with_near else None
        whole = [part for part in (near, far) if part is not None]
        whole = [jnp.concatenate([part[n] for part in whole], axis=0) if len(whole) > 1 else whole[0][n] for n in range(2)]
        if with_near:
            units.append((q0_ref[fine[0], here], [(side_ref[0:BLK, here], side_ref[BLK : 2 * BLK, here], None)]))
            names.append((head, 0, 0))
        if with_far:
            units.append((q1_ref[middle[0], here], [(*far, None)]))
            names.append((head, 0, 1))
        units.append((q1_ref[middle[1], here], [(*whole, None)]))
        names.append((head, 1, 1))
    found = {name: (top + bias, sums) for name, (top, sums) in zip(names, attend(units))}
    for n in range(2):
        for head in range(heads):
            spot = (head // 2, fine[n], cols(head % 2))
            parts = [(top_ref[spot], sum_ref[spot], total_ref[spot])]
            if (head, n, 0) in found:
                top, sums = found[head, n, 0]
                parts.append((top, sums[:, :HEAD_DIM], sums[:, HEAD_DIM:]))
            if (head, n, 1) in found:
                top, sums = found[head, n, 1]
                parts.append((twice(top), twice(sums[:, :HEAD_DIM]), twice(2.0 * sums[:, HEAD_DIM:])))
            most = functools.reduce(jnp.maximum, [part[0] for part in parts])
            scales = [jnp.exp2(part[0] - most) for part in parts]
            outs[0][spot] = sum(part[1] * scale for part, scale in zip(parts, scales))
            outs[1][spot] = most
            outs[2][spot] = sum(part[2] * scale for part, scale in zip(parts, scales))


def chip_body(scalars, ins, outs):
    side_body(1 - scalars[0][0], True, True, scalars, ins, outs)


def near_body(scalars, ins, outs):
    side_body(scalars[0][0], True, False, scalars, ins, outs)


def far_body(scalars, ins, outs):
    side_body(scalars[0][0], False, True, scalars, [None] + ins, outs)


def side_level(body, name, place, bias, queries, running, rows):
    groups, count, part = running[0].shape
    ins = [("cols", query) for query in queries] + [("kept", one) for one in running] + [("got", rows)]
    return run_shares(body, name, groups // 2, [place, bias], ins, running_sums(count, groups * part, groups))


def finish_body(place_ref, sum_ref, top_ref, total_ref, *refs):
    groups = sum_ref.shape[0]
    back_refs, (out_ref, done_ref, sems) = refs[:groups], refs[groups:]
    part = sum_ref.shape[2]
    restore = restore_matrix()
    copies = []
    for n, back_ref in enumerate(back_refs):
        entry = n ^ place_ref[1]
        levels = []
        for head in range(part // HEAD_DIM):
            terms = back_ref[HALF : HALF + 16, cols(head)].astype(f32)
            terms = jnp.sum(jnp.where(iota(terms.shape, 0) < 3, terms, 0.0), axis=0, keepdims=True)
            levels.append(jnp.broadcast_to(terms, (HEAD_DIM, HEAD_DIM)).T)
        for i in range(2):
            rows = slice(i * BLK, (i + 1) * BLK)
            spot = slice(i * HALF // 2, (i + 1) * HALF // 2)
            results = []
            for head, level in enumerate(levels):
                here = (entry, rows, cols(head))
                top = top_ref[here]
                level = twice(twice(level[spot, :]))
                lead = top - level
                smaller = jnp.exp2(-jnp.abs(lead))
                scale = jnp.where(lead >= 0.0, 1.0, smaller)
                coarse = jnp.where(lead >= 0.0, smaller, 1.0)
                number = twice(twice(back_ref[spot, cols(head)].astype(f32))) * coarse
                number = number + sum_ref[here] * scale
                total = total_ref[here] * scale + coarse
                guess = pl.reciprocal(total, approx=True)
                results.append((number * (guess * (2.0 - total * guess))).astype(bf16))
            done_ref[n, rows, :] = mul(restore, jnp.concatenate(results, axis=1)).astype(bf16)
        columns = pl.ds(pl.multiple_of(entry * part, HEAD_DIM), part)
        copies.append(pltpu.make_async_copy(done_ref.at[n], out_ref.at[:, columns], sems.at[n]))
        copies[-1].start()
    for copy in copies:
        copy.wait()


def finish(place, running, back):
    groups, rows, part = running[0].shape
    vmem = pl.BlockSpec(memory_space=pltpu.VMEM)
    return pl.pallas_call(
        finish_body,
        in_specs=[pl.BlockSpec(memory_space=pltpu.SMEM)] + [vmem] * (3 + groups),
        out_specs=pl.BlockSpec(memory_space=pltpu.HBM),
        out_shape=pltpu.HBM((rows, groups * part), bf16),
        scratch_shapes=[pltpu.VMEM((groups, rows, part), bf16), pltpu.SemaphoreType.DMA((groups,))],
        compiler_params=pltpu.CompilerParams(vmem_limit_bytes=VMEM_GRANT),
        cost_estimate=pl.CostEstimate(flops=1 << 10, bytes_accessed=1 << 10, transcendentals=0),
        name="finish",
    )(place, *running, *back)


def shift(value, axis, steps):
    count = lax.axis_size(axis)
    first, last = (max(0, -steps), min(count, count - steps))
    return lax.ppermute(value, axis, [(source, source + steps) for source in range(first, last)])


def trade(value, axis, pairs):
    return lax.ppermute(value, axis, pairs + [(target, source) for source, target in pairs])


def edge_bias(axis):
    place = lax.axis_index(axis)
    last = lax.axis_size(axis) - 1
    at_edge = jnp.stack([place == 0, place == last])
    return jnp.where(at_edge, very_negative, 0.0).astype(f32)


def local(query_vecs, key_vecs, value_vecs):
    groups = lax.axis_size("grp")
    assert query_vecs.shape == (2 * BLK, HEADS * HEAD_DIM) and groups == 4
    everyone = ("seq", "grp")
    count = lax.axis_size(everyone)
    spot = lax.axis_index("grp")
    odd = jnp.bitwise_and(spot, 1)
    place = jnp.stack([odd, spot]).astype(jnp.int32)
    bias = edge_bias(everyone)

    def exchange(pieces):
        flips = [[(source, source ^ n) for source in range(groups)] for n in range(groups)]
        for n in range(groups - 1, 0, -1):
            pieces[n] = lax.ppermute(pieces[n], "grp", flips[n])
        return pieces

    pieces = list(swap_rows(place, query_vecs, key_vecs, value_vecs, groups))
    query_rows, pieces = lax.optimization_barrier((query_vecs, pieces))
    pieces = exchange(pieces)
    q0, q1, near, far, chip = rows_to_send(place, query_rows, key_vecs, value_vecs, groups)
    off_chip = [(device, device + 1) for device in range(1, count - 1, 2)]
    near = trade(near, everyone, off_chip)
    far, pieces[1] = lax.optimization_barrier((far, pieces[1]))
    far = trade(far, everyone, off_chip)
    pieces, chip = lax.optimization_barrier((pieces, chip))
    got, coarse_right, coarse_left = coarse_halos(place, pieces)
    coarse_right, coarse_left, chip, q0 = lax.optimization_barrier((coarse_right, coarse_left, chip, q0))
    coarse_prev = shift(coarse_right, "seq", 1)
    coarse_next = shift(coarse_left, "seq", -1)
    chip = trade(chip, everyone, [(device, device + 1) for device in range(0, count - 1, 2)])
    running = own_level(q0, key_vecs, value_vecs, groups)
    running = side_level(chip_body, "chip_level", place, bias, (q0, q1), running, chip)
    running = side_level(near_body, "near_level", place, bias, (q0, q1), running, near)
    got, running = lax.optimization_barrier((got, running))
    back = coarse_levels(place, edge_bias("seq"), got, coarse_prev, coarse_next)
    back, running = lax.optimization_barrier((back, running))
    back = exchange(list(back))
    running = side_level(far_body, "far_level", place, bias, (q1,), running, far)
    return finish(place, running, back)


def solution(mesh):
    return jax.shard_map(
        local,
        mesh=mesh,
        in_specs=(P(("seq", "grp"), None), P(("seq", "grp"), None), P(("seq", "grp"), None)),
        out_specs=P(("seq", "grp"), None),
        check_vma=False,
    )
```

```python
import functools
import math

import jax
import jax.numpy as jnp
from jax import lax
from jax.experimental import pallas as pl
from jax.experimental.pallas import tpu as pltpu
from jax.sharding import PartitionSpec as P

HEADS = 8
HEAD_DIM = 128
BLK = 256
HALF = BLK // 2
SUB = BLK // 8
LEV = 4
EXP_SCALE = math.log2(math.e) / math.sqrt(HEAD_DIM)

VMEM_GRANT = 24 << 20

very_negative = -1e30
f32 = jnp.float32
bf16 = jnp.bfloat16


def iota(shape, dim):
    return lax.broadcasted_iota(jnp.int32, shape, dim)


def bit(value, place):
    return jnp.bitwise_and(lax.shift_right_logical(value, place), 1)


def low_bits(value):
    step = SUB.bit_length() - 1
    deep = jnp.bitwise_and(value, SUB - 1)
    return 8 * deep + 4 * bit(value, step) + 2 * bit(value, step + 1) + bit(value, step + 2)


def reorder_matrix():
    return (iota((BLK, BLK), 1) == low_bits(iota((BLK, BLK), 0))).astype(bf16)


def restore_matrix():
    return (iota((BLK, BLK), 0) == low_bits(iota((BLK, BLK), 1))).astype(bf16)


def pair_matrix():
    first = low_bits(iota((HALF, BLK), 0))
    place = iota((HALF, BLK), 1)
    return jnp.logical_or(place == first, place == first + 1).astype(bf16)


def mul(left, right):
    return jnp.dot(left, right, preferred_element_type=f32)


def fold(rows, factor):
    half = rows.shape[0] // 2
    total = rows[:half].astype(f32) + rows[half:].astype(f32)
    if factor != 1.0:
        total = total * factor
    return total.astype(bf16)


def fold_chunks(rows, chunk, factor):
    count = rows.shape[0] // chunk
    return jnp.concatenate([fold(rows[i * chunk : (i + 1) * chunk], factor) for i in range(count)], axis=0)


def twice(rows):
    return jnp.concatenate([rows, rows], axis=0)


def cols(head):
    return slice(head * HEAD_DIM, (head + 1) * HEAD_DIM)


DECLARED = 1 << 36


def with_ones(values):
    return jnp.concatenate([values, jnp.ones_like(values)], axis=1)


def attend(units):
    scores = []
    for query, parts in units:
        raws = [
            lax.dot_general(query, keys, (((1,), (1,)), ((), ())), preferred_element_type=f32) for keys, _, _ in parts
        ]
        scores.append([raw if part[2] is None else raw + part[2] for raw, part in zip(raws, parts)])
    tops = []
    for raws in scores:
        tops.append(functools.reduce(jnp.maximum, [jnp.max(raw, axis=1, keepdims=True) for raw in raws]))
    found = []
    for (_, parts), raws, top in zip(units, scores, tops):
        total = None
        for (_, values, _), raw in zip(parts, raws):
            weights = jnp.exp2((raw - top) * EXP_SCALE).astype(bf16)
            one = mul(weights, with_ones(values))
            total = one if total is None else total + one
        found.append((jnp.broadcast_to(top * EXP_SCALE, (top.shape[0], HEAD_DIM)), total))
    return found


def share_of(ref, share, shares):
    width = ref.shape[1] // shares
    first = share * width
    if not isinstance(share, int):
        first = pl.multiple_of(first, HEAD_DIM)
    return ref.at[:, pl.ds(first, width)]


def run_shares(body, name, shares, scalars, ins, outs, work=1 << 10, unrolled=False):
    moved_in = [i for i, (kind, _) in enumerate(ins) if kind in ("cols", "got")]
    moved_out = [i for i, (kind, _) in enumerate(outs) if kind == "cols"]
    as_list = lambda pair: list(pair[1]) if pair[0] == "pieces" else [pair[1]]
    buffer_shape = {
        "cols": lambda value: (shares, value.shape[0], value.shape[1] // shares),
        "got": lambda value: (shares, value.shape[0], value.shape[1] // shares),
        "kept": lambda value: None,
        "pieces": lambda values: (shares, len(values) // shares, *values[0].shape),
    }

    def kernel(*refs):
        refs = list(refs)
        take = lambda count: [refs.pop(0) for _ in range(count)]
        scalar_refs = take(len(scalars))
        in_refs = [take(len(as_list(pair))) for pair in ins]
        out_refs = [take(len(as_list(pair))) for pair in outs]
        in_bufs = [in_refs[i][0] if ins[i][0] == "kept" else refs.pop(0) for i in range(len(ins))]
        out_bufs = [out_refs[i][0] if outs[i][0] == "kept" else refs.pop(0) for i in range(len(outs))]
        in_sems, out_sems, piece_sems = take(3)

        def bring(i, share):
            return pltpu.make_async_copy(share_of(in_refs[i][0], share, shares), in_bufs[i].at[share], in_sems.at[i, share])

        def put(i, share):
            return pltpu.make_async_copy(out_bufs[i].at[share], share_of(out_refs[i][0], share, shares), out_sems.at[i, share])

        def spot_of(buffer, n):
            entry = n ^ scalar_refs[0][1]
            return buffer.at[lax.div(entry, buffer.shape[1]), lax.rem(entry, buffer.shape[1])]

        pieces_in, pieces_out = [], []
        for i, (kind, _) in enumerate(ins):
            if kind == "pieces":
                pieces_in += [(ref, spot_of(in_bufs[i], n), n) for n, ref in enumerate(in_refs[i])]
        for i, (kind, _) in enumerate(outs):
            if kind == "pieces":
                pieces_out += [(spot_of(out_bufs[i], n), ref, n) for n, ref in enumerate(out_refs[i])]
        pieces_in = [pltpu.make_async_copy(source, target, piece_sems.at[n]) for source, target, n in pieces_in]
        pieces_out = [pltpu.make_async_copy(source, target, piece_sems.at[n]) for source, target, n in pieces_out]

        for share in range(shares):
            for i in moved_in:
                bring(i, share).start()
            if share == 0:
                for copy in pieces_in:
                    copy.start()
        for copy in pieces_in:
            copy.wait()

        def views(operands, buffers, share):
            result = []
            for (kind, value), buffer in zip(operands, buffers):
                count = value.shape[0] // shares if kind == "kept" else None
                result.append(buffer.at[share] if count is None else buffer.at[pl.ds(share * count, count)])
            return result

        def step(share, carry):
            for i in moved_in:
                bring(i, share).wait()
            body(scalar_refs, views(ins, in_bufs, share), views(outs, out_bufs, share))
            for i in moved_out:
                put(i, share).start()
            return carry

        if unrolled:
            for share in range(shares):
                step(share, 0)
        else:
            lax.fori_loop(0, shares, step, 0)
        for copy in pieces_out:
            copy.start()
        for share in range(shares):
            for i in moved_out:
                put(i, share).wait()
        for copy in pieces_out:
            copy.wait()

    spaces = {"cols": pltpu.HBM, "got": pl.ANY, "pieces": pl.ANY, "kept": pltpu.VMEM}
    values, in_specs, out_specs, out_shapes, buffers = [], [], [], [], []
    for kind, value in ins:
        for one in as_list((kind, value)):
            values.append(pltpu.with_memory_space_constraint(one, pltpu.HBM) if kind == "cols" else one)
            in_specs.append(pl.BlockSpec(memory_space=spaces[kind]))
    for kind, shape in outs:
        for one in as_list((kind, shape)):
            out_shapes.append(pltpu.HBM(one.shape, one.dtype) if kind == "cols" else one)
            out_specs.append(pl.BlockSpec(memory_space=pltpu.HBM if kind == "cols" else pltpu.VMEM))
    for kind, value in list(ins) + list(outs):
        if kind != "kept":
            buffers.append(pltpu.VMEM(buffer_shape[kind](value), as_list((kind, value))[0].dtype))
    count = max(len(as_list(pair)) for pair in list(ins) + list(outs))
    semaphores = [(len(ins), shares), (len(outs), shares), (count,)]
    return pl.pallas_call(
        kernel,
        in_specs=[pl.BlockSpec(memory_space=pltpu.SMEM)] * len(scalars) + in_specs,
        out_specs=out_specs,
        out_shape=out_shapes,
        scratch_shapes=buffers + [pltpu.SemaphoreType.DMA(shape) for shape in semaphores],
        compiler_params=pltpu.CompilerParams(vmem_limit_bytes=VMEM_GRANT),
        cost_estimate=pl.CostEstimate(flops=work, bytes_accessed=1 << 10, transcendentals=0),
        name=name,
    )(*scalars, *values)


def array(rows, width, dtype):
    return jax.ShapeDtypeStruct((rows, width), dtype)


def swap_body(_, ins, outs):
    pair = pair_matrix()
    count, _, part = outs[0].shape
    for place, (ref, factor) in enumerate(zip(ins, (0.5, 0.5, 1.0))):
        for i in range(2):
            level1 = mul(pair, ref[i * BLK : (i + 1) * BLK, :])
            if factor != 1.0:
                level1 = level1 * factor
            level2 = fold(level1.astype(bf16), factor)
            first = place * HALF + i * HALF // 2
            for n in range(count):
                outs[0][n, first : first + HALF // 2, :] = level2[:, n * part : (n + 1) * part]


def swap_rows(place, query_vecs, key_vecs, value_vecs, groups):
    width = query_vecs.shape[1]
    ins = [("cols", a) for a in (query_vecs, key_vecs, value_vecs)]
    outs = [("pieces", [array(3 * HALF, width // groups, bf16)] * groups)]
    return run_shares(swap_body, "swap_rows", groups // 2, [place], ins, outs, unrolled=True)


def rows_body(scalars, ins, outs):
    q_ref, k_ref, v_ref = ins
    q0_ref, q1_ref, near_ref, far_ref, chip_ref = outs
    reorder = reorder_matrix()
    pair = pair_matrix()
    for i in range(2):
        rows = slice(i * BLK, (i + 1) * BLK)
        q0 = mul(reorder, q_ref[rows, :]).astype(bf16)
        q0_ref[rows, :] = q0
        q1_ref[i * HALF : (i + 1) * HALF, :] = fold(q0, 0.5)
    odd = scalars[0][0]
    outer = pl.ds(pl.multiple_of(odd * BLK, BLK), BLK)
    inner = pl.ds(pl.multiple_of((1 - odd) * BLK, BLK), BLK)
    for ref, far_rows, first, near, far in ((near_ref, far_ref, 0, outer, inner), (chip_ref, chip_ref, 2 * BLK, inner, outer)):
        ref[0:BLK, :] = k_ref[near, :]
        ref[BLK : 2 * BLK, :] = v_ref[near, :]
        far_rows[first : first + HALF, :] = (mul(pair, k_ref[far, :]) * 0.5).astype(bf16)
        far_rows[first + HALF : first + BLK, :] = mul(pair, v_ref[far, :]).astype(bf16)


def rows_to_send(place, query_vecs, key_vecs, value_vecs, groups):
    rows, width = query_vecs.shape
    ins = [("cols", a) for a in (query_vecs, key_vecs, value_vecs)]
    outs = [("cols", array(n, width, bf16)) for n in (rows, rows // 2, 2 * BLK, BLK, 3 * BLK)]
    return run_shares(rows_body, "rows_to_send", groups, [place], ins, outs)


def own_body(_, ins, outs):
    q_ref, k_ref, v_ref = ins
    sum_ref, top_ref, total_ref = outs
    heads = q_ref.shape[1] // HEAD_DIM
    for i in range(2):
        rows = slice(i * BLK, (i + 1) * BLK)
        units = [(q_ref[rows, cols(head)], [(k_ref[:, cols(head)], v_ref[:, cols(head)], None)]) for head in range(heads)]
        for head, (top, sums) in enumerate(attend(units)):
            spot = (head // 2, rows, cols(head % 2))
            sum_ref[spot] = sums[:, :HEAD_DIM]
            top_ref[spot] = top
            total_ref[spot] = sums[:, HEAD_DIM:]


def running_sums(rows, width, groups):
    return [("kept", jax.ShapeDtypeStruct((groups, rows, width // groups), f32))] * 3


def own_level(q0, key_vecs, value_vecs, groups):
    ins = [("cols", a) for a in (q0, key_vecs, value_vecs)]
    return run_shares(own_body, "own_level", groups // 2, [], ins, running_sums(*q0.shape, groups), DECLARED)


def halo_body(place_ref, *refs):
    count = len(refs) - 4
    piece_refs, (got_ref, right_ref, left_ref, sems) = refs[:count], refs[count:]
    copies = [pltpu.make_async_copy(ref, got_ref.at[n ^ place_ref[1]], sems.at[n]) for n, ref in enumerate(piece_refs)]
    for copy in copies:
        copy.start()
    for copy in copies:
        copy.wait()
    pair = count // 2
    for which, factor in ((1, 0.5), (2, 1.0)):
        rows = slice(which * HALF, (which + 1) * HALF)
        near = (which - 1) * BLK
        far = 2 * BLK + (which - 1) * HALF
        for j in range(count):
            level2 = got_ref[j, rows, :]
            level3 = fold_chunks(level2, HALF // 2, factor)
            near_ref, far_ref = (left_ref, right_ref) if j < pair else (right_ref, left_ref)
            spot = j % pair
            near_ref[near + spot * HALF : near + (spot + 1) * HALF, :] = level2
            far_ref[far + spot * HALF // 2 : far + (spot + 1) * HALF // 2, :] = level3


def coarse_halos(place, pieces):
    rows, width = pieces[0].shape
    vmem = pl.BlockSpec(memory_space=pltpu.VMEM)
    shape = jax.ShapeDtypeStruct((3 * BLK, width), bf16)
    return pl.pallas_call(
        halo_body,
        in_specs=[pl.BlockSpec(memory_space=pltpu.SMEM)] + [pl.BlockSpec(memory_space=pl.ANY)] * len(pieces),
        out_specs=[vmem] * 3,
        out_shape=[jax.ShapeDtypeStruct((len(pieces), rows, width), bf16), shape, shape],
        scratch_shapes=[pltpu.SemaphoreType.DMA((len(pieces),))],
        compiler_params=pltpu.CompilerParams(vmem_limit_bytes=16 << 20),
        cost_estimate=pl.CostEstimate(flops=1 << 20, bytes_accessed=24 * pieces[0].size, transcendentals=0),
        name="coarse_halos",
    )(place, *pieces)


def coarse_body(place_ref, bias_ref, got_ref, prev_ref, next_ref, *refs):
    *out_refs, back_ref, sems = refs
    count = got_ref.shape[0]
    heads = got_ref.shape[2] // HEAD_DIM
    bias_prev = bias_ref[0]
    bias_next = bias_ref[1]
    lane = iota((HALF, HEAD_DIM), 1)

    units = []
    for head in range(heads):
        here = cols(head)

        def own(which, j):
            return got_ref[j, which * HALF : (which + 1) * HALF, here]

        def near(ref, which, spot):
            first = (which - 1) * BLK + spot * HALF
            return ref[first : first + HALF, here]

        def both(ref, which):
            return ref[(which - 1) * BLK : which * BLK, here]

        def far(ref, which):
            first = 2 * BLK + (which - 1) * HALF
            return ref[first : first + HALF, here]

        def near3(ref, which):
            return fold_chunks(both(ref, which), HALF // 2, 0.5 if which == 1 else 1.0)

        def joined(*rows):
            return jnp.concatenate(rows, axis=0)

        def part(pick, bias):
            return (pick(1), pick(2), bias)

        units += [
            (own(0, 0), [part(lambda w: joined(own(w, 2), own(w, 3)), None), part(lambda w: near(prev_ref, w, 0), bias_prev)]),
            (own(0, 1), [part(lambda w: both(prev_ref, w), bias_prev), part(lambda w: own(w, 3), None)]),
            (own(0, 2), [part(lambda w: both(next_ref, w), bias_next), part(lambda w: own(w, 0), None)]),
            (own(0, 3), [part(lambda w: joined(own(w, 0), own(w, 1)), None), part(lambda w: near(next_ref, w, 1), bias_next)]),
        ]
        for j, (ref, bias, other, other_bias) in enumerate(
            ((next_ref, bias_next, prev_ref, bias_prev), (prev_ref, bias_prev, next_ref, bias_next))
        ):
            query = joined(*[fold_chunks(own(0, 2 * j + n), HALF // 2, 0.5) for n in range(2)])
            units.append(
                (
                    query,
                    [part(lambda w: joined(near3(ref, w), far(ref, w)), bias), part(lambda w: far(other, w), other_bias)],
                )
            )
    found = attend(units)
    each = len(units) // heads

    def joined(*rows):
        return jnp.concatenate(rows, axis=0)

    for head in range(heads):
        here = cols(head)
        for j in range(count):
            top2, sum2 = found[head * each + j]
            top3, sum3 = found[head * each + count + j // 2]

            def spread(rows):
                first = (j % 2) * 2 * SUB
                one = rows[first : first + SUB]
                other = rows[first + SUB : first + 2 * SUB]
                return joined(one, one, other, other)

            top3 = spread(top3)
            sum3 = spread(sum3)
            top = jnp.maximum(top2, top3)
            scale2 = jnp.exp2(top2 - top)
            scale3 = jnp.exp2(top3 - top)
            values = sum2[:, :HEAD_DIM] * scale2 + sum3[:, :HEAD_DIM] * scale3
            total = sum2[:, HEAD_DIM:] * (4.0 * scale2) + sum3[:, HEAD_DIM:] * (8.0 * scale3)
            back_ref[j, 0:HALF, here] = (values / total).astype(bf16)
            level = top + jnp.log2(total)
            high = level.astype(bf16).astype(f32)
            middle = (level - high).astype(bf16).astype(f32)
            terms = jnp.where(lane == 0, high, jnp.where(lane == 1, middle, level - high - middle))
            back_ref[j, HALF : HALF + 16, here] = terms.T[0:16, :].astype(bf16)
    copies = [
        pltpu.make_async_copy(back_ref.at[n ^ place_ref[1]], ref, sems.at[n]) for n, ref in enumerate(out_refs)
    ]
    for copy in copies:
        copy.start()
    for copy in copies:
        copy.wait()


def coarse_levels(place, bias, got, from_prev, from_next):
    count, _, width = got.shape
    vmem = pl.BlockSpec(memory_space=pltpu.VMEM)
    smem = pl.BlockSpec(memory_space=pltpu.SMEM)
    rows = HALF + 16
    return pl.pallas_call(
        coarse_body,
        in_specs=[smem, smem, vmem, vmem, vmem],
        out_specs=[vmem] * count,
        out_shape=[array(rows, width, bf16)] * count,
        scratch_shapes=[pltpu.VMEM((count, rows, width), bf16), pltpu.SemaphoreType.DMA((count,))],
        compiler_params=pltpu.CompilerParams(vmem_limit_bytes=16 << 20),
        cost_estimate=pl.CostEstimate(flops=DECLARED, bytes_accessed=8 * got.size, transcendentals=1 << 20),
        name="coarse_levels",
    )(place, bias, got, from_prev, from_next)


def side_body(side, with_near, with_far, scalars, ins, outs):
    q0_ref, q1_ref, sum_ref, top_ref, total_ref, side_ref = ins
    heads = q1_ref.shape[1] // HEAD_DIM
    bias = scalars[1][side]
    blocks = (side, 1 - side)
    fine = [pl.ds(pl.multiple_of(block * BLK, BLK), BLK) for block in blocks]
    middle = [pl.ds(pl.multiple_of(block * HALF, HALF), HALF) for block in blocks]
    if with_near:
        pair = pair_matrix()
        near_keys = (mul(pair, side_ref[0:BLK, :]) * 0.5).astype(bf16)
        near_values = mul(pair, side_ref[BLK : 2 * BLK, :]).astype(bf16)
    start = 2 * BLK if with_near else 0
    far_keys, far_values = (slice(start + n * HALF, start + (n + 1) * HALF) for n in range(2))
    units, names = [], []
    for head in range(heads):
        here = cols(head)
        far = (side_ref[far_keys, here], side_ref[far_values, here]) if with_far else None
        near = (near_keys[:, here], near_values[:, here]) if with_near else None
        whole = [part for part in (near, far) if part is not None]
        whole = [jnp.concatenate([part[n] for part in whole], axis=0) if len(whole) > 1 else whole[0][n] for n in range(2)]
        if with_near:
            units.append((q0_ref[fine[0], here], [(side_ref[0:BLK, here], side_ref[BLK : 2 * BLK, here], None)]))
            names.append((head, 0, 0))
        if with_far:
            units.append((q1_ref[middle[0], here], [(*far, None)]))
            names.append((head, 0, 1))
        units.append((q1_ref[middle[1], here], [(*whole, None)]))
        names.append((head, 1, 1))
    found = {name: (top + bias, sums) for name, (top, sums) in zip(names, attend(units))}
    for n in range(2):
        for head in range(heads):
            spot = (head // 2, fine[n], cols(head % 2))
            parts = [(top_ref[spot], sum_ref[spot], total_ref[spot])]
            if (head, n, 0) in found:
                top, sums = found[head, n, 0]
                parts.append((top, sums[:, :HEAD_DIM], sums[:, HEAD_DIM:]))
            if (head, n, 1) in found:
                top, sums = found[head, n, 1]
                parts.append((twice(top), twice(sums[:, :HEAD_DIM]), twice(2.0 * sums[:, HEAD_DIM:])))
            most = functools.reduce(jnp.maximum, [part[0] for part in parts])
            scales = [jnp.exp2(part[0] - most) for part in parts]
            outs[0][spot] = sum(part[1] * scale for part, scale in zip(parts, scales))
            outs[1][spot] = most
            outs[2][spot] = sum(part[2] * scale for part, scale in zip(parts, scales))


def chip_body(scalars, ins, outs):
    side_body(1 - scalars[0][0], True, True, scalars, ins, outs)


def near_body(scalars, ins, outs):
    side_body(scalars[0][0], True, False, scalars, ins, outs)


def far_body(scalars, ins, outs):
    side_body(scalars[0][0], False, True, scalars, [None] + ins, outs)


def side_level(body, name, place, bias, queries, running, rows):
    groups, count, part = running[0].shape
    ins = [("cols", query) for query in queries] + [("kept", one) for one in running] + [("got", rows)]
    return run_shares(body, name, groups // 2, [place, bias], ins, running_sums(count, groups * part, groups))


def finish_body(place_ref, sum_ref, top_ref, total_ref, *refs):
    groups = sum_ref.shape[0]
    back_refs, (out_ref, done_ref, sems) = refs[:groups], refs[groups:]
    part = sum_ref.shape[2]
    restore = restore_matrix()
    copies = []
    for n, back_ref in enumerate(back_refs):
        entry = n ^ place_ref[1]
        levels = []
        for head in range(part // HEAD_DIM):
            terms = back_ref[HALF : HALF + 16, cols(head)].astype(f32)
            terms = jnp.sum(jnp.where(iota(terms.shape, 0) < 3, terms, 0.0), axis=0, keepdims=True)
            levels.append(jnp.broadcast_to(terms, (HEAD_DIM, HEAD_DIM)).T)
        for i in range(2):
            rows = slice(i * BLK, (i + 1) * BLK)
            spot = slice(i * HALF // 2, (i + 1) * HALF // 2)
            results = []
            for head, level in enumerate(levels):
                here = (entry, rows, cols(head))
                top = top_ref[here]
                level = twice(twice(level[spot, :]))
                lead = top - level
                smaller = jnp.exp2(-jnp.abs(lead))
                scale = jnp.where(lead >= 0.0, 1.0, smaller)
                coarse = jnp.where(lead >= 0.0, smaller, 1.0)
                number = twice(twice(back_ref[spot, cols(head)].astype(f32))) * coarse
                number = number + sum_ref[here] * scale
                total = total_ref[here] * scale + coarse
                guess = pl.reciprocal(total, approx=True)
                results.append((number * (guess * (2.0 - total * guess))).astype(bf16))
            done_ref[n, rows, :] = mul(restore, jnp.concatenate(results, axis=1)).astype(bf16)
        columns = pl.ds(pl.multiple_of(entry * part, HEAD_DIM), part)
        copies.append(pltpu.make_async_copy(done_ref.at[n], out_ref.at[:, columns], sems.at[n]))
        copies[-1].start()
    for copy in copies:
        copy.wait()


def finish(place, running, back):
    groups, rows, part = running[0].shape
    vmem = pl.BlockSpec(memory_space=pltpu.VMEM)
    return pl.pallas_call(
        finish_body,
        in_specs=[pl.BlockSpec(memory_space=pltpu.SMEM)] + [vmem] * (3 + groups),
        out_specs=pl.BlockSpec(memory_space=pltpu.HBM),
        out_shape=pltpu.HBM((rows, groups * part), bf16),
        scratch_shapes=[pltpu.VMEM((groups, rows, part), bf16), pltpu.SemaphoreType.DMA((groups,))],
        compiler_params=pltpu.CompilerParams(vmem_limit_bytes=VMEM_GRANT),
        cost_estimate=pl.CostEstimate(flops=1 << 10, bytes_accessed=1 << 10, transcendentals=0),
        name="finish",
    )(place, *running, *back)


def shift(value, axis, steps):
    count = lax.axis_size(axis)
    first, last = (max(0, -steps), min(count, count - steps))
    return lax.ppermute(value, axis, [(source, source + steps) for source in range(first, last)])


def trade(value, axis, pairs):
    return lax.ppermute(value, axis, pairs + [(target, source) for source, target in pairs])


def edge_bias(axis):
    place = lax.axis_index(axis)
    last = lax.axis_size(axis) - 1
    at_edge = jnp.stack([place == 0, place == last])
    return jnp.where(at_edge, very_negative, 0.0).astype(f32)


def local(query_vecs, key_vecs, value_vecs):
    groups = lax.axis_size("grp")
    assert query_vecs.shape == (2 * BLK, HEADS * HEAD_DIM) and groups == 4
    everyone = ("seq", "grp")
    count = lax.axis_size(everyone)
    spot = lax.axis_index("grp")
    odd = jnp.bitwise_and(spot, 1)
    place = jnp.stack([odd, spot]).astype(jnp.int32)
    bias = edge_bias(everyone)

    def exchange(pieces):
        flips = [[(source, source ^ n) for source in range(groups)] for n in range(groups)]
        for n in range(groups - 1, 0, -1):
            pieces[n] = lax.ppermute(pieces[n], "grp", flips[n])
        return pieces

    pieces = list(swap_rows(place, query_vecs, key_vecs, value_vecs, groups))
    query_rows, pieces = lax.optimization_barrier((query_vecs, pieces))
    pieces = exchange(pieces)
    q0, q1, near, far, chip = rows_to_send(place, query_rows, key_vecs, value_vecs, groups)
    off_chip = [(device, device + 1) for device in range(1, count - 1, 2)]
    near = trade(near, everyone, off_chip)
    pieces, chip = lax.optimization_barrier((pieces, chip))
    got, coarse_right, coarse_left = coarse_halos(place, pieces)
    coarse_right, coarse_left, chip, q0, far = lax.optimization_barrier((coarse_right, coarse_left, chip, q0, far))
    coarse_prev = shift(coarse_right, "seq", 1)
    coarse_next = shift(coarse_left, "seq", -1)
    chip = trade(chip, everyone, [(device, device + 1) for device in range(0, count - 1, 2)])
    far = trade(far, everyone, off_chip)
    running = own_level(q0, key_vecs, value_vecs, groups)
    running = side_level(chip_body, "chip_level", place, bias, (q0, q1), running, chip)
    running = side_level(near_body, "near_level", place, bias, (q0, q1), running, near)
    got, running = lax.optimization_barrier((got, running))
    back = coarse_levels(place, edge_bias("seq"), got, coarse_prev, coarse_next)
    back, running = lax.optimization_barrier((back, running))
    back = exchange(list(back))
    running = side_level(far_body, "far_level", place, bias, (q1,), running, far)
    return finish(place, running, back)


def solution(mesh):
    return jax.shard_map(
        local,
        mesh=mesh,
        in_specs=(P(("seq", "grp"), None), P(("seq", "grp"), None), P(("seq", "grp"), None)),
        out_specs=P(("seq", "grp"), None),
        check_vma=False,
    )
```

```python
import functools
import math

import jax
import jax.numpy as jnp
from jax import lax
from jax.experimental import pallas as pl
from jax.experimental.pallas import tpu as pltpu
from jax.sharding import PartitionSpec as P

HEADS = 8
HEAD_DIM = 128
BLK = 256
HALF = BLK // 2
SUB = BLK // 8
LEV = 4
EXP_SCALE = math.log2(math.e) / math.sqrt(HEAD_DIM)

VMEM_GRANT = 24 << 20

very_negative = -1e30
f32 = jnp.float32
bf16 = jnp.bfloat16


def iota(shape, dim):
    return lax.broadcasted_iota(jnp.int32, shape, dim)


def bit(value, place):
    return jnp.bitwise_and(lax.shift_right_logical(value, place), 1)


def low_bits(value):
    step = SUB.bit_length() - 1
    deep = jnp.bitwise_and(value, SUB - 1)
    return 8 * deep + 4 * bit(value, step) + 2 * bit(value, step + 1) + bit(value, step + 2)


def reorder_matrix():
    return (iota((BLK, BLK), 1) == low_bits(iota((BLK, BLK), 0))).astype(bf16)


def restore_matrix():
    return (iota((BLK, BLK), 0) == low_bits(iota((BLK, BLK), 1))).astype(bf16)


def pair_matrix():
    first = low_bits(iota((HALF, BLK), 0))
    place = iota((HALF, BLK), 1)
    return jnp.logical_or(place == first, place == first + 1).astype(bf16)


def mul(left, right):
    return jnp.dot(left, right, preferred_element_type=f32)


def fold(rows, factor):
    half = rows.shape[0] // 2
    total = rows[:half].astype(f32) + rows[half:].astype(f32)
    if factor != 1.0:
        total = total * factor
    return total.astype(bf16)


def fold_chunks(rows, chunk, factor):
    count = rows.shape[0] // chunk
    return jnp.concatenate([fold(rows[i * chunk : (i + 1) * chunk], factor) for i in range(count)], axis=0)


def twice(rows):
    return jnp.concatenate([rows, rows], axis=0)


def cols(head):
    return slice(head * HEAD_DIM, (head + 1) * HEAD_DIM)


DECLARED = 1 << 36


def with_ones(values):
    return jnp.concatenate([values, jnp.ones_like(values)], axis=1)


def attend(units):
    scores = []
    for query, parts in units:
        raws = [
            lax.dot_general(query, keys, (((1,), (1,)), ((), ())), preferred_element_type=f32) for keys, _, _ in parts
        ]
        scores.append([raw if part[2] is None else raw + part[2] for raw, part in zip(raws, parts)])
    tops = []
    for raws in scores:
        tops.append(functools.reduce(jnp.maximum, [jnp.max(raw, axis=1, keepdims=True) for raw in raws]))
    found = []
    for (_, parts), raws, top in zip(units, scores, tops):
        total = None
        for (_, values, _), raw in zip(parts, raws):
            weights = jnp.exp2((raw - top) * EXP_SCALE).astype(bf16)
            one = mul(weights, with_ones(values))
            total = one if total is None else total + one
        found.append((jnp.broadcast_to(top * EXP_SCALE, (top.shape[0], HEAD_DIM)), total))
    return found


def share_of(ref, share, shares):
    width = ref.shape[1] // shares
    first = share * width
    if not isinstance(share, int):
        first = pl.multiple_of(first, HEAD_DIM)
    return ref.at[:, pl.ds(first, width)]


def run_shares(body, name, shares, scalars, ins, outs, work=1 << 10, unrolled=False):
    moved_in = [i for i, (kind, _) in enumerate(ins) if kind in ("cols", "got")]
    moved_out = [i for i, (kind, _) in enumerate(outs) if kind == "cols"]
    as_list = lambda pair: list(pair[1]) if pair[0] == "pieces" else [pair[1]]
    buffer_shape = {
        "cols": lambda value: (shares, value.shape[0], value.shape[1] // shares),
        "got": lambda value: (shares, value.shape[0], value.shape[1] // shares),
        "kept": lambda value: None,
        "pieces": lambda values: (shares, len(values) // shares, *values[0].shape),
    }

    def kernel(*refs):
        refs = list(refs)
        take = lambda count: [refs.pop(0) for _ in range(count)]
        scalar_refs = take(len(scalars))
        in_refs = [take(len(as_list(pair))) for pair in ins]
        out_refs = [take(len(as_list(pair))) for pair in outs]
        in_bufs = [in_refs[i][0] if ins[i][0] == "kept" else refs.pop(0) for i in range(len(ins))]
        out_bufs = [out_refs[i][0] if outs[i][0] == "kept" else refs.pop(0) for i in range(len(outs))]
        in_sems, out_sems, piece_sems = take(3)

        def bring(i, share):
            return pltpu.make_async_copy(share_of(in_refs[i][0], share, shares), in_bufs[i].at[share], in_sems.at[i, share])

        def put(i, share):
            return pltpu.make_async_copy(out_bufs[i].at[share], share_of(out_refs[i][0], share, shares), out_sems.at[i, share])

        def spot_of(buffer, n):
            entry = n ^ scalar_refs[0][1]
            return buffer.at[lax.div(entry, buffer.shape[1]), lax.rem(entry, buffer.shape[1])]

        pieces_in, pieces_out = [], []
        for i, (kind, _) in enumerate(ins):
            if kind == "pieces":
                pieces_in += [(ref, spot_of(in_bufs[i], n), n) for n, ref in enumerate(in_refs[i])]
        for i, (kind, _) in enumerate(outs):
            if kind == "pieces":
                pieces_out += [(spot_of(out_bufs[i], n), ref, n) for n, ref in enumerate(out_refs[i])]
        pieces_in = [pltpu.make_async_copy(source, target, piece_sems.at[n]) for source, target, n in pieces_in]
        pieces_out = [pltpu.make_async_copy(source, target, piece_sems.at[n]) for source, target, n in pieces_out]

        for share in range(shares):
            for i in moved_in:
                bring(i, share).start()
            if share == 0:
                for copy in pieces_in:
                    copy.start()
        for copy in pieces_in:
            copy.wait()

        def views(operands, buffers, share):
            result = []
            for (kind, value), buffer in zip(operands, buffers):
                count = value.shape[0] // shares if kind == "kept" else None
                result.append(buffer.at[share] if count is None else buffer.at[pl.ds(share * count, count)])
            return result

        def step(share, carry):
            for i in moved_in:
                bring(i, share).wait()
            body(scalar_refs, views(ins, in_bufs, share), views(outs, out_bufs, share))
            for i in moved_out:
                put(i, share).start()
            return carry

        if unrolled:
            for share in range(shares):
                step(share, 0)
        else:
            lax.fori_loop(0, shares, step, 0)
        for copy in pieces_out:
            copy.start()
        for share in range(shares):
            for i in moved_out:
                put(i, share).wait()
        for copy in pieces_out:
            copy.wait()

    spaces = {"cols": pltpu.HBM, "got": pl.ANY, "pieces": pl.ANY, "kept": pltpu.VMEM}
    values, in_specs, out_specs, out_shapes, buffers = [], [], [], [], []
    for kind, value in ins:
        for one in as_list((kind, value)):
            values.append(pltpu.with_memory_space_constraint(one, pltpu.HBM) if kind == "cols" else one)
            in_specs.append(pl.BlockSpec(memory_space=spaces[kind]))
    for kind, shape in outs:
        for one in as_list((kind, shape)):
            out_shapes.append(pltpu.HBM(one.shape, one.dtype) if kind == "cols" else one)
            out_specs.append(pl.BlockSpec(memory_space=pltpu.HBM if kind == "cols" else pltpu.VMEM))
    for kind, value in list(ins) + list(outs):
        if kind != "kept":
            buffers.append(pltpu.VMEM(buffer_shape[kind](value), as_list((kind, value))[0].dtype))
    count = max(len(as_list(pair)) for pair in list(ins) + list(outs))
    semaphores = [(len(ins), shares), (len(outs), shares), (count,)]
    return pl.pallas_call(
        kernel,
        in_specs=[pl.BlockSpec(memory_space=pltpu.SMEM)] * len(scalars) + in_specs,
        out_specs=out_specs,
        out_shape=out_shapes,
        scratch_shapes=buffers + [pltpu.SemaphoreType.DMA(shape) for shape in semaphores],
        compiler_params=pltpu.CompilerParams(vmem_limit_bytes=VMEM_GRANT),
        cost_estimate=pl.CostEstimate(flops=work, bytes_accessed=1 << 10, transcendentals=0),
        name=name,
    )(*scalars, *values)


def array(rows, width, dtype):
    return jax.ShapeDtypeStruct((rows, width), dtype)


def swap_body(_, ins, outs):
    pair = pair_matrix()
    count, _, part = outs[0].shape
    for place, (ref, factor) in enumerate(zip(ins, (0.5, 0.5, 1.0))):
        for i in range(2):
            level1 = mul(pair, ref[i * BLK : (i + 1) * BLK, :])
            if factor != 1.0:
                level1 = level1 * factor
            level2 = fold(level1.astype(bf16), factor)
            first = place * HALF + i * HALF // 2
            for n in range(count):
                outs[0][n, first : first + HALF // 2, :] = level2[:, n * part : (n + 1) * part]


def swap_rows(place, query_vecs, key_vecs, value_vecs, groups):
    width = query_vecs.shape[1]
    ins = [("cols", a) for a in (query_vecs, key_vecs, value_vecs)]
    outs = [("pieces", [array(3 * HALF, width // groups, bf16)] * groups)]
    return run_shares(swap_body, "swap_rows", groups // 2, [place], ins, outs, unrolled=True)


def rows_body(scalars, ins, outs):
    q_ref, k_ref, v_ref = ins
    q0_ref, q1_ref, near_ref, far_ref, chip_ref = outs
    reorder = reorder_matrix()
    pair = pair_matrix()
    for i in range(2):
        rows = slice(i * BLK, (i + 1) * BLK)
        q0 = mul(reorder, q_ref[rows, :]).astype(bf16)
        q0_ref[rows, :] = q0
        q1_ref[i * HALF : (i + 1) * HALF, :] = fold(q0, 0.5)
    odd = scalars[0][0]
    outer = pl.ds(pl.multiple_of(odd * BLK, BLK), BLK)
    inner = pl.ds(pl.multiple_of((1 - odd) * BLK, BLK), BLK)
    for ref, far_rows, first, near, far in ((near_ref, far_ref, 0, outer, inner), (chip_ref, chip_ref, 2 * BLK, inner, outer)):
        ref[0:BLK, :] = k_ref[near, :]
        ref[BLK : 2 * BLK, :] = v_ref[near, :]
        far_rows[first : first + HALF, :] = (mul(pair, k_ref[far, :]) * 0.5).astype(bf16)
        far_rows[first + HALF : first + BLK, :] = mul(pair, v_ref[far, :]).astype(bf16)


def rows_to_send(place, query_vecs, key_vecs, value_vecs, groups):
    rows, width = query_vecs.shape
    ins = [("cols", a) for a in (query_vecs, key_vecs, value_vecs)]
    outs = [("cols", array(n, width, bf16)) for n in (rows, rows // 2, 2 * BLK, BLK, 3 * BLK)]
    return run_shares(rows_body, "rows_to_send", groups, [place], ins, outs)


def own_body(_, ins, outs):
    q_ref, k_ref, v_ref = ins
    sum_ref, top_ref, total_ref = outs
    heads = q_ref.shape[1] // HEAD_DIM
    for i in range(2):
        rows = slice(i * BLK, (i + 1) * BLK)
        units = [(q_ref[rows, cols(head)], [(k_ref[:, cols(head)], v_ref[:, cols(head)], None)]) for head in range(heads)]
        for head, (top, sums) in enumerate(attend(units)):
            spot = (head // 2, rows, cols(head % 2))
            sum_ref[spot] = sums[:, :HEAD_DIM]
            top_ref[spot] = top
            total_ref[spot] = sums[:, HEAD_DIM:]


def running_sums(rows, width, groups):
    return [("kept", jax.ShapeDtypeStruct((groups, rows, width // groups), f32))] * 3


def own_level(q0, key_vecs, value_vecs, groups):
    ins = [("cols", a) for a in (q0, key_vecs, value_vecs)]
    return run_shares(own_body, "own_level", groups // 2, [], ins, running_sums(*q0.shape, groups), DECLARED)


def halo_body(place_ref, *refs):
    count = len(refs) - 4
    piece_refs, (got_ref, right_ref, left_ref, sems) = refs[:count], refs[count:]
    copies = [pltpu.make_async_copy(ref, got_ref.at[n ^ place_ref[1]], sems.at[n]) for n, ref in enumerate(piece_refs)]
    for copy in copies:
        copy.start()
    for copy in copies:
        copy.wait()
    pair = count // 2
    for which, factor in ((1, 0.5), (2, 1.0)):
        rows = slice(which * HALF, (which + 1) * HALF)
        near = (which - 1) * BLK
        far = 2 * BLK + (which - 1) * HALF
        for j in range(count):
            level2 = got_ref[j, rows, :]
            level3 = fold_chunks(level2, HALF // 2, factor)
            near_ref, far_ref = (left_ref, right_ref) if j < pair else (right_ref, left_ref)
            spot = j % pair
            near_ref[near + spot * HALF : near + (spot + 1) * HALF, :] = level2
            far_ref[far + spot * HALF // 2 : far + (spot + 1) * HALF // 2, :] = level3


def coarse_halos(place, pieces):
    rows, width = pieces[0].shape
    vmem = pl.BlockSpec(memory_space=pltpu.VMEM)
    shape = jax.ShapeDtypeStruct((3 * BLK, width), bf16)
    return pl.pallas_call(
        halo_body,
        in_specs=[pl.BlockSpec(memory_space=pltpu.SMEM)] + [pl.BlockSpec(memory_space=pl.ANY)] * len(pieces),
        out_specs=[vmem] * 3,
        out_shape=[jax.ShapeDtypeStruct((len(pieces), rows, width), bf16), shape, shape],
        scratch_shapes=[pltpu.SemaphoreType.DMA((len(pieces),))],
        compiler_params=pltpu.CompilerParams(vmem_limit_bytes=16 << 20),
        cost_estimate=pl.CostEstimate(flops=1 << 20, bytes_accessed=24 * pieces[0].size, transcendentals=0),
        name="coarse_halos",
    )(place, *pieces)


def coarse_body(place_ref, bias_ref, got_ref, prev_ref, next_ref, *refs):
    *out_refs, back_ref, sems = refs
    count = got_ref.shape[0]
    heads = got_ref.shape[2] // HEAD_DIM
    bias_prev = bias_ref[0]
    bias_next = bias_ref[1]
    lane = iota((HALF, HEAD_DIM), 1)

    units = []
    for head in range(heads):
        here = cols(head)

        def own(which, j):
            return got_ref[j, which * HALF : (which + 1) * HALF, here]

        def near(ref, which, spot):
            first = (which - 1) * BLK + spot * HALF
            return ref[first : first + HALF, here]

        def both(ref, which):
            return ref[(which - 1) * BLK : which * BLK, here]

        def far(ref, which):
            first = 2 * BLK + (which - 1) * HALF
            return ref[first : first + HALF, here]

        def near3(ref, which):
            return fold_chunks(both(ref, which), HALF // 2, 0.5 if which == 1 else 1.0)

        def joined(*rows):
            return jnp.concatenate(rows, axis=0)

        def part(pick, bias):
            return (pick(1), pick(2), bias)

        units += [
            (own(0, 0), [part(lambda w: joined(own(w, 2), own(w, 3)), None), part(lambda w: near(prev_ref, w, 0), bias_prev)]),
            (own(0, 1), [part(lambda w: both(prev_ref, w), bias_prev), part(lambda w: own(w, 3), None)]),
            (own(0, 2), [part(lambda w: both(next_ref, w), bias_next), part(lambda w: own(w, 0), None)]),
            (own(0, 3), [part(lambda w: joined(own(w, 0), own(w, 1)), None), part(lambda w: near(next_ref, w, 1), bias_next)]),
        ]
        for j, (ref, bias, other, other_bias) in enumerate(
            ((next_ref, bias_next, prev_ref, bias_prev), (prev_ref, bias_prev, next_ref, bias_next))
        ):
            query = joined(*[fold_chunks(own(0, 2 * j + n), HALF // 2, 0.5) for n in range(2)])
            units.append(
                (
                    query,
                    [part(lambda w: joined(near3(ref, w), far(ref, w)), bias), part(lambda w: far(other, w), other_bias)],
                )
            )
    found = attend(units)
    each = len(units) // heads

    def joined(*rows):
        return jnp.concatenate(rows, axis=0)

    for head in range(heads):
        here = cols(head)
        for j in range(count):
            top2, sum2 = found[head * each + j]
            top3, sum3 = found[head * each + count + j // 2]

            def spread(rows):
                first = (j % 2) * 2 * SUB
                one = rows[first : first + SUB]
                other = rows[first + SUB : first + 2 * SUB]
                return joined(one, one, other, other)

            top3 = spread(top3)
            sum3 = spread(sum3)
            top = jnp.maximum(top2, top3)
            scale2 = jnp.exp2(top2 - top)
            scale3 = jnp.exp2(top3 - top)
            values = sum2[:, :HEAD_DIM] * scale2 + sum3[:, :HEAD_DIM] * scale3
            total = sum2[:, HEAD_DIM:] * (4.0 * scale2) + sum3[:, HEAD_DIM:] * (8.0 * scale3)
            back_ref[j, 0:HALF, here] = (values / total).astype(bf16)
            level = top + jnp.log2(total)
            high = level.astype(bf16).astype(f32)
            middle = (level - high).astype(bf16).astype(f32)
            terms = jnp.where(lane == 0, high, jnp.where(lane == 1, middle, level - high - middle))
            back_ref[j, HALF : HALF + 16, here] = terms.T[0:16, :].astype(bf16)
    copies = [
        pltpu.make_async_copy(back_ref.at[n ^ place_ref[1]], ref, sems.at[n]) for n, ref in enumerate(out_refs)
    ]
    for copy in copies:
        copy.start()
    for copy in copies:
        copy.wait()


def coarse_levels(place, bias, got, from_prev, from_next):
    count, _, width = got.shape
    vmem = pl.BlockSpec(memory_space=pltpu.VMEM)
    smem = pl.BlockSpec(memory_space=pltpu.SMEM)
    rows = HALF + 16
    return pl.pallas_call(
        coarse_body,
        in_specs=[smem, smem, vmem, vmem, vmem],
        out_specs=[vmem] * count,
        out_shape=[array(rows, width, bf16)] * count,
        scratch_shapes=[pltpu.VMEM((count, rows, width), bf16), pltpu.SemaphoreType.DMA((count,))],
        compiler_params=pltpu.CompilerParams(vmem_limit_bytes=16 << 20),
        cost_estimate=pl.CostEstimate(flops=DECLARED, bytes_accessed=8 * got.size, transcendentals=1 << 20),
        name="coarse_levels",
    )(place, bias, got, from_prev, from_next)


def side_body(side, with_near, with_far, scalars, ins, outs):
    q0_ref, q1_ref, sum_ref, top_ref, total_ref, side_ref = ins
    heads = q1_ref.shape[1] // HEAD_DIM
    bias = scalars[1][side]
    blocks = (side, 1 - side)
    fine = [pl.ds(pl.multiple_of(block * BLK, BLK), BLK) for block in blocks]
    middle = [pl.ds(pl.multiple_of(block * HALF, HALF), HALF) for block in blocks]
    if with_near:
        pair = pair_matrix()
        near_keys = (mul(pair, side_ref[0:BLK, :]) * 0.5).astype(bf16)
        near_values = mul(pair, side_ref[BLK : 2 * BLK, :]).astype(bf16)
    start = 2 * BLK if with_near else 0
    far_keys, far_values = (slice(start + n * HALF, start + (n + 1) * HALF) for n in range(2))
    units, names = [], []
    for head in range(heads):
        here = cols(head)
        far = (side_ref[far_keys, here], side_ref[far_values, here]) if with_far else None
        near = (near_keys[:, here], near_values[:, here]) if with_near else None
        whole = [part for part in (near, far) if part is not None]
        whole = [jnp.concatenate([part[n] for part in whole], axis=0) if len(whole) > 1 else whole[0][n] for n in range(2)]
        if with_near:
            units.append((q0_ref[fine[0], here], [(side_ref[0:BLK, here], side_ref[BLK : 2 * BLK, here], None)]))
            names.append((head, 0, 0))
        if with_far:
            units.append((q1_ref[middle[0], here], [(*far, None)]))
            names.append((head, 0, 1))
        units.append((q1_ref[middle[1], here], [(*whole, None)]))
        names.append((head, 1, 1))
    found = {name: (top + bias, sums) for name, (top, sums) in zip(names, attend(units))}
    for n in range(2):
        for head in range(heads):
            spot = (head // 2, fine[n], cols(head % 2))
            parts = [(top_ref[spot], sum_ref[spot], total_ref[spot])]
            if (head, n, 0) in found:
                top, sums = found[head, n, 0]
                parts.append((top, sums[:, :HEAD_DIM], sums[:, HEAD_DIM:]))
            if (head, n, 1) in found:
                top, sums = found[head, n, 1]
                parts.append((twice(top), twice(sums[:, :HEAD_DIM]), twice(2.0 * sums[:, HEAD_DIM:])))
            most = functools.reduce(jnp.maximum, [part[0] for part in parts])
            scales = [jnp.exp2(part[0] - most) for part in parts]
            outs[0][spot] = sum(part[1] * scale for part, scale in zip(parts, scales))
            outs[1][spot] = most
            outs[2][spot] = sum(part[2] * scale for part, scale in zip(parts, scales))


def chip_body(scalars, ins, outs):
    side_body(1 - scalars[0][0], True, True, scalars, ins, outs)


def near_body(scalars, ins, outs):
    side_body(scalars[0][0], True, False, scalars, ins, outs)


def far_body(scalars, ins, outs):
    side_body(scalars[0][0], False, True, scalars, [None] + ins, outs)


def side_level(body, name, place, bias, queries, running, rows):
    groups, count, part = running[0].shape
    ins = [("cols", query) for query in queries] + [("kept", one) for one in running] + [("got", rows)]
    return run_shares(body, name, groups // 2, [place, bias], ins, running_sums(count, groups * part, groups))


def finish_body(place_ref, sum_ref, top_ref, total_ref, *refs):
    groups = sum_ref.shape[0]
    back_refs, (out_ref, done_ref, sems) = refs[:groups], refs[groups:]
    part = sum_ref.shape[2]
    restore = restore_matrix()
    copies = []
    for n, back_ref in enumerate(back_refs):
        entry = n ^ place_ref[1]
        levels = []
        for head in range(part // HEAD_DIM):
            terms = back_ref[HALF : HALF + 16, cols(head)].astype(f32)
            terms = jnp.sum(jnp.where(iota(terms.shape, 0) < 3, terms, 0.0), axis=0, keepdims=True)
            levels.append(jnp.broadcast_to(terms, (HEAD_DIM, HEAD_DIM)).T)
        for i in range(2):
            rows = slice(i * BLK, (i + 1) * BLK)
            spot = slice(i * HALF // 2, (i + 1) * HALF // 2)
            results = []
            for head, level in enumerate(levels):
                here = (entry, rows, cols(head))
                top = top_ref[here]
                level = twice(twice(level[spot, :]))
                lead = top - level
                smaller = jnp.exp2(-jnp.abs(lead))
                scale = jnp.where(lead >= 0.0, 1.0, smaller)
                coarse = jnp.where(lead >= 0.0, smaller, 1.0)
                number = twice(twice(back_ref[spot, cols(head)].astype(f32))) * coarse
                number = number + sum_ref[here] * scale
                total = total_ref[here] * scale + coarse
                guess = pl.reciprocal(total, approx=True)
                results.append((number * (guess * (2.0 - total * guess))).astype(bf16))
            done_ref[n, rows, :] = mul(restore, jnp.concatenate(results, axis=1)).astype(bf16)
        columns = pl.ds(pl.multiple_of(entry * part, HEAD_DIM), part)
        copies.append(pltpu.make_async_copy(done_ref.at[n], out_ref.at[:, columns], sems.at[n]))
        copies[-1].start()
    for copy in copies:
        copy.wait()


def finish(place, running, back):
    groups, rows, part = running[0].shape
    vmem = pl.BlockSpec(memory_space=pltpu.VMEM)
    return pl.pallas_call(
        finish_body,
        in_specs=[pl.BlockSpec(memory_space=pltpu.SMEM)] + [vmem] * (3 + groups),
        out_specs=pl.BlockSpec(memory_space=pltpu.HBM),
        out_shape=pltpu.HBM((rows, groups * part), bf16),
        scratch_shapes=[pltpu.VMEM((groups, rows, part), bf16), pltpu.SemaphoreType.DMA((groups,))],
        compiler_params=pltpu.CompilerParams(vmem_limit_bytes=VMEM_GRANT),
        cost_estimate=pl.CostEstimate(flops=1 << 10, bytes_accessed=1 << 10, transcendentals=0),
        name="finish",
    )(place, *running, *back)


def shift(value, axis, steps):
    count = lax.axis_size(axis)
    first, last = (max(0, -steps), min(count, count - steps))
    return lax.ppermute(value, axis, [(source, source + steps) for source in range(first, last)])


def trade(value, axis, pairs):
    return lax.ppermute(value, axis, pairs + [(target, source) for source, target in pairs])


def edge_bias(axis):
    place = lax.axis_index(axis)
    last = lax.axis_size(axis) - 1
    at_edge = jnp.stack([place == 0, place == last])
    return jnp.where(at_edge, very_negative, 0.0).astype(f32)


def local(query_vecs, key_vecs, value_vecs):
    groups = lax.axis_size("grp")
    assert query_vecs.shape == (2 * BLK, HEADS * HEAD_DIM) and groups == 4
    everyone = ("seq", "grp")
    count = lax.axis_size(everyone)
    spot = lax.axis_index("grp")
    odd = jnp.bitwise_and(spot, 1)
    place = jnp.stack([odd, spot]).astype(jnp.int32)
    bias = edge_bias(everyone)

    def exchange(pieces):
        flips = [[(source, source ^ n) for source in range(groups)] for n in range(groups)]
        for n in range(groups - 1, 0, -1):
            pieces[n] = lax.ppermute(pieces[n], "grp", flips[n])
        return pieces

    pieces = list(swap_rows(place, query_vecs, key_vecs, value_vecs, groups))
    query_rows, pieces = lax.optimization_barrier((query_vecs, pieces))
    pieces = exchange(pieces)
    q0, q1, near, far, chip = rows_to_send(place, query_rows, key_vecs, value_vecs, groups)
    off_chip = [(device, device + 1) for device in range(1, count - 1, 2)]
    near_out = trade(near, everyone, [pair for pair in off_chip if pair[1] % groups == 0])
    pieces, chip = lax.optimization_barrier((pieces, chip))
    got, coarse_right, coarse_left = coarse_halos(place, pieces)
    coarse_right, coarse_left, chip, q0, far, near = lax.optimization_barrier(
        (coarse_right, coarse_left, chip, q0, far, near)
    )
    coarse_prev = shift(coarse_right, "seq", 1)
    coarse_next = shift(coarse_left, "seq", -1)
    chip = trade(chip, everyone, [(device, device + 1) for device in range(0, count - 1, 2)])
    near_in = trade(near, everyone, [pair for pair in off_chip if pair[1] % groups != 0])
    running = own_level(q0, key_vecs, value_vecs, groups)
    far, running = lax.optimization_barrier((far, running))
    far = trade(far, everyone, off_chip)
    running = side_level(chip_body, "chip_level", place, bias, (q0, q1), running, chip)
    near_out, near_in, running = lax.optimization_barrier((near_out, near_in, running))
    near = near_out + near_in
    running = side_level(near_body, "near_level", place, bias, (q0, q1), running, near)
    got, running = lax.optimization_barrier((got, running))
    back = coarse_levels(place, edge_bias("seq"), got, coarse_prev, coarse_next)
    back, running = lax.optimization_barrier((back, running))
    back = exchange(list(back))
    running = side_level(far_body, "far_level", place, bias, (q1,), running, far)
    return finish(place, running, back)


def solution(mesh):
    return jax.shard_map(
        local,
        mesh=mesh,
        in_specs=(P(("seq", "grp"), None), P(("seq", "grp"), None), P(("seq", "grp"), None)),
        out_specs=P(("seq", "grp"), None),
        check_vma=False,
    )
```

```python
import functools
import math

import jax
import jax.numpy as jnp
from jax import lax
from jax.experimental import pallas as pl
from jax.experimental.pallas import tpu as pltpu
from jax.sharding import PartitionSpec as P

HEADS = 8
HEAD_DIM = 128
BLK = 256
HALF = BLK // 2
SUB = BLK // 8
LEV = 4
EXP_SCALE = math.log2(math.e) / math.sqrt(HEAD_DIM)

VMEM_GRANT = 24 << 20

very_negative = -1e30
f32 = jnp.float32
bf16 = jnp.bfloat16


def iota(shape, dim):
    return lax.broadcasted_iota(jnp.int32, shape, dim)


def bit(value, place):
    return jnp.bitwise_and(lax.shift_right_logical(value, place), 1)


def low_bits(value):
    step = SUB.bit_length() - 1
    deep = jnp.bitwise_and(value, SUB - 1)
    return 8 * deep + 4 * bit(value, step) + 2 * bit(value, step + 1) + bit(value, step + 2)


def reorder_matrix():
    return (iota((BLK, BLK), 1) == low_bits(iota((BLK, BLK), 0))).astype(bf16)


def restore_matrix():
    return (iota((BLK, BLK), 0) == low_bits(iota((BLK, BLK), 1))).astype(bf16)


def pair_matrix():
    first = low_bits(iota((HALF, BLK), 0))
    place = iota((HALF, BLK), 1)
    return jnp.logical_or(place == first, place == first + 1).astype(bf16)


def mul(left, right):
    return jnp.dot(left, right, preferred_element_type=f32)


def fold(rows, factor):
    half = rows.shape[0] // 2
    total = rows[:half].astype(f32) + rows[half:].astype(f32)
    if factor != 1.0:
        total = total * factor
    return total.astype(bf16)


def fold_chunks(rows, chunk, factor):
    count = rows.shape[0] // chunk
    return jnp.concatenate([fold(rows[i * chunk : (i + 1) * chunk], factor) for i in range(count)], axis=0)


def twice(rows):
    return jnp.concatenate([rows, rows], axis=0)


def cols(head):
    return slice(head * HEAD_DIM, (head + 1) * HEAD_DIM)


DECLARED = 1 << 36


def with_ones(values):
    return jnp.concatenate([values, jnp.ones_like(values)], axis=1)


def attend(units):
    scores = []
    for query, parts in units:
        raws = [
            lax.dot_general(query, keys, (((1,), (1,)), ((), ())), preferred_element_type=f32) for keys, _, _ in parts
        ]
        scores.append([raw if part[2] is None else raw + part[2] for raw, part in zip(raws, parts)])
    tops = []
    for raws in scores:
        tops.append(functools.reduce(jnp.maximum, [jnp.max(raw, axis=1, keepdims=True) for raw in raws]))
    found = []
    for (_, parts), raws, top in zip(units, scores, tops):
        total = None
        for (_, values, _), raw in zip(parts, raws):
            weights = jnp.exp2((raw - top) * EXP_SCALE).astype(bf16)
            one = mul(weights, with_ones(values))
            total = one if total is None else total + one
        found.append((jnp.broadcast_to(top * EXP_SCALE, (top.shape[0], HEAD_DIM)), total))
    return found


def share_of(ref, share, shares):
    width = ref.shape[1] // shares
    first = share * width
    if not isinstance(share, int):
        first = pl.multiple_of(first, HEAD_DIM)
    return ref.at[:, pl.ds(first, width)]


def run_shares(body, name, shares, scalars, ins, outs, work=1 << 10, unrolled=False):
    moved_in = [i for i, (kind, _) in enumerate(ins) if kind in ("cols", "got")]
    moved_out = [i for i, (kind, _) in enumerate(outs) if kind == "cols"]
    as_list = lambda pair: list(pair[1]) if pair[0] == "pieces" else [pair[1]]
    buffer_shape = {
        "cols": lambda value: (shares, value.shape[0], value.shape[1] // shares),
        "got": lambda value: (shares, value.shape[0], value.shape[1] // shares),
        "kept": lambda value: None,
        "pieces": lambda values: (shares, len(values) // shares, *values[0].shape),
    }

    def kernel(*refs):
        refs = list(refs)
        take = lambda count: [refs.pop(0) for _ in range(count)]
        scalar_refs = take(len(scalars))
        in_refs = [take(len(as_list(pair))) for pair in ins]
        out_refs = [take(len(as_list(pair))) for pair in outs]
        in_bufs = [in_refs[i][0] if ins[i][0] == "kept" else refs.pop(0) for i in range(len(ins))]
        out_bufs = [out_refs[i][0] if outs[i][0] == "kept" else refs.pop(0) for i in range(len(outs))]
        in_sems, out_sems, piece_sems = take(3)

        def bring(i, share):
            return pltpu.make_async_copy(share_of(in_refs[i][0], share, shares), in_bufs[i].at[share], in_sems.at[i, share])

        def put(i, share):
            return pltpu.make_async_copy(out_bufs[i].at[share], share_of(out_refs[i][0], share, shares), out_sems.at[i, share])

        def spot_of(buffer, n):
            entry = n ^ scalar_refs[0][1]
            return buffer.at[lax.div(entry, buffer.shape[1]), lax.rem(entry, buffer.shape[1])]

        pieces_in, pieces_out = [], []
        for i, (kind, _) in enumerate(ins):
            if kind == "pieces":
                pieces_in += [(ref, spot_of(in_bufs[i], n), n) for n, ref in enumerate(in_refs[i])]
        for i, (kind, _) in enumerate(outs):
            if kind == "pieces":
                pieces_out += [(spot_of(out_bufs[i], n), ref, n) for n, ref in enumerate(out_refs[i])]
        pieces_in = [pltpu.make_async_copy(source, target, piece_sems.at[n]) for source, target, n in pieces_in]
        pieces_out = [pltpu.make_async_copy(source, target, piece_sems.at[n]) for source, target, n in pieces_out]

        for share in range(shares):
            for i in moved_in:
                bring(i, share).start()
            if share == 0:
                for copy in pieces_in:
                    copy.start()
        for copy in pieces_in:
            copy.wait()

        def views(operands, buffers, share):
            result = []
            for (kind, value), buffer in zip(operands, buffers):
                count = value.shape[0] // shares if kind == "kept" else None
                result.append(buffer.at[share] if count is None else buffer.at[pl.ds(share * count, count)])
            return result

        def step(share, carry):
            for i in moved_in:
                bring(i, share).wait()
            body(scalar_refs, views(ins, in_bufs, share), views(outs, out_bufs, share))
            for i in moved_out:
                put(i, share).start()
            return carry

        if unrolled:
            for share in range(shares):
                step(share, 0)
        else:
            lax.fori_loop(0, shares, step, 0)
        for copy in pieces_out:
            copy.start()
        for share in range(shares):
            for i in moved_out:
                put(i, share).wait()
        for copy in pieces_out:
            copy.wait()

    spaces = {"cols": pltpu.HBM, "got": pl.ANY, "pieces": pl.ANY, "kept": pltpu.VMEM}
    values, in_specs, out_specs, out_shapes, buffers = [], [], [], [], []
    for kind, value in ins:
        for one in as_list((kind, value)):
            values.append(pltpu.with_memory_space_constraint(one, pltpu.HBM) if kind == "cols" else one)
            in_specs.append(pl.BlockSpec(memory_space=spaces[kind]))
    for kind, shape in outs:
        for one in as_list((kind, shape)):
            out_shapes.append(pltpu.HBM(one.shape, one.dtype) if kind == "cols" else one)
            out_specs.append(pl.BlockSpec(memory_space=pltpu.HBM if kind == "cols" else pltpu.VMEM))
    for kind, value in list(ins) + list(outs):
        if kind != "kept":
            buffers.append(pltpu.VMEM(buffer_shape[kind](value), as_list((kind, value))[0].dtype))
    count = max(len(as_list(pair)) for pair in list(ins) + list(outs))
    semaphores = [(len(ins), shares), (len(outs), shares), (count,)]
    return pl.pallas_call(
        kernel,
        in_specs=[pl.BlockSpec(memory_space=pltpu.SMEM)] * len(scalars) + in_specs,
        out_specs=out_specs,
        out_shape=out_shapes,
        scratch_shapes=buffers + [pltpu.SemaphoreType.DMA(shape) for shape in semaphores],
        compiler_params=pltpu.CompilerParams(vmem_limit_bytes=VMEM_GRANT),
        cost_estimate=pl.CostEstimate(flops=work, bytes_accessed=1 << 10, transcendentals=0),
        name=name,
    )(*scalars, *values)


def array(rows, width, dtype):
    return jax.ShapeDtypeStruct((rows, width), dtype)


def swap_body(_, ins, outs):
    pair = pair_matrix()
    count, _, part = outs[0].shape
    for place, (ref, factor) in enumerate(zip(ins, (0.5, 0.5, 1.0))):
        for i in range(2):
            level1 = mul(pair, ref[i * BLK : (i + 1) * BLK, :])
            if factor != 1.0:
                level1 = level1 * factor
            level2 = fold(level1.astype(bf16), factor)
            first = place * HALF + i * HALF // 2
            for n in range(count):
                outs[0][n, first : first + HALF // 2, :] = level2[:, n * part : (n + 1) * part]


def swap_rows(place, query_vecs, key_vecs, value_vecs, groups):
    width = query_vecs.shape[1]
    ins = [("cols", a) for a in (query_vecs, key_vecs, value_vecs)]
    outs = [("pieces", [array(3 * HALF, width // groups, bf16)] * groups)]
    return run_shares(swap_body, "swap_rows", groups // 2, [place], ins, outs, unrolled=True)


def rows_body(scalars, ins, outs):
    q_ref, k_ref, v_ref = ins
    q0_ref, q1_ref, near_ref, far_ref, chip_ref = outs
    reorder = reorder_matrix()
    pair = pair_matrix()
    for i in range(2):
        rows = slice(i * BLK, (i + 1) * BLK)
        q0 = mul(reorder, q_ref[rows, :]).astype(bf16)
        q0_ref[rows, :] = q0
        q1_ref[i * HALF : (i + 1) * HALF, :] = fold(q0, 0.5)
    odd = scalars[0][0]
    outer = pl.ds(pl.multiple_of(odd * BLK, BLK), BLK)
    inner = pl.ds(pl.multiple_of((1 - odd) * BLK, BLK), BLK)
    for ref, far_rows, first, near, far in ((near_ref, far_ref, 0, outer, inner), (chip_ref, chip_ref, 2 * BLK, inner, outer)):
        ref[0:BLK, :] = k_ref[near, :]
        ref[BLK : 2 * BLK, :] = v_ref[near, :]
        far_rows[first : first + HALF, :] = (mul(pair, k_ref[far, :]) * 0.5).astype(bf16)
        far_rows[first + HALF : first + BLK, :] = mul(pair, v_ref[far, :]).astype(bf16)


def rows_to_send(place, query_vecs, key_vecs, value_vecs, groups):
    rows, width = query_vecs.shape
    ins = [("cols", a) for a in (query_vecs, key_vecs, value_vecs)]
    outs = [("cols", array(n, width, bf16)) for n in (rows, rows // 2, 2 * BLK, BLK, 3 * BLK)]
    return run_shares(rows_body, "rows_to_send", groups, [place], ins, outs)


def own_body(_, ins, outs):
    q_ref, k_ref, v_ref = ins
    sum_ref, top_ref, total_ref = outs
    heads = q_ref.shape[1] // HEAD_DIM
    for i in range(2):
        rows = slice(i * BLK, (i + 1) * BLK)
        units = [(q_ref[rows, cols(head)], [(k_ref[:, cols(head)], v_ref[:, cols(head)], None)]) for head in range(heads)]
        for head, (top, sums) in enumerate(attend(units)):
            spot = (head // 2, rows, cols(head % 2))
            sum_ref[spot] = sums[:, :HEAD_DIM]
            top_ref[spot] = top
            total_ref[spot] = sums[:, HEAD_DIM:]


def running_sums(rows, width, groups):
    return [("kept", jax.ShapeDtypeStruct((groups, rows, width // groups), f32))] * 3


def own_level(q0, key_vecs, value_vecs, groups):
    ins = [("cols", a) for a in (q0, key_vecs, value_vecs)]
    return run_shares(own_body, "own_level", groups // 2, [], ins, running_sums(*q0.shape, groups), DECLARED)


def halo_body(place_ref, *refs):
    count = len(refs) - 4
    piece_refs, (got_ref, right_ref, left_ref, sems) = refs[:count], refs[count:]
    copies = [pltpu.make_async_copy(ref, got_ref.at[n ^ place_ref[1]], sems.at[n]) for n, ref in enumerate(piece_refs)]
    for copy in copies:
        copy.start()
    for copy in copies:
        copy.wait()
    pair = count // 2
    for which, factor in ((1, 0.5), (2, 1.0)):
        rows = slice(which * HALF, (which + 1) * HALF)
        near = (which - 1) * BLK
        far = 2 * BLK + (which - 1) * HALF
        for j in range(count):
            level2 = got_ref[j, rows, :]
            level3 = fold_chunks(level2, HALF // 2, factor)
            near_ref, far_ref = (left_ref, right_ref) if j < pair else (right_ref, left_ref)
            spot = j % pair
            near_ref[near + spot * HALF : near + (spot + 1) * HALF, :] = level2
            far_ref[far + spot * HALF // 2 : far + (spot + 1) * HALF // 2, :] = level3


def coarse_halos(place, pieces):
    rows, width = pieces[0].shape
    vmem = pl.BlockSpec(memory_space=pltpu.VMEM)
    shape = jax.ShapeDtypeStruct((3 * BLK, width), bf16)
    return pl.pallas_call(
        halo_body,
        in_specs=[pl.BlockSpec(memory_space=pltpu.SMEM)] + [pl.BlockSpec(memory_space=pl.ANY)] * len(pieces),
        out_specs=[vmem] * 3,
        out_shape=[jax.ShapeDtypeStruct((len(pieces), rows, width), bf16), shape, shape],
        scratch_shapes=[pltpu.SemaphoreType.DMA((len(pieces),))],
        compiler_params=pltpu.CompilerParams(vmem_limit_bytes=16 << 20),
        cost_estimate=pl.CostEstimate(flops=1 << 20, bytes_accessed=24 * pieces[0].size, transcendentals=0),
        name="coarse_halos",
    )(place, *pieces)


def coarse_body(place_ref, bias_ref, got_ref, prev_ref, next_ref, *refs):
    *out_refs, back_ref, sems = refs
    count = got_ref.shape[0]
    heads = got_ref.shape[2] // HEAD_DIM
    bias_prev = bias_ref[0]
    bias_next = bias_ref[1]
    lane = iota((HALF, HEAD_DIM), 1)

    units = []
    for head in range(heads):
        here = cols(head)

        def own(which, j):
            return got_ref[j, which * HALF : (which + 1) * HALF, here]

        def near(ref, which, spot):
            first = (which - 1) * BLK + spot * HALF
            return ref[first : first + HALF, here]

        def both(ref, which):
            return ref[(which - 1) * BLK : which * BLK, here]

        def far(ref, which):
            first = 2 * BLK + (which - 1) * HALF
            return ref[first : first + HALF, here]

        def near3(ref, which):
            return fold_chunks(both(ref, which), HALF // 2, 0.5 if which == 1 else 1.0)

        def joined(*rows):
            return jnp.concatenate(rows, axis=0)

        def part(pick, bias):
            return (pick(1), pick(2), bias)

        units += [
            (own(0, 0), [part(lambda w: joined(own(w, 2), own(w, 3)), None), part(lambda w: near(prev_ref, w, 0), bias_prev)]),
            (own(0, 1), [part(lambda w: both(prev_ref, w), bias_prev), part(lambda w: own(w, 3), None)]),
            (own(0, 2), [part(lambda w: both(next_ref, w), bias_next), part(lambda w: own(w, 0), None)]),
            (own(0, 3), [part(lambda w: joined(own(w, 0), own(w, 1)), None), part(lambda w: near(next_ref, w, 1), bias_next)]),
        ]
        for j, (ref, bias, other, other_bias) in enumerate(
            ((next_ref, bias_next, prev_ref, bias_prev), (prev_ref, bias_prev, next_ref, bias_next))
        ):
            query = joined(*[fold_chunks(own(0, 2 * j + n), HALF // 2, 0.5) for n in range(2)])
            units.append(
                (
                    query,
                    [part(lambda w: joined(near3(ref, w), far(ref, w)), bias), part(lambda w: far(other, w), other_bias)],
                )
            )
    found = attend(units)
    each = len(units) // heads

    def joined(*rows):
        return jnp.concatenate(rows, axis=0)

    for head in range(heads):
        here = cols(head)
        for j in range(count):
            top2, sum2 = found[head * each + j]
            top3, sum3 = found[head * each + count + j // 2]

            def spread(rows):
                first = (j % 2) * 2 * SUB
                one = rows[first : first + SUB]
                other = rows[first + SUB : first + 2 * SUB]
                return joined(one, one, other, other)

            top3 = spread(top3)
            sum3 = spread(sum3)
            top = jnp.maximum(top2, top3)
            scale2 = jnp.exp2(top2 - top)
            scale3 = jnp.exp2(top3 - top)
            values = sum2[:, :HEAD_DIM] * scale2 + sum3[:, :HEAD_DIM] * scale3
            total = sum2[:, HEAD_DIM:] * (4.0 * scale2) + sum3[:, HEAD_DIM:] * (8.0 * scale3)
            back_ref[j, 0:HALF, here] = (values / total).astype(bf16)
            level = top + jnp.log2(total)
            high = level.astype(bf16).astype(f32)
            middle = (level - high).astype(bf16).astype(f32)
            terms = jnp.where(lane == 0, high, jnp.where(lane == 1, middle, level - high - middle))
            back_ref[j, HALF : HALF + 16, here] = terms.T[0:16, :].astype(bf16)
    copies = [
        pltpu.make_async_copy(back_ref.at[n ^ place_ref[1]], ref, sems.at[n]) for n, ref in enumerate(out_refs)
    ]
    for copy in copies:
        copy.start()
    for copy in copies:
        copy.wait()


def coarse_levels(place, bias, got, from_prev, from_next):
    count, _, width = got.shape
    vmem = pl.BlockSpec(memory_space=pltpu.VMEM)
    smem = pl.BlockSpec(memory_space=pltpu.SMEM)
    rows = HALF + 16
    return pl.pallas_call(
        coarse_body,
        in_specs=[smem, smem, vmem, vmem, vmem],
        out_specs=[vmem] * count,
        out_shape=[array(rows, width, bf16)] * count,
        scratch_shapes=[pltpu.VMEM((count, rows, width), bf16), pltpu.SemaphoreType.DMA((count,))],
        compiler_params=pltpu.CompilerParams(vmem_limit_bytes=16 << 20),
        cost_estimate=pl.CostEstimate(flops=DECLARED, bytes_accessed=8 * got.size, transcendentals=1 << 20),
        name="coarse_levels",
    )(place, bias, got, from_prev, from_next)


def side_body(side, with_near, with_far, scalars, ins, outs):
    q0_ref, q1_ref, sum_ref, top_ref, total_ref, side_ref = ins
    heads = q1_ref.shape[1] // HEAD_DIM
    bias = scalars[1][side]
    blocks = (side, 1 - side)
    fine = [pl.ds(pl.multiple_of(block * BLK, BLK), BLK) for block in blocks]
    middle = [pl.ds(pl.multiple_of(block * HALF, HALF), HALF) for block in blocks]
    if with_near:
        pair = pair_matrix()
        near_keys = (mul(pair, side_ref[0:BLK, :]) * 0.5).astype(bf16)
        near_values = mul(pair, side_ref[BLK : 2 * BLK, :]).astype(bf16)
    start = 2 * BLK if with_near else 0
    far_keys, far_values = (slice(start + n * HALF, start + (n + 1) * HALF) for n in range(2))
    units, names = [], []
    for head in range(heads):
        here = cols(head)
        far = (side_ref[far_keys, here], side_ref[far_values, here]) if with_far else None
        near = (near_keys[:, here], near_values[:, here]) if with_near else None
        whole = [part for part in (near, far) if part is not None]
        whole = [jnp.concatenate([part[n] for part in whole], axis=0) if len(whole) > 1 else whole[0][n] for n in range(2)]
        if with_near:
            units.append((q0_ref[fine[0], here], [(side_ref[0:BLK, here], side_ref[BLK : 2 * BLK, here], None)]))
            names.append((head, 0, 0))
        if with_far:
            units.append((q1_ref[middle[0], here], [(*far, None)]))
            names.append((head, 0, 1))
        units.append((q1_ref[middle[1], here], [(*whole, None)]))
        names.append((head, 1, 1))
    found = {name: (top + bias, sums) for name, (top, sums) in zip(names, attend(units))}
    for n in range(2):
        for head in range(heads):
            spot = (head // 2, fine[n], cols(head % 2))
            parts = [(top_ref[spot], sum_ref[spot], total_ref[spot])]
            if (head, n, 0) in found:
                top, sums = found[head, n, 0]
                parts.append((top, sums[:, :HEAD_DIM], sums[:, HEAD_DIM:]))
            if (head, n, 1) in found:
                top, sums = found[head, n, 1]
                parts.append((twice(top), twice(sums[:, :HEAD_DIM]), twice(2.0 * sums[:, HEAD_DIM:])))
            most = functools.reduce(jnp.maximum, [part[0] for part in parts])
            scales = [jnp.exp2(part[0] - most) for part in parts]
            outs[0][spot] = sum(part[1] * scale for part, scale in zip(parts, scales))
            outs[1][spot] = most
            outs[2][spot] = sum(part[2] * scale for part, scale in zip(parts, scales))


def chip_body(scalars, ins, outs):
    side_body(1 - scalars[0][0], True, True, scalars, ins, outs)


def near_body(scalars, ins, outs):
    side_body(scalars[0][0], True, False, scalars, ins, outs)


def far_body(scalars, ins, outs):
    side_body(scalars[0][0], False, True, scalars, [None] + ins, outs)


def side_level(body, name, place, bias, queries, running, rows):
    groups, count, part = running[0].shape
    ins = [("cols", query) for query in queries] + [("kept", one) for one in running] + [("got", rows)]
    return run_shares(body, name, groups // 2, [place, bias], ins, running_sums(count, groups * part, groups))


def finish_body(place_ref, sum_ref, top_ref, total_ref, *refs):
    groups = sum_ref.shape[0]
    back_refs, (out_ref, done_ref, sems) = refs[:groups], refs[groups:]
    part = sum_ref.shape[2]
    restore = restore_matrix()
    copies = []
    for n, back_ref in enumerate(back_refs):
        entry = n ^ place_ref[1]
        levels = []
        for head in range(part // HEAD_DIM):
            terms = back_ref[HALF : HALF + 16, cols(head)].astype(f32)
            terms = jnp.sum(jnp.where(iota(terms.shape, 0) < 3, terms, 0.0), axis=0, keepdims=True)
            levels.append(jnp.broadcast_to(terms, (HEAD_DIM, HEAD_DIM)).T)
        for i in range(2):
            rows = slice(i * BLK, (i + 1) * BLK)
            spot = slice(i * HALF // 2, (i + 1) * HALF // 2)
            results = []
            for head, level in enumerate(levels):
                here = (entry, rows, cols(head))
                top = top_ref[here]
                level = twice(twice(level[spot, :]))
                lead = top - level
                smaller = jnp.exp2(-jnp.abs(lead))
                scale = jnp.where(lead >= 0.0, 1.0, smaller)
                coarse = jnp.where(lead >= 0.0, smaller, 1.0)
                number = twice(twice(back_ref[spot, cols(head)].astype(f32))) * coarse
                number = number + sum_ref[here] * scale
                total = total_ref[here] * scale + coarse
                guess = pl.reciprocal(total, approx=True)
                results.append((number * (guess * (2.0 - total * guess))).astype(bf16))
            done_ref[n, rows, :] = mul(restore, jnp.concatenate(results, axis=1)).astype(bf16)
        columns = pl.ds(pl.multiple_of(entry * part, HEAD_DIM), part)
        copies.append(pltpu.make_async_copy(done_ref.at[n], out_ref.at[:, columns], sems.at[n]))
        copies[-1].start()
    for copy in copies:
        copy.wait()


def finish(place, running, back):
    groups, rows, part = running[0].shape
    vmem = pl.BlockSpec(memory_space=pltpu.VMEM)
    return pl.pallas_call(
        finish_body,
        in_specs=[pl.BlockSpec(memory_space=pltpu.SMEM)] + [vmem] * (3 + groups),
        out_specs=pl.BlockSpec(memory_space=pltpu.HBM),
        out_shape=pltpu.HBM((rows, groups * part), bf16),
        scratch_shapes=[pltpu.VMEM((groups, rows, part), bf16), pltpu.SemaphoreType.DMA((groups,))],
        compiler_params=pltpu.CompilerParams(vmem_limit_bytes=VMEM_GRANT),
        cost_estimate=pl.CostEstimate(flops=1 << 10, bytes_accessed=1 << 10, transcendentals=0),
        name="finish",
    )(place, *running, *back)


def shift(value, axis, steps):
    count = lax.axis_size(axis)
    first, last = (max(0, -steps), min(count, count - steps))
    return lax.ppermute(value, axis, [(source, source + steps) for source in range(first, last)])


def trade(value, axis, pairs):
    return lax.ppermute(value, axis, pairs + [(target, source) for source, target in pairs])


def edge_bias(axis):
    place = lax.axis_index(axis)
    last = lax.axis_size(axis) - 1
    at_edge = jnp.stack([place == 0, place == last])
    return jnp.where(at_edge, very_negative, 0.0).astype(f32)


def local(query_vecs, key_vecs, value_vecs):
    groups = lax.axis_size("grp")
    assert query_vecs.shape == (2 * BLK, HEADS * HEAD_DIM) and groups == 4
    everyone = ("seq", "grp")
    count = lax.axis_size(everyone)
    spot = lax.axis_index("grp")
    odd = jnp.bitwise_and(spot, 1)
    place = jnp.stack([odd, spot]).astype(jnp.int32)
    bias = edge_bias(everyone)

    def exchange(pieces, places):
        for n in places:
            flips = [(source, source ^ n) for source in range(groups)]
            pieces[n] = lax.ppermute(pieces[n], "grp", flips)
        return pieces

    off = range(2, groups)
    pieces = list(swap_rows(place, query_vecs, key_vecs, value_vecs, groups))
    query_rows, pieces = lax.optimization_barrier((query_vecs, pieces))
    pieces = exchange(pieces, off)
    q0, q1, near, far, chip = rows_to_send(place, query_rows, key_vecs, value_vecs, groups)
    pieces[1], far = lax.optimization_barrier((pieces[1], far))
    pieces = exchange(pieces, [1])
    off_chip = [(device, device + 1) for device in range(1, count - 1, 2)]
    near = trade(near, everyone, off_chip)
    pieces, chip = lax.optimization_barrier((pieces, chip))
    got, coarse_right, coarse_left = coarse_halos(place, pieces)
    coarse_right, coarse_left, chip, q0, far = lax.optimization_barrier((coarse_right, coarse_left, chip, q0, far))
    coarse_prev = shift(coarse_right, "seq", 1)
    coarse_next = shift(coarse_left, "seq", -1)
    chip = trade(chip, everyone, [(device, device + 1) for device in range(0, count - 1, 2)])
    far = trade(far, everyone, off_chip)
    running = own_level(q0, key_vecs, value_vecs, groups)
    running = side_level(chip_body, "chip_level", place, bias, (q0, q1), running, chip)
    running = side_level(near_body, "near_level", place, bias, (q0, q1), running, near)
    got, running = lax.optimization_barrier((got, running))
    back = coarse_levels(place, edge_bias("seq"), got, coarse_prev, coarse_next)
    back, running = lax.optimization_barrier((back, running))
    back = exchange(list(back), [*off, 1])
    running = side_level(far_body, "far_level", place, bias, (q1,), running, far)
    return finish(place, running, back)


def solution(mesh):
    return jax.shard_map(
        local,
        mesh=mesh,
        in_specs=(P(("seq", "grp"), None), P(("seq", "grp"), None), P(("seq", "grp"), None)),
        out_specs=P(("seq", "grp"), None),
        check_vma=False,
    )
```

```python
import functools
import math

import jax
import jax.numpy as jnp
from jax import lax
from jax.experimental import pallas as pl
from jax.experimental.pallas import tpu as pltpu
from jax.sharding import PartitionSpec as P

HEADS = 8
HEAD_DIM = 128
BLK = 256
HALF = BLK // 2
SUB = BLK // 8
LEV = 4
EXP_SCALE = math.log2(math.e) / math.sqrt(HEAD_DIM)

VMEM_GRANT = 24 << 20

very_negative = -1e30
f32 = jnp.float32
bf16 = jnp.bfloat16


def iota(shape, dim):
    return lax.broadcasted_iota(jnp.int32, shape, dim)


def bit(value, place):
    return jnp.bitwise_and(lax.shift_right_logical(value, place), 1)


def low_bits(value):
    step = SUB.bit_length() - 1
    deep = jnp.bitwise_and(value, SUB - 1)
    return 8 * deep + 4 * bit(value, step) + 2 * bit(value, step + 1) + bit(value, step + 2)


def reorder_matrix():
    return (iota((BLK, BLK), 1) == low_bits(iota((BLK, BLK), 0))).astype(bf16)


def restore_matrix():
    return (iota((BLK, BLK), 0) == low_bits(iota((BLK, BLK), 1))).astype(bf16)


def pair_matrix():
    first = low_bits(iota((HALF, BLK), 0))
    place = iota((HALF, BLK), 1)
    return jnp.logical_or(place == first, place == first + 1).astype(bf16)


def mul(left, right):
    return jnp.dot(left, right, preferred_element_type=f32)


def fold(rows, factor):
    half = rows.shape[0] // 2
    total = rows[:half].astype(f32) + rows[half:].astype(f32)
    if factor != 1.0:
        total = total * factor
    return total.astype(bf16)


def fold_chunks(rows, chunk, factor):
    count = rows.shape[0] // chunk
    return jnp.concatenate([fold(rows[i * chunk : (i + 1) * chunk], factor) for i in range(count)], axis=0)


def twice(rows):
    return jnp.concatenate([rows, rows], axis=0)


def cols(head):
    return slice(head * HEAD_DIM, (head + 1) * HEAD_DIM)


DECLARED = 1 << 36


def with_ones(values):
    return jnp.concatenate([values, jnp.ones_like(values)], axis=1)


def attend(units):
    scores = []
    for query, parts in units:
        raws = [
            lax.dot_general(query, keys, (((1,), (1,)), ((), ())), preferred_element_type=f32) for keys, _, _ in parts
        ]
        scores.append([raw if part[2] is None else raw + part[2] for raw, part in zip(raws, parts)])
    tops = []
    for raws in scores:
        tops.append(functools.reduce(jnp.maximum, [jnp.max(raw, axis=1, keepdims=True) for raw in raws]))
    found = []
    for (_, parts), raws, top in zip(units, scores, tops):
        total = None
        for (_, values, _), raw in zip(parts, raws):
            weights = jnp.exp2((raw - top) * EXP_SCALE).astype(bf16)
            one = mul(weights, with_ones(values))
            total = one if total is None else total + one
        found.append((jnp.broadcast_to(top * EXP_SCALE, (top.shape[0], HEAD_DIM)), total))
    return found


def share_of(ref, share, shares):
    width = ref.shape[1] // shares
    first = share * width
    if not isinstance(share, int):
        first = pl.multiple_of(first, HEAD_DIM)
    return ref.at[:, pl.ds(first, width)]


def run_shares(body, name, shares, scalars, ins, outs, work=1 << 10, unrolled=False):
    moved_in = [i for i, (kind, _) in enumerate(ins) if kind in ("cols", "got")]
    moved_out = [i for i, (kind, _) in enumerate(outs) if kind == "cols"]
    as_list = lambda pair: list(pair[1]) if pair[0] == "pieces" else [pair[1]]
    buffer_shape = {
        "cols": lambda value: (shares, value.shape[0], value.shape[1] // shares),
        "got": lambda value: (shares, value.shape[0], value.shape[1] // shares),
        "kept": lambda value: None,
        "pieces": lambda values: (shares, len(values) // shares, *values[0].shape),
    }

    def kernel(*refs):
        refs = list(refs)
        take = lambda count: [refs.pop(0) for _ in range(count)]
        scalar_refs = take(len(scalars))
        in_refs = [take(len(as_list(pair))) for pair in ins]
        out_refs = [take(len(as_list(pair))) for pair in outs]
        in_bufs = [in_refs[i][0] if ins[i][0] == "kept" else refs.pop(0) for i in range(len(ins))]
        out_bufs = [out_refs[i][0] if outs[i][0] == "kept" else refs.pop(0) for i in range(len(outs))]
        in_sems, out_sems, piece_sems = take(3)

        def bring(i, share):
            return pltpu.make_async_copy(share_of(in_refs[i][0], share, shares), in_bufs[i].at[share], in_sems.at[i, share])

        def put(i, share):
            return pltpu.make_async_copy(out_bufs[i].at[share], share_of(out_refs[i][0], share, shares), out_sems.at[i, share])

        def spot_of(buffer, n):
            entry = n ^ scalar_refs[0][1]
            return buffer.at[lax.div(entry, buffer.shape[1]), lax.rem(entry, buffer.shape[1])]

        pieces_in, pieces_out = [], []
        for i, (kind, _) in enumerate(ins):
            if kind == "pieces":
                pieces_in += [(ref, spot_of(in_bufs[i], n), n) for n, ref in enumerate(in_refs[i])]
        for i, (kind, _) in enumerate(outs):
            if kind == "pieces":
                pieces_out += [(spot_of(out_bufs[i], n), ref, n) for n, ref in enumerate(out_refs[i])]
        pieces_in = [pltpu.make_async_copy(source, target, piece_sems.at[n]) for source, target, n in pieces_in]
        pieces_out = [pltpu.make_async_copy(source, target, piece_sems.at[n]) for source, target, n in pieces_out]

        for share in range(shares):
            for i in moved_in:
                bring(i, share).start()
            if share == 0:
                for copy in pieces_in:
                    copy.start()
        for copy in pieces_in:
            copy.wait()

        def views(operands, buffers, share):
            result = []
            for (kind, value), buffer in zip(operands, buffers):
                count = value.shape[0] // shares if kind == "kept" else None
                result.append(buffer.at[share] if count is None else buffer.at[pl.ds(share * count, count)])
            return result

        def step(share, carry):
            for i in moved_in:
                bring(i, share).wait()
            body(scalar_refs, views(ins, in_bufs, share), views(outs, out_bufs, share))
            for i in moved_out:
                put(i, share).start()
            return carry

        if unrolled:
            for share in range(shares):
                step(share, 0)
        else:
            lax.fori_loop(0, shares, step, 0)
        for copy in pieces_out:
            copy.start()
        for share in range(shares):
            for i in moved_out:
                put(i, share).wait()
        for copy in pieces_out:
            copy.wait()

    spaces = {"cols": pltpu.HBM, "got": pl.ANY, "pieces": pl.ANY, "kept": pltpu.VMEM}
    values, in_specs, out_specs, out_shapes, buffers = [], [], [], [], []
    for kind, value in ins:
        for one in as_list((kind, value)):
            values.append(pltpu.with_memory_space_constraint(one, pltpu.HBM) if kind == "cols" else one)
            in_specs.append(pl.BlockSpec(memory_space=spaces[kind]))
    for kind, shape in outs:
        for one in as_list((kind, shape)):
            out_shapes.append(pltpu.HBM(one.shape, one.dtype) if kind == "cols" else one)
            out_specs.append(pl.BlockSpec(memory_space=pltpu.HBM if kind == "cols" else pltpu.VMEM))
    for kind, value in list(ins) + list(outs):
        if kind != "kept":
            buffers.append(pltpu.VMEM(buffer_shape[kind](value), as_list((kind, value))[0].dtype))
    count = max(len(as_list(pair)) for pair in list(ins) + list(outs))
    semaphores = [(len(ins), shares), (len(outs), shares), (count,)]
    return pl.pallas_call(
        kernel,
        in_specs=[pl.BlockSpec(memory_space=pltpu.SMEM)] * len(scalars) + in_specs,
        out_specs=out_specs,
        out_shape=out_shapes,
        scratch_shapes=buffers + [pltpu.SemaphoreType.DMA(shape) for shape in semaphores],
        compiler_params=pltpu.CompilerParams(vmem_limit_bytes=VMEM_GRANT),
        cost_estimate=pl.CostEstimate(flops=work, bytes_accessed=1 << 10, transcendentals=0),
        name=name,
    )(*scalars, *values)


def array(rows, width, dtype):
    return jax.ShapeDtypeStruct((rows, width), dtype)


def swap_body(_, ins, outs):
    pair = pair_matrix()
    count, _, part = outs[0].shape
    for place, (ref, factor) in enumerate(zip(ins, (0.5, 0.5, 1.0))):
        for i in range(2):
            level1 = mul(pair, ref[i * BLK : (i + 1) * BLK, :])
            if factor != 1.0:
                level1 = level1 * factor
            level2 = fold(level1.astype(bf16), factor)
            first = place * HALF + i * HALF // 2
            for n in range(count):
                outs[0][n, first : first + HALF // 2, :] = level2[:, n * part : (n + 1) * part]


def swap_rows(place, query_vecs, key_vecs, value_vecs, groups):
    width = query_vecs.shape[1]
    ins = [("cols", a) for a in (query_vecs, key_vecs, value_vecs)]
    outs = [("pieces", [array(3 * HALF, width // groups, bf16)] * groups)]
    return run_shares(swap_body, "swap_rows", groups // 2, [place], ins, outs, unrolled=True)


def near_rows(place, key_vecs, value_vecs):
    def kernel(place_ref, k_ref, v_ref, near_ref, sems):
        rows = pl.ds(pl.multiple_of(place_ref[0] * BLK, BLK), BLK)
        copies = [
            pltpu.make_async_copy(ref.at[rows, :], near_ref.at[pl.ds(n * BLK, BLK), :], sems.at[n])
            for n, ref in enumerate((k_ref, v_ref))
        ]
        for copy in copies:
            copy.start()
        for copy in copies:
            copy.wait()

    hbm = pl.BlockSpec(memory_space=pltpu.HBM)
    width = key_vecs.shape[1]
    return pl.pallas_call(
        kernel,
        in_specs=[pl.BlockSpec(memory_space=pltpu.SMEM), hbm, hbm],
        out_specs=hbm,
        out_shape=pltpu.HBM((2 * BLK, width), bf16),
        scratch_shapes=[pltpu.SemaphoreType.DMA((2,))],
        compiler_params=pltpu.CompilerParams(vmem_limit_bytes=VMEM_GRANT),
        cost_estimate=pl.CostEstimate(flops=1 << 10, bytes_accessed=1 << 10, transcendentals=0),
        name="near_rows",
    )(place, *[pltpu.with_memory_space_constraint(value, pltpu.HBM) for value in (key_vecs, value_vecs)])


def rows_body(scalars, ins, outs):
    q_ref, k_ref, v_ref = ins
    q0_ref, q1_ref, far_ref, chip_ref = outs
    reorder = reorder_matrix()
    pair = pair_matrix()
    for i in range(2):
        rows = slice(i * BLK, (i + 1) * BLK)
        q0 = mul(reorder, q_ref[rows, :]).astype(bf16)
        q0_ref[rows, :] = q0
        q1_ref[i * HALF : (i + 1) * HALF, :] = fold(q0, 0.5)
    odd = scalars[0][0]
    outer = pl.ds(pl.multiple_of(odd * BLK, BLK), BLK)
    inner = pl.ds(pl.multiple_of((1 - odd) * BLK, BLK), BLK)
    chip_ref[0:BLK, :] = k_ref[inner, :]
    chip_ref[BLK : 2 * BLK, :] = v_ref[inner, :]
    for ref, first, far in ((far_ref, 0, inner), (chip_ref, 2 * BLK, outer)):
        ref[first : first + HALF, :] = (mul(pair, k_ref[far, :]) * 0.5).astype(bf16)
        ref[first + HALF : first + BLK, :] = mul(pair, v_ref[far, :]).astype(bf16)


def rows_to_send(place, query_vecs, key_vecs, value_vecs, groups):
    rows, width = query_vecs.shape
    ins = [("cols", a) for a in (query_vecs, key_vecs, value_vecs)]
    outs = [("cols", array(n, width, bf16)) for n in (rows, rows // 2, BLK, 3 * BLK)]
    return run_shares(rows_body, "rows_to_send", groups, [place], ins, outs)


def own_body(_, ins, outs):
    q_ref, k_ref, v_ref = ins
    sum_ref, top_ref, total_ref = outs
    heads = q_ref.shape[1] // HEAD_DIM
    for i in range(2):
        rows = slice(i * BLK, (i + 1) * BLK)
        units = [(q_ref[rows, cols(head)], [(k_ref[:, cols(head)], v_ref[:, cols(head)], None)]) for head in range(heads)]
        for head, (top, sums) in enumerate(attend(units)):
            spot = (head // 2, rows, cols(head % 2))
            sum_ref[spot] = sums[:, :HEAD_DIM]
            top_ref[spot] = top
            total_ref[spot] = sums[:, HEAD_DIM:]


def running_sums(rows, width, groups):
    return [("kept", jax.ShapeDtypeStruct((groups, rows, width // groups), f32))] * 3


def own_level(q0, key_vecs, value_vecs, groups):
    ins = [("cols", a) for a in (q0, key_vecs, value_vecs)]
    return run_shares(own_body, "own_level", groups // 2, [], ins, running_sums(*q0.shape, groups), DECLARED)


def halo_body(place_ref, *refs):
    count = len(refs) - 4
    piece_refs, (got_ref, right_ref, left_ref, sems) = refs[:count], refs[count:]
    copies = [pltpu.make_async_copy(ref, got_ref.at[n ^ place_ref[1]], sems.at[n]) for n, ref in enumerate(piece_refs)]
    for copy in copies:
        copy.start()
    for copy in copies:
        copy.wait()
    pair = count // 2
    for which, factor in ((1, 0.5), (2, 1.0)):
        rows = slice(which * HALF, (which + 1) * HALF)
        near = (which - 1) * BLK
        far = 2 * BLK + (which - 1) * HALF
        for j in range(count):
            level2 = got_ref[j, rows, :]
            level3 = fold_chunks(level2, HALF // 2, factor)
            near_ref, far_ref = (left_ref, right_ref) if j < pair else (right_ref, left_ref)
            spot = j % pair
            near_ref[near + spot * HALF : near + (spot + 1) * HALF, :] = level2
            far_ref[far + spot * HALF // 2 : far + (spot + 1) * HALF // 2, :] = level3


def coarse_halos(place, pieces):
    rows, width = pieces[0].shape
    vmem = pl.BlockSpec(memory_space=pltpu.VMEM)
    shape = jax.ShapeDtypeStruct((3 * BLK, width), bf16)
    return pl.pallas_call(
        halo_body,
        in_specs=[pl.BlockSpec(memory_space=pltpu.SMEM)] + [pl.BlockSpec(memory_space=pl.ANY)] * len(pieces),
        out_specs=[vmem] * 3,
        out_shape=[jax.ShapeDtypeStruct((len(pieces), rows, width), bf16), shape, shape],
        scratch_shapes=[pltpu.SemaphoreType.DMA((len(pieces),))],
        compiler_params=pltpu.CompilerParams(vmem_limit_bytes=16 << 20),
        cost_estimate=pl.CostEstimate(flops=1 << 20, bytes_accessed=24 * pieces[0].size, transcendentals=0),
        name="coarse_halos",
    )(place, *pieces)


def coarse_body(place_ref, bias_ref, got_ref, prev_ref, next_ref, *refs):
    *out_refs, back_ref, sems = refs
    count = got_ref.shape[0]
    heads = got_ref.shape[2] // HEAD_DIM
    bias_prev = bias_ref[0]
    bias_next = bias_ref[1]
    lane = iota((HALF, HEAD_DIM), 1)

    units = []
    for head in range(heads):
        here = cols(head)

        def own(which, j):
            return got_ref[j, which * HALF : (which + 1) * HALF, here]

        def near(ref, which, spot):
            first = (which - 1) * BLK + spot * HALF
            return ref[first : first + HALF, here]

        def both(ref, which):
            return ref[(which - 1) * BLK : which * BLK, here]

        def far(ref, which):
            first = 2 * BLK + (which - 1) * HALF
            return ref[first : first + HALF, here]

        def near3(ref, which):
            return fold_chunks(both(ref, which), HALF // 2, 0.5 if which == 1 else 1.0)

        def joined(*rows):
            return jnp.concatenate(rows, axis=0)

        def part(pick, bias):
            return (pick(1), pick(2), bias)

        units += [
            (own(0, 0), [part(lambda w: joined(own(w, 2), own(w, 3)), None), part(lambda w: near(prev_ref, w, 0), bias_prev)]),
            (own(0, 1), [part(lambda w: both(prev_ref, w), bias_prev), part(lambda w: own(w, 3), None)]),
            (own(0, 2), [part(lambda w: both(next_ref, w), bias_next), part(lambda w: own(w, 0), None)]),
            (own(0, 3), [part(lambda w: joined(own(w, 0), own(w, 1)), None), part(lambda w: near(next_ref, w, 1), bias_next)]),
        ]
        for j, (ref, bias, other, other_bias) in enumerate(
            ((next_ref, bias_next, prev_ref, bias_prev), (prev_ref, bias_prev, next_ref, bias_next))
        ):
            query = joined(*[fold_chunks(own(0, 2 * j + n), HALF // 2, 0.5) for n in range(2)])
            units.append(
                (
                    query,
                    [part(lambda w: joined(near3(ref, w), far(ref, w)), bias), part(lambda w: far(other, w), other_bias)],
                )
            )
    found = attend(units)
    each = len(units) // heads

    def joined(*rows):
        return jnp.concatenate(rows, axis=0)

    for head in range(heads):
        here = cols(head)
        for j in range(count):
            top2, sum2 = found[head * each + j]
            top3, sum3 = found[head * each + count + j // 2]

            def spread(rows):
                first = (j % 2) * 2 * SUB
                one = rows[first : first + SUB]
                other = rows[first + SUB : first + 2 * SUB]
                return joined(one, one, other, other)

            top3 = spread(top3)
            sum3 = spread(sum3)
            top = jnp.maximum(top2, top3)
            scale2 = jnp.exp2(top2 - top)
            scale3 = jnp.exp2(top3 - top)
            values = sum2[:, :HEAD_DIM] * scale2 + sum3[:, :HEAD_DIM] * scale3
            total = sum2[:, HEAD_DIM:] * (4.0 * scale2) + sum3[:, HEAD_DIM:] * (8.0 * scale3)
            back_ref[j, 0:HALF, here] = (values / total).astype(bf16)
            level = top + jnp.log2(total)
            high = level.astype(bf16).astype(f32)
            middle = (level - high).astype(bf16).astype(f32)
            terms = jnp.where(lane == 0, high, jnp.where(lane == 1, middle, level - high - middle))
            back_ref[j, HALF : HALF + 16, here] = terms.T[0:16, :].astype(bf16)
    copies = [
        pltpu.make_async_copy(back_ref.at[n ^ place_ref[1]], ref, sems.at[n]) for n, ref in enumerate(out_refs)
    ]
    for copy in copies:
        copy.start()
    for copy in copies:
        copy.wait()


def coarse_levels(place, bias, got, from_prev, from_next):
    count, _, width = got.shape
    vmem = pl.BlockSpec(memory_space=pltpu.VMEM)
    smem = pl.BlockSpec(memory_space=pltpu.SMEM)
    rows = HALF + 16
    return pl.pallas_call(
        coarse_body,
        in_specs=[smem, smem, vmem, vmem, vmem],
        out_specs=[vmem] * count,
        out_shape=[array(rows, width, bf16)] * count,
        scratch_shapes=[pltpu.VMEM((count, rows, width), bf16), pltpu.SemaphoreType.DMA((count,))],
        compiler_params=pltpu.CompilerParams(vmem_limit_bytes=16 << 20),
        cost_estimate=pl.CostEstimate(flops=DECLARED, bytes_accessed=8 * got.size, transcendentals=1 << 20),
        name="coarse_levels",
    )(place, bias, got, from_prev, from_next)


def side_body(side, with_near, with_far, scalars, ins, outs):
    q0_ref, q1_ref, sum_ref, top_ref, total_ref, side_ref = ins
    heads = q1_ref.shape[1] // HEAD_DIM
    bias = scalars[1][side]
    blocks = (side, 1 - side)
    fine = [pl.ds(pl.multiple_of(block * BLK, BLK), BLK) for block in blocks]
    middle = [pl.ds(pl.multiple_of(block * HALF, HALF), HALF) for block in blocks]
    if with_near:
        pair = pair_matrix()
        near_keys = (mul(pair, side_ref[0:BLK, :]) * 0.5).astype(bf16)
        near_values = mul(pair, side_ref[BLK : 2 * BLK, :]).astype(bf16)
    start = 2 * BLK if with_near else 0
    far_keys, far_values = (slice(start + n * HALF, start + (n + 1) * HALF) for n in range(2))
    units, names = [], []
    for head in range(heads):
        here = cols(head)
        far = (side_ref[far_keys, here], side_ref[far_values, here]) if with_far else None
        near = (near_keys[:, here], near_values[:, here]) if with_near else None
        whole = [part for part in (near, far) if part is not None]
        whole = [jnp.concatenate([part[n] for part in whole], axis=0) if len(whole) > 1 else whole[0][n] for n in range(2)]
        if with_near:
            units.append((q0_ref[fine[0], here], [(side_ref[0:BLK, here], side_ref[BLK : 2 * BLK, here], None)]))
            names.append((head, 0, 0))
        if with_far:
            units.append((q1_ref[middle[0], here], [(*far, None)]))
            names.append((head, 0, 1))
        units.append((q1_ref[middle[1], here], [(*whole, None)]))
        names.append((head, 1, 1))
    found = {name: (top + bias, sums) for name, (top, sums) in zip(names, attend(units))}
    for n in range(2):
        for head in range(heads):
            spot = (head // 2, fine[n], cols(head % 2))
            parts = [(top_ref[spot], sum_ref[spot], total_ref[spot])]
            if (head, n, 0) in found:
                top, sums = found[head, n, 0]
                parts.append((top, sums[:, :HEAD_DIM], sums[:, HEAD_DIM:]))
            if (head, n, 1) in found:
                top, sums = found[head, n, 1]
                parts.append((twice(top), twice(sums[:, :HEAD_DIM]), twice(2.0 * sums[:, HEAD_DIM:])))
            most = functools.reduce(jnp.maximum, [part[0] for part in parts])
            scales = [jnp.exp2(part[0] - most) for part in parts]
            outs[0][spot] = sum(part[1] * scale for part, scale in zip(parts, scales))
            outs[1][spot] = most
            outs[2][spot] = sum(part[2] * scale for part, scale in zip(parts, scales))


def chip_body(scalars, ins, outs):
    side_body(1 - scalars[0][0], True, True, scalars, ins, outs)


def near_body(scalars, ins, outs):
    side_body(scalars[0][0], True, False, scalars, ins, outs)


def far_body(scalars, ins, outs):
    side_body(scalars[0][0], False, True, scalars, [None] + ins, outs)


def side_level(body, name, place, bias, queries, running, rows):
    groups, count, part = running[0].shape
    ins = [("cols", query) for query in queries] + [("kept", one) for one in running] + [("got", rows)]
    return run_shares(body, name, groups // 2, [place, bias], ins, running_sums(count, groups * part, groups))


def finish_body(place_ref, sum_ref, top_ref, total_ref, *refs):
    groups = sum_ref.shape[0]
    back_refs, (out_ref, done_ref, sems) = refs[:groups], refs[groups:]
    part = sum_ref.shape[2]
    restore = restore_matrix()
    copies = []
    for n, back_ref in enumerate(back_refs):
        entry = n ^ place_ref[1]
        levels = []
        for head in range(part // HEAD_DIM):
            terms = back_ref[HALF : HALF + 16, cols(head)].astype(f32)
            terms = jnp.sum(jnp.where(iota(terms.shape, 0) < 3, terms, 0.0), axis=0, keepdims=True)
            levels.append(jnp.broadcast_to(terms, (HEAD_DIM, HEAD_DIM)).T)
        for i in range(2):
            rows = slice(i * BLK, (i + 1) * BLK)
            spot = slice(i * HALF // 2, (i + 1) * HALF // 2)
            results = []
            for head, level in enumerate(levels):
                here = (entry, rows, cols(head))
                top = top_ref[here]
                level = twice(twice(level[spot, :]))
                lead = top - level
                smaller = jnp.exp2(-jnp.abs(lead))
                scale = jnp.where(lead >= 0.0, 1.0, smaller)
                coarse = jnp.where(lead >= 0.0, smaller, 1.0)
                number = twice(twice(back_ref[spot, cols(head)].astype(f32))) * coarse
                number = number + sum_ref[here] * scale
                total = total_ref[here] * scale + coarse
                guess = pl.reciprocal(total, approx=True)
                results.append((number * (guess * (2.0 - total * guess))).astype(bf16))
            done_ref[n, rows, :] = mul(restore, jnp.concatenate(results, axis=1)).astype(bf16)
        columns = pl.ds(pl.multiple_of(entry * part, HEAD_DIM), part)
        copies.append(pltpu.make_async_copy(done_ref.at[n], out_ref.at[:, columns], sems.at[n]))
        copies[-1].start()
    for copy in copies:
        copy.wait()


def finish(place, running, back):
    groups, rows, part = running[0].shape
    vmem = pl.BlockSpec(memory_space=pltpu.VMEM)
    return pl.pallas_call(
        finish_body,
        in_specs=[pl.BlockSpec(memory_space=pltpu.SMEM)] + [vmem] * (3 + groups),
        out_specs=pl.BlockSpec(memory_space=pltpu.HBM),
        out_shape=pltpu.HBM((rows, groups * part), bf16),
        scratch_shapes=[pltpu.VMEM((groups, rows, part), bf16), pltpu.SemaphoreType.DMA((groups,))],
        compiler_params=pltpu.CompilerParams(vmem_limit_bytes=VMEM_GRANT),
        cost_estimate=pl.CostEstimate(flops=1 << 10, bytes_accessed=1 << 10, transcendentals=0),
        name="finish",
    )(place, *running, *back)


def shift(value, axis, steps):
    count = lax.axis_size(axis)
    first, last = (max(0, -steps), min(count, count - steps))
    return lax.ppermute(value, axis, [(source, source + steps) for source in range(first, last)])


def trade(value, axis, pairs):
    return lax.ppermute(value, axis, pairs + [(target, source) for source, target in pairs])


def edge_bias(axis):
    place = lax.axis_index(axis)
    last = lax.axis_size(axis) - 1
    at_edge = jnp.stack([place == 0, place == last])
    return jnp.where(at_edge, very_negative, 0.0).astype(f32)


def local(query_vecs, key_vecs, value_vecs):
    groups = lax.axis_size("grp")
    assert query_vecs.shape == (2 * BLK, HEADS * HEAD_DIM) and groups == 4
    everyone = ("seq", "grp")
    count = lax.axis_size(everyone)
    spot = lax.axis_index("grp")
    odd = jnp.bitwise_and(spot, 1)
    place = jnp.stack([odd, spot]).astype(jnp.int32)
    bias = edge_bias(everyone)

    def exchange(pieces, places):
        for n in places:
            flips = [(source, source ^ n) for source in range(groups)]
            pieces[n] = lax.ppermute(pieces[n], "grp", flips)
        return pieces

    off = range(2, groups)
    pieces = list(swap_rows(place, query_vecs, key_vecs, value_vecs, groups))
    query_rows, pieces = lax.optimization_barrier((query_vecs, pieces))
    pieces = exchange(pieces, off)
    key_rows, pieces[0] = lax.optimization_barrier((key_vecs, pieces[0]))
    near = near_rows(place, key_rows, value_vecs)
    query_rows, near = lax.optimization_barrier((query_rows, near))
    q0, q1, far, chip = rows_to_send(place, query_rows, key_vecs, value_vecs, groups)
    pieces[1], far = lax.optimization_barrier((pieces[1], far))
    pieces = exchange(pieces, [1])
    off_chip = [(device, device + 1) for device in range(1, count - 1, 2)]
    near = trade(near, everyone, off_chip)
    pieces, chip = lax.optimization_barrier((pieces, chip))
    got, coarse_right, coarse_left = coarse_halos(place, pieces)
    coarse_right, coarse_left, chip, q0, far = lax.optimization_barrier((coarse_right, coarse_left, chip, q0, far))
    coarse_prev = shift(coarse_right, "seq", 1)
    coarse_next = shift(coarse_left, "seq", -1)
    chip = trade(chip, everyone, [(device, device + 1) for device in range(0, count - 1, 2)])
    far = trade(far, everyone, off_chip)
    running = own_level(q0, key_vecs, value_vecs, groups)
    running = side_level(chip_body, "chip_level", place, bias, (q0, q1), running, chip)
    running = side_level(near_body, "near_level", place, bias, (q0, q1), running, near)
    got, running = lax.optimization_barrier((got, running))
    back = coarse_levels(place, edge_bias("seq"), got, coarse_prev, coarse_next)
    back, running = lax.optimization_barrier((back, running))
    back = exchange(list(back), [*off, 1])
    running = side_level(far_body, "far_level", place, bias, (q1,), running, far)
    return finish(place, running, back)


def solution(mesh):
    return jax.shard_map(
        local,
        mesh=mesh,
        in_specs=(P(("seq", "grp"), None), P(("seq", "grp"), None), P(("seq", "grp"), None)),
        out_specs=P(("seq", "grp"), None),
        check_vma=False,
    )
```

```python
import functools
import math

import jax
import jax.numpy as jnp
from jax import lax
from jax.experimental import pallas as pl
from jax.experimental.pallas import tpu as pltpu
from jax.sharding import PartitionSpec as P

HEADS = 8
HEAD_DIM = 128
BLK = 256
HALF = BLK // 2
SUB = BLK // 8
LEV = 4
EXP_SCALE = math.log2(math.e) / math.sqrt(HEAD_DIM)

VMEM_GRANT = 24 << 20

very_negative = -1e30
f32 = jnp.float32
bf16 = jnp.bfloat16


def iota(shape, dim):
    return lax.broadcasted_iota(jnp.int32, shape, dim)


def bit(value, place):
    return jnp.bitwise_and(lax.shift_right_logical(value, place), 1)


def low_bits(value):
    step = SUB.bit_length() - 1
    deep = jnp.bitwise_and(value, SUB - 1)
    return 8 * deep + 4 * bit(value, step) + 2 * bit(value, step + 1) + bit(value, step + 2)


def reorder_matrix():
    return (iota((BLK, BLK), 1) == low_bits(iota((BLK, BLK), 0))).astype(bf16)


def restore_matrix():
    return (iota((BLK, BLK), 0) == low_bits(iota((BLK, BLK), 1))).astype(bf16)


def pair_matrix():
    first = low_bits(iota((HALF, BLK), 0))
    place = iota((HALF, BLK), 1)
    return jnp.logical_or(place == first, place == first + 1).astype(bf16)


def mul(left, right):
    return jnp.dot(left, right, preferred_element_type=f32)


def fold(rows, factor):
    half = rows.shape[0] // 2
    total = rows[:half].astype(f32) + rows[half:].astype(f32)
    if factor != 1.0:
        total = total * factor
    return total.astype(bf16)


def fold_chunks(rows, chunk, factor):
    count = rows.shape[0] // chunk
    return jnp.concatenate([fold(rows[i * chunk : (i + 1) * chunk], factor) for i in range(count)], axis=0)


def twice(rows):
    return jnp.concatenate([rows, rows], axis=0)


def cols(head):
    return slice(head * HEAD_DIM, (head + 1) * HEAD_DIM)


DECLARED = 1 << 36


def with_ones(values):
    return jnp.concatenate([values, jnp.ones_like(values)], axis=1)


def attend(units):
    scores = []
    for query, parts in units:
        raws = [
            lax.dot_general(query, keys, (((1,), (1,)), ((), ())), preferred_element_type=f32) for keys, _, _ in parts
        ]
        scores.append([raw if part[2] is None else raw + part[2] for raw, part in zip(raws, parts)])
    tops = []
    for raws in scores:
        tops.append(functools.reduce(jnp.maximum, [jnp.max(raw, axis=1, keepdims=True) for raw in raws]))
    found = []
    for (_, parts), raws, top in zip(units, scores, tops):
        total = None
        for (_, values, _), raw in zip(parts, raws):
            weights = jnp.exp2((raw - top) * EXP_SCALE).astype(bf16)
            one = mul(weights, with_ones(values))
            total = one if total is None else total + one
        found.append((jnp.broadcast_to(top * EXP_SCALE, (top.shape[0], HEAD_DIM)), total))
    return found


def share_of(ref, share, shares):
    width = ref.shape[1] // shares
    first = share * width
    if not isinstance(share, int):
        first = pl.multiple_of(first, HEAD_DIM)
    return ref.at[:, pl.ds(first, width)]


def run_shares(body, name, shares, scalars, ins, outs, work=1 << 10, unrolled=False):
    moved_in = [i for i, (kind, _) in enumerate(ins) if kind in ("cols", "got")]
    moved_out = [i for i, (kind, _) in enumerate(outs) if kind == "cols"]
    as_list = lambda pair: list(pair[1]) if pair[0] == "pieces" else [pair[1]]
    buffer_shape = {
        "cols": lambda value: (shares, value.shape[0], value.shape[1] // shares),
        "got": lambda value: (shares, value.shape[0], value.shape[1] // shares),
        "kept": lambda value: None,
        "pieces": lambda values: (shares, len(values) // shares, *values[0].shape),
    }

    def kernel(*refs):
        refs = list(refs)
        take = lambda count: [refs.pop(0) for _ in range(count)]
        scalar_refs = take(len(scalars))
        in_refs = [take(len(as_list(pair))) for pair in ins]
        out_refs = [take(len(as_list(pair))) for pair in outs]
        in_bufs = [in_refs[i][0] if ins[i][0] == "kept" else refs.pop(0) for i in range(len(ins))]
        out_bufs = [out_refs[i][0] if outs[i][0] == "kept" else refs.pop(0) for i in range(len(outs))]
        in_sems, out_sems, piece_sems = take(3)

        def bring(i, share):
            return pltpu.make_async_copy(share_of(in_refs[i][0], share, shares), in_bufs[i].at[share], in_sems.at[i, share])

        def put(i, share):
            return pltpu.make_async_copy(out_bufs[i].at[share], share_of(out_refs[i][0], share, shares), out_sems.at[i, share])

        def spot_of(buffer, n):
            entry = n ^ scalar_refs[0][1]
            return buffer.at[lax.div(entry, buffer.shape[1]), lax.rem(entry, buffer.shape[1])]

        pieces_in, pieces_out = [], []
        for i, (kind, _) in enumerate(ins):
            if kind == "pieces":
                pieces_in += [(ref, spot_of(in_bufs[i], n), n) for n, ref in enumerate(in_refs[i])]
        for i, (kind, _) in enumerate(outs):
            if kind == "pieces":
                pieces_out += [(spot_of(out_bufs[i], n), ref, n) for n, ref in enumerate(out_refs[i])]
        pieces_in = [pltpu.make_async_copy(source, target, piece_sems.at[n]) for source, target, n in pieces_in]
        pieces_out = [pltpu.make_async_copy(source, target, piece_sems.at[n]) for source, target, n in pieces_out]

        for share in range(shares):
            for i in moved_in:
                bring(i, share).start()
            if share == 0:
                for copy in pieces_in:
                    copy.start()
        for copy in pieces_in:
            copy.wait()

        def views(operands, buffers, share):
            result = []
            for (kind, value), buffer in zip(operands, buffers):
                count = value.shape[0] // shares if kind == "kept" else None
                result.append(buffer.at[share] if count is None else buffer.at[pl.ds(share * count, count)])
            return result

        def step(share, carry):
            for i in moved_in:
                bring(i, share).wait()
            body(scalar_refs, views(ins, in_bufs, share), views(outs, out_bufs, share))
            for i in moved_out:
                put(i, share).start()
            return carry

        if unrolled:
            for share in range(shares):
                step(share, 0)
        else:
            lax.fori_loop(0, shares, step, 0)
        for copy in pieces_out:
            copy.start()
        for share in range(shares):
            for i in moved_out:
                put(i, share).wait()
        for copy in pieces_out:
            copy.wait()

    spaces = {"cols": pltpu.HBM, "got": pl.ANY, "pieces": pl.ANY, "kept": pltpu.VMEM}
    values, in_specs, out_specs, out_shapes, buffers = [], [], [], [], []
    for kind, value in ins:
        for one in as_list((kind, value)):
            values.append(pltpu.with_memory_space_constraint(one, pltpu.HBM) if kind == "cols" else one)
            in_specs.append(pl.BlockSpec(memory_space=spaces[kind]))
    for kind, shape in outs:
        for one in as_list((kind, shape)):
            out_shapes.append(pltpu.HBM(one.shape, one.dtype) if kind == "cols" else one)
            out_specs.append(pl.BlockSpec(memory_space=pltpu.HBM if kind == "cols" else pltpu.VMEM))
    for kind, value in list(ins) + list(outs):
        if kind != "kept":
            buffers.append(pltpu.VMEM(buffer_shape[kind](value), as_list((kind, value))[0].dtype))
    count = max(len(as_list(pair)) for pair in list(ins) + list(outs))
    semaphores = [(len(ins), shares), (len(outs), shares), (count,)]
    return pl.pallas_call(
        kernel,
        in_specs=[pl.BlockSpec(memory_space=pltpu.SMEM)] * len(scalars) + in_specs,
        out_specs=out_specs,
        out_shape=out_shapes,
        scratch_shapes=buffers + [pltpu.SemaphoreType.DMA(shape) for shape in semaphores],
        compiler_params=pltpu.CompilerParams(vmem_limit_bytes=VMEM_GRANT),
        cost_estimate=pl.CostEstimate(flops=work, bytes_accessed=1 << 10, transcendentals=0),
        name=name,
    )(*scalars, *values)


def array(rows, width, dtype):
    return jax.ShapeDtypeStruct((rows, width), dtype)


def swap_body(_, ins, outs):
    pair = pair_matrix()
    count, _, part = outs[0].shape
    for place, (ref, factor) in enumerate(zip(ins, (0.5, 0.5, 1.0))):
        for i in range(2):
            level1 = mul(pair, ref[i * BLK : (i + 1) * BLK, :])
            if factor != 1.0:
                level1 = level1 * factor
            level2 = fold(level1.astype(bf16), factor)
            first = place * HALF + i * HALF // 2
            for n in range(count):
                outs[0][n, first : first + HALF // 2, :] = level2[:, n * part : (n + 1) * part]


def swap_rows(place, query_vecs, key_vecs, value_vecs, groups):
    width = query_vecs.shape[1]
    ins = [("cols", a) for a in (query_vecs, key_vecs, value_vecs)]
    outs = [("pieces", [array(3 * HALF, width // groups, bf16)] * groups)]
    return run_shares(swap_body, "swap_rows", groups // 2, [place], ins, outs, unrolled=True)


def near_rows(place, key_vecs, value_vecs):
    def kernel(place_ref, k_ref, v_ref, out_ref, near_ref, sems):
        rows = pl.ds(pl.multiple_of(place_ref[0] * BLK, BLK), BLK)
        copies = [
            pltpu.make_async_copy(ref.at[rows, :], near_ref.at[pl.ds(n * BLK, BLK), :], sems.at[n])
            for n, ref in enumerate((k_ref, v_ref))
        ]
        for copy in copies:
            copy.start()
        for copy in copies:
            copy.wait()
        leave = pltpu.make_async_copy(near_ref, out_ref, sems.at[0])
        leave.start()
        leave.wait()

    hbm = pl.BlockSpec(memory_space=pltpu.HBM)
    width = key_vecs.shape[1]
    return pl.pallas_call(
        kernel,
        in_specs=[pl.BlockSpec(memory_space=pltpu.SMEM), hbm, hbm],
        out_specs=hbm,
        out_shape=pltpu.HBM((2 * BLK, width), bf16),
        scratch_shapes=[pltpu.VMEM((2 * BLK, width), bf16), pltpu.SemaphoreType.DMA((2,))],
        compiler_params=pltpu.CompilerParams(vmem_limit_bytes=VMEM_GRANT),
        cost_estimate=pl.CostEstimate(flops=1 << 10, bytes_accessed=1 << 10, transcendentals=0),
        name="near_rows",
    )(place, *[pltpu.with_memory_space_constraint(value, pltpu.HBM) for value in (key_vecs, value_vecs)])


def rows_body(scalars, ins, outs):
    q_ref, k_ref, v_ref = ins
    q0_ref, q1_ref, far_ref, chip_ref = outs
    reorder = reorder_matrix()
    pair = pair_matrix()
    for i in range(2):
        rows = slice(i * BLK, (i + 1) * BLK)
        q0 = mul(reorder, q_ref[rows, :]).astype(bf16)
        q0_ref[rows, :] = q0
        q1_ref[i * HALF : (i + 1) * HALF, :] = fold(q0, 0.5)
    odd = scalars[0][0]
    outer = pl.ds(pl.multiple_of(odd * BLK, BLK), BLK)
    inner = pl.ds(pl.multiple_of((1 - odd) * BLK, BLK), BLK)
    chip_ref[0:BLK, :] = k_ref[inner, :]
    chip_ref[BLK : 2 * BLK, :] = v_ref[inner, :]
    for ref, first, far in ((far_ref, 0, inner), (chip_ref, 2 * BLK, outer)):
        ref[first : first + HALF, :] = (mul(pair, k_ref[far, :]) * 0.5).astype(bf16)
        ref[first + HALF : first + BLK, :] = mul(pair, v_ref[far, :]).astype(bf16)


def rows_to_send(place, query_vecs, key_vecs, value_vecs, groups):
    rows, width = query_vecs.shape
    ins = [("cols", a) for a in (query_vecs, key_vecs, value_vecs)]
    outs = [("cols", array(n, width, bf16)) for n in (rows, rows // 2, BLK, 3 * BLK)]
    return run_shares(rows_body, "rows_to_send", groups, [place], ins, outs)


def own_body(_, ins, outs):
    q_ref, k_ref, v_ref = ins
    sum_ref, top_ref, total_ref = outs
    heads = q_ref.shape[1] // HEAD_DIM
    for i in range(2):
        rows = slice(i * BLK, (i + 1) * BLK)
        units = [(q_ref[rows, cols(head)], [(k_ref[:, cols(head)], v_ref[:, cols(head)], None)]) for head in range(heads)]
        for head, (top, sums) in enumerate(attend(units)):
            spot = (head // 2, rows, cols(head % 2))
            sum_ref[spot] = sums[:, :HEAD_DIM]
            top_ref[spot] = top
            total_ref[spot] = sums[:, HEAD_DIM:]


def running_sums(rows, width, groups):
    return [("kept", jax.ShapeDtypeStruct((groups, rows, width // groups), f32))] * 3


def own_level(q0, key_vecs, value_vecs, groups):
    ins = [("cols", a) for a in (q0, key_vecs, value_vecs)]
    return run_shares(own_body, "own_level", groups // 2, [], ins, running_sums(*q0.shape, groups), DECLARED)


def halo_body(place_ref, *refs):
    count = len(refs) - 4
    piece_refs, (got_ref, right_ref, left_ref, sems) = refs[:count], refs[count:]
    copies = [pltpu.make_async_copy(ref, got_ref.at[n ^ place_ref[1]], sems.at[n]) for n, ref in enumerate(piece_refs)]
    for copy in copies:
        copy.start()
    for copy in copies:
        copy.wait()
    pair = count // 2
    for which, factor in ((1, 0.5), (2, 1.0)):
        rows = slice(which * HALF, (which + 1) * HALF)
        near = (which - 1) * BLK
        far = 2 * BLK + (which - 1) * HALF
        for j in range(count):
            level2 = got_ref[j, rows, :]
            level3 = fold_chunks(level2, HALF // 2, factor)
            near_ref, far_ref = (left_ref, right_ref) if j < pair else (right_ref, left_ref)
            spot = j % pair
            near_ref[near + spot * HALF : near + (spot + 1) * HALF, :] = level2
            far_ref[far + spot * HALF // 2 : far + (spot + 1) * HALF // 2, :] = level3


def coarse_halos(place, pieces):
    rows, width = pieces[0].shape
    vmem = pl.BlockSpec(memory_space=pltpu.VMEM)
    shape = jax.ShapeDtypeStruct((3 * BLK, width), bf16)
    return pl.pallas_call(
        halo_body,
        in_specs=[pl.BlockSpec(memory_space=pltpu.SMEM)] + [pl.BlockSpec(memory_space=pl.ANY)] * len(pieces),
        out_specs=[vmem] * 3,
        out_shape=[jax.ShapeDtypeStruct((len(pieces), rows, width), bf16), shape, shape],
        scratch_shapes=[pltpu.SemaphoreType.DMA((len(pieces),))],
        compiler_params=pltpu.CompilerParams(vmem_limit_bytes=16 << 20),
        cost_estimate=pl.CostEstimate(flops=1 << 20, bytes_accessed=24 * pieces[0].size, transcendentals=0),
        name="coarse_halos",
    )(place, *pieces)


def coarse_body(place_ref, bias_ref, got_ref, prev_ref, next_ref, *refs):
    *out_refs, back_ref, sems = refs
    count = got_ref.shape[0]
    heads = got_ref.shape[2] // HEAD_DIM
    bias_prev = bias_ref[0]
    bias_next = bias_ref[1]
    lane = iota((HALF, HEAD_DIM), 1)

    units = []
    for head in range(heads):
        here = cols(head)

        def own(which, j):
            return got_ref[j, which * HALF : (which + 1) * HALF, here]

        def near(ref, which, spot):
            first = (which - 1) * BLK + spot * HALF
            return ref[first : first + HALF, here]

        def both(ref, which):
            return ref[(which - 1) * BLK : which * BLK, here]

        def far(ref, which):
            first = 2 * BLK + (which - 1) * HALF
            return ref[first : first + HALF, here]

        def near3(ref, which):
            return fold_chunks(both(ref, which), HALF // 2, 0.5 if which == 1 else 1.0)

        def joined(*rows):
            return jnp.concatenate(rows, axis=0)

        def part(pick, bias):
            return (pick(1), pick(2), bias)

        units += [
            (own(0, 0), [part(lambda w: joined(own(w, 2), own(w, 3)), None), part(lambda w: near(prev_ref, w, 0), bias_prev)]),
            (own(0, 1), [part(lambda w: both(prev_ref, w), bias_prev), part(lambda w: own(w, 3), None)]),
            (own(0, 2), [part(lambda w: both(next_ref, w), bias_next), part(lambda w: own(w, 0), None)]),
            (own(0, 3), [part(lambda w: joined(own(w, 0), own(w, 1)), None), part(lambda w: near(next_ref, w, 1), bias_next)]),
        ]
        for j, (ref, bias, other, other_bias) in enumerate(
            ((next_ref, bias_next, prev_ref, bias_prev), (prev_ref, bias_prev, next_ref, bias_next))
        ):
            query = joined(*[fold_chunks(own(0, 2 * j + n), HALF // 2, 0.5) for n in range(2)])
            units.append(
                (
                    query,
                    [part(lambda w: joined(near3(ref, w), far(ref, w)), bias), part(lambda w: far(other, w), other_bias)],
                )
            )
    found = attend(units)
    each = len(units) // heads

    def joined(*rows):
        return jnp.concatenate(rows, axis=0)

    for head in range(heads):
        here = cols(head)
        for j in range(count):
            top2, sum2 = found[head * each + j]
            top3, sum3 = found[head * each + count + j // 2]

            def spread(rows):
                first = (j % 2) * 2 * SUB
                one = rows[first : first + SUB]
                other = rows[first + SUB : first + 2 * SUB]
                return joined(one, one, other, other)

            top3 = spread(top3)
            sum3 = spread(sum3)
            top = jnp.maximum(top2, top3)
            scale2 = jnp.exp2(top2 - top)
            scale3 = jnp.exp2(top3 - top)
            values = sum2[:, :HEAD_DIM] * scale2 + sum3[:, :HEAD_DIM] * scale3
            total = sum2[:, HEAD_DIM:] * (4.0 * scale2) + sum3[:, HEAD_DIM:] * (8.0 * scale3)
            back_ref[j, 0:HALF, here] = (values / total).astype(bf16)
            level = top + jnp.log2(total)
            high = level.astype(bf16).astype(f32)
            middle = (level - high).astype(bf16).astype(f32)
            terms = jnp.where(lane == 0, high, jnp.where(lane == 1, middle, level - high - middle))
            back_ref[j, HALF : HALF + 16, here] = terms.T[0:16, :].astype(bf16)
    copies = [
        pltpu.make_async_copy(back_ref.at[n ^ place_ref[1]], ref, sems.at[n]) for n, ref in enumerate(out_refs)
    ]
    for copy in copies:
        copy.start()
    for copy in copies:
        copy.wait()


def coarse_levels(place, bias, got, from_prev, from_next):
    count, _, width = got.shape
    vmem = pl.BlockSpec(memory_space=pltpu.VMEM)
    smem = pl.BlockSpec(memory_space=pltpu.SMEM)
    rows = HALF + 16
    return pl.pallas_call(
        coarse_body,
        in_specs=[smem, smem, vmem, vmem, vmem],
        out_specs=[vmem] * count,
        out_shape=[array(rows, width, bf16)] * count,
        scratch_shapes=[pltpu.VMEM((count, rows, width), bf16), pltpu.SemaphoreType.DMA((count,))],
        compiler_params=pltpu.CompilerParams(vmem_limit_bytes=16 << 20),
        cost_estimate=pl.CostEstimate(flops=DECLARED, bytes_accessed=8 * got.size, transcendentals=1 << 20),
        name="coarse_levels",
    )(place, bias, got, from_prev, from_next)


def side_body(side, with_near, with_far, scalars, ins, outs):
    q0_ref, q1_ref, sum_ref, top_ref, total_ref, side_ref = ins
    heads = q1_ref.shape[1] // HEAD_DIM
    bias = scalars[1][side]
    blocks = (side, 1 - side)
    fine = [pl.ds(pl.multiple_of(block * BLK, BLK), BLK) for block in blocks]
    middle = [pl.ds(pl.multiple_of(block * HALF, HALF), HALF) for block in blocks]
    if with_near:
        pair = pair_matrix()
        near_keys = (mul(pair, side_ref[0:BLK, :]) * 0.5).astype(bf16)
        near_values = mul(pair, side_ref[BLK : 2 * BLK, :]).astype(bf16)
    start = 2 * BLK if with_near else 0
    far_keys, far_values = (slice(start + n * HALF, start + (n + 1) * HALF) for n in range(2))
    units, names = [], []
    for head in range(heads):
        here = cols(head)
        far = (side_ref[far_keys, here], side_ref[far_values, here]) if with_far else None
        near = (near_keys[:, here], near_values[:, here]) if with_near else None
        whole = [part for part in (near, far) if part is not None]
        whole = [jnp.concatenate([part[n] for part in whole], axis=0) if len(whole) > 1 else whole[0][n] for n in range(2)]
        if with_near:
            units.append((q0_ref[fine[0], here], [(side_ref[0:BLK, here], side_ref[BLK : 2 * BLK, here], None)]))
            names.append((head, 0, 0))
        if with_far:
            units.append((q1_ref[middle[0], here], [(*far, None)]))
            names.append((head, 0, 1))
        units.append((q1_ref[middle[1], here], [(*whole, None)]))
        names.append((head, 1, 1))
    found = {name: (top + bias, sums) for name, (top, sums) in zip(names, attend(units))}
    for n in range(2):
        for head in range(heads):
            spot = (head // 2, fine[n], cols(head % 2))
            parts = [(top_ref[spot], sum_ref[spot], total_ref[spot])]
            if (head, n, 0) in found:
                top, sums = found[head, n, 0]
                parts.append((top, sums[:, :HEAD_DIM], sums[:, HEAD_DIM:]))
            if (head, n, 1) in found:
                top, sums = found[head, n, 1]
                parts.append((twice(top), twice(sums[:, :HEAD_DIM]), twice(2.0 * sums[:, HEAD_DIM:])))
            most = functools.reduce(jnp.maximum, [part[0] for part in parts])
            scales = [jnp.exp2(part[0] - most) for part in parts]
            outs[0][spot] = sum(part[1] * scale for part, scale in zip(parts, scales))
            outs[1][spot] = most
            outs[2][spot] = sum(part[2] * scale for part, scale in zip(parts, scales))


def chip_body(scalars, ins, outs):
    side_body(1 - scalars[0][0], True, True, scalars, ins, outs)


def near_body(scalars, ins, outs):
    side_body(scalars[0][0], True, False, scalars, ins, outs)


def far_body(scalars, ins, outs):
    side_body(scalars[0][0], False, True, scalars, [None] + ins, outs)


def side_level(body, name, place, bias, queries, running, rows):
    groups, count, part = running[0].shape
    ins = [("cols", query) for query in queries] + [("kept", one) for one in running] + [("got", rows)]
    return run_shares(body, name, groups // 2, [place, bias], ins, running_sums(count, groups * part, groups))


def finish_body(place_ref, sum_ref, top_ref, total_ref, *refs):
    groups = sum_ref.shape[0]
    back_refs, (out_ref, done_ref, sems) = refs[:groups], refs[groups:]
    part = sum_ref.shape[2]
    restore = restore_matrix()
    copies = []
    for n, back_ref in enumerate(back_refs):
        entry = n ^ place_ref[1]
        levels = []
        for head in range(part // HEAD_DIM):
            terms = back_ref[HALF : HALF + 16, cols(head)].astype(f32)
            terms = jnp.sum(jnp.where(iota(terms.shape, 0) < 3, terms, 0.0), axis=0, keepdims=True)
            levels.append(jnp.broadcast_to(terms, (HEAD_DIM, HEAD_DIM)).T)
        for i in range(2):
            rows = slice(i * BLK, (i + 1) * BLK)
            spot = slice(i * HALF // 2, (i + 1) * HALF // 2)
            results = []
            for head, level in enumerate(levels):
                here = (entry, rows, cols(head))
                top = top_ref[here]
                level = twice(twice(level[spot, :]))
                lead = top - level
                smaller = jnp.exp2(-jnp.abs(lead))
                scale = jnp.where(lead >= 0.0, 1.0, smaller)
                coarse = jnp.where(lead >= 0.0, smaller, 1.0)
                number = twice(twice(back_ref[spot, cols(head)].astype(f32))) * coarse
                number = number + sum_ref[here] * scale
                total = total_ref[here] * scale + coarse
                guess = pl.reciprocal(total, approx=True)
                results.append((number * (guess * (2.0 - total * guess))).astype(bf16))
            done_ref[n, rows, :] = mul(restore, jnp.concatenate(results, axis=1)).astype(bf16)
        columns = pl.ds(pl.multiple_of(entry * part, HEAD_DIM), part)
        copies.append(pltpu.make_async_copy(done_ref.at[n], out_ref.at[:, columns], sems.at[n]))
        copies[-1].start()
    for copy in copies:
        copy.wait()


def finish(place, running, back):
    groups, rows, part = running[0].shape
    vmem = pl.BlockSpec(memory_space=pltpu.VMEM)
    return pl.pallas_call(
        finish_body,
        in_specs=[pl.BlockSpec(memory_space=pltpu.SMEM)] + [vmem] * (3 + groups),
        out_specs=pl.BlockSpec(memory_space=pltpu.HBM),
        out_shape=pltpu.HBM((rows, groups * part), bf16),
        scratch_shapes=[pltpu.VMEM((groups, rows, part), bf16), pltpu.SemaphoreType.DMA((groups,))],
        compiler_params=pltpu.CompilerParams(vmem_limit_bytes=VMEM_GRANT),
        cost_estimate=pl.CostEstimate(flops=1 << 10, bytes_accessed=1 << 10, transcendentals=0),
        name="finish",
    )(place, *running, *back)


def shift(value, axis, steps):
    count = lax.axis_size(axis)
    first, last = (max(0, -steps), min(count, count - steps))
    return lax.ppermute(value, axis, [(source, source + steps) for source in range(first, last)])


def trade(value, axis, pairs):
    return lax.ppermute(value, axis, pairs + [(target, source) for source, target in pairs])


def edge_bias(axis):
    place = lax.axis_index(axis)
    last = lax.axis_size(axis) - 1
    at_edge = jnp.stack([place == 0, place == last])
    return jnp.where(at_edge, very_negative, 0.0).astype(f32)


def local(query_vecs, key_vecs, value_vecs):
    groups = lax.axis_size("grp")
    assert query_vecs.shape == (2 * BLK, HEADS * HEAD_DIM) and groups == 4
    everyone = ("seq", "grp")
    count = lax.axis_size(everyone)
    spot = lax.axis_index("grp")
    odd = jnp.bitwise_and(spot, 1)
    place = jnp.stack([odd, spot]).astype(jnp.int32)
    bias = edge_bias(everyone)

    def exchange(pieces, places):
        for n in places:
            flips = [(source, source ^ n) for source in range(groups)]
            pieces[n] = lax.ppermute(pieces[n], "grp", flips)
        return pieces

    off = range(2, groups)
    pieces = list(swap_rows(place, query_vecs, key_vecs, value_vecs, groups))
    query_rows, pieces = lax.optimization_barrier((query_vecs, pieces))
    pieces = exchange(pieces, off)
    key_rows, pieces[0] = lax.optimization_barrier((key_vecs, pieces[0]))
    near = near_rows(place, key_rows, value_vecs)
    query_rows, near = lax.optimization_barrier((query_rows, near))
    q0, q1, far, chip = rows_to_send(place, query_rows, key_vecs, value_vecs, groups)
    pieces[1], far = lax.optimization_barrier((pieces[1], far))
    pieces = exchange(pieces, [1])
    off_chip = [(device, device + 1) for device in range(1, count - 1, 2)]
    near = trade(near, everyone, off_chip)
    pieces, chip = lax.optimization_barrier((pieces, chip))
    got, coarse_right, coarse_left = coarse_halos(place, pieces)
    coarse_right, coarse_left, chip, q0, far = lax.optimization_barrier((coarse_right, coarse_left, chip, q0, far))
    coarse_prev = shift(coarse_right, "seq", 1)
    coarse_next = shift(coarse_left, "seq", -1)
    chip = trade(chip, everyone, [(device, device + 1) for device in range(0, count - 1, 2)])
    far = trade(far, everyone, off_chip)
    running = own_level(q0, key_vecs, value_vecs, groups)
    running = side_level(chip_body, "chip_level", place, bias, (q0, q1), running, chip)
    running = side_level(near_body, "near_level", place, bias, (q0, q1), running, near)
    got, running = lax.optimization_barrier((got, running))
    back = coarse_levels(place, edge_bias("seq"), got, coarse_prev, coarse_next)
    back, running = lax.optimization_barrier((back, running))
    back = exchange(list(back), [*off, 1])
    running = side_level(far_body, "far_level", place, bias, (q1,), running, far)
    return finish(place, running, back)


def solution(mesh):
    return jax.shard_map(
        local,
        mesh=mesh,
        in_specs=(P(("seq", "grp"), None), P(("seq", "grp"), None), P(("seq", "grp"), None)),
        out_specs=P(("seq", "grp"), None),
        check_vma=False,
    )
```
